32 devices in a mesh: edge: 16 (over z, y, core), col: 2 (over x).
Axes of the slice: x: 2, y: 2, z: 4, core: 2. Of those that a mesh axis runs over, the one named last changes fastest.
Arguments:
- head_ids: int32 [131072], P('edge'), may hold values from 0 to 126975, as said below
- relation_ids: int32 [131072], P('edge'), may hold values from 0 to 3199
- tail_ids: int32 [131072], P('edge'), may hold values from 0 to 126975, as said below
- negative_ids: int32 [128, 1024], P('edge'), may hold values from 0 to 126975, as said below
- live_counts: int32 [128], P('edge'), may hold values from 1 to 1024, as said below
- rel_weight: float32 [3200], replicated, may hold values from 0.5 to 2
- rel_count: int32 [3200], replicated, may hold values from 1 to 4
- entity_table: float32 [400, 126976], P('col', 'edge'), may hold values from -0.6 to 0.6
- entity_first: float32 [400, 126976], P('col', 'edge'), may hold values from -0.3 to 0.3
- entity_second: float32 [400, 126976], P('col', 'edge'), may hold values from 0.0025 to 0.01
- relation_table: float32 [3200, 400], P('edge', 'col'), may hold values from -0.6 to 0.6
- relation_first: float32 [3200, 400], P('edge', 'col'), may hold values from -1.2 to 1.2
- relation_second: float32 [3200, 400], P('edge', 'col'), may hold values from 0.04 to 0.16
Outputs:
- loss_pair: float32 [2], replicated
- new_entity: float32 [400, 126976], P('col', 'edge')
- new_entity_first: float32 [400, 126976], P('col', 'edge')
- new_entity_second: float32 [400, 126976], P('col', 'edge')
- new_relation: float32 [3200, 400], P('edge', 'col')
- new_relation_first: float32 [3200, 400], P('edge', 'col')
- new_relation_second: float32 [3200, 400], P('edge', 'col')
The draws below stay inside these ranges and needn't reach their ends.
Inputs may be any that keep to these rules, and one draw needn't show every extreme that they name: `head_ids`: entity ids. Of the ids that one index of edge names (its heads, tails and negative tails together), at most 2048 lie among the entities of any one index of edge, and exactly 2048 among those of one of them. `tail_ids`: as for head_ids. `negative_ids`: as for head_ids. `live_counts`: some block has all 1024 slots live.
All inputs are finite; a program needn't handle non-finite values.
Results may differ from the reference program's by a relative error of at most 0.005.
Values may be sent and summed in bfloat16 or wider, within the bound.
No kernel may reach another device: no remote copies, remote signals or barrier semaphores. Data moves between devices by JAX's collectives and lax.ppermute only.
A program may use at most 256 MiB of HBM per device.

```python
import math
import jax
import jax.numpy as jnp
import numpy as np
from jax import lax

D = 400
ENT_DEV = 7936
SPAN = 1024
NEG = 1024
CH_DEV = 8
STEP = 5
ENTS = 126976
RELS = 3200
SPANS = 128
EDGES = 131072
IDS_DEV = 24576
CAP = 2048
N_EDGE = 16


def owner_layout(key):
    key_list = jax.random.split(key, N_EDGE)

    def one_device(device_key):
        star_key, rest_key, order_key, local_key = jax.random.split(device_key, 4)
        star = jax.random.randint(star_key, (), 0, N_EDGE)
        labels = (jnp.arange(N_EDGE * CAP, dtype=jnp.int32) // CAP + star) % N_EDGE
        others = jax.random.permutation(rest_key, labels[CAP:])
        chosen = jnp.concatenate([labels[:CAP], others[:IDS_DEV - CAP]])
        chosen = jax.random.permutation(order_key, chosen)
        local_rows = jax.random.randint(local_key, (IDS_DEV,), 0, ENT_DEV)
        return chosen * ENT_DEV + local_rows
    return jax.vmap(one_device)(key_list)


def draw_head_ids(key, part):
    layout = owner_layout(key)
    return layout[:, :CH_DEV * SPAN].reshape(-1).astype(jnp.int32)


def draw_tail_ids(key, part):
    layout = owner_layout(key)
    return layout[:, CH_DEV * SPAN:2 * CH_DEV * SPAN].reshape(-1).astype(jnp.int32)


def draw_negative_ids(key, part):
    layout = owner_layout(key)
    return layout[:, 2 * CH_DEV * SPAN:].reshape(SPANS, NEG).astype(jnp.int32)


def draw_live_counts(key, part):
    key = jax.random.fold_in(key, 7)
    device = jnp.arange(SPANS, dtype=jnp.int32) // CH_DEV
    upper_end = SPAN // 3 + (SPAN - SPAN // 3) * device // max(N_EDGE - 1, 1)
    lower_end = jnp.maximum(1, upper_end * 4 // 5)
    counts = jax.random.randint(key, (SPANS,), lower_end, upper_end + 1)
    return counts.at[SPANS - 1].set(SPAN).astype(jnp.int32)


def with_ends(array, own_key, smallest, high):
    longest = array.shape.index(max(array.shape))
    spots = []
    for shift in (0, 1):
        where = [jax.random.randint(jax.random.fold_in(own_key, axis), (), 0, length) for axis, length in enumerate(array.shape)]
        where[longest] = (where[longest] + shift) % array.shape[longest]
        spots.append(tuple(where))
    return array.at[spots[0]].set(smallest).at[spots[1]].set(high)


def block_levels(key, shape, cuts, smallest, top_value):
    gain = 1.0
    for position, parts in cuts:
        draws = jax.random.uniform(jax.random.fold_in(jax.random.fold_in(key, 6), position), (parts,), jnp.float32, smallest / len(cuts), top_value / len(cuts))
        gain = gain * jnp.repeat(jnp.exp(draws), shape[position] // parts).reshape((-1,) + (1,) * (len(shape) - 1 - position))
    return gain


def cumulative_ranks(number_of, slope):
    portions = [(1 << 20) // math.isqrt(standing ** slope) + 1 for standing in range(1, number_of + 1)]
    width = 1 + sum(portions) // (1 << 30)
    return np.cumsum(np.array([max(1, weight // width) for weight in portions]))


def skewed_ids(own_key, shape, count, slope):
    table = cumulative_ranks(count, slope)
    lot = jax.random.randint(jax.random.fold_in(own_key, 1), shape, 0, int(table[count - 1]))
    rank = jnp.searchsorted(jnp.asarray(table, jnp.int32), lot, side="right")
    return jax.random.permutation(jax.random.fold_in(own_key, 2), count)[rank].astype(jnp.int32)


def centred(rng, dims, deviation, bound, cuts=(), kind=jnp.bfloat16):
    gain = block_levels(rng, dims, cuts, -0.22, 0.18) if cuts else 1.0
    entries = jax.random.normal(rng, dims, jnp.float32) * deviation * gain
    return jnp.minimum(jnp.maximum(entries, -bound), bound).astype(kind)


def setup_inputs(seed: int = 0) -> dict:
    streams_of = jax.random.split(jax.random.key(seed), 14)
    return {
        "head_ids": draw_head_ids(jax.random.fold_in(streams_of[13], 71), 0),
        "relation_ids": with_ends(skewed_ids(streams_of[1], (EDGES,), RELS, 2), jax.random.fold_in(streams_of[1], 3), 0, RELS - 1).astype(jnp.int32),
        "tail_ids": draw_tail_ids(jax.random.fold_in(streams_of[13], 71), 0),
        "negative_ids": draw_negative_ids(jax.random.fold_in(streams_of[13], 71), 0),
        "live_counts": draw_live_counts(jax.random.fold_in(streams_of[13], 71), 0),
        "rel_weight": jnp.clip(jnp.exp(jax.random.uniform(streams_of[5], (RELS,), jnp.float32, math.log(0.5), math.log(2.0))), 0.5, 2.0),
        "rel_count": with_ends(jax.random.randint(streams_of[6], (RELS,), 1, 5), jax.random.fold_in(streams_of[6], 1), 1, 4).astype(jnp.int32),
        "entity_table": centred(streams_of[7], (D, ENTS), 0.1, 0.6, ((0, 2), (1, 16)), jnp.float32),
        "entity_first": centred(streams_of[8], (D, ENTS), 0.05, 0.3, ((0, 2), (1, 16)), jnp.float32),
        "entity_second": jnp.clip(jnp.exp(math.log(0.01) - 1.3862944 * jax.random.uniform(streams_of[9], (D, ENTS), jnp.float32) ** block_levels(streams_of[9], (D, ENTS), ((0, 2), (1, 16)), -0.2, 0.2)), 0.0025, 0.01),
        "relation_table": centred(streams_of[10], (RELS, D), 0.1, 0.6, ((0, 16), (1, 2)), jnp.float32),
        "relation_first": centred(streams_of[11], (RELS, D), 0.2, 1.2, ((0, 16), (1, 2)), jnp.float32),
        "relation_second": jnp.clip(jnp.exp(math.log(0.16) - 1.3862944 * jax.random.uniform(streams_of[12], (RELS, D), jnp.float32) ** block_levels(streams_of[12], (RELS, D), ((0, 16), (1, 2)), -0.2, 0.2)), 0.04, 0.16),
    }


MARGIN = 0.1
LEARN_RATE = 0.1
BETA_ONE = 0.5
BETA_TWO = 0.5
EPSILON = 1e-08
DECAY = 0.01

@jax.custom_vjp
def low(v):
    return lax.optimization_barrier(v.astype(jnp.bfloat16)).astype(jnp.float32)

@jax.custom_vjp
def low_back(v):
    return v

def low_keep(v):
    return (low(v), None)

def low_pass(kept, grad):
    return (grad,)

def back_keep(v):
    return (v, None)

def back_low(kept, grad):
    return (low(grad),)
low.defvjp(low_keep, low_pass)
low_back.defvjp(back_keep, back_low)

def adamw_update(weights, gradient, first, second):
    new_first = BETA_ONE * first + (1.0 - BETA_ONE) * gradient
    new_second = BETA_TWO * second + (1.0 - BETA_TWO) * gradient * gradient
    first_hat = new_first / (1.0 - BETA_ONE ** STEP)
    second_hat = new_second / (1.0 - BETA_TWO ** STEP)
    updated = weights - LEARN_RATE * (first_hat / (jnp.sqrt(second_hat) + EPSILON) + DECAY * weights)
    return (updated, new_first, new_second)

def reference(head_ids, relation_ids, tail_ids, negative_ids, live_counts, rel_weight, rel_count, entity_table, entity_first, entity_second, relation_table, relation_first, relation_second):
    blocks = negative_ids.shape[0]
    rel_total = rel_weight.shape[0]
    rel_scale = rel_weight * (rel_total / jnp.sum(rel_weight)) / rel_count.astype(jnp.float32)
    live_mask = (jnp.arange(SPAN, dtype=jnp.int32)[None, :] < live_counts[:, None]).astype(jnp.float32)
    edge_weight = rel_scale[relation_ids].reshape(blocks, SPAN) * live_mask / NEG

    def block_loss(loss_sum, pieces):
        head_part, rel_part, tail_part, neg_part, weight_part = pieces
        shifted = head_part + rel_part
        positive = lax.optimization_barrier(jnp.sum((shifted - tail_part) ** 2, axis=-1))
        crossed = low_back(jnp.dot(low(shifted), neg_part.T, precision=lax.Precision.HIGHEST))
        negative = lax.optimization_barrier(jnp.sum(shifted * shifted, axis=-1))[:, None] - 2.0 * crossed + lax.optimization_barrier(jnp.sum(neg_part * neg_part, axis=-1))[None, :]
        margins = MARGIN + positive[:, None] - negative
        return (loss_sum + jnp.sum(weight_part[:, None] * jax.nn.softplus(margins)), None)

    def forward(entities, relations):
        head_rows = low(jnp.take(entities, head_ids, axis=1).T).reshape(blocks, SPAN, D)
        tail_rows = low(jnp.take(entities, tail_ids, axis=1).T).reshape(blocks, SPAN, D)
        neg_rows = low(jnp.take(entities, negative_ids.reshape(-1), axis=1).T).reshape(blocks, NEG, D)
        rel_rows = low(relations[relation_ids]).reshape(blocks, SPAN, D)
        loss_sum, unused = lax.scan(jax.checkpoint(block_loss), jnp.zeros((), jnp.float32), (head_rows, rel_rows, tail_rows, neg_rows, edge_weight))
        return loss_sum
    loss_sum, pullback = jax.vjp(forward, entity_table, relation_table)
    entity_grad, relation_grad = pullback(jnp.ones((), jnp.float32))
    loss_pair = jnp.stack([loss_sum, jnp.sum(live_mask)])
    new_entity, new_entity_first, new_entity_second = adamw_update(entity_table, entity_grad, entity_first, entity_second)
    new_relation, new_relation_first, new_relation_second = adamw_update(relation_table, relation_grad, relation_first, relation_second)
    return (loss_pair, new_entity, new_entity_first, new_entity_second, new_relation, new_relation_first, new_relation_second)
```

```python
import functools

import jax
import jax.numpy as jnp
from jax import lax
from jax.experimental import pallas as pl
from jax.experimental.pallas import tpu as pltpu
from jax.sharding import PartitionSpec as P

STEP = 5


MARGIN = 0.1
LEARN_RATE = 0.1
BETA_ONE = 0.5
BETA_TWO = 0.5
EPSILON = 1e-08
DECAY = 0.01
LANES = 128
UNROLL = 8
PARTS = 4
NN = (((1,), (0,)), ((), ()))
NT = (((1,), (1,)), ((), ()))
TN = (((0,), (0,)), ((), ()))
F32 = jnp.float32
BF16 = jnp.bfloat16
SMEM = pltpu.SMEM
VMEM = pltpu.VMEM


def params():
    return pltpu.CompilerParams(vmem_limit_bytes=60 << 20)


def cost(flops, moved):
    return pl.CostEstimate(flops=int(flops), bytes_accessed=int(moved), transcendentals=0)


def whole(space):
    return pl.BlockSpec(memory_space=space)


def adamw_update(weights, gradient, first, second):
    new_first = BETA_ONE * first + (1.0 - BETA_ONE) * gradient
    new_second = BETA_TWO * second + (1.0 - BETA_TWO) * gradient * gradient
    first_hat = new_first / (1.0 - BETA_ONE**STEP)
    second_hat = new_second / (1.0 - BETA_TWO**STEP)
    updated = weights - LEARN_RATE * (
        first_hat / (jnp.sqrt(second_hat) + EPSILON) + DECAY * weights
    )
    return (updated, new_first, new_second)


def width_slices(width):
    return [(at, min(LANES, width - at)) for at in range(0, width, LANES)]


def owner_lists(all_ids, groups, capacity, ent_rows):
    count = all_ids.shape[0]
    owners = all_ids // ent_rows
    local_rows = all_ids - owners * ent_rows
    chunk = 256
    mine = owners[None, :] == jnp.arange(groups, dtype=jnp.int32)[:, None]
    mine = mine.astype(BF16).reshape(groups, count // chunk, chunk)
    before = jnp.triu(jnp.ones((chunk, chunk), BF16), 1)
    inner = jnp.dot(mine, before, preferred_element_type=F32)
    sums = jnp.sum(mine.astype(F32), axis=2)
    carry = jnp.cumsum(sums, axis=1) - sums
    ranks = jnp.sum(mine.astype(F32) * (inner + carry[:, :, None]), axis=0)
    ranks = ranks.astype(jnp.int32).reshape(count)
    counts = jnp.sum(sums, axis=1).astype(jnp.int32)
    high = owners * (capacity // LANES) + ranks // LANES
    low = ranks % LANES
    tall = groups * capacity // LANES
    left = (jnp.arange(tall, dtype=jnp.int32)[:, None] == high[None, :]).astype(BF16)
    right = (jnp.arange(LANES, dtype=jnp.int32)[:, None] == low[None, :]).astype(BF16)
    places = jnp.arange(1, count + 1, dtype=jnp.int32)
    parts = jnp.stack([places // 256, places % 256, local_rows // 256, local_rows % 256])
    right = (parts.astype(BF16)[:, None, :] * right[None]).reshape(PARTS * LANES, count)
    found = lax.dot_general(left, right, NT, preferred_element_type=F32).astype(jnp.int32)
    found = found.reshape(tall, PARTS, LANES)
    place = found[:, 0] * 256 + found[:, 1]
    place_list = jnp.where(place > 0, place - 1, count).reshape(groups, capacity)
    row_list = jnp.where(place > 0, found[:, 2] * 256 + found[:, 3], ent_rows)
    return place_list, row_list.reshape(groups, capacity), counts


def relation_rows_kernel(n_slices, ids_ref, *refs):
    tables, outs = refs[:n_slices], refs[n_slices:]
    count = outs[0].shape[0]

    def body(step, carry):
        for lane in range(UNROLL):
            at = step * UNROLL + lane
            row = ids_ref[at]
            for table, out in zip(tables, outs):
                out[pl.ds(at, 1), :] = table[pl.ds(row, 1), :]
        return carry

    lax.fori_loop(0, count // UNROLL, body, 0)


def relation_rows(relation_ids, tables):
    count = relation_ids.shape[0]
    n = len(tables)
    return pl.pallas_call(
        functools.partial(relation_rows_kernel, n),
        out_shape=[jax.ShapeDtypeStruct((count, LANES), F32)] * n,
        in_specs=[whole(SMEM)] + [whole(VMEM)] * n,
        out_specs=[whole(VMEM)] * n,
        compiler_params=params(),
        cost_estimate=cost(0, 30e6 * n),
        name="relation_rows",
    )(relation_ids, *tables)


def fetch_kernel(capacity, counts_ref, place_ref, row_ref, dense_ref, out_ref, rows):
    shard = pl.program_id(0)
    depth, ent_rows = dense_ref.shape[1:]
    step_cols = 256 if ent_rows % 256 == 0 else 128

    if depth < LANES:

        @pl.when(shard == 0)
        def _():
            rows[...] = jnp.zeros_like(rows)

    def turn(step, carry):
        cols = pl.ds(pl.multiple_of(step * step_cols, step_cols), step_cols)
        rows[cols, :depth] = dense_ref[0, :, cols].astype(F32).T
        return carry

    lax.fori_loop(0, ent_rows // step_cols, turn, 0)
    trips = (counts_ref[shard] + UNROLL - 1) // UNROLL

    def body(step, carry):
        for lane in range(UNROLL):
            at = shard * capacity + step * UNROLL + lane
            out_ref[pl.ds(place_ref[at], 1), :] = rows[pl.ds(row_ref[at], 1), :]
        return carry

    lax.fori_loop(0, trips, body, 0)


def fetch(counts, place_list, row_list, dense):
    groups, depth, ent_rows = dense.shape
    capacity = place_list.shape[1]
    id_count = 3 * groups * capacity // 4
    return pl.pallas_call(
        functools.partial(fetch_kernel, capacity),
        out_shape=jax.ShapeDtypeStruct((id_count + 8, LANES), F32),
        grid=(groups,),
        in_specs=[whole(SMEM)] * 3
        + [pl.BlockSpec((1, depth, ent_rows), lambda shard: (shard, 0, 0))],
        out_specs=whole(VMEM),
        scratch_shapes=[pltpu.VMEM((ent_rows + 8, LANES), F32)],
        compiler_params=params(),
        cost_estimate=cost(0, 250e6),
        name="fetch_rows",
    )(counts, place_list.reshape(-1), row_list.reshape(-1), dense)


def prepare_kernel(depth, head_ref, tail_ref, neg_ref, rel_ref, off_ref, tail_out, pair_ref, sums_ref):
    lane = lax.broadcasted_iota(jnp.int32, head_ref.shape, 1)
    inside = lane < depth
    rel = rel_ref[...]
    tail = tail_ref[...]
    shifted = head_ref[...] + jnp.where(inside, rel, 0.0)
    off_ref[...] = jnp.where(inside, shifted - tail, rel)
    tail_out[...] = tail.astype(BF16)
    shifted_t = shifted.T
    offset_t = (shifted - tail).T
    neg_t = neg_ref[...].T
    pair_ref[0] = shifted_t[:depth].astype(BF16)
    pair_ref[1] = neg_t[:depth].astype(BF16)
    sums_ref[0:1, :] = jnp.sum(offset_t * offset_t, axis=0, keepdims=True) - jnp.sum(
        shifted_t * shifted_t, axis=0, keepdims=True
    )
    sums_ref[1:2, :] = jnp.sum(neg_t * neg_t, axis=0, keepdims=True)


def prepare(fetched, rel_rows, depth, blocks, block_len):
    edge_count = blocks * block_len

    def rows(at):
        return pl.BlockSpec((block_len, LANES), lambda b: (at * blocks + b, 0))

    return pl.pallas_call(
        functools.partial(prepare_kernel, depth),
        out_shape=[
            jax.ShapeDtypeStruct((edge_count, LANES), F32),
            jax.ShapeDtypeStruct((edge_count, LANES), BF16),
            jax.ShapeDtypeStruct((2, depth, edge_count), BF16),
            jax.ShapeDtypeStruct((2, edge_count), F32),
        ],
        grid=(blocks,),
        in_specs=[rows(0), rows(1), rows(2), rows(0)],
        out_specs=[
            rows(0),
            rows(0),
            pl.BlockSpec((2, depth, block_len), lambda b: (0, 0, b)),
            pl.BlockSpec((2, block_len), lambda b: (0, b)),
        ],
        compiler_params=params(),
        cost_estimate=cost(0, 40e6),
        name="prepare",
    )(fetched, fetched, fetched, rel_rows)


def block_kernel(slices, n_col, live_ref, *refs):
    n = len(slices)
    pairs = [refs[k * n : (k + 1) * n] for k in range(n_col)]
    at = n * n_col
    sums_ref = refs[at]
    offs = refs[at + 1 : at + 1 + n]
    tails = refs[at + 1 + n : at + 1 + 2 * n]
    grads = refs[at + 1 + 2 * n : at + 1 + 3 * n]
    loss_ref = refs[at + 1 + 3 * n]
    shift_scr, neg_scr, cross, slopes, row_bias, row_sum = refs[at + 2 + 3 * n :]
    block = pl.program_id(0)
    length = cross.shape[0]
    width = sum(depth for _, depth in slices)
    for k in range(n_col):
        for (start, depth), pair in zip(slices, pairs[k]):
            shift_scr[k, start : start + depth, :] = pair[0]
            neg_scr[k, start : start + depth, :] = pair[1]
    bias = jnp.sum(sums_ref[:, 0, :], axis=0, keepdims=True) + MARGIN
    neg_norm = jnp.sum(sums_ref[:, 1, :], axis=0, keepdims=True)
    row_bias[...] = jnp.broadcast_to(bias, (LANES, length)).T

    tile = min(256, length)

    def matmul(step, carry):
        part = pl.ds(pl.multiple_of(step * tile, tile), tile)
        total = None
        for k in range(n_col):
            term = lax.dot_general(
                shift_scr[k, :, part], neg_scr[k], TN, preferred_element_type=F32
            )
            total = term if total is None else total + term
        cross[part, :] = total
        return carry

    lax.fori_loop(0, length // tile, matmul, 0)

    live = live_ref[block]
    small = 64

    def pairwise(step, carry):
        loss, cols = carry
        begin = pl.multiple_of(step * small, small)
        part = pl.ds(begin, small)
        place = begin + lax.broadcasted_iota(jnp.int32, (small, 1), 0)
        scale = offs[-1][part, LANES - 1 : LANES]
        weight = jnp.where(place < live, scale, 0.0) / length
        margins = 2.0 * cross[part, :] + (row_bias[part, 0:1] - neg_norm)
        fall = jnp.exp(-jnp.abs(margins))
        under = 1.0 + fall
        inverse = 1.0 / under
        logs = jnp.where(fall < 2.0**-11, fall * (1.0 - 0.5 * fall), jnp.log(under))
        soft = jnp.maximum(margins, 0.0) + logs
        slope = weight * jnp.where(margins >= 0.0, inverse, fall * inverse)
        row_sum[part, :] = jnp.broadcast_to(
            jnp.sum(slope, axis=1, keepdims=True), (small, LANES)
        )
        slopes[part, :] = (2.0 * slope).astype(BF16)
        loss = loss + jnp.sum((weight * soft).reshape(small // 8, 8, length), axis=0)
        cols = cols + jnp.sum(slope.reshape(small // 8, 8, length), axis=0)
        return loss, cols

    zero = jnp.zeros((8, length), F32)
    loss, cols = lax.fori_loop(0, length // small, pairwise, (zero, zero))
    col_sum = jnp.sum(cols, axis=0, keepdims=True)
    loss_part = jnp.sum(loss.reshape(8, length // LANES, LANES), axis=1)

    @pl.when(block == 0)
    def _():
        loss_ref[...] = loss_part

    @pl.when(block > 0)
    def _():
        loss_ref[...] += loss_part

    def edges(step, carry):
        part = pl.ds(pl.multiple_of(step * tile, tile), tile)
        moved = lax.dot_general(slopes[part, :], neg_scr[0], NT, preferred_element_type=F32)
        twice = -2.0 * row_sum[part, :]
        for (start, depth), off, tail, grad in zip(slices, offs, tails, grads):
            grad[0, part, :depth] = (
                twice[:, :depth] * tail[part, :depth].astype(F32) + moved[:, start : start + depth]
            )
            grad[1, part, :] = twice * off[part, :]
        return carry

    lax.fori_loop(0, length // tile, edges, 0)

    moved = lax.dot_general(shift_scr[0], slopes[...], NN, preferred_element_type=F32)
    moved = moved - 2.0 * col_sum * neg_scr[0].astype(F32)
    for (start, depth), grad in zip(slices, grads):
        grad[2, :, :depth] = moved[start : start + depth, :].T


def block_math(live_counts, pairs, sums, offs, tails, slices, block_len):
    n, n_col = len(slices), len(pairs)
    blocks = live_counts.shape[0]
    edge_count = blocks * block_len
    width = sum(depth for _, depth in slices)
    flat = [piece for per_col in pairs for piece in per_col]

    def rows():
        return pl.BlockSpec((block_len, LANES), lambda b: (b, 0))

    return pl.pallas_call(
        functools.partial(block_kernel, slices, n_col),
        out_shape=[jax.ShapeDtypeStruct((3, edge_count, LANES), F32)] * n
        + [jax.ShapeDtypeStruct((8, LANES), F32)],
        grid=(blocks,),
        in_specs=[whole(SMEM)]
        + [
            pl.BlockSpec((2, piece.shape[1], block_len), lambda b: (0, 0, b)) for piece in flat
        ]
        + [pl.BlockSpec((sums.shape[0], 2, block_len), lambda b: (0, 0, b))]
        + [rows() for _ in range(2 * n)],
        out_specs=[pl.BlockSpec((3, block_len, LANES), lambda b: (0, b, 0))] * n
        + [pl.BlockSpec((8, LANES), lambda b: (0, 0))],
        scratch_shapes=[
            pltpu.VMEM((n_col, width, block_len), BF16),
            pltpu.VMEM((n_col, width, block_len), BF16),
            pltpu.VMEM((block_len, block_len), F32),
            pltpu.VMEM((block_len, block_len), BF16),
            pltpu.VMEM((block_len, LANES), F32),
            pltpu.VMEM((block_len, LANES), F32),
        ],
        compiler_params=params(),
        cost_estimate=cost(blocks * 8 * block_len * block_len * width, 200e6),
        name="block_math",
    )(live_counts, *flat, sums, *offs, *tails)


def outgoing_kernel(slices, capacity, begin, counts_ref, place_ref, *refs):
    n = len(slices)
    grads, out_ref, tiles = refs[:n], refs[n], refs[n + 1 :]
    groups, width, chunk = out_ref.shape

    def owner(group, carry):
        wanted = jnp.clip(counts_ref[group] - begin, 0, chunk)

        def body(step, inner):
            for lane in range(UNROLL):
                at = step * UNROLL + lane
                place = place_ref[group * capacity + begin + at]
                for grad, tile in zip(grads, tiles):
                    tile[pl.ds(at, 1), :] = grad[pl.ds(place, 1), :]
            return inner

        lax.fori_loop(0, (wanted + UNROLL - 1) // UNROLL, body, 0)
        for (start, depth), tile in zip(slices, tiles):
            out_ref[group, start : start + depth, :] = tile[...].T[:depth].astype(BF16)
        return carry

    lax.fori_loop(0, groups, owner, 0)


def outgoing(counts, place_list, grads, slices, begin, chunk):
    groups, capacity = place_list.shape
    n = len(slices)
    width = sum(depth for _, depth in slices)
    return pl.pallas_call(
        functools.partial(outgoing_kernel, slices, capacity, begin),
        out_shape=jax.ShapeDtypeStruct((groups, width, chunk), BF16),
        in_specs=[whole(SMEM)] * 2 + [whole(VMEM)] * n,
        out_specs=whole(VMEM),
        scratch_shapes=[pltpu.VMEM((chunk, LANES), F32)] * n,
        compiler_params=params(),
        cost_estimate=cost(0, 80e6),
        name="outgoing",
    )(counts, place_list.reshape(-1), *grads)


def collect_kernel(slices, capacity, begin, first, counts_ref, row_ref, came_ref, *refs):
    n = len(slices)
    olds = () if first else refs[:n]
    refs = refs if first else refs[n:]
    totals, tiles = refs[:n], refs[n:]
    groups, width, chunk = came_ref.shape
    for k in range(n):
        totals[k][...] = jnp.zeros_like(totals[k]) if first else olds[k][...]

    def source(group, carry):
        wanted = jnp.clip(counts_ref[group] - begin, 0, chunk)

        @pl.when(wanted > 0)
        def _():
            for (start, depth), tile in zip(slices, tiles):
                tile[:, :depth] = came_ref[group, start : start + depth, :].astype(F32).T

            def body(step, inner):
                for lane in range(UNROLL):
                    at = step * UNROLL + lane
                    row = row_ref[group * capacity + begin + at]
                    for total, tile in zip(totals, tiles):
                        total[pl.ds(row, 1), :] = total[pl.ds(row, 1), :] + tile[pl.ds(at, 1), :]
                return inner

            lax.fori_loop(0, (wanted + UNROLL - 1) // UNROLL, body, 0)

        return carry

    lax.fori_loop(0, groups, source, 0)


def collect(counts, row_list, came, totals, slices, begin, ent_rows):
    capacity = row_list.shape[1]
    chunk = came.shape[2]
    n = len(slices)
    first = totals is None
    given = () if first else tuple(totals)
    return pl.pallas_call(
        functools.partial(collect_kernel, slices, capacity, begin, first),
        out_shape=[jax.ShapeDtypeStruct((ent_rows + 8, LANES), F32)] * n,
        in_specs=[whole(SMEM)] * 2 + [whole(VMEM)] * (1 + len(given)),
        out_specs=[whole(VMEM)] * n,
        scratch_shapes=[pltpu.VMEM((chunk, LANES), F32)] * n,
        compiler_params=params(),
        cost_estimate=cost(0, 120e6),
        name="collect",
    )(counts, row_list.reshape(-1), came, *given)


def relation_sums_kernel(n, ids_ref, *refs):
    grads, totals = refs[:n], refs[n:]
    count = grads[0].shape[1]
    for total in totals:
        total[...] = jnp.zeros_like(total)

    def body(step, carry):
        for lane in range(UNROLL):
            at = step * UNROLL + lane
            row = ids_ref[at]
            for grad, total in zip(grads, totals):
                total[pl.ds(row, 1), :] = total[pl.ds(row, 1), :] + grad[0, pl.ds(at, 1), :]
        return carry

    lax.fori_loop(0, count // UNROLL, body, 0)


def relation_sums(relation_ids, grads, rel_total):
    n = len(grads)
    count = relation_ids.shape[0]
    return pl.pallas_call(
        functools.partial(relation_sums_kernel, n),
        out_shape=[jax.ShapeDtypeStruct((rel_total, LANES), F32)] * n,
        grid=(1,),
        in_specs=[whole(SMEM)]
        + [pl.BlockSpec((1, count, LANES), lambda i: (0, 0, 0))] * n,
        out_specs=[whole(VMEM)] * n,
        compiler_params=params(),
        cost_estimate=cost(0, 120e6),
        name="relation_sums",
    )(relation_ids, *grads)


def update_kernel(slices, weights_ref, first_ref, second_ref, *refs):
    n = len(slices)
    totals, outs, scr = refs[:n], refs[n : n + 3], refs[n + 3]
    for (start, depth), total in zip(slices, totals):
        scr[start : start + depth, :] = total[...].T[:depth]
    results = adamw_update(weights_ref[...], scr[...], first_ref[...], second_ref[...])
    for out, result in zip(outs, results):
        out[...] = result


def update_entities(weights, totals, first, second, slices):
    width, ent_rows = weights.shape
    cols = 256 if ent_rows % 256 == 0 else 128
    n = len(slices)
    table = pl.BlockSpec((width, cols), lambda i: (0, i))
    return pl.pallas_call(
        functools.partial(update_kernel, slices),
        out_shape=[jax.ShapeDtypeStruct((width, ent_rows), F32)] * 3,
        grid=(ent_rows // cols,),
        in_specs=[table] * 3 + [pl.BlockSpec((cols, LANES), lambda i: (i, 0))] * n,
        out_specs=[table] * 3,
        scratch_shapes=[pltpu.VMEM((width, cols), F32)],
        compiler_params=params(),
        cost_estimate=cost(0, 60e6),
        name="update_entities",
    )(weights, first, second, *totals)


def shards(
    head_ids,
    relation_ids,
    tail_ids,
    negative_ids,
    live_counts,
    rel_weight,
    rel_count,
    entity_table,
    entity_first,
    entity_second,
    relation_table,
    relation_first,
    relation_second,
):
    groups = lax.axis_size("edge")
    n_col = lax.axis_size("col")
    width, ent_rows = entity_table.shape
    blocks, neg_count = negative_ids.shape
    block_len = head_ids.shape[0] // blocks
    edge_count = blocks * block_len
    slices = width_slices(width)
    n = len(slices)
    all_ids = jnp.concatenate([head_ids, tail_ids, negative_ids.reshape(-1)])
    id_count = all_ids.shape[0]
    capacity = (4 * id_count + 3 * groups - 1) // (3 * groups)
    rel_total = rel_weight.shape[0]

    table_low = entity_table.astype(BF16)
    rel_table = lax.all_gather(relation_table.astype(BF16), "edge", axis=0, tiled=True)
    dense = [
        lax.all_gather(table_low[start : start + depth], "edge", axis=0, tiled=False)
        for start, depth in slices
    ]

    place_list, row_list, counts = owner_lists(all_ids, groups, capacity, ent_rows)
    asked = lax.all_to_all(row_list, "edge", split_axis=0, concat_axis=0, tiled=True)
    asked_counts = jnp.sum((asked < ent_rows).astype(jnp.int32), axis=1)
    safe_places = jnp.minimum(place_list, id_count - 1)

    rel_scale = rel_weight * (rel_total / jnp.sum(rel_weight)) / rel_count.astype(F32)
    rel_slices = []
    for k, (start, depth) in enumerate(slices):
        piece = rel_table[:, start : start + depth].astype(F32)
        if k < n - 1:
            rel_slices.append(piece)
        else:
            gap = jnp.zeros((rel_total, LANES - 1 - depth), F32)
            rel_slices.append(jnp.concatenate([piece, gap, rel_scale[:, None]], axis=1))
    rel_rows = relation_rows(relation_ids, rel_slices)

    offs, tails, own, others, sums = [], [], [], [[] for _ in range(n_col - 1)], []
    for k, (start, depth) in enumerate(slices):
        fetched = fetch(counts, place_list, row_list, dense[k])
        off, tail, pair, part = prepare(fetched, rel_rows[k], depth, blocks, block_len)
        offs.append(off)
        tails.append(tail)
        own.append(pair)
        sums.append(part)
        for away in range(1, n_col):
            turn = [(c, (c + away) % n_col) for c in range(n_col)]
            others[away - 1].append(lax.ppermute(pair, "col", turn))
            sums.append(lax.ppermute(part, "col", turn))
    sums = jnp.stack(sums)

    *grads, loss_tile = block_math(
        live_counts, [own] + others, sums, offs, tails, slices, block_len
    )
    live = jnp.sum(jnp.minimum(live_counts, block_len)).astype(F32)
    whole_pair = lax.psum(jnp.stack([jnp.sum(loss_tile), live]), ("edge", "col"))
    loss_pair = whole_pair / n_col

    flat = [grad.reshape(id_count, LANES) for grad in grads]
    chunks = 4
    chunk = capacity // chunks
    arrived = []
    for k in range(chunks):
        sent = outgoing(counts, safe_places, flat, slices, k * chunk, chunk)
        arrived.append(lax.all_to_all(sent, "edge", split_axis=0, concat_axis=0, tiled=True))
    totals = None
    for k in range(chunks):
        totals = collect(asked_counts, asked, arrived[k], totals, slices, k * chunk, ent_rows)

    rel_terms = relation_sums(relation_ids, grads, rel_total)
    rel_terms = jnp.concatenate(
        [term[:, :depth] for (start, depth), term in zip(slices, rel_terms)], axis=1
    )
    relation_grad = lax.psum_scatter(rel_terms, "edge", scatter_dimension=0, tiled=True)
    new_entity, new_entity_first, new_entity_second = update_entities(
        entity_table, totals, entity_first, entity_second, slices
    )
    new_relation, new_relation_first, new_relation_second = adamw_update(
        relation_table, relation_grad, relation_first, relation_second
    )
    return (
        loss_pair,
        new_entity,
        new_entity_first,
        new_entity_second,
        new_relation,
        new_relation_first,
        new_relation_second,
    )


def solution(mesh):
    placed = (
        P("edge"),
        P("edge"),
        P("edge"),
        P("edge", None),
        P("edge"),
        P(),
        P(),
        P("col", "edge"),
        P("col", "edge"),
        P("col", "edge"),
        P("edge", "col"),
        P("edge", "col"),
        P("edge", "col"),
    )
    return jax.shard_map(
        shards,
        mesh=mesh,
        in_specs=placed,
        out_specs=(
            P(),
            P("col", "edge"),
            P("col", "edge"),
            P("col", "edge"),
            P("edge", "col"),
            P("edge", "col"),
            P("edge", "col"),
        ),
        check_vma=False,
    )
```

```python
import functools

import jax
import jax.numpy as jnp
from jax import lax
from jax.experimental import pallas as pl
from jax.experimental.pallas import tpu as pltpu
from jax.sharding import PartitionSpec as P

STEP = 5


MARGIN = 0.1
LEARN_RATE = 0.1
BETA_ONE = 0.5
BETA_TWO = 0.5
EPSILON = 1e-08
DECAY = 0.01
LANES = 128
UNROLL = 8
PARTS = 4
PIECES = 4
HALVES = 2
CHUNKS = 4
REL_PAD = 256
NN = (((1,), (0,)), ((), ()))
NT = (((1,), (1,)), ((), ()))
TN = (((0,), (0,)), ((), ()))
F32 = jnp.float32
BF16 = jnp.bfloat16
SMEM = pltpu.SMEM
VMEM = pltpu.VMEM


def params():
    return pltpu.CompilerParams(vmem_limit_bytes=60 << 20)


def cost(flops, moved):
    return pl.CostEstimate(flops=int(flops), bytes_accessed=int(moved), transcendentals=0)


def whole(space):
    return pl.BlockSpec(memory_space=space)


def adamw_update(weights, gradient, first, second):
    new_first = BETA_ONE * first + (1.0 - BETA_ONE) * gradient
    new_second = BETA_TWO * second + (1.0 - BETA_TWO) * gradient * gradient
    first_hat = new_first / (1.0 - BETA_ONE**STEP)
    second_hat = new_second / (1.0 - BETA_TWO**STEP)
    updated = weights - LEARN_RATE * (
        first_hat / (jnp.sqrt(second_hat) + EPSILON) + DECAY * weights
    )
    return (updated, new_first, new_second)


def width_slices(width):
    return [(at, min(LANES, width - at)) for at in range(0, width, LANES)]


def piece_bounds(ent_rows):
    tiles = ent_rows // LANES
    cuts = [LANES * ((tiles * k + PIECES - 1) // PIECES) for k in range(PIECES)]
    return cuts + [ent_rows]


def owner_lists(all_ids, groups, capacity, ent_rows):
    count = all_ids.shape[0]
    owners = all_ids // ent_rows
    local_rows = all_ids - owners * ent_rows
    chunk = 256
    pieces = sum((local_rows >= cut).astype(jnp.int32) for cut in piece_bounds(ent_rows)[1:-1])
    buckets = owners * PIECES + pieces
    mine = buckets[None, :] == jnp.arange(groups * PIECES, dtype=jnp.int32)[:, None]
    mine = mine.astype(BF16).reshape(groups * PIECES, count // chunk, chunk)
    before = jnp.triu(jnp.ones((chunk, chunk), BF16), 1)
    inner = jnp.dot(mine, before, preferred_element_type=F32)
    sums = jnp.sum(mine.astype(F32), axis=2)
    in_bucket = jnp.sum(sums, axis=1).reshape(groups, PIECES)
    ends = jnp.cumsum(in_bucket, axis=1)
    carry = jnp.cumsum(sums, axis=1) - sums + (ends - in_bucket).reshape(-1, 1)
    ranks = jnp.sum(mine.astype(F32) * (inner + carry[:, :, None]), axis=0)
    ranks = ranks.astype(jnp.int32).reshape(count)
    starts = jnp.concatenate([jnp.zeros((groups, 1), F32), ends], axis=1).astype(jnp.int32)
    high = owners * (capacity // LANES) + ranks // LANES
    low = ranks % LANES
    tall = groups * capacity // LANES
    left = (jnp.arange(tall, dtype=jnp.int32)[:, None] == high[None, :]).astype(BF16)
    right = (jnp.arange(LANES, dtype=jnp.int32)[:, None] == low[None, :]).astype(BF16)
    places = jnp.arange(1, count + 1, dtype=jnp.int32)
    parts = jnp.stack([places // 256, places % 256, local_rows // 256, local_rows % 256])
    right = (parts.astype(BF16)[:, None, :] * right[None]).reshape(PARTS * LANES, count)
    found = lax.dot_general(left, right, NT, preferred_element_type=F32).astype(jnp.int32)
    found = found.reshape(tall, PARTS, LANES)
    place = found[:, 0] * 256 + found[:, 1]
    place_list = jnp.where(place > 0, place - 1, count).reshape(groups, capacity)
    row_list = jnp.where(place > 0, found[:, 2] * 256 + found[:, 3], ent_rows)
    return place_list, row_list.reshape(groups, capacity), starts


def relation_rows_kernel(ids_ref, table_ref, scale_ref, out_ref, columns, rows):
    groups, depth, span = table_ref.shape
    columns[...] = jnp.zeros_like(columns)

    def turn(group, carry):
        columns[:depth, :] = table_ref[group].astype(F32)
        if depth < LANES:
            columns[LANES - 1 :, :] = scale_ref[pl.ds(group, 1), :]
        rows[pl.ds(pl.multiple_of(group * span, span), span), :] = columns[...].T
        return carry

    lax.fori_loop(0, groups, turn, 0)

    def body(step, carry):
        for lane in range(UNROLL):
            at = step * UNROLL + lane
            out_ref[pl.ds(at, 1), :] = rows[pl.ds(ids_ref[at], 1), :]
        return carry

    lax.fori_loop(0, out_ref.shape[0] // UNROLL, body, 0)


def relation_rows(places, dense, scale):
    count = places.shape[0]
    groups, depth, span = dense.shape
    return pl.pallas_call(
        relation_rows_kernel,
        out_shape=jax.ShapeDtypeStruct((count, LANES), F32),
        grid=(1,),
        in_specs=[
            whole(SMEM),
            pl.BlockSpec((groups, depth, REL_PAD), lambda i: (0, 0, span // REL_PAD - 1)),
            whole(VMEM),
        ],
        out_specs=whole(VMEM),
        scratch_shapes=[
            pltpu.VMEM((LANES, REL_PAD), F32),
            pltpu.VMEM((groups * REL_PAD, LANES), F32),
        ],
        compiler_params=params(),
        cost_estimate=cost(0, 30e6),
        name="relation_rows",
    )(places, dense, scale)


def fetch_kernel(capacity, piece, begin, end, starts_ref, place_ref, row_ref, dense_ref, *refs):
    (old_ref,) = refs[:1] if piece > 0 else (None,)
    out_ref, rows, kept, sem = refs[-4:]
    shard = pl.program_id(0)
    depth = dense_ref.shape[1]
    step_cols = 256 if begin % 256 == 0 and end % 256 == 0 else 128

    if piece > 0:

        @pl.when(shard == 0)
        def _():
            pltpu.make_async_copy(old_ref, kept, sem).start()

    if depth < LANES:

        @pl.when(shard == 0)
        def _():
            rows[...] = jnp.zeros_like(rows)

    def turn(step, carry):
        cols = pl.ds(pl.multiple_of(step * step_cols, step_cols), step_cols)
        into = pl.ds(pl.multiple_of(begin + step * step_cols, step_cols), step_cols)
        rows[into, :depth] = dense_ref[0, :, cols].astype(F32).T
        return carry

    lax.fori_loop(0, (end - begin) // step_cols, turn, 0, unroll=True)

    if piece > 0:

        @pl.when(shard == 0)
        def _():
            pltpu.make_async_copy(old_ref, kept, sem).wait()

    first = starts_ref[shard * (PIECES + 1) + piece] + shard * capacity
    wanted = starts_ref[shard * (PIECES + 1) + piece + 1] + shard * capacity - first

    def move(at):
        kept[pl.ds(place_ref[at], 1), :] = rows[pl.ds(row_ref[at], 1), :]

    def body(step, carry):
        for lane in range(UNROLL):
            move(first + step * UNROLL + lane)
        return carry

    def last(step, carry):
        move(first + step)
        return carry

    trips = wanted // UNROLL
    lax.fori_loop(0, trips, body, 0)
    lax.fori_loop(trips * UNROLL, wanted, last, 0)

    @pl.when(shard == pl.num_programs(0) - 1)
    def _():
        copy = pltpu.make_async_copy(kept, out_ref, sem)
        copy.start()
        copy.wait()


def fetch(starts, place_list, row_list, dense, old, piece, begin, end, ent_rows, id_count):
    groups, depth, _ = dense.shape
    capacity = place_list.shape[0] // groups
    given = [] if old is None else [old]
    return pl.pallas_call(
        functools.partial(fetch_kernel, capacity, piece, begin, end),
        out_shape=jax.ShapeDtypeStruct((id_count, LANES), F32),
        grid=(groups,),
        in_specs=[whole(SMEM)] * 3
        + [pl.BlockSpec((1, depth, end - begin), lambda shard: (shard, 0, 0))]
        + [whole(pl.ANY)] * len(given),
        out_specs=whole(pl.ANY),
        input_output_aliases={4: 0} if given else {},
        scratch_shapes=[
            pltpu.VMEM((ent_rows, LANES), F32),
            pltpu.VMEM((id_count, LANES), F32),
            pltpu.SemaphoreType.DMA,
        ],
        compiler_params=params(),
        cost_estimate=cost(0, 100e6),
        name="fetch_rows",
    )(starts, place_list, row_list, dense, *given)


def prepare_kernel(depth, head_ref, tail_ref, neg_ref, rel_ref, off_ref, tail_out, pair_ref, sums_ref):
    lane = lax.broadcasted_iota(jnp.int32, head_ref.shape, 1)
    inside = lane < depth
    rel = rel_ref[...]
    tail = tail_ref[...]
    shifted = head_ref[...] + jnp.where(inside, rel, 0.0)
    off_ref[...] = jnp.where(inside, shifted - tail, rel)
    tail_out[...] = tail.astype(BF16)
    shifted_t = shifted.T
    offset_t = (shifted - tail).T
    neg_t = neg_ref[...].T
    pair_ref[0] = shifted_t[:depth].astype(BF16)
    pair_ref[1] = neg_t[:depth].astype(BF16)
    sums_ref[0:1, :] = jnp.sum(offset_t * offset_t, axis=0, keepdims=True) - jnp.sum(
        shifted_t * shifted_t, axis=0, keepdims=True
    )
    sums_ref[1:2, :] = jnp.sum(neg_t * neg_t, axis=0, keepdims=True)


def prepare(fetched, rel_rows, depth, blocks, block_len, half):
    part = blocks // HALVES
    edge_count = part * block_len

    def rows(at):
        return pl.BlockSpec((block_len, LANES), lambda b: (at * blocks + half * part + b, 0))

    def outs(*shape):
        return pl.BlockSpec(shape + (block_len,), lambda b: (0,) * len(shape) + (b,))

    return pl.pallas_call(
        functools.partial(prepare_kernel, depth),
        out_shape=[
            jax.ShapeDtypeStruct((edge_count, LANES), F32),
            jax.ShapeDtypeStruct((edge_count, LANES), BF16),
            jax.ShapeDtypeStruct((2, depth, edge_count), BF16),
            jax.ShapeDtypeStruct((2, edge_count), F32),
        ],
        grid=(part,),
        in_specs=[rows(0), rows(1), rows(2), rows(0)],
        out_specs=[
            pl.BlockSpec((block_len, LANES), lambda b: (b, 0)),
            pl.BlockSpec((block_len, LANES), lambda b: (b, 0)),
            outs(2, depth),
            outs(2),
        ],
        compiler_params=params(),
        cost_estimate=cost(0, 20e6),
        name="prepare",
    )(fetched, fetched, fetched, rel_rows)


def block_kernel(slices, n_col, half, me_ref, live_ref, *refs):
    n = len(slices)
    pairs = [refs[k * n : (k + 1) * n] for k in range(n_col)]
    refs = refs[n_col * n :]
    sums_refs, refs = refs[:n_col], refs[n_col:]
    offs, tails, refs = refs[:n], refs[n : 2 * n], refs[2 * n :]
    if half > 0:
        refs = refs[n:]
    grads, refs = refs[:n], refs[n:]
    loss_ref, shift_scr, neg_scr, sums_scr, cross, slopes, row_bias, row_sum = refs
    block = pl.program_id(0)
    length = cross.shape[0]
    me = me_ref[0]
    for k in range(n_col):
        slot = lax.rem(me + (n_col - k), n_col)
        for (start, depth), pair in zip(slices, pairs[k]):
            shift_scr[slot, start : start + depth, :] = pair[0]
            neg_scr[slot, start : start + depth, :] = pair[1]
        sums_scr[slot] = sums_refs[k][...]
    bias = jnp.sum(sums_scr[:, 0, :], axis=0, keepdims=True) + MARGIN
    neg_norm = jnp.sum(sums_scr[:, 1, :], axis=0, keepdims=True)
    row_bias[...] = jnp.broadcast_to(bias, (LANES, length)).T

    tile = min(256, length)

    def matmul(step, carry):
        part = pl.ds(pl.multiple_of(step * tile, tile), tile)
        total = None
        for k in range(n_col):
            term = lax.dot_general(
                shift_scr[k, :, part], neg_scr[k], TN, preferred_element_type=F32
            )
            total = term if total is None else total + term
        cross[part, :] = total
        return carry

    lax.fori_loop(0, length // tile, matmul, 0)

    live = live_ref[half * pl.num_programs(0) + block]
    small = 64

    def pairwise(step, carry):
        loss, cols = carry
        begin = pl.multiple_of(step * small, small)
        part = pl.ds(begin, small)
        place = begin + lax.broadcasted_iota(jnp.int32, (small, 1), 0)
        scale = offs[-1][part, LANES - 1 : LANES]
        weight = jnp.where(place < live, scale, 0.0) / length
        margins = 2.0 * cross[part, :] + (row_bias[part, 0:1] - neg_norm)
        fall = jnp.exp(-jnp.abs(margins))
        under = 1.0 + fall
        inverse = 1.0 / under
        logs = jnp.where(fall < 2.0**-11, fall * (1.0 - 0.5 * fall), jnp.log(under))
        soft = jnp.maximum(margins, 0.0) + logs
        slope = weight * jnp.where(margins >= 0.0, inverse, fall * inverse)
        row_sum[part, :] = jnp.broadcast_to(
            jnp.sum(slope, axis=1, keepdims=True), (small, LANES)
        )
        slopes[part, :] = (2.0 * slope).astype(BF16)
        loss = loss + jnp.sum((weight * soft).reshape(small // 8, 8, length), axis=0)
        cols = cols + jnp.sum(slope.reshape(small // 8, 8, length), axis=0)
        return loss, cols

    zero = jnp.zeros((8, length), F32)
    loss, cols = lax.fori_loop(0, length // small, pairwise, (zero, zero))
    col_sum = jnp.sum(cols, axis=0, keepdims=True)
    loss_part = jnp.sum(loss.reshape(8, length // LANES, LANES), axis=1)

    @pl.when(block == 0)
    def _():
        loss_ref[...] = loss_part

    @pl.when(block > 0)
    def _():
        loss_ref[...] += loss_part

    def edges(step, carry):
        part = pl.ds(pl.multiple_of(step * tile, tile), tile)
        moved = lax.dot_general(slopes[part, :], neg_scr[me], NT, preferred_element_type=F32)
        twice = -2.0 * row_sum[part, :]
        for (start, depth), off, tail, grad in zip(slices, offs, tails, grads):
            grad[0, part, :depth] = (
                twice[:, :depth] * tail[part, :depth].astype(F32) + moved[:, start : start + depth]
            )
            grad[1, part, :] = twice * off[part, :]
        return carry

    lax.fori_loop(0, length // tile, edges, 0)

    moved = lax.dot_general(shift_scr[me], slopes[...], NN, preferred_element_type=F32)
    moved = moved - 2.0 * col_sum * neg_scr[me].astype(F32)
    for (start, depth), grad in zip(slices, grads):
        grad[2, :, :depth] = moved[start : start + depth, :].T


def block_math(me, live_counts, pairs, sums, offs, tails, old, slices, block_len, half):
    n, n_col = len(slices), len(pairs)
    blocks = live_counts.shape[0]
    part = blocks // HALVES
    width = sum(depth for _, depth in slices)
    flat = [piece for per_col in pairs for piece in per_col]
    given = [] if old is None else old

    def rows():
        return pl.BlockSpec((block_len, LANES), lambda b: (b, 0))

    first_old = 2 + len(flat) + n_col + 2 * n
    return pl.pallas_call(
        functools.partial(block_kernel, slices, n_col, half),
        out_shape=[jax.ShapeDtypeStruct((3, blocks * block_len, LANES), F32)] * n
        + [jax.ShapeDtypeStruct((8, LANES), F32)],
        grid=(part,),
        in_specs=[whole(SMEM)] * 2
        + [
            pl.BlockSpec((2, piece.shape[1], block_len), lambda b: (0, 0, b)) for piece in flat
        ]
        + [pl.BlockSpec((2, block_len), lambda b: (0, b))] * n_col
        + [rows() for _ in range(2 * n)]
        + [whole(pl.ANY)] * len(given),
        out_specs=[
            pl.BlockSpec((3, block_len, LANES), lambda b: (0, half * part + b, 0))
        ]
        * n
        + [pl.BlockSpec((8, LANES), lambda b: (0, 0))],
        input_output_aliases={first_old + k: k for k in range(len(given))},
        scratch_shapes=[
            pltpu.VMEM((n_col, width, block_len), BF16),
            pltpu.VMEM((n_col, width, block_len), BF16),
            pltpu.VMEM((n_col, 2, block_len), F32),
            pltpu.VMEM((block_len, block_len), F32),
            pltpu.VMEM((block_len, block_len), BF16),
            pltpu.VMEM((block_len, LANES), F32),
            pltpu.VMEM((block_len, LANES), F32),
        ],
        compiler_params=params(),
        cost_estimate=cost(part * 8 * block_len * block_len * width, 120e6),
        name="block_math",
    )(me, live_counts, *flat, *sums, *offs, *tails, *given)


def outgoing_kernel(slices, capacity, begin, counts_ref, place_ref, *refs):
    n = len(slices)
    grads, out_ref, tiles = refs[:n], refs[-n - 1], refs[-n:]
    groups, width, chunk = out_ref.shape

    def owner(group, carry):
        wanted = jnp.clip(counts_ref[group] - begin, 0, chunk)

        def body(step, inner):
            for lane in range(UNROLL):
                at = step * UNROLL + lane
                place = place_ref[group * capacity + begin + at]
                for grad, tile in zip(grads, tiles):
                    tile[pl.ds(at, 1), :] = grad[pl.ds(place, 1), :]
            return inner

        lax.fori_loop(0, (wanted + UNROLL - 1) // UNROLL, body, 0)
        for (start, depth), tile in zip(slices, tiles):
            out_ref[group, start : start + depth, :] = tile[...].T[:depth].astype(BF16)
        return carry

    lax.fori_loop(0, groups, owner, 0)


def outgoing(counts, place_list, grads, slices, begin, chunk, after):
    groups, capacity = place_list.shape
    n = len(slices)
    width = sum(depth for _, depth in slices)
    return pl.pallas_call(
        functools.partial(outgoing_kernel, slices, capacity, begin),
        out_shape=jax.ShapeDtypeStruct((groups, width, chunk), BF16),
        in_specs=[whole(SMEM)] * 2 + [whole(VMEM)] * n + [whole(pl.ANY)] * len(after),
        out_specs=whole(VMEM),
        scratch_shapes=[pltpu.VMEM((chunk, LANES), F32)] * n,
        compiler_params=params(),
        cost_estimate=cost(0, 80e6),
        name="outgoing",
    )(counts, place_list.reshape(-1), *grads, *after)


def collect_kernel(slices, capacity, begin, first, counts_ref, row_ref, came_ref, *refs):
    n = len(slices)
    olds = () if first else refs[:n]
    refs = refs if first else refs[n:]
    totals, tiles = refs[:n], refs[n:]
    groups, width, chunk = came_ref.shape
    for k in range(n):
        totals[k][...] = jnp.zeros_like(totals[k]) if first else olds[k][...]

    def source(group, carry):
        wanted = jnp.clip(counts_ref[group] - begin, 0, chunk)

        @pl.when(wanted > 0)
        def _():
            for (start, depth), tile in zip(slices, tiles):
                tile[:, :depth] = came_ref[group, start : start + depth, :].astype(F32).T

            def body(step, inner):
                for lane in range(UNROLL):
                    at = step * UNROLL + lane
                    row = row_ref[group * capacity + begin + at]
                    for total, tile in zip(totals, tiles):
                        total[pl.ds(row, 1), :] = total[pl.ds(row, 1), :] + tile[pl.ds(at, 1), :]
                return inner

            lax.fori_loop(0, (wanted + UNROLL - 1) // UNROLL, body, 0)

        return carry

    lax.fori_loop(0, groups, source, 0)


def collect(counts, row_list, came, totals, slices, begin, ent_rows):
    capacity = row_list.shape[1]
    chunk = came.shape[2]
    n = len(slices)
    first = totals is None
    given = () if first else tuple(totals)
    return pl.pallas_call(
        functools.partial(collect_kernel, slices, capacity, begin, first),
        out_shape=[jax.ShapeDtypeStruct((ent_rows + 8, LANES), F32)] * n,
        in_specs=[whole(SMEM)] * 2 + [whole(VMEM)] * (1 + len(given)),
        out_specs=[whole(VMEM)] * n,
        scratch_shapes=[pltpu.VMEM((chunk, LANES), F32)] * n,
        compiler_params=params(),
        cost_estimate=cost(0, 120e6),
        name="collect",
    )(counts, row_list.reshape(-1), came, *given)


def relation_sums_kernel(n, ids_ref, *refs):
    grads, totals = refs[:n], refs[n:]
    count = grads[0].shape[1]
    for total in totals:
        total[...] = jnp.zeros_like(total)

    def body(step, carry):
        for lane in range(UNROLL):
            at = step * UNROLL + lane
            row = ids_ref[at]
            for grad, total in zip(grads, totals):
                total[pl.ds(row, 1), :] = total[pl.ds(row, 1), :] + grad[0, pl.ds(at, 1), :]
        return carry

    lax.fori_loop(0, count // UNROLL, body, 0)


def relation_sums(relation_ids, grads, rel_total):
    n = len(grads)
    count = relation_ids.shape[0]
    return pl.pallas_call(
        functools.partial(relation_sums_kernel, n),
        out_shape=[jax.ShapeDtypeStruct((rel_total, LANES), F32)] * n,
        grid=(1,),
        in_specs=[whole(SMEM)]
        + [pl.BlockSpec((1, count, LANES), lambda i: (0, 0, 0))] * n,
        out_specs=[whole(VMEM)] * n,
        compiler_params=params(),
        cost_estimate=cost(0, 120e6),
        name="relation_sums",
    )(relation_ids, *grads)


def update_kernel(slices, weights_ref, first_ref, second_ref, *refs):
    n = len(slices)
    totals, outs, scr = refs[:n], refs[n : n + 3], refs[n + 3]
    for (start, depth), total in zip(slices, totals):
        scr[start : start + depth, :] = total[...].T[:depth]
    results = adamw_update(weights_ref[...], scr[...], first_ref[...], second_ref[...])
    for out, result in zip(outs, results):
        out[...] = result


def update_entities(weights, totals, first, second, slices):
    width, ent_rows = weights.shape
    cols = 1024
    n = len(slices)
    table = pl.BlockSpec((width, cols), lambda i: (0, i))
    return pl.pallas_call(
        functools.partial(update_kernel, slices),
        out_shape=[jax.ShapeDtypeStruct((width, ent_rows), F32)] * 3,
        grid=(pl.cdiv(ent_rows, cols),),
        in_specs=[table] * 3 + [pl.BlockSpec((cols, LANES), lambda i: (i, 0))] * n,
        out_specs=[table] * 3,
        scratch_shapes=[pltpu.VMEM((width, cols), F32)],
        compiler_params=params(),
        cost_estimate=cost(0, 60e6),
        name="update_entities",
    )(weights, first, second, *totals)


def shards(
    head_ids,
    relation_ids,
    tail_ids,
    negative_ids,
    live_counts,
    rel_weight,
    rel_count,
    entity_table,
    entity_first,
    entity_second,
    relation_table,
    relation_first,
    relation_second,
):
    groups = lax.axis_size("edge")
    n_col = lax.axis_size("col")
    width, ent_rows = entity_table.shape
    blocks, neg_count = negative_ids.shape
    block_len = head_ids.shape[0] // blocks
    edge_count = blocks * block_len
    slices = width_slices(width)
    n = len(slices)
    all_ids = jnp.concatenate([head_ids, tail_ids, negative_ids.reshape(-1)])
    id_count = all_ids.shape[0]
    capacity = (4 * id_count + 3 * groups - 1) // (3 * groups)
    rel_total = rel_weight.shape[0]

    table_low = entity_table.astype(BF16)
    rel_own = rel_total // groups
    rel_low = jnp.pad(relation_table.astype(BF16).T, ((0, 0), (0, REL_PAD - rel_own)))
    bounds = piece_bounds(ent_rows)
    dense = []
    for start, depth in slices:
        for piece in range(PIECES):
            sent = table_low[start : start + depth, bounds[piece] : bounds[piece + 1]]
            if piece == 0:
                sent = jnp.concatenate([sent, rel_low[start : start + depth]], axis=1)
            dense.append(lax.all_gather(sent, "edge", axis=0, tiled=False))

    place_list, row_list, starts = owner_lists(all_ids, groups, capacity, ent_rows)
    counts = starts[:, PIECES]
    asked = lax.all_to_all(row_list, "edge", split_axis=0, concat_axis=0, tiled=True)
    asked_counts = jnp.sum((asked < ent_rows).astype(jnp.int32), axis=1)
    safe_places = jnp.minimum(place_list, id_count - 1)
    starts, place_flat, row_flat = starts.reshape(-1), place_list.reshape(-1), row_list.reshape(-1)

    rel_scale = rel_weight * (rel_total / jnp.sum(rel_weight)) / rel_count.astype(F32)
    rel_scale = jnp.pad(rel_scale.reshape(groups, rel_own), ((0, 0), (0, REL_PAD - rel_own)))
    rel_places = relation_ids + (relation_ids // rel_own) * (REL_PAD - rel_own)

    me = lax.axis_index("col").astype(jnp.int32).reshape(1)
    offs = [[] for _ in range(HALVES)]
    tails = [[] for _ in range(HALVES)]
    pairs = [[[] for _ in range(n_col)] for _ in range(HALVES)]
    parts = [[] for _ in range(HALVES)]
    for k, (start, depth) in enumerate(slices):
        rel_rows = relation_rows(rel_places, dense[k * PIECES], rel_scale)
        fetched = None
        for piece in range(PIECES):
            fetched = fetch(
                starts,
                place_flat,
                row_flat,
                dense[k * PIECES + piece],
                fetched,
                piece,
                bounds[piece],
                bounds[piece + 1],
                ent_rows,
                id_count,
            )
        for half in range(HALVES):
            off, tail, pair, part = prepare(fetched, rel_rows, depth, blocks, block_len, half)
            offs[half].append(off)
            tails[half].append(tail)
            parts[half].append(part)
            pairs[half][0].append(pair)
            for away in range(1, n_col):
                turn = [(c, (c + away) % n_col) for c in range(n_col)]
                pairs[half][away].append(lax.ppermute(pair, "col", turn))

    grads, loss_tiles = None, []
    for half in range(HALVES):
        part = functools.reduce(jnp.add, parts[half])
        sums = [part]
        for away in range(1, n_col):
            turn = [(c, (c + away) % n_col) for c in range(n_col)]
            sums.append(lax.ppermute(part, "col", turn))
        *grads, loss_tile = block_math(
            me, live_counts, pairs[half], sums, offs[half], tails[half], grads, slices, block_len, half
        )
        loss_tiles.append(loss_tile)
    live = jnp.sum(jnp.minimum(live_counts, block_len)).astype(F32)
    loss_own = jnp.sum(functools.reduce(jnp.add, loss_tiles))
    loss_row = jnp.zeros((8, LANES), F32).at[0, 0].set(loss_own).at[0, 1].set(live)
    loss_all = lax.all_gather(loss_row, "edge", axis=0, tiled=False)
    loss_pair = jnp.sum(loss_all[:, 0, :2], axis=0)

    rel_terms = relation_sums(relation_ids, grads, rel_total)
    flat = [grad.reshape(id_count, LANES) for grad in grads]
    chunk = capacity // CHUNKS
    arrived, totals, after = [], None, rel_terms[:1]
    for k in range(CHUNKS):
        sent = outgoing(
            counts, safe_places, flat, slices, k * chunk, chunk, after if k > 0 else []
        )
        arrived.append(lax.all_to_all(sent, "edge", split_axis=0, concat_axis=0, tiled=True))
        if k > 0:
            totals = collect(
                asked_counts, asked, arrived[k - 1], totals, slices, (k - 1) * chunk, ent_rows
            )
            after = totals[:1]
    k = CHUNKS - 1
    totals = collect(asked_counts, asked, arrived[k], totals, slices, k * chunk, ent_rows)

    rel_terms = jnp.concatenate(
        [term[:, :depth] for (start, depth), term in zip(slices, rel_terms)], axis=1
    )
    relation_grad = lax.psum_scatter(rel_terms, "edge", scatter_dimension=0, tiled=True)
    new_entity, new_entity_first, new_entity_second = update_entities(
        entity_table, totals, entity_first, entity_second, slices
    )
    new_relation, new_relation_first, new_relation_second = adamw_update(
        relation_table, relation_grad, relation_first, relation_second
    )
    return (
        loss_pair,
        new_entity,
        new_entity_first,
        new_entity_second,
        new_relation,
        new_relation_first,
        new_relation_second,
    )


def solution(mesh):
    placed = (
        P("edge"),
        P("edge"),
        P("edge"),
        P("edge", None),
        P("edge"),
        P(),
        P(),
        P("col", "edge"),
        P("col", "edge"),
        P("col", "edge"),
        P("edge", "col"),
        P("edge", "col"),
        P("edge", "col"),
    )
    return jax.shard_map(
        shards,
        mesh=mesh,
        in_specs=placed,
        out_specs=(
            P(),
            P("col", "edge"),
            P("col", "edge"),
            P("col", "edge"),
            P("edge", "col"),
            P("edge", "col"),
            P("edge", "col"),
        ),
        check_vma=False,
    )
```

```python
import functools

import jax
import jax.numpy as jnp
from jax import lax
from jax.experimental import pallas as pl
from jax.experimental.pallas import tpu as pltpu
from jax.sharding import PartitionSpec as P

STEP = 5


MARGIN = 0.1
LEARN_RATE = 0.1
BETA_ONE = 0.5
BETA_TWO = 0.5
EPSILON = 1e-08
DECAY = 0.01
LANES = 128
UNROLL = 8
PARTS = 4
HALVES = 2
TURN = 512
NN = (((1,), (0,)), ((), ()))
NT = (((1,), (1,)), ((), ()))
TN = (((0,), (0,)), ((), ()))
F32 = jnp.float32
BF16 = jnp.bfloat16
SMEM = pltpu.SMEM
VMEM = pltpu.VMEM


def params():
    return pltpu.CompilerParams(vmem_limit_bytes=60 << 20)


def cost(flops, moved):
    return pl.CostEstimate(flops=int(flops), bytes_accessed=int(moved), transcendentals=0)


def whole(space):
    return pl.BlockSpec(memory_space=space)


def adamw_update(weights, gradient, first, second):
    new_first = BETA_ONE * first + (1.0 - BETA_ONE) * gradient
    new_second = BETA_TWO * second + (1.0 - BETA_TWO) * gradient * gradient
    first_hat = new_first / (1.0 - BETA_ONE**STEP)
    second_hat = new_second / (1.0 - BETA_TWO**STEP)
    updated = weights - LEARN_RATE * (
        first_hat / (jnp.sqrt(second_hat) + EPSILON) + DECAY * weights
    )
    return (updated, new_first, new_second)


def width_slices(width):
    return [(at, min(LANES, width - at)) for at in range(0, width, LANES)]


def owner_lists(all_ids, groups, capacity, ent_rows):
    count = all_ids.shape[0]
    owners = all_ids // ent_rows
    local_rows = all_ids - owners * ent_rows
    chunk = 256
    mine = owners[None, :] == jnp.arange(groups, dtype=jnp.int32)[:, None]
    mine = mine.astype(BF16).reshape(groups, count // chunk, chunk)
    before = jnp.triu(jnp.ones((chunk, chunk), BF16), 1)
    inner = jnp.dot(mine, before, preferred_element_type=F32)
    sums = jnp.sum(mine.astype(F32), axis=2)
    carry = jnp.cumsum(sums, axis=1) - sums
    ranks = jnp.sum(mine.astype(F32) * (inner + carry[:, :, None]), axis=0)
    ranks = ranks.astype(jnp.int32).reshape(count)
    counts = jnp.sum(sums, axis=1).astype(jnp.int32)
    high = owners * (capacity // LANES) + ranks // LANES
    low = ranks % LANES
    tall = groups * capacity // LANES
    left = (jnp.arange(tall, dtype=jnp.int32)[:, None] == high[None, :]).astype(BF16)
    right = (jnp.arange(LANES, dtype=jnp.int32)[:, None] == low[None, :]).astype(BF16)
    places = jnp.arange(1, count + 1, dtype=jnp.int32)
    parts = jnp.stack([places // 256, places % 256, local_rows // 256, local_rows % 256])
    right = (parts.astype(BF16)[:, None, :] * right[None]).reshape(PARTS * LANES, count)
    found = lax.dot_general(left, right, NT, preferred_element_type=F32).astype(jnp.int32)
    found = found.reshape(tall, PARTS, LANES)
    place = found[:, 0] * 256 + found[:, 1]
    place_list = jnp.where(place > 0, place - 1, count).reshape(groups, capacity)
    row_list = jnp.where(place > 0, found[:, 2] * 256 + found[:, 3], ent_rows)
    return place_list, row_list.reshape(groups, capacity), counts


def relation_rows_kernel(n_slices, ids_ref, *refs):
    tables, outs = refs[:n_slices], refs[n_slices:]
    count = outs[0].shape[0]

    def body(step, carry):
        for lane in range(UNROLL):
            at = step * UNROLL + lane
            row = ids_ref[at]
            for table, out in zip(tables, outs):
                out[pl.ds(at, 1), :] = table[pl.ds(row, 1), :]
        return carry

    lax.fori_loop(0, count // UNROLL, body, 0)


def relation_rows(relation_ids, tables):
    count = relation_ids.shape[0]
    n = len(tables)
    return pl.pallas_call(
        functools.partial(relation_rows_kernel, n),
        out_shape=[jax.ShapeDtypeStruct((count, LANES), F32)] * n,
        in_specs=[whole(SMEM)] + [whole(VMEM)] * n,
        out_specs=[whole(VMEM)] * n,
        compiler_params=params(),
        cost_estimate=cost(0, 30e6 * n),
        name="relation_rows",
    )(relation_ids, *tables)


def fetch_kernel(capacity, moves, counts_ref, place_ref, row_ref, dense_ref, out_ref, *rows):
    shard = pl.program_id(0)
    last = pl.num_programs(0) - 1
    depth, ent_rows = dense_ref.shape[1:]
    turns = ent_rows // TURN
    rest = ent_rows - turns * TURN

    if depth < LANES:

        @pl.when(shard == 0)
        def _():
            for ref in rows:
                ref[...] = jnp.zeros_like(ref)

    def turn(into, begin, size):
        cols = pl.ds(begin, size)
        into[cols, :depth] = dense_ref[0, :, cols].astype(F32).T

    def move(source, at):
        out_ref[pl.ds(place_ref[at], 1), :] = source[pl.ds(row_ref[at], 1), :]

    def step(into, source):
        base = (shard - 1) * capacity

        def remaining(first):
            def body(trip, carry):
                for lane in range(UNROLL):
                    move(source, base + first + trip * UNROLL + lane)
                return carry

            wanted = counts_ref[jnp.maximum(shard - 1, 0)] - first
            lax.fori_loop(0, (wanted + UNROLL - 1) // UNROLL, body, 0)

        def only_turn(trip, carry):
            turn(into, pl.multiple_of(trip * TURN, TURN), TURN)
            return carry

        def both(trip, carry):
            turn(into, pl.multiple_of(trip * TURN, TURN), TURN)
            for lane in range(moves):
                move(source, base + trip * moves + lane)
            return carry

        @pl.when(shard == 0)
        def _():
            lax.fori_loop(0, turns, only_turn, 0)

        @pl.when((shard > 0) & (shard < last))
        def _():
            lax.fori_loop(0, turns, both, 0)
            remaining(turns * moves)

        @pl.when(shard == last)
        def _():
            remaining(0)

        if rest:

            @pl.when(shard < last)
            def _():
                turn(into, turns * TURN, rest)

    for parity in range(2):

        @pl.when(lax.rem(shard, 2) == parity)
        def _():
            step(rows[parity], rows[1 - parity])


def fetch(counts, place_list, row_list, dense, id_count):
    groups, depth, ent_rows = dense.shape
    capacity = place_list.shape[0] // groups
    moves = (id_count // groups) // (ent_rows // TURN) // UNROLL * UNROLL
    return pl.pallas_call(
        functools.partial(fetch_kernel, capacity, moves),
        out_shape=jax.ShapeDtypeStruct((id_count + 8, LANES), F32),
        grid=(groups + 1,),
        in_specs=[whole(SMEM)] * 3
        + [
            pl.BlockSpec(
                (1, depth, ent_rows), lambda shard: (jnp.minimum(shard, groups - 1), 0, 0)
            )
        ],
        out_specs=whole(VMEM),
        scratch_shapes=[pltpu.VMEM((ent_rows + 8, LANES), F32)] * 2,
        compiler_params=params(),
        cost_estimate=cost(0, 170e6),
        name="fetch_rows",
    )(counts, place_list, row_list, dense)


def prepare_kernel(depth, head_ref, tail_ref, neg_ref, rel_ref, off_ref, tail_out, pair_ref, sums_ref):
    lane = lax.broadcasted_iota(jnp.int32, head_ref.shape, 1)
    inside = lane < depth
    rel = rel_ref[...]
    tail = tail_ref[...]
    shifted = head_ref[...] + jnp.where(inside, rel, 0.0)
    off_ref[...] = jnp.where(inside, shifted - tail, rel)
    tail_out[...] = tail.astype(BF16)
    shifted_t = shifted.T
    offset_t = (shifted - tail).T
    neg_t = neg_ref[...].T
    pair_ref[0] = shifted_t[:depth].astype(BF16)
    pair_ref[1] = neg_t[:depth].astype(BF16)
    sums_ref[0:1, :] = jnp.sum(offset_t * offset_t, axis=0, keepdims=True) - jnp.sum(
        shifted_t * shifted_t, axis=0, keepdims=True
    )
    sums_ref[1:2, :] = jnp.sum(neg_t * neg_t, axis=0, keepdims=True)


def prepare(fetched, rel_rows, depth, blocks, block_len, half):
    part = blocks // HALVES
    edge_count = part * block_len

    def rows(at):
        return pl.BlockSpec((block_len, LANES), lambda b: (at * blocks + half * part + b, 0))

    def outs(*shape):
        return pl.BlockSpec(shape + (block_len,), lambda b: (0,) * len(shape) + (b,))

    return pl.pallas_call(
        functools.partial(prepare_kernel, depth),
        out_shape=[
            jax.ShapeDtypeStruct((edge_count, LANES), F32),
            jax.ShapeDtypeStruct((edge_count, LANES), BF16),
            jax.ShapeDtypeStruct((2, depth, edge_count), BF16),
            jax.ShapeDtypeStruct((2, edge_count), F32),
        ],
        grid=(part,),
        in_specs=[rows(0), rows(1), rows(2), rows(0)],
        out_specs=[
            pl.BlockSpec((block_len, LANES), lambda b: (b, 0)),
            pl.BlockSpec((block_len, LANES), lambda b: (b, 0)),
            outs(2, depth),
            outs(2),
        ],
        compiler_params=params(),
        cost_estimate=cost(0, 20e6),
        name="prepare",
    )(fetched, fetched, fetched, rel_rows)


def block_kernel(slices, n_col, half, me_ref, live_ref, *refs):
    n = len(slices)
    pairs = [refs[k * n : (k + 1) * n] for k in range(n_col)]
    refs = refs[n_col * n :]
    sums_refs, refs = refs[:n_col], refs[n_col:]
    offs, tails, refs = refs[:n], refs[n : 2 * n], refs[2 * n :]
    if half > 0:
        refs = refs[n:]
    grads, refs = refs[:n], refs[n:]
    loss_ref, shift_scr, neg_scr, sums_scr, cross, slopes, row_bias, row_sum = refs
    block = pl.program_id(0)
    length = cross.shape[0]
    me = me_ref[0]
    for k in range(n_col):
        slot = lax.rem(me + (n_col - k), n_col)
        for (start, depth), pair in zip(slices, pairs[k]):
            shift_scr[slot, start : start + depth, :] = 2.0 * pair[0]
            neg_scr[slot, start : start + depth, :] = pair[1]
        sums_scr[slot] = sums_refs[k][...]
    bias = jnp.sum(sums_scr[:, 0, :], axis=0, keepdims=True) + MARGIN
    neg_norm = jnp.sum(sums_scr[:, 1, :], axis=0, keepdims=True)
    row_bias[...] = jnp.broadcast_to(bias, (LANES, length)).T

    live = live_ref[half * pl.num_programs(0) + block]
    tile = 256
    small = 128
    lane_tiles = [slice(at, at + LANES) for at in range(0, length, LANES)]
    cols = jnp.zeros((8, length), F32)
    loss = jnp.zeros((8, LANES), F32)
    def products(at):
        part = slice(at, at + tile)
        doubled = None
        for k in range(n_col):
            term = lax.dot_general(
                shift_scr[k, :, part], neg_scr[k], TN, preferred_element_type=F32
            )
            doubled = term if doubled is None else doubled + term
        cross[part, :] = doubled

    def moves(at):
        part = slice(at, at + tile)
        moved = lax.dot_general(slopes[part, :], neg_scr[me], NT, preferred_element_type=F32)
        fade = -row_sum[part, :]
        for (start, depth), off, tail, grad in zip(slices, offs, tails, grads):
            grad[0, part, :depth] = (
                fade[:, :depth] * tail[part, :depth].astype(F32) + moved[:, start : start + depth]
            )
            grad[1, part, :] = fade * off[part, :]

    products(0)
    for begin in range(0, length, tile):
        if begin + tile < length:
            products(begin + tile)
        for at in range(begin, begin + tile, small):
            part = slice(at, at + small)
            place = at + lax.broadcasted_iota(jnp.int32, (small, 1), 0)
            scale = offs[-1][part, LANES - 1 : LANES]
            weight = jnp.where(place < live, scale, 0.0) / length
            margins = cross[part, :] + (row_bias[part, 0:1] - neg_norm)
            fall = jnp.exp(-jnp.abs(margins))
            under = 1.0 + fall
            guess = pl.reciprocal(under, approx=True)
            inverse = guess * (2.0 - under * guess)
            twice = (2.0 * weight) * (jnp.where(margins >= 0.0, 1.0, fall) * inverse)
            row_sum[part, :] = jnp.broadcast_to(
                jnp.sum(twice, axis=1, keepdims=True), (small, LANES)
            )
            slopes[part, :] = twice.astype(BF16)
            cols = cols + jnp.sum(twice.reshape(small // 8, 8, length), axis=0)
            over = jnp.maximum(margins, 0.0)
            lifts = [fall[:, lanes] for lanes in lane_tiles]
            while len(lifts) > 1:
                lifts = [a + b + a * b for a, b in zip(lifts[::2], lifts[1::2])]
            lift = lifts[0]
            soft = functools.reduce(jnp.add, [over[:, lanes] for lanes in lane_tiles]) + jnp.where(
                lift < 2.0**-11, lift * (1.0 - 0.5 * lift), jnp.log(1.0 + lift)
            )
            loss = loss + jnp.sum((weight * soft).reshape(small // 8, 8, LANES), axis=0)
        moves(begin)
    col_sum = jnp.sum(cols, axis=0, keepdims=True)

    @pl.when(block == 0)
    def _():
        loss_ref[...] = loss

    @pl.when(block > 0)
    def _():
        loss_ref[...] += loss

    moved = lax.dot_general(shift_scr[me], slopes[...], NN, preferred_element_type=F32)
    moved = 0.5 * moved - col_sum * neg_scr[me].astype(F32)
    for (start, depth), grad in zip(slices, grads):
        grad[2, :, :depth] = moved[start : start + depth, :].T


def block_math(me, live_counts, pairs, sums, offs, tails, old, slices, block_len, half):
    n, n_col = len(slices), len(pairs)
    blocks = live_counts.shape[0]
    part = blocks // HALVES
    width = sum(depth for _, depth in slices)
    flat = [piece for per_col in pairs for piece in per_col]
    given = [] if old is None else old

    def rows():
        return pl.BlockSpec((block_len, LANES), lambda b: (b, 0))

    first_old = 2 + len(flat) + n_col + 2 * n
    return pl.pallas_call(
        functools.partial(block_kernel, slices, n_col, half),
        out_shape=[jax.ShapeDtypeStruct((3, blocks * block_len, LANES), F32)] * n
        + [jax.ShapeDtypeStruct((8, LANES), F32)],
        grid=(part,),
        in_specs=[whole(SMEM)] * 2
        + [
            pl.BlockSpec((2, piece.shape[1], block_len), lambda b: (0, 0, b)) for piece in flat
        ]
        + [pl.BlockSpec((2, block_len), lambda b: (0, b))] * n_col
        + [rows() for _ in range(2 * n)]
        + [whole(pl.ANY)] * len(given),
        out_specs=[
            pl.BlockSpec((3, block_len, LANES), lambda b: (0, half * part + b, 0))
        ]
        * n
        + [pl.BlockSpec((8, LANES), lambda b: (0, 0))],
        input_output_aliases={first_old + k: k for k in range(len(given))},
        scratch_shapes=[
            pltpu.VMEM((n_col, width, block_len), BF16),
            pltpu.VMEM((n_col, width, block_len), BF16),
            pltpu.VMEM((n_col, 2, block_len), F32),
            pltpu.VMEM((block_len, block_len), F32),
            pltpu.VMEM((block_len, block_len), BF16),
            pltpu.VMEM((block_len, LANES), F32),
            pltpu.VMEM((block_len, LANES), F32),
        ],
        compiler_params=params(),
        cost_estimate=cost(part * 8 * block_len * block_len * width, 120e6),
        name="block_math",
    )(me, live_counts, *flat, *sums, *offs, *tails, *given)


def outgoing_kernel(slices, capacity, begin, counts_ref, place_ref, *refs):
    n = len(slices)
    grads, out_ref, tiles = refs[:n], refs[-n - 1], refs[-n:]
    groups, width, chunk = out_ref.shape

    def owner(group, carry):
        wanted = jnp.clip(counts_ref[group] - begin, 0, chunk)

        def body(step, inner):
            for lane in range(UNROLL):
                at = step * UNROLL + lane
                place = place_ref[group * capacity + begin + at]
                for grad, tile in zip(grads, tiles):
                    tile[pl.ds(at, 1), :] = grad[pl.ds(place, 1), :]
            return inner

        lax.fori_loop(0, (wanted + UNROLL - 1) // UNROLL, body, 0)
        for (start, depth), tile in zip(slices, tiles):
            out_ref[group, start : start + depth, :] = tile[...].T[:depth].astype(BF16)
        return carry

    lax.fori_loop(0, groups, owner, 0)


def outgoing(counts, place_list, grads, slices, begin, chunk, after):
    groups, capacity = place_list.shape
    n = len(slices)
    width = sum(depth for _, depth in slices)
    return pl.pallas_call(
        functools.partial(outgoing_kernel, slices, capacity, begin),
        out_shape=jax.ShapeDtypeStruct((groups, width, chunk), BF16),
        in_specs=[whole(SMEM)] * 2 + [whole(VMEM)] * n + [whole(pl.ANY)] * len(after),
        out_specs=whole(VMEM),
        scratch_shapes=[pltpu.VMEM((chunk, LANES), F32)] * n,
        compiler_params=params(),
        cost_estimate=cost(0, 80e6),
        name="outgoing",
    )(counts, place_list.reshape(-1), *grads, *after)


def collect_kernel(slices, capacity, begin, first, counts_ref, row_ref, came_ref, *refs):
    n = len(slices)
    olds = () if first else refs[:n]
    refs = refs if first else refs[n:]
    totals, tiles = refs[:n], refs[n:]
    groups, width, chunk = came_ref.shape
    for k in range(n):
        totals[k][...] = jnp.zeros_like(totals[k]) if first else olds[k][...]

    def source(group, carry):
        wanted = jnp.clip(counts_ref[group] - begin, 0, chunk)

        @pl.when(wanted > 0)
        def _():
            for (start, depth), tile in zip(slices, tiles):
                tile[:, :depth] = came_ref[group, start : start + depth, :].astype(F32).T

            def body(step, inner):
                for lane in range(UNROLL):
                    at = step * UNROLL + lane
                    row = row_ref[group * capacity + begin + at]
                    for total, tile in zip(totals, tiles):
                        total[pl.ds(row, 1), :] = total[pl.ds(row, 1), :] + tile[pl.ds(at, 1), :]
                return inner

            lax.fori_loop(0, (wanted + UNROLL - 1) // UNROLL, body, 0)

        return carry

    lax.fori_loop(0, groups, source, 0)


def collect(counts, row_list, came, totals, slices, begin, ent_rows):
    capacity = row_list.shape[1]
    chunk = came.shape[2]
    n = len(slices)
    first = totals is None
    given = () if first else tuple(totals)
    return pl.pallas_call(
        functools.partial(collect_kernel, slices, capacity, begin, first),
        out_shape=[jax.ShapeDtypeStruct((ent_rows + 8, LANES), F32)] * n,
        in_specs=[whole(SMEM)] * 2 + [whole(VMEM)] * (1 + len(given)),
        out_specs=[whole(VMEM)] * n,
        scratch_shapes=[pltpu.VMEM((chunk, LANES), F32)] * n,
        compiler_params=params(),
        cost_estimate=cost(0, 120e6),
        name="collect",
    )(counts, row_list.reshape(-1), came, *given)


def relation_sums_kernel(n, ids_ref, *refs):
    grads, totals = refs[:n], refs[-n:]
    count = grads[0].shape[1]
    for total in totals:
        total[...] = jnp.zeros_like(total)

    def body(step, carry):
        for lane in range(UNROLL):
            at = step * UNROLL + lane
            row = ids_ref[at]
            for grad, total in zip(grads, totals):
                total[pl.ds(row, 1), :] = total[pl.ds(row, 1), :] + grad[0, pl.ds(at, 1), :]
        return carry

    lax.fori_loop(0, count // UNROLL, body, 0)


def relation_sums(relation_ids, grads, rel_total, after):
    n = len(grads)
    count = relation_ids.shape[0]
    return pl.pallas_call(
        functools.partial(relation_sums_kernel, n),
        out_shape=[jax.ShapeDtypeStruct((rel_total, LANES), F32)] * n,
        grid=(1,),
        in_specs=[whole(SMEM)]
        + [pl.BlockSpec((1, count, LANES), lambda i: (0, 0, 0))] * n
        + [whole(pl.ANY)] * len(after),
        out_specs=[whole(VMEM)] * n,
        compiler_params=params(),
        cost_estimate=cost(0, 120e6),
        name="relation_sums",
    )(relation_ids, *grads, *after)


def update_kernel(slices, weights_ref, first_ref, second_ref, *refs):
    n = len(slices)
    totals, outs, scr = refs[:n], refs[n : n + 3], refs[n + 3]
    for (start, depth), total in zip(slices, totals):
        scr[start : start + depth, :] = total[...].T[:depth]
    results = adamw_update(weights_ref[...], scr[...], first_ref[...], second_ref[...])
    for out, result in zip(outs, results):
        out[...] = result


def update_entities(weights, totals, first, second, slices):
    width, ent_rows = weights.shape
    cols = 1024
    n = len(slices)
    table = pl.BlockSpec((width, cols), lambda i: (0, i))
    return pl.pallas_call(
        functools.partial(update_kernel, slices),
        out_shape=[jax.ShapeDtypeStruct((width, ent_rows), F32)] * 3,
        grid=(pl.cdiv(ent_rows, cols),),
        in_specs=[table] * 3 + [pl.BlockSpec((cols, LANES), lambda i: (i, 0))] * n,
        out_specs=[table] * 3,
        scratch_shapes=[pltpu.VMEM((width, cols), F32)],
        compiler_params=params(),
        cost_estimate=cost(0, 60e6),
        name="update_entities",
    )(weights, first, second, *totals)


def chunk_bounds(capacity):
    units = capacity // LANES
    small = max(1, 3 * units // 16)
    large = (units - 2 * small) // 2
    sizes = [small, large, units - 2 * small - large, small]
    bounds = [0]
    for size in sizes:
        bounds.append(bounds[-1] + size * LANES)
    return bounds


def shards(
    head_ids,
    relation_ids,
    tail_ids,
    negative_ids,
    live_counts,
    rel_weight,
    rel_count,
    entity_table,
    entity_first,
    entity_second,
    relation_table,
    relation_first,
    relation_second,
):
    groups = lax.axis_size("edge")
    n_col = lax.axis_size("col")
    width, ent_rows = entity_table.shape
    blocks, neg_count = negative_ids.shape
    block_len = head_ids.shape[0] // blocks
    edge_count = blocks * block_len
    slices = width_slices(width)
    n = len(slices)
    all_ids = jnp.concatenate([head_ids, tail_ids, negative_ids.reshape(-1)])
    id_count = all_ids.shape[0]
    capacity = (4 * id_count + 3 * groups - 1) // (3 * groups)
    rel_total = rel_weight.shape[0]

    table_low = entity_table.astype(BF16)
    dense = [
        lax.all_gather(table_low[start : start + depth], "edge", axis=0, tiled=False)
        for start, depth in slices
    ]
    rel_own = rel_total // groups
    rel_low = jnp.broadcast_to(relation_table.astype(BF16)[None], (groups, rel_own, width))
    rel_table = lax.all_to_all(rel_low, "edge", split_axis=0, concat_axis=0, tiled=True)
    rel_table = rel_table.reshape(rel_total, width)

    place_list, row_list, counts = owner_lists(all_ids, groups, capacity, ent_rows)
    asked = lax.all_to_all(row_list, "edge", split_axis=0, concat_axis=0, tiled=True)
    asked_counts = jnp.sum((asked < ent_rows).astype(jnp.int32), axis=1)
    safe_places = jnp.minimum(place_list, id_count - 1)
    place_flat, row_flat = place_list.reshape(-1), row_list.reshape(-1)

    rel_scale = rel_weight * (rel_total / jnp.sum(rel_weight)) / rel_count.astype(F32)
    rel_slices = []
    for k, (start, depth) in enumerate(slices):
        piece = rel_table[:, start : start + depth].astype(F32)
        if k == n - 1:
            gap = jnp.zeros((rel_total, LANES - 1 - depth), F32)
            piece = jnp.concatenate([piece, gap, rel_scale[:, None]], axis=1)
        rel_slices.append(piece)
    rel_rows = relation_rows(relation_ids, rel_slices)

    me = lax.axis_index("col").astype(jnp.int32).reshape(1)
    offs = [[] for _ in range(HALVES)]
    tails = [[] for _ in range(HALVES)]
    pairs = [[[] for _ in range(n_col)] for _ in range(HALVES)]
    parts = [[] for _ in range(HALVES)]
    for k, (start, depth) in enumerate(slices):
        fetched = fetch(counts, place_flat, row_flat, dense[k], id_count)
        for half in range(HALVES):
            off, tail, pair, part = prepare(fetched, rel_rows[k], depth, blocks, block_len, half)
            offs[half].append(off)
            tails[half].append(tail)
            parts[half].append(part)
            pairs[half][0].append(pair)
            for away in range(1, n_col):
                turn = [(c, (c + away) % n_col) for c in range(n_col)]
                pairs[half][away].append(lax.ppermute(pair, "col", turn))

    grads, loss_tiles = None, []
    for half in range(HALVES):
        part = functools.reduce(jnp.add, parts[half])
        sums = [part]
        for away in range(1, n_col):
            turn = [(c, (c + away) % n_col) for c in range(n_col)]
            sums.append(lax.ppermute(part, "col", turn))
        *grads, loss_tile = block_math(
            me, live_counts, pairs[half], sums, offs[half], tails[half], grads, slices, block_len, half
        )
        loss_tiles.append(loss_tile)
    live = jnp.sum(jnp.minimum(live_counts, block_len)).astype(F32)
    loss_own = jnp.sum(functools.reduce(jnp.add, loss_tiles))
    loss_row = jnp.zeros((LANES,), F32).at[0].set(loss_own).at[1].set(live)
    loss_all = lax.all_to_all(
        jnp.broadcast_to(loss_row, (groups, 1, LANES)), "edge", split_axis=0, concat_axis=0, tiled=True
    )
    loss_pair = jnp.sum(loss_all[:, 0, :2], axis=0)

    flat = [grad.reshape(id_count, LANES) for grad in grads]
    bounds = chunk_bounds(capacity)
    chunks = len(bounds) - 1
    arrived, totals, after = [], None, []
    for k in range(chunks):
        sent = outgoing(
            counts, safe_places, flat, slices, bounds[k], bounds[k + 1] - bounds[k], after
        )
        arrived.append(lax.all_to_all(sent, "edge", split_axis=0, concat_axis=0, tiled=True))
        after = []
        if k > 0:
            totals = collect(
                asked_counts, asked, arrived[k - 1], totals, slices, bounds[k - 1], ent_rows
            )
            after = totals[:1]
        if k == 1:
            rel_terms = relation_sums(relation_ids, grads, rel_total, [totals[0], loss_all])
            after = rel_terms[:1]
            rel_terms = jnp.concatenate(
                [term[:, :depth] for (start, depth), term in zip(slices, rel_terms)], axis=1
            )
            relation_grad = lax.psum_scatter(rel_terms, "edge", scatter_dimension=0, tiled=True)
        if k == chunks - 2:
            after = [totals[0], relation_grad]
    k = chunks - 1
    totals = collect(asked_counts, asked, arrived[k], totals, slices, bounds[k], ent_rows)

    new_entity, new_entity_first, new_entity_second = update_entities(
        entity_table, totals, entity_first, entity_second, slices
    )
    new_relation, new_relation_first, new_relation_second = adamw_update(
        relation_table, relation_grad, relation_first, relation_second
    )
    return (
        loss_pair,
        new_entity,
        new_entity_first,
        new_entity_second,
        new_relation,
        new_relation_first,
        new_relation_second,
    )


def solution(mesh):
    placed = (
        P("edge"),
        P("edge"),
        P("edge"),
        P("edge", None),
        P("edge"),
        P(),
        P(),
        P("col", "edge"),
        P("col", "edge"),
        P("col", "edge"),
        P("edge", "col"),
        P("edge", "col"),
        P("edge", "col"),
    )
    return jax.shard_map(
        shards,
        mesh=mesh,
        in_specs=placed,
        out_specs=(
            P(),
            P("col", "edge"),
            P("col", "edge"),
            P("col", "edge"),
            P("edge", "col"),
            P("edge", "col"),
            P("edge", "col"),
        ),
        check_vma=False,
    )
```

```python
import functools

import jax
import jax.numpy as jnp
from jax import lax
from jax.experimental import pallas as pl
from jax.experimental.pallas import tpu as pltpu
from jax.sharding import PartitionSpec as P

STEP = 5


MARGIN = 0.1
LEARN_RATE = 0.1
BETA_ONE = 0.5
BETA_TWO = 0.5
EPSILON = 1e-08
DECAY = 0.01
LANES = 128
UNROLL = 8
PARTS = 4
HALVES = 2
TURN = 512
REL_PAD = 256
TERMS = 3
NN = (((1,), (0,)), ((), ()))
NT = (((1,), (1,)), ((), ()))
TN = (((0,), (0,)), ((), ()))
F32 = jnp.float32
BF16 = jnp.bfloat16
SMEM = pltpu.SMEM
VMEM = pltpu.VMEM


def params():
    return pltpu.CompilerParams(vmem_limit_bytes=60 << 20)


def cost(flops, moved):
    return pl.CostEstimate(flops=int(flops), bytes_accessed=int(moved), transcendentals=0)


def whole(space):
    return pl.BlockSpec(memory_space=space)


def adamw_update(weights, gradient, first, second):
    new_first = BETA_ONE * first + (1.0 - BETA_ONE) * gradient
    new_second = BETA_TWO * second + (1.0 - BETA_TWO) * gradient * gradient
    first_hat = new_first / (1.0 - BETA_ONE**STEP)
    second_hat = new_second / (1.0 - BETA_TWO**STEP)
    updated = weights - LEARN_RATE * (
        first_hat / (jnp.sqrt(second_hat) + EPSILON) + DECAY * weights
    )
    return (updated, new_first, new_second)


def width_slices(width):
    return [(at, min(LANES, width - at)) for at in range(0, width, LANES)]


def owner_lists(all_ids, groups, capacity, ent_rows):
    count = all_ids.shape[0]
    owners = all_ids // ent_rows
    local_rows = all_ids - owners * ent_rows
    chunk = 256
    mine = owners[None, :] == jnp.arange(groups, dtype=jnp.int32)[:, None]
    mine = mine.astype(BF16).reshape(groups, count // chunk, chunk)
    before = jnp.triu(jnp.ones((chunk, chunk), BF16), 1)
    inner = jnp.dot(mine, before, preferred_element_type=F32)
    sums = jnp.sum(mine.astype(F32), axis=2)
    carry = jnp.cumsum(sums, axis=1) - sums
    ranks = jnp.sum(mine.astype(F32) * (inner + carry[:, :, None]), axis=0)
    ranks = ranks.astype(jnp.int32).reshape(count)
    counts = jnp.sum(sums, axis=1).astype(jnp.int32)
    high = owners * (capacity // LANES) + ranks // LANES
    low = ranks % LANES
    tall = groups * capacity // LANES
    left = (jnp.arange(tall, dtype=jnp.int32)[:, None] == high[None, :]).astype(BF16)
    right = (jnp.arange(LANES, dtype=jnp.int32)[:, None] == low[None, :]).astype(BF16)
    places = jnp.arange(1, count + 1, dtype=jnp.int32)
    parts = jnp.stack([places // 256, places % 256, local_rows // 256, local_rows % 256])
    right = (parts.astype(BF16)[:, None, :] * right[None]).reshape(PARTS * LANES, count)
    found = lax.dot_general(left, right, NT, preferred_element_type=F32).astype(jnp.int32)
    found = found.reshape(tall, PARTS, LANES)
    place = found[:, 0] * 256 + found[:, 1]
    place_list = jnp.where(place > 0, place - 1, count).reshape(groups, capacity)
    row_list = jnp.where(place > 0, found[:, 2] * 256 + found[:, 3], ent_rows)
    return place_list, row_list.reshape(groups, capacity), counts


def relation_rows_kernel(slices, ids_ref, scale_ref, *refs):
    n = len(slices)
    tables, outs = refs[:n], refs[-2 * n - 1 : -n - 1]
    columns, rows = refs[-n - 1], refs[-n:]
    groups = tables[0].shape[0]
    for (_, depth), table, into in zip(slices, tables, rows):
        columns[...] = jnp.zeros_like(columns)

        def turn(group, carry):
            columns[:depth, :] = table[group, :depth].astype(F32)
            if depth < LANES:
                columns[LANES - 1 :, :] = scale_ref[pl.ds(group, 1), :]
            into[pl.ds(pl.multiple_of(group * REL_PAD, REL_PAD), REL_PAD), :] = columns[...].T
            return carry

        lax.fori_loop(0, groups, turn, 0, unroll=4)

    def body(step, carry):
        for lane in range(UNROLL):
            at = step * UNROLL + lane
            row = ids_ref[at]
            for source, out in zip(rows, outs):
                out[pl.ds(at, 1), :] = source[pl.ds(row, 1), :]
        return carry

    lax.fori_loop(0, outs[0].shape[0] // UNROLL, body, 0)


def relation_rows(places, dense, scale, slices, after):
    count = places.shape[0]
    groups, depth, span = dense.shape
    n = len(slices)
    first = span // REL_PAD - n

    def columns(k):
        return pl.BlockSpec((groups, depth, REL_PAD), lambda i: (0, 0, first + k))

    return pl.pallas_call(
        functools.partial(relation_rows_kernel, slices),
        out_shape=[jax.ShapeDtypeStruct((count, LANES), F32)] * n,
        grid=(1,),
        in_specs=[whole(SMEM), whole(VMEM)]
        + [columns(k) for k in range(n)]
        + [whole(pl.ANY)] * len(after),
        out_specs=[whole(VMEM)] * n,
        scratch_shapes=[pltpu.VMEM((LANES, REL_PAD), F32)]
        + [pltpu.VMEM((groups * REL_PAD, LANES), F32)] * n,
        compiler_params=params(),
        cost_estimate=cost(0, 80e6),
        name="relation_rows",
    )(places, scale, *[dense] * n, *after)


def fetch_kernel(
    capacity, moves, ent_rows, counts_ref, place_ref, row_ref, dense_ref, *refs
):
    shard = pl.program_id(0)
    last = pl.num_programs(0) - 1
    out_ref, rows = refs[-3], refs[-2:]
    depth = dense_ref.shape[1]
    turns = ent_rows // TURN
    rest = ent_rows - turns * TURN

    if depth < LANES:

        @pl.when(shard == 0)
        def _():
            for ref in rows:
                ref[...] = jnp.zeros_like(ref)

    def turn(into, begin, size):
        cols = pl.ds(begin, size)
        into[cols, :depth] = dense_ref[0, :, cols].astype(F32).T

    def move(source, at):
        out_ref[pl.ds(place_ref[at], 1), :] = source[pl.ds(row_ref[at], 1), :]

    def step(into, source):
        base = (shard - 1) * capacity

        def remaining(first):
            def body(trip, carry):
                for lane in range(UNROLL):
                    move(source, base + first + trip * UNROLL + lane)
                return carry

            wanted = counts_ref[jnp.maximum(shard - 1, 0)] - first
            lax.fori_loop(0, (wanted + UNROLL - 1) // UNROLL, body, 0)

        def only_turn(trip, carry):
            turn(into, pl.multiple_of(trip * TURN, TURN), TURN)
            return carry

        def both(trip, carry):
            turn(into, pl.multiple_of(trip * TURN, TURN), TURN)
            for lane in range(moves):
                move(source, base + trip * moves + lane)
            return carry

        @pl.when(shard == 0)
        def _():
            lax.fori_loop(0, turns, only_turn, 0)

        @pl.when((shard > 0) & (shard < last))
        def _():
            lax.fori_loop(0, turns, both, 0)
            remaining(turns * moves)

        @pl.when(shard == last)
        def _():
            remaining(0)

        if rest:

            @pl.when(shard < last)
            def _():
                turn(into, turns * TURN, rest)

    for parity in range(2):

        @pl.when(lax.rem(shard, 2) == parity)
        def _():
            step(rows[parity], rows[1 - parity])


def fetch(counts, place_list, row_list, dense, id_count, ent_rows, after):
    groups, depth, _ = dense.shape
    capacity = place_list.shape[0] // groups
    moves = (id_count // groups) // (ent_rows // TURN) // UNROLL * UNROLL
    return pl.pallas_call(
        functools.partial(fetch_kernel, capacity, moves, ent_rows),
        out_shape=jax.ShapeDtypeStruct((id_count + 8, LANES), F32),
        grid=(groups + 1,),
        in_specs=[whole(SMEM)] * 3
        + [
            pl.BlockSpec(
                (1, depth, ent_rows), lambda shard: (jnp.minimum(shard, groups - 1), 0, 0)
            )
        ]
        + [whole(pl.ANY)] * len(after),
        out_specs=whole(VMEM),
        scratch_shapes=[pltpu.VMEM((ent_rows + 8, LANES), F32)] * 2,
        compiler_params=params(),
        cost_estimate=cost(0, 170e6),
        name="fetch_rows",
    )(counts, place_list, row_list, dense, *after)


def column_sum(values):
    return jnp.sum(values * values, axis=0, keepdims=True)


def negatives_kernel(neg_ref, low_ref, norm_ref):
    neg_t = neg_ref[...].T
    low_ref[...] = neg_t[: low_ref.shape[0]].astype(BF16)
    norm_ref[...] = column_sum(neg_t)


def negatives(fetched, depth, blocks, block_len):
    count = blocks * block_len
    return pl.pallas_call(
        negatives_kernel,
        out_shape=[
            jax.ShapeDtypeStruct((depth, count), BF16),
            jax.ShapeDtypeStruct((1, count), F32),
        ],
        grid=(blocks,),
        in_specs=[pl.BlockSpec((block_len, LANES), lambda b: (2 * blocks + b, 0))],
        out_specs=[
            pl.BlockSpec((depth, block_len), lambda b: (0, b)),
            pl.BlockSpec((1, block_len), lambda b: (0, b)),
        ],
        compiler_params=params(),
        cost_estimate=cost(0, 10e6),
        name="negatives",
    )(fetched)


def edge_parts(depth, head_ref, tail_ref, rel_ref, off_ref, tail_out):
    lane = lax.broadcasted_iota(jnp.int32, head_ref.shape, 1)
    inside = lane < depth
    rel = rel_ref[...]
    tail = tail_ref[...]
    shifted = head_ref[...] + jnp.where(inside, rel, 0.0)
    off_ref[...] = jnp.where(inside, shifted - tail, rel)
    tail_out[...] = tail.astype(BF16)
    shifted_t = shifted.T
    return shifted_t, column_sum((shifted - tail).T) - column_sum(shifted_t)


def edges_kernel(depth, head_ref, tail_ref, rel_ref, off_ref, tail_out, low_ref, bias_ref):
    shifted_t, bias = edge_parts(depth, head_ref, tail_ref, rel_ref, off_ref, tail_out)
    low_ref[...] = shifted_t[:depth].astype(BF16)
    bias_ref[...] = bias


def edges(fetched, rel_rows, depth, blocks, block_len):
    count = blocks * block_len

    def rows(at):
        return pl.BlockSpec((block_len, LANES), lambda b: (at * blocks + b, 0))

    return pl.pallas_call(
        functools.partial(edges_kernel, depth),
        out_shape=[
            jax.ShapeDtypeStruct((count, LANES), F32),
            jax.ShapeDtypeStruct((count, LANES), BF16),
            jax.ShapeDtypeStruct((depth, count), BF16),
            jax.ShapeDtypeStruct((1, count), F32),
        ],
        grid=(blocks,),
        in_specs=[rows(0), rows(1), rows(0)],
        out_specs=[
            rows(0),
            rows(0),
            pl.BlockSpec((depth, block_len), lambda b: (0, b)),
            pl.BlockSpec((1, block_len), lambda b: (0, b)),
        ],
        compiler_params=params(),
        cost_estimate=cost(0, 30e6),
        name="edges",
    )(fetched, fetched, rel_rows)


def last_rows(depth):
    return (depth + 7) // 8 * 8


def with_terms(columns, total, depth):
    place = lax.broadcasted_iota(jnp.int32, (8, total.shape[1]), 0)
    left = total
    terms = jnp.zeros(place.shape, F32)
    for k in range(TERMS):
        term = left.astype(BF16).astype(F32)
        left = left - term
        terms = jnp.where(place == k, term, terms)
    return jnp.concatenate([columns[: last_rows(depth)], terms], axis=0).astype(BF16)


def last_kernel(depth, n_given, head_ref, tail_ref, neg_ref, rel_ref, *refs):
    biases, norms = refs[:n_given], refs[n_given : 2 * n_given]
    off_ref, tail_out, pair_ref = refs[2 * n_given :]
    shifted_t, bias = edge_parts(depth, head_ref, tail_ref, rel_ref, off_ref, tail_out)
    neg_t = neg_ref[...].T
    norm = column_sum(neg_t)
    for ref in biases:
        bias = bias + ref[...]
    for ref in norms:
        norm = norm + ref[...]
    pair_ref[0] = with_terms(shifted_t, bias, depth)
    pair_ref[1] = with_terms(neg_t, norm, depth)


def last_slice(fetched, rel_rows, biases, norms, depth, blocks, block_len, half):
    part = blocks // HALVES
    count = part * block_len
    tall = last_rows(depth) + 8

    def rows(at):
        return pl.BlockSpec((block_len, LANES), lambda b: (at * blocks + half * part + b, 0))

    return pl.pallas_call(
        functools.partial(last_kernel, depth, len(biases)),
        out_shape=[
            jax.ShapeDtypeStruct((count, LANES), F32),
            jax.ShapeDtypeStruct((count, LANES), BF16),
            jax.ShapeDtypeStruct((2, tall, count), BF16),
        ],
        grid=(part,),
        in_specs=[rows(0), rows(1), rows(2), rows(0)]
        + [pl.BlockSpec((1, block_len), lambda b: (0, half * part + b))]
        * (len(biases) + len(norms)),
        out_specs=[
            pl.BlockSpec((block_len, LANES), lambda b: (b, 0)),
            pl.BlockSpec((block_len, LANES), lambda b: (b, 0)),
            pl.BlockSpec((2, tall, block_len), lambda b: (0, 0, b)),
        ],
        compiler_params=params(),
        cost_estimate=cost(0, 20e6),
        name="last_slice",
    )(fetched, fetched, fetched, rel_rows, *biases, *norms)


def block_kernel(slices, n_col, half, me_ref, live_ref, *refs):
    n = len(slices)
    per_col = 2 * n - 1
    given = [refs[k * per_col : (k + 1) * per_col] for k in range(n_col)]
    refs = refs[n_col * per_col :]
    offs, tails, refs = refs[:n], refs[n : 2 * n], refs[2 * n :]
    if half > 0:
        refs = refs[n:]
    grads, refs = refs[:n], refs[n:]
    loss_ref, shift_scr, neg_scr, sums_scr, cross, slopes, row_bias, row_sum = refs
    block = pl.program_id(0)
    length = cross.shape[0]
    me = me_ref[0]
    for k in range(n_col):
        slot = lax.rem(me + (n_col - k), n_col)
        for m, (start, depth) in enumerate(slices):
            if m < n - 1:
                shift, neg = given[k][2 * m][...], given[k][2 * m + 1][...]
            else:
                pair = given[k][-1]
                shift, neg = pair[0, :depth, :], pair[1, :depth, :]
                for row in range(2):
                    terms = pair[row, last_rows(depth) : last_rows(depth) + 8, :].astype(F32)
                    sums_scr[slot, row : row + 1] = jnp.sum(terms, axis=0, keepdims=True)
            shift_scr[slot, start : start + depth, :] = 2.0 * shift
            neg_scr[slot, start : start + depth, :] = neg
    bias = jnp.sum(sums_scr[:, 0, :], axis=0, keepdims=True) + MARGIN
    neg_norm = jnp.sum(sums_scr[:, 1, :], axis=0, keepdims=True)
    row_bias[...] = jnp.broadcast_to(bias, (LANES, length)).T

    live = live_ref[half * pl.num_programs(0) + block]
    tile = 256
    small = 128
    lane_tiles = [slice(at, at + LANES) for at in range(0, length, LANES)]
    cols = jnp.zeros((8, length), F32)
    loss = jnp.zeros((8, LANES), F32)
    def products(at):
        part = slice(at, at + tile)
        doubled = None
        for k in range(n_col):
            term = lax.dot_general(
                shift_scr[k, :, part], neg_scr[k], TN, preferred_element_type=F32
            )
            doubled = term if doubled is None else doubled + term
        cross[part, :] = doubled

    def moves(at):
        part = slice(at, at + tile)
        moved = lax.dot_general(slopes[part, :], neg_scr[me], NT, preferred_element_type=F32)
        fade = -row_sum[part, :]
        for (start, depth), off, tail, grad in zip(slices, offs, tails, grads):
            grad[0, part, :depth] = (
                fade[:, :depth] * tail[part, :depth].astype(F32) + moved[:, start : start + depth]
            )
            grad[1, part, :] = fade * off[part, :]

    products(0)
    for begin in range(0, length, tile):
        if begin + tile < length:
            products(begin + tile)
        for at in range(begin, begin + tile, small):
            part = slice(at, at + small)
            place = at + lax.broadcasted_iota(jnp.int32, (small, 1), 0)
            scale = offs[-1][part, LANES - 1 : LANES]
            weight = jnp.where(place < live, scale, 0.0) / length
            margins = cross[part, :] + (row_bias[part, 0:1] - neg_norm)
            fall = jnp.exp(-jnp.abs(margins))
            under = 1.0 + fall
            guess = pl.reciprocal(under, approx=True)
            inverse = guess * (2.0 - under * guess)
            twice = (2.0 * weight) * (jnp.where(margins >= 0.0, 1.0, fall) * inverse)
            row_sum[part, :] = jnp.broadcast_to(
                jnp.sum(twice, axis=1, keepdims=True), (small, LANES)
            )
            slopes[part, :] = twice.astype(BF16)
            cols = cols + jnp.sum(twice.reshape(small // 8, 8, length), axis=0)
            over = jnp.maximum(margins, 0.0)
            lifts = [fall[:, lanes] for lanes in lane_tiles]
            while len(lifts) > 1:
                lifts = [a + b + a * b for a, b in zip(lifts[::2], lifts[1::2])]
            lift = lifts[0]
            soft = functools.reduce(jnp.add, [over[:, lanes] for lanes in lane_tiles]) + jnp.where(
                lift < 2.0**-11, lift * (1.0 - 0.5 * lift), jnp.log(1.0 + lift)
            )
            loss = loss + jnp.sum((weight * soft).reshape(small // 8, 8, LANES), axis=0)
        moves(begin)
    col_sum = jnp.sum(cols, axis=0, keepdims=True)

    @pl.when(block == 0)
    def _():
        loss_ref[...] = loss

    @pl.when(block > 0)
    def _():
        loss_ref[...] += loss

    moved = lax.dot_general(shift_scr[me], slopes[...], NN, preferred_element_type=F32)
    moved = 0.5 * moved - col_sum * neg_scr[me].astype(F32)
    for (start, depth), grad in zip(slices, grads):
        grad[2, :, :depth] = moved[start : start + depth, :].T


def block_math(me, live_counts, given, offs, tails, old, slices, block_len, half):
    n, n_col = len(slices), len(given)
    blocks = live_counts.shape[0]
    part = blocks // HALVES
    width = sum(depth for _, depth in slices)
    flat = [piece for per_col in given for piece in per_col]
    kept = [] if old is None else old

    def columns(piece):
        if piece.ndim == 3:
            return pl.BlockSpec((2, piece.shape[1], block_len), lambda b: (0, 0, b))
        return pl.BlockSpec((piece.shape[0], block_len), lambda b: (0, half * part + b))

    def rows(array):
        first = half * part if array.shape[0] > part * block_len else 0
        return pl.BlockSpec((block_len, LANES), lambda b: (first + b, 0))

    first_old = 2 + len(flat) + 2 * n
    return pl.pallas_call(
        functools.partial(block_kernel, slices, n_col, half),
        out_shape=[jax.ShapeDtypeStruct((3, blocks * block_len, LANES), F32)] * n
        + [jax.ShapeDtypeStruct((8, LANES), F32)],
        grid=(part,),
        in_specs=[whole(SMEM)] * 2
        + [columns(piece) for piece in flat]
        + [rows(array) for array in offs + tails]
        + [whole(pl.ANY)] * len(kept),
        out_specs=[
            pl.BlockSpec((3, block_len, LANES), lambda b: (0, half * part + b, 0))
        ]
        * n
        + [pl.BlockSpec((8, LANES), lambda b: (0, 0))],
        input_output_aliases={first_old + k: k for k in range(len(kept))},
        scratch_shapes=[
            pltpu.VMEM((n_col, width, block_len), BF16),
            pltpu.VMEM((n_col, width, block_len), BF16),
            pltpu.VMEM((n_col, 2, block_len), F32),
            pltpu.VMEM((block_len, block_len), F32),
            pltpu.VMEM((block_len, block_len), BF16),
            pltpu.VMEM((block_len, LANES), F32),
            pltpu.VMEM((block_len, LANES), F32),
        ],
        compiler_params=params(),
        cost_estimate=cost(part * 8 * block_len * block_len * width, 120e6),
        name="block_math",
    )(me, live_counts, *flat, *offs, *tails, *kept)


def outgoing_kernel(slices, capacity, begin, counts_ref, place_ref, *refs):
    n = len(slices)
    grads, out_ref, tiles = refs[:n], refs[-n - 1], refs[-n:]
    groups, width, chunk = out_ref.shape

    def owner(group, carry):
        wanted = jnp.clip(counts_ref[group] - begin, 0, chunk)

        def body(step, inner):
            for lane in range(UNROLL):
                at = step * UNROLL + lane
                place = place_ref[group * capacity + begin + at]
                for grad, tile in zip(grads, tiles):
                    tile[pl.ds(at, 1), :] = grad[pl.ds(place, 1), :]
            return inner

        lax.fori_loop(0, (wanted + UNROLL - 1) // UNROLL, body, 0)
        for (start, depth), tile in zip(slices, tiles):
            out_ref[group, start : start + depth, :] = tile[...].T[:depth].astype(BF16)
        return carry

    lax.fori_loop(0, groups, owner, 0)


def outgoing(counts, place_list, grads, slices, begin, chunk, after):
    groups, capacity = place_list.shape
    n = len(slices)
    width = sum(depth for _, depth in slices)
    return pl.pallas_call(
        functools.partial(outgoing_kernel, slices, capacity, begin),
        out_shape=jax.ShapeDtypeStruct((groups, width, chunk), BF16),
        in_specs=[whole(SMEM)] * 2 + [whole(VMEM)] * n + [whole(pl.ANY)] * len(after),
        out_specs=whole(VMEM),
        scratch_shapes=[pltpu.VMEM((chunk, LANES), F32)] * n,
        compiler_params=params(),
        cost_estimate=cost(0, 80e6),
        name="outgoing",
    )(counts, place_list.reshape(-1), *grads, *after)


def collect_kernel(slices, capacity, begin, first, counts_ref, row_ref, came_ref, *refs):
    n = len(slices)
    olds = () if first else refs[:n]
    totals, tiles = refs[-2 * n : -n], refs[-n:]
    groups, width, chunk = came_ref.shape
    for k in range(n):
        totals[k][...] = jnp.zeros_like(totals[k]) if first else olds[k][...]

    def source(group, carry):
        wanted = jnp.clip(counts_ref[group] - begin, 0, chunk)

        @pl.when(wanted > 0)
        def _():
            for (start, depth), tile in zip(slices, tiles):
                tile[:, :depth] = came_ref[group, start : start + depth, :].astype(F32).T

            def body(step, inner):
                for lane in range(UNROLL):
                    at = step * UNROLL + lane
                    row = row_ref[group * capacity + begin + at]
                    for total, tile in zip(totals, tiles):
                        total[pl.ds(row, 1), :] = total[pl.ds(row, 1), :] + tile[pl.ds(at, 1), :]
                return inner

            lax.fori_loop(0, (wanted + UNROLL - 1) // UNROLL, body, 0)

        return carry

    lax.fori_loop(0, groups, source, 0)


def collect(counts, row_list, came, totals, slices, begin, ent_rows, after):
    capacity = row_list.shape[1]
    chunk = came.shape[2]
    n = len(slices)
    first = totals is None
    given = () if first else tuple(totals)
    return pl.pallas_call(
        functools.partial(collect_kernel, slices, capacity, begin, first),
        out_shape=[jax.ShapeDtypeStruct((ent_rows + 8, LANES), F32)] * n,
        in_specs=[whole(SMEM)] * 2
        + [whole(VMEM)] * (1 + len(given))
        + [whole(pl.ANY)] * len(after),
        out_specs=[whole(VMEM)] * n,
        scratch_shapes=[pltpu.VMEM((chunk, LANES), F32)] * n,
        compiler_params=params(),
        cost_estimate=cost(0, 120e6),
        name="collect",
    )(counts, row_list.reshape(-1), came, *given, *after)


def relation_sums_kernel(n, ids_ref, *refs):
    grads, totals = refs[:n], refs[-n:]
    count = grads[0].shape[1]
    for total in totals:
        total[...] = jnp.zeros_like(total)

    def body(step, carry):
        for lane in range(UNROLL):
            at = step * UNROLL + lane
            row = ids_ref[at]
            for grad, total in zip(grads, totals):
                total[pl.ds(row, 1), :] = total[pl.ds(row, 1), :] + grad[0, pl.ds(at, 1), :]
        return carry

    lax.fori_loop(0, count // UNROLL, body, 0)


def relation_sums(relation_ids, grads, rel_total, after):
    n = len(grads)
    count = relation_ids.shape[0]
    return pl.pallas_call(
        functools.partial(relation_sums_kernel, n),
        out_shape=[jax.ShapeDtypeStruct((rel_total, LANES), F32)] * n,
        grid=(1,),
        in_specs=[whole(SMEM)]
        + [pl.BlockSpec((1, count, LANES), lambda i: (0, 0, 0))] * n
        + [whole(pl.ANY)] * len(after),
        out_specs=[whole(VMEM)] * n,
        compiler_params=params(),
        cost_estimate=cost(0, 120e6),
        name="relation_sums",
    )(relation_ids, *grads, *after)


def update_kernel(slices, weights_ref, first_ref, second_ref, *refs):
    n = len(slices)
    totals, outs, scr = refs[:n], refs[n : n + 3], refs[n + 3]
    for (start, depth), total in zip(slices, totals):
        scr[start : start + depth, :] = total[...].T[:depth]
    results = adamw_update(weights_ref[...], scr[...], first_ref[...], second_ref[...])
    for out, result in zip(outs, results):
        out[...] = result


def update_entities(weights, totals, first, second, slices):
    width, ent_rows = weights.shape
    cols = 1024
    n = len(slices)
    table = pl.BlockSpec((width, cols), lambda i: (0, i))
    return pl.pallas_call(
        functools.partial(update_kernel, slices),
        out_shape=[jax.ShapeDtypeStruct((width, ent_rows), F32)] * 3,
        grid=(pl.cdiv(ent_rows, cols),),
        in_specs=[table] * 3 + [pl.BlockSpec((cols, LANES), lambda i: (i, 0))] * n,
        out_specs=[table] * 3,
        scratch_shapes=[pltpu.VMEM((width, cols), F32)],
        compiler_params=params(),
        cost_estimate=cost(0, 60e6),
        name="update_entities",
    )(weights, first, second, *totals)


def chunk_bounds(capacity):
    units = capacity // LANES
    sizes = [3, 6, 5, 2] if units == 16 else [units // 4] * 3 + [units - 3 * (units // 4)]
    bounds = [0]
    for size in sizes:
        bounds.append(bounds[-1] + size * LANES)
    return bounds


def shards(
    head_ids,
    relation_ids,
    tail_ids,
    negative_ids,
    live_counts,
    rel_weight,
    rel_count,
    entity_table,
    entity_first,
    entity_second,
    relation_table,
    relation_first,
    relation_second,
):
    groups = lax.axis_size("edge")
    n_col = lax.axis_size("col")
    width, ent_rows = entity_table.shape
    blocks, neg_count = negative_ids.shape
    block_len = head_ids.shape[0] // blocks
    edge_count = blocks * block_len
    slices = width_slices(width)
    n = len(slices)
    all_ids = jnp.concatenate([head_ids, tail_ids, negative_ids.reshape(-1)])
    id_count = all_ids.shape[0]
    capacity = (4 * id_count + 3 * groups - 1) // (3 * groups)
    rel_total = rel_weight.shape[0]

    rel_own = rel_total // groups
    rel_low = jnp.pad(relation_table.astype(BF16).T, ((0, 0), (0, REL_PAD - rel_own)))
    dense = []
    for k, (start, depth) in enumerate(slices):
        sent = entity_table[start : start + depth].astype(BF16)
        if k == 0:
            behind = [
                jnp.pad(rel_low[at : at + size], ((0, depth - size), (0, 0))) for at, size in slices
            ]
            sent = jnp.concatenate([sent] + behind, axis=1)
        dense.append(lax.all_gather(sent, "edge", axis=0, tiled=False))

    place_list, row_list, counts = owner_lists(all_ids, groups, capacity, ent_rows)
    asked = lax.all_to_all(row_list, "edge", split_axis=0, concat_axis=0, tiled=True)
    asked_counts = jnp.sum((asked < ent_rows).astype(jnp.int32), axis=1)
    safe_places = jnp.minimum(place_list, id_count - 1)
    place_flat, row_flat = place_list.reshape(-1), row_list.reshape(-1)

    rel_scale = rel_weight * (rel_total / jnp.sum(rel_weight)) / rel_count.astype(F32)
    rel_scale = jnp.pad(rel_scale.reshape(groups, rel_own), ((0, 0), (0, REL_PAD - rel_own)))
    rel_places = relation_ids + (relation_ids // rel_own) * (REL_PAD - rel_own)

    def from_others(array):
        turns = [[(c, (c + away) % n_col) for c in range(n_col)] for away in range(1, n_col)]
        return [lax.ppermute(array, "col", turn) for turn in turns]

    me = lax.axis_index("col").astype(jnp.int32).reshape(1)
    given = [[[] for _ in range(n_col)] for _ in range(HALVES)]
    offs = [[] for _ in range(HALVES)]
    tails = [[] for _ in range(HALVES)]
    biases, norms, first_sent, rel_rows = [], [], [], None
    for k, (start, depth) in enumerate(slices):
        early = [asked] + first_sent if k > 0 else []
        fetched = fetch(counts, place_flat, row_flat, dense[k], id_count, ent_rows, early)
        if k < n - 1:
            neg_low, norm = negatives(fetched, depth, blocks, block_len)
            neg_all = [neg_low] + from_others(neg_low)
            if rel_rows is None:
                rel_rows = relation_rows(rel_places, dense[0], rel_scale, slices, [neg_low])
            off, tail, low, bias = edges(fetched, rel_rows[k], depth, blocks, block_len)
            low_all = [low] + from_others(low)
            first_sent = neg_all[1:]
            biases.append(bias)
            norms.append(norm)
            for half in range(HALVES):
                offs[half].append(off)
                tails[half].append(tail)
                for col in range(n_col):
                    given[half][col] += [low_all[col], neg_all[col]]
            continue
        if rel_rows is None:
            rel_rows = relation_rows(rel_places, dense[0], rel_scale, slices, [])
        for half in range(HALVES):
            off, tail, pair = last_slice(
                fetched, rel_rows[k], biases, norms, depth, blocks, block_len, half
            )
            offs[half].append(off)
            tails[half].append(tail)
            for col, piece in enumerate([pair] + from_others(pair)):
                given[half][col].append(piece)

    grads, loss_tiles = None, []
    for half in range(HALVES):
        *grads, loss_tile = block_math(
            me, live_counts, given[half], offs[half], tails[half], grads, slices, block_len, half
        )
        loss_tiles.append(loss_tile)
    live = jnp.sum(jnp.minimum(live_counts, block_len)).astype(F32)
    loss_own = jnp.sum(functools.reduce(jnp.add, loss_tiles))
    loss_row = jnp.zeros((LANES,), F32).at[0].set(loss_own).at[1].set(live)
    loss_all = lax.all_to_all(
        jnp.broadcast_to(loss_row, (groups, 1, LANES)), "edge", split_axis=0, concat_axis=0, tiled=True
    )
    loss_pair = jnp.sum(loss_all[:, 0, :2], axis=0)

    flat = [grad.reshape(id_count, LANES) for grad in grads]
    bounds = chunk_bounds(capacity)
    chunks = len(bounds) - 1
    arrived, totals, after = [], None, []
    for k in range(chunks):
        sent = outgoing(
            counts, safe_places, flat, slices, bounds[k], bounds[k + 1] - bounds[k], after
        )
        arrived.append(lax.all_to_all(sent, "edge", split_axis=0, concat_axis=0, tiled=True))
        after = []
        if k == 1:
            rel_terms = relation_sums(relation_ids, grads, rel_total, [arrived[0], loss_all])
            after = rel_terms[:1]
            rel_terms = jnp.concatenate(
                [term[:, :depth] for (start, depth), term in zip(slices, rel_terms)], axis=1
            )
            relation_grad = lax.psum_scatter(rel_terms, "edge", scatter_dimension=0, tiled=True)
        if k == chunks - 1:
            after = [relation_grad]
        if k > 0:
            totals = collect(
                asked_counts,
                asked,
                arrived[k - 1],
                totals,
                slices,
                bounds[k - 1],
                ent_rows,
                after,
            )
            after = [totals[0], rel_terms]
    k = chunks - 1
    totals = collect(asked_counts, asked, arrived[k], totals, slices, bounds[k], ent_rows, [])

    new_entity, new_entity_first, new_entity_second = update_entities(
        entity_table, totals, entity_first, entity_second, slices
    )
    new_relation, new_relation_first, new_relation_second = adamw_update(
        relation_table, relation_grad, relation_first, relation_second
    )
    return (
        loss_pair,
        new_entity,
        new_entity_first,
        new_entity_second,
        new_relation,
        new_relation_first,
        new_relation_second,
    )


def solution(mesh):
    placed = (
        P("edge"),
        P("edge"),
        P("edge"),
        P("edge", None),
        P("edge"),
        P(),
        P(),
        P("col", "edge"),
        P("col", "edge"),
        P("col", "edge"),
        P("edge", "col"),
        P("edge", "col"),
        P("edge", "col"),
    )
    return jax.shard_map(
        shards,
        mesh=mesh,
        in_specs=placed,
        out_specs=(
            P(),
            P("col", "edge"),
            P("col", "edge"),
            P("col", "edge"),
            P("edge", "col"),
            P("edge", "col"),
            P("edge", "col"),
        ),
        check_vma=False,
    )
```

```python
import functools

import jax
import jax.numpy as jnp
from jax import lax
from jax.experimental import pallas as pl
from jax.experimental.pallas import tpu as pltpu
from jax.sharding import PartitionSpec as P

STEP = 5


MARGIN = 0.1
LEARN_RATE = 0.1
BETA_ONE = 0.5
BETA_TWO = 0.5
EPSILON = 1e-08
DECAY = 0.01
LANES = 128
UNROLL = 8
PARTS = 4
HALVES = 4
TURN = 512
REL_PAD = 256
TERMS = 3
NN = (((1,), (0,)), ((), ()))
NT = (((1,), (1,)), ((), ()))
TN = (((0,), (0,)), ((), ()))
F32 = jnp.float32
BF16 = jnp.bfloat16
SMEM = pltpu.SMEM
VMEM = pltpu.VMEM


def params():
    return pltpu.CompilerParams(vmem_limit_bytes=60 << 20)


def cost(flops, moved):
    return pl.CostEstimate(flops=int(flops), bytes_accessed=int(moved), transcendentals=0)


def whole(space):
    return pl.BlockSpec(memory_space=space)


def adamw_update(weights, gradient, first, second):
    new_first = BETA_ONE * first + (1.0 - BETA_ONE) * gradient
    new_second = BETA_TWO * second + (1.0 - BETA_TWO) * gradient * gradient
    first_hat = new_first / (1.0 - BETA_ONE**STEP)
    second_hat = new_second / (1.0 - BETA_TWO**STEP)
    updated = weights - LEARN_RATE * (
        first_hat / (jnp.sqrt(second_hat) + EPSILON) + DECAY * weights
    )
    return (updated, new_first, new_second)


def width_slices(width):
    return [(at, min(LANES, width - at)) for at in range(0, width, LANES)]


def owner_lists(all_ids, groups, capacity, ent_rows):
    count = all_ids.shape[0]
    owners = all_ids // ent_rows
    local_rows = all_ids - owners * ent_rows
    chunk = 256
    mine = owners[None, :] == jnp.arange(groups, dtype=jnp.int32)[:, None]
    mine = mine.astype(BF16).reshape(groups, count // chunk, chunk)
    before = jnp.triu(jnp.ones((chunk, chunk), BF16), 1)
    inner = jnp.dot(mine, before, preferred_element_type=F32)
    sums = jnp.sum(mine.astype(F32), axis=2)
    carry = jnp.cumsum(sums, axis=1) - sums
    ranks = jnp.sum(mine.astype(F32) * (inner + carry[:, :, None]), axis=0)
    ranks = ranks.astype(jnp.int32).reshape(count)
    counts = jnp.sum(sums, axis=1).astype(jnp.int32)
    high = owners * (capacity // LANES) + ranks // LANES
    low = ranks % LANES
    tall = groups * capacity // LANES
    left = (jnp.arange(tall, dtype=jnp.int32)[:, None] == high[None, :]).astype(BF16)
    right = (jnp.arange(LANES, dtype=jnp.int32)[:, None] == low[None, :]).astype(BF16)
    places = jnp.arange(1, count + 1, dtype=jnp.int32)
    parts = jnp.stack([places // 256, places % 256, local_rows // 256, local_rows % 256])
    right = (parts.astype(BF16)[:, None, :] * right[None]).reshape(PARTS * LANES, count)
    found = lax.dot_general(left, right, NT, preferred_element_type=F32).astype(jnp.int32)
    found = found.reshape(tall, PARTS, LANES)
    place = found[:, 0] * 256 + found[:, 1]
    place_list = jnp.where(place > 0, place - 1, count).reshape(groups, capacity)
    row_list = jnp.where(place > 0, found[:, 2] * 256 + found[:, 3], ent_rows)
    return place_list, row_list.reshape(groups, capacity), counts


def relation_rows_kernel(slices, ids_ref, scale_ref, *refs):
    n = len(slices)
    tables, outs = refs[:n], refs[-2 * n - 1 : -n - 1]
    columns, rows = refs[-n - 1], refs[-n:]
    groups = tables[0].shape[0]
    for (_, depth), table, into in zip(slices, tables, rows):
        columns[...] = jnp.zeros_like(columns)

        def turn(group, carry):
            columns[:depth, :] = table[group, :depth].astype(F32)
            if depth < LANES:
                columns[LANES - 1 :, :] = scale_ref[pl.ds(group, 1), :]
            into[pl.ds(pl.multiple_of(group * REL_PAD, REL_PAD), REL_PAD), :] = columns[...].T
            return carry

        lax.fori_loop(0, groups, turn, 0, unroll=4)

    def body(step, carry):
        for lane in range(UNROLL):
            at = step * UNROLL + lane
            row = ids_ref[at]
            for source, out in zip(rows, outs):
                out[pl.ds(at, 1), :] = source[pl.ds(row, 1), :]
        return carry

    lax.fori_loop(0, outs[0].shape[0] // UNROLL, body, 0)


def relation_rows(places, dense, scale, slices, after):
    count = places.shape[0]
    groups, depth, span = dense.shape
    n = len(slices)
    first = span // REL_PAD - n

    def columns(k):
        return pl.BlockSpec((groups, depth, REL_PAD), lambda i: (0, 0, first + k))

    return pl.pallas_call(
        functools.partial(relation_rows_kernel, slices),
        out_shape=[jax.ShapeDtypeStruct((count, LANES), F32)] * n,
        grid=(1,),
        in_specs=[whole(SMEM), whole(VMEM)]
        + [columns(k) for k in range(n)]
        + [whole(pl.ANY)] * len(after),
        out_specs=[whole(VMEM)] * n,
        scratch_shapes=[pltpu.VMEM((LANES, REL_PAD), F32)]
        + [pltpu.VMEM((groups * REL_PAD, LANES), F32)] * n,
        compiler_params=params(),
        cost_estimate=cost(0, 80e6),
        name="relation_rows",
    )(places, scale, *[dense] * n, *after)


def fetch_kernel(
    capacity, moves, ent_rows, counts_ref, place_ref, row_ref, dense_ref, *refs
):
    shard = pl.program_id(0)
    last = pl.num_programs(0) - 1
    out_ref, rows = refs[-3], refs[-2:]
    depth = dense_ref.shape[1]
    turns = ent_rows // TURN
    rest = ent_rows - turns * TURN

    if depth < LANES:

        @pl.when(shard == 0)
        def _():
            for ref in rows:
                ref[...] = jnp.zeros_like(ref)

    def turn(into, begin, size):
        cols = pl.ds(begin, size)
        into[cols, :depth] = dense_ref[0, :, cols].astype(F32).T

    def move(source, at):
        out_ref[pl.ds(place_ref[at], 1), :] = source[pl.ds(row_ref[at], 1), :]

    def step(into, source):
        base = (shard - 1) * capacity

        def remaining(first):
            def body(trip, carry):
                for lane in range(UNROLL):
                    move(source, base + first + trip * UNROLL + lane)
                return carry

            wanted = counts_ref[jnp.maximum(shard - 1, 0)] - first
            lax.fori_loop(0, (wanted + UNROLL - 1) // UNROLL, body, 0)

        def only_turn(trip, carry):
            turn(into, pl.multiple_of(trip * TURN, TURN), TURN)
            return carry

        def both(trip, carry):
            turn(into, pl.multiple_of(trip * TURN, TURN), TURN)
            for lane in range(moves):
                move(source, base + trip * moves + lane)
            return carry

        @pl.when(shard == 0)
        def _():
            lax.fori_loop(0, turns, only_turn, 0)

        @pl.when((shard > 0) & (shard < last))
        def _():
            lax.fori_loop(0, turns, both, 0)
            remaining(turns * moves)

        @pl.when(shard == last)
        def _():
            remaining(0)

        if rest:

            @pl.when(shard < last)
            def _():
                turn(into, turns * TURN, rest)

    for parity in range(2):

        @pl.when(lax.rem(shard, 2) == parity)
        def _():
            step(rows[parity], rows[1 - parity])


def fetch(counts, place_list, row_list, dense, id_count, ent_rows, after):
    groups, depth, _ = dense.shape
    capacity = place_list.shape[0] // groups
    moves = (id_count // groups) // (ent_rows // TURN) // UNROLL * UNROLL
    return pl.pallas_call(
        functools.partial(fetch_kernel, capacity, moves, ent_rows),
        out_shape=jax.ShapeDtypeStruct((id_count + 8, LANES), F32),
        grid=(groups + 1,),
        in_specs=[whole(SMEM)] * 3
        + [
            pl.BlockSpec(
                (1, depth, ent_rows), lambda shard: (jnp.minimum(shard, groups - 1), 0, 0)
            )
        ]
        + [whole(pl.ANY)] * len(after),
        out_specs=whole(VMEM),
        scratch_shapes=[pltpu.VMEM((ent_rows + 8, LANES), F32)] * 2,
        compiler_params=params(),
        cost_estimate=cost(0, 170e6),
        name="fetch_rows",
    )(counts, place_list, row_list, dense, *after)


def column_sum(values):
    return jnp.sum(values * values, axis=0, keepdims=True)


def negatives_kernel(neg_ref, low_ref, norm_ref):
    neg_t = neg_ref[...].T
    low_ref[...] = neg_t[: low_ref.shape[0]].astype(BF16)
    norm_ref[...] = column_sum(neg_t)


def negatives(fetched, depth, blocks, block_len):
    count = blocks * block_len
    return pl.pallas_call(
        negatives_kernel,
        out_shape=[
            jax.ShapeDtypeStruct((depth, count), BF16),
            jax.ShapeDtypeStruct((1, count), F32),
        ],
        grid=(blocks,),
        in_specs=[pl.BlockSpec((block_len, LANES), lambda b: (2 * blocks + b, 0))],
        out_specs=[
            pl.BlockSpec((depth, block_len), lambda b: (0, b)),
            pl.BlockSpec((1, block_len), lambda b: (0, b)),
        ],
        compiler_params=params(),
        cost_estimate=cost(0, 10e6),
        name="negatives",
    )(fetched)


def edge_parts(depth, head_ref, tail_ref, rel_ref, off_ref, tail_out):
    lane = lax.broadcasted_iota(jnp.int32, head_ref.shape, 1)
    inside = lane < depth
    rel = rel_ref[...]
    tail = tail_ref[...]
    shifted = head_ref[...] + jnp.where(inside, rel, 0.0)
    off_ref[...] = jnp.where(inside, shifted - tail, rel)
    tail_out[...] = tail.astype(BF16)
    shifted_t = shifted.T
    return shifted_t, column_sum((shifted - tail).T) - column_sum(shifted_t)


def edges_kernel(depth, head_ref, tail_ref, rel_ref, off_ref, tail_out, low_ref, bias_ref):
    shifted_t, bias = edge_parts(depth, head_ref, tail_ref, rel_ref, off_ref, tail_out)
    low_ref[...] = shifted_t[:depth].astype(BF16)
    bias_ref[...] = bias


def edges(fetched, rel_rows, depth, blocks, block_len):
    count = blocks * block_len

    def rows(at):
        return pl.BlockSpec((block_len, LANES), lambda b: (at * blocks + b, 0))

    return pl.pallas_call(
        functools.partial(edges_kernel, depth),
        out_shape=[
            jax.ShapeDtypeStruct((count, LANES), F32),
            jax.ShapeDtypeStruct((count, LANES), BF16),
            jax.ShapeDtypeStruct((depth, count), BF16),
            jax.ShapeDtypeStruct((1, count), F32),
        ],
        grid=(blocks,),
        in_specs=[rows(0), rows(1), rows(0)],
        out_specs=[
            rows(0),
            rows(0),
            pl.BlockSpec((depth, block_len), lambda b: (0, b)),
            pl.BlockSpec((1, block_len), lambda b: (0, b)),
        ],
        compiler_params=params(),
        cost_estimate=cost(0, 30e6),
        name="edges",
    )(fetched, fetched, rel_rows)


def last_rows(depth):
    return (depth + 7) // 8 * 8


def with_terms(columns, total, depth):
    place = lax.broadcasted_iota(jnp.int32, (8, total.shape[1]), 0)
    left = total
    terms = jnp.zeros(place.shape, F32)
    for k in range(TERMS):
        term = left.astype(BF16).astype(F32)
        left = left - term
        terms = jnp.where(place == k, term, terms)
    return jnp.concatenate([columns[: last_rows(depth)], terms], axis=0).astype(BF16)


def last_kernel(depth, n_given, head_ref, tail_ref, neg_ref, rel_ref, *refs):
    biases, norms = refs[:n_given], refs[n_given : 2 * n_given]
    off_ref, tail_out, pair_ref = refs[-3:]
    shifted_t, bias = edge_parts(depth, head_ref, tail_ref, rel_ref, off_ref, tail_out)
    neg_t = neg_ref[...].T
    norm = column_sum(neg_t)
    for ref in biases:
        bias = bias + ref[...]
    for ref in norms:
        norm = norm + ref[...]
    pair_ref[0] = with_terms(shifted_t, bias, depth)
    pair_ref[1] = with_terms(neg_t, norm, depth)


def last_slice(fetched, rel_rows, biases, norms, depth, blocks, block_len, half, after):
    part = blocks // HALVES
    count = part * block_len
    tall = last_rows(depth) + 8

    def rows(at):
        return pl.BlockSpec((block_len, LANES), lambda b: (at * blocks + half * part + b, 0))

    return pl.pallas_call(
        functools.partial(last_kernel, depth, len(biases)),
        out_shape=[
            jax.ShapeDtypeStruct((count, LANES), F32),
            jax.ShapeDtypeStruct((count, LANES), BF16),
            jax.ShapeDtypeStruct((2, tall, count), BF16),
        ],
        grid=(part,),
        in_specs=[rows(0), rows(1), rows(2), rows(0)]
        + [pl.BlockSpec((1, block_len), lambda b: (0, half * part + b))]
        * (len(biases) + len(norms))
        + [whole(pl.ANY)] * len(after),
        out_specs=[
            pl.BlockSpec((block_len, LANES), lambda b: (b, 0)),
            pl.BlockSpec((block_len, LANES), lambda b: (b, 0)),
            pl.BlockSpec((2, tall, block_len), lambda b: (0, 0, b)),
        ],
        compiler_params=params(),
        cost_estimate=cost(0, 20e6),
        name="last_slice",
    )(fetched, fetched, fetched, rel_rows, *biases, *norms, *after)


def block_kernel(slices, n_col, half, me_ref, live_ref, *refs):
    n = len(slices)
    per_col = 2 * n - 1
    given = [refs[k * per_col : (k + 1) * per_col] for k in range(n_col)]
    refs = refs[n_col * per_col :]
    offs, tails, refs = refs[:n], refs[n : 2 * n], refs[2 * n :]
    grad, refs = refs[-9], refs[-8:]
    loss_ref, shift_scr, neg_scr, sums_scr, cross, slopes, row_bias, row_sum = refs
    block = pl.program_id(0)
    length = cross.shape[0]
    me = me_ref[0]
    for k in range(n_col):
        slot = lax.rem(me + (n_col - k), n_col)
        for m, (start, depth) in enumerate(slices):
            if m < n - 1:
                shift, neg = given[k][2 * m][...], given[k][2 * m + 1][...]
            else:
                pair = given[k][-1]
                shift, neg = pair[0, :depth, :], pair[1, :depth, :]
                for row in range(2):
                    terms = pair[row, last_rows(depth) : last_rows(depth) + 8, :].astype(F32)
                    sums_scr[slot, row : row + 1] = jnp.sum(terms, axis=0, keepdims=True)
            shift_scr[slot, start : start + depth, :] = 2.0 * shift
            neg_scr[slot, start : start + depth, :] = neg
    bias = jnp.sum(sums_scr[:, 0, :], axis=0, keepdims=True) + MARGIN
    neg_norm = jnp.sum(sums_scr[:, 1, :], axis=0, keepdims=True)
    row_bias[...] = jnp.broadcast_to(bias, (LANES, length)).T

    live = live_ref[half * pl.num_programs(0) + block]
    tile = 256
    small = 128
    lane_tiles = [slice(at, at + LANES) for at in range(0, length, LANES)]
    cols = jnp.zeros((8, length), F32)
    loss = jnp.zeros((8, LANES), F32)
    def products(at):
        part = slice(at, at + tile)
        doubled = None
        for k in range(n_col):
            term = lax.dot_general(
                shift_scr[k, :, part], neg_scr[k], TN, preferred_element_type=F32
            )
            doubled = term if doubled is None else doubled + term
        cross[part, :] = doubled

    def moves(at):
        part = slice(at, at + tile)
        moved = lax.dot_general(slopes[part, :], neg_scr[me], NT, preferred_element_type=F32)
        fade = -row_sum[part, :]
        for m, (start, depth) in enumerate(slices):
            into = pl.ds(n * at + m, tile, stride=n)
            grad[0, into, :depth] = (
                fade[:, :depth] * tails[m][part, :depth].astype(F32)
                + moved[:, start : start + depth]
            )
            grad[1, into, :] = fade * offs[m][part, :]

    products(0)
    for begin in range(0, length, tile):
        if begin + tile < length:
            products(begin + tile)
        for at in range(begin, begin + tile, small):
            part = slice(at, at + small)
            place = at + lax.broadcasted_iota(jnp.int32, (small, 1), 0)
            scale = offs[-1][part, LANES - 1 : LANES]
            weight = jnp.where(place < live, scale, 0.0) / length
            margins = cross[part, :] + (row_bias[part, 0:1] - neg_norm)
            fall = jnp.exp(-jnp.abs(margins))
            under = 1.0 + fall
            guess = pl.reciprocal(under, approx=True)
            inverse = guess * (2.0 - under * guess)
            twice = (2.0 * weight) * (jnp.where(margins >= 0.0, 1.0, fall) * inverse)
            row_sum[part, :] = jnp.broadcast_to(
                jnp.sum(twice, axis=1, keepdims=True), (small, LANES)
            )
            slopes[part, :] = twice.astype(BF16)
            cols = cols + jnp.sum(twice.reshape(small // 8, 8, length), axis=0)
            over = jnp.maximum(margins, 0.0)
            lifts = [fall[:, lanes] for lanes in lane_tiles]
            while len(lifts) > 1:
                lifts = [a + b + a * b for a, b in zip(lifts[::2], lifts[1::2])]
            lift = lifts[0]
            soft = functools.reduce(jnp.add, [over[:, lanes] for lanes in lane_tiles]) + jnp.where(
                lift < 2.0**-11, lift * (1.0 - 0.5 * lift), jnp.log(1.0 + lift)
            )
            loss = loss + jnp.sum((weight * soft).reshape(small // 8, 8, LANES), axis=0)
        moves(begin)
    col_sum = jnp.sum(cols, axis=0, keepdims=True)

    @pl.when(block == 0)
    def _():
        loss_ref[...] = loss

    @pl.when(block > 0)
    def _():
        loss_ref[...] += loss

    moved = lax.dot_general(shift_scr[me], slopes[...], NN, preferred_element_type=F32)
    moved = 0.5 * moved - col_sum * neg_scr[me].astype(F32)
    for m, (start, depth) in enumerate(slices):
        grad[2, pl.ds(m, length, stride=n), :depth] = moved[start : start + depth, :].T


def block_math(me, live_counts, given, offs, tails, old, slices, block_len, half, after):
    n, n_col = len(slices), len(given)
    blocks = live_counts.shape[0]
    part = blocks // HALVES
    width = sum(depth for _, depth in slices)
    flat = [piece for per_col in given for piece in per_col]
    kept = [] if old is None else [old]

    def columns(piece):
        if piece.ndim == 3:
            return pl.BlockSpec((2, piece.shape[1], block_len), lambda b: (0, 0, b))
        return pl.BlockSpec((piece.shape[0], block_len), lambda b: (0, half * part + b))

    def rows(array):
        first = half * part if array.shape[0] > part * block_len else 0
        return pl.BlockSpec((block_len, LANES), lambda b: (first + b, 0))

    first_old = 2 + len(flat) + 2 * n
    return pl.pallas_call(
        functools.partial(block_kernel, slices, n_col, half),
        out_shape=[
            jax.ShapeDtypeStruct((3, n * blocks * block_len, LANES), F32),
            jax.ShapeDtypeStruct((8, LANES), F32),
        ],
        grid=(part,),
        in_specs=[whole(SMEM)] * 2
        + [columns(piece) for piece in flat]
        + [rows(array) for array in offs + tails]
        + [whole(pl.ANY)] * len(kept + after),
        out_specs=[
            pl.BlockSpec((3, n * block_len, LANES), lambda b: (0, half * part + b, 0)),
            pl.BlockSpec((8, LANES), lambda b: (0, 0)),
        ],
        input_output_aliases={first_old + k: k for k in range(len(kept))},
        scratch_shapes=[
            pltpu.VMEM((n_col, width, block_len), BF16),
            pltpu.VMEM((n_col, width, block_len), BF16),
            pltpu.VMEM((n_col, 2, block_len), F32),
            pltpu.VMEM((block_len, block_len), F32),
            pltpu.VMEM((block_len, block_len), BF16),
            pltpu.VMEM((block_len, LANES), F32),
            pltpu.VMEM((block_len, LANES), F32),
        ],
        compiler_params=params(),
        cost_estimate=cost(part * 8 * block_len * block_len * width, 120e6),
        name="block_math",
    )(me, live_counts, *flat, *offs, *tails, *kept, *after)


def pair_of(row, n):
    return pl.ds(pl.multiple_of(row * n, n), n)


def outgoing_kernel(slices, capacity, begin, counts_ref, place_ref, grad, *refs):
    n = len(slices)
    out_ref, tile = refs[-2:]
    groups, width, chunk = out_ref.shape

    def owner(group, carry):
        wanted = jnp.clip(counts_ref[group] - begin, 0, chunk)

        def body(step, inner):
            for lane in range(UNROLL):
                at = step * UNROLL + lane
                place = place_ref[group * capacity + begin + at]
                tile[pair_of(at, n), :] = grad[pair_of(place, n), :]
            return inner

        lax.fori_loop(0, (wanted + UNROLL - 1) // UNROLL, body, 0)
        for m, (start, depth) in enumerate(slices):
            piece = tile[pl.ds(m, chunk, stride=n), :].T
            out_ref[group, start : start + depth, :] = piece[:depth].astype(BF16)
        return carry

    lax.fori_loop(0, groups, owner, 0)


def outgoing(counts, place_list, grad, slices, begin, chunk, after):
    groups, capacity = place_list.shape
    n = len(slices)
    width = sum(depth for _, depth in slices)
    return pl.pallas_call(
        functools.partial(outgoing_kernel, slices, capacity, begin),
        out_shape=jax.ShapeDtypeStruct((groups, width, chunk), BF16),
        in_specs=[whole(SMEM)] * 2 + [whole(VMEM)] + [whole(pl.ANY)] * len(after),
        out_specs=whole(VMEM),
        scratch_shapes=[pltpu.VMEM((n * chunk, LANES), F32)],
        compiler_params=params(),
        cost_estimate=cost(0, 80e6),
        name="outgoing",
    )(counts, place_list.reshape(-1), grad, *after)


def collect_kernel(slices, capacity, begin, first, counts_ref, row_ref, came_ref, *refs):
    n = len(slices)
    total, tile = refs[-2:]
    groups, width, chunk = came_ref.shape
    total[...] = jnp.zeros_like(total) if first else refs[0][...]

    def source(group, carry):
        wanted = jnp.clip(counts_ref[group] - begin, 0, chunk)

        @pl.when(wanted > 0)
        def _():
            for m, (start, depth) in enumerate(slices):
                piece = came_ref[group, start : start + depth, :].astype(F32)
                tile[pl.ds(m, chunk, stride=n), :depth] = piece.T

            def body(step, inner):
                for lane in range(UNROLL):
                    at = step * UNROLL + lane
                    into = pair_of(row_ref[group * capacity + begin + at], n)
                    total[into, :] = total[into, :] + tile[pair_of(at, n), :]
                return inner

            lax.fori_loop(0, (wanted + UNROLL - 1) // UNROLL, body, 0)

        return carry

    lax.fori_loop(0, groups, source, 0)


def collect(counts, row_list, came, total, slices, begin, ent_rows, after):
    capacity = row_list.shape[1]
    chunk = came.shape[2]
    n = len(slices)
    given = [] if total is None else [total]
    return pl.pallas_call(
        functools.partial(collect_kernel, slices, capacity, begin, total is None),
        out_shape=jax.ShapeDtypeStruct((n * (ent_rows + 8), LANES), F32),
        in_specs=[whole(SMEM)] * 2
        + [whole(VMEM)] * (1 + len(given))
        + [whole(pl.ANY)] * len(after),
        out_specs=whole(VMEM),
        scratch_shapes=[pltpu.VMEM((n * chunk, LANES), F32)],
        compiler_params=params(),
        cost_estimate=cost(0, 120e6),
        name="collect",
    )(counts, row_list.reshape(-1), came, *given, *after)


def relation_sums_kernel(n, ids_ref, grad, *refs):
    total = refs[-1]
    total[...] = jnp.zeros_like(total)

    def body(step, carry):
        for lane in range(UNROLL):
            at = step * UNROLL + lane
            into = pair_of(ids_ref[at], n)
            total[into, :] = total[into, :] + grad[0, pair_of(at, n), :]
        return carry

    lax.fori_loop(0, grad.shape[1] // n // UNROLL, body, 0)


def relation_sums(relation_ids, grad, n, rel_total, after):
    count = relation_ids.shape[0]
    return pl.pallas_call(
        functools.partial(relation_sums_kernel, n),
        out_shape=jax.ShapeDtypeStruct((n * rel_total, LANES), F32),
        grid=(1,),
        in_specs=[whole(SMEM), pl.BlockSpec((1, n * count, LANES), lambda i: (0, 0, 0))]
        + [whole(pl.ANY)] * len(after),
        out_specs=whole(VMEM),
        compiler_params=params(),
        cost_estimate=cost(0, 120e6),
        name="relation_sums",
    )(relation_ids, grad, *after)


def update_kernel(slices, weights_ref, first_ref, second_ref, total, *refs):
    n = len(slices)
    outs, scr = refs[:3], refs[3]
    cols = weights_ref.shape[1]
    for m, (start, depth) in enumerate(slices):
        scr[start : start + depth, :] = total[pl.ds(m, cols, stride=n), :].T[:depth]
    results = adamw_update(weights_ref[...], scr[...], first_ref[...], second_ref[...])
    for out, result in zip(outs, results):
        out[...] = result


def update_entities(weights, total, first, second, slices):
    width, ent_rows = weights.shape
    cols = 1024
    n = len(slices)
    table = pl.BlockSpec((width, cols), lambda i: (0, i))
    return pl.pallas_call(
        functools.partial(update_kernel, slices),
        out_shape=[jax.ShapeDtypeStruct((width, ent_rows), F32)] * 3,
        grid=(pl.cdiv(ent_rows, cols),),
        in_specs=[table] * 3 + [pl.BlockSpec((n * cols, LANES), lambda i: (i, 0))],
        out_specs=[table] * 3,
        scratch_shapes=[pltpu.VMEM((width, cols), F32)],
        compiler_params=params(),
        cost_estimate=cost(0, 60e6),
        name="update_entities",
    )(weights, first, second, total)


def add_across(value, groups, step):
    turn = [(g, g ^ step) for g in range(groups)]
    return value + lax.ppermute(value, "edge", turn)


def chunk_bounds(capacity):
    units = capacity // LANES
    sizes = [3, 6, 5, 2] if units == 16 else [units // 4] * 3 + [units - 3 * (units // 4)]
    bounds = [0]
    for size in sizes:
        bounds.append(bounds[-1] + size * LANES)
    return bounds


def shards(
    head_ids,
    relation_ids,
    tail_ids,
    negative_ids,
    live_counts,
    rel_weight,
    rel_count,
    entity_table,
    entity_first,
    entity_second,
    relation_table,
    relation_first,
    relation_second,
):
    groups = lax.axis_size("edge")
    n_col = lax.axis_size("col")
    width, ent_rows = entity_table.shape
    blocks, neg_count = negative_ids.shape
    block_len = head_ids.shape[0] // blocks
    edge_count = blocks * block_len
    slices = width_slices(width)
    n = len(slices)
    all_ids = jnp.concatenate([head_ids, tail_ids, negative_ids.reshape(-1)])
    id_count = all_ids.shape[0]
    capacity = (4 * id_count + 3 * groups - 1) // (3 * groups)
    rel_total = rel_weight.shape[0]

    rel_own = rel_total // groups
    rel_low = jnp.pad(relation_table.astype(BF16).T, ((0, 0), (0, REL_PAD - rel_own)))
    dense = []
    for k, (start, depth) in enumerate(slices):
        sent = entity_table[start : start + depth].astype(BF16)
        if k == 0:
            behind = [
                jnp.pad(rel_low[at : at + size], ((0, depth - size), (0, 0))) for at, size in slices
            ]
            sent = jnp.concatenate([sent] + behind, axis=1)
        dense.append(lax.all_gather(sent, "edge", axis=0, tiled=False))

    place_list, row_list, counts = owner_lists(all_ids, groups, capacity, ent_rows)
    asked = lax.all_to_all(row_list, "edge", split_axis=0, concat_axis=0, tiled=True)
    asked_counts = jnp.sum((asked < ent_rows).astype(jnp.int32), axis=1)
    safe_places = jnp.minimum(place_list, id_count - 1)
    place_flat, row_flat = place_list.reshape(-1), row_list.reshape(-1)

    rel_scale = rel_weight * (rel_total / jnp.sum(rel_weight)) / rel_count.astype(F32)
    rel_scale = jnp.pad(rel_scale.reshape(groups, rel_own), ((0, 0), (0, REL_PAD - rel_own)))
    rel_places = relation_ids + (relation_ids // rel_own) * (REL_PAD - rel_own)

    def from_others(array):
        turns = [[(c, (c + away) % n_col) for c in range(n_col)] for away in range(1, n_col)]
        return [lax.ppermute(array, "col", turn) for turn in turns]

    me = lax.axis_index("col").astype(jnp.int32).reshape(1)
    given = [[[] for _ in range(n_col)] for _ in range(HALVES)]
    offs = [[] for _ in range(HALVES)]
    tails = [[] for _ in range(HALVES)]
    biases, norms, first_sent, rel_rows = [], [], [], None
    for k, (start, depth) in enumerate(slices):
        early = first_sent if k > 0 else [asked]
        fetched = fetch(counts, place_flat, row_flat, dense[k], id_count, ent_rows, early)
        if k < n - 1:
            neg_low, norm = negatives(fetched, depth, blocks, block_len)
            neg_all = [neg_low] + from_others(neg_low)
            if rel_rows is None:
                rel_rows = relation_rows(rel_places, dense[0], rel_scale, slices, [neg_low])
            off, tail, low, bias = edges(fetched, rel_rows[k], depth, blocks, block_len)
            low_all = [low] + from_others(low)
            first_sent = neg_all[1:]
            biases.append(bias)
            norms.append(norm)
            for half in range(HALVES):
                offs[half].append(off)
                tails[half].append(tail)
                for col in range(n_col):
                    given[half][col] += [low_all[col], neg_all[col]]
            continue
        if rel_rows is None:
            rel_rows = relation_rows(rel_places, dense[0], rel_scale, slices, [])

    def finish(half, after):
        off, tail, pair = last_slice(
            fetched, rel_rows[-1], biases, norms, slices[-1][1], blocks, block_len, half, after
        )
        offs[half].append(off)
        tails[half].append(tail)
        for col, piece in enumerate([pair] + from_others(pair)):
            given[half][col].append(piece)

    grad, loss_tiles = None, []
    finish(0, [])
    for half in range(HALVES):
        after = []
        if half + 1 < HALVES:
            finish(half + 1, [given[half][-1][-1]] + loss_tiles[-1:])
            after = offs[half + 1][-1:]
        grad, loss_tile = block_math(
            me,
            live_counts,
            given[half],
            offs[half],
            tails[half],
            grad,
            slices,
            block_len,
            half,
            after,
        )
        loss_tiles.append(loss_tile)
    live = jnp.sum(jnp.minimum(live_counts, block_len)).astype(F32)
    loss_own = jnp.sum(functools.reduce(jnp.add, loss_tiles))
    lane = jnp.arange(LANES, dtype=jnp.int32)[None, :]
    loss_row = jnp.where(lane == 0, loss_own, jnp.where(lane == 1, live, 0.0))
    step = 1
    loss_rows = []
    while step < groups:
        loss_row = add_across(loss_row, groups, step)
        loss_rows.append(loss_row)
        step *= 2

    def loss_step(k):
        return loss_rows[min(k, len(loss_rows) - 1)]

    flat = grad.reshape(n * id_count, LANES)
    bounds = chunk_bounds(capacity)
    chunks = len(bounds) - 1
    arrived, total, after = [], None, []
    for k in range(chunks):
        after = after + [loss_step(0)] if k == 1 else after
        sent = outgoing(
            counts, safe_places, flat, slices, bounds[k], bounds[k + 1] - bounds[k], after
        )
        arrived.append(lax.all_to_all(sent, "edge", split_axis=0, concat_axis=0, tiled=True))
        after = []
        if k == 1:
            rel_terms = relation_sums(
                relation_ids, grad, n, rel_total, [arrived[0], loss_step(1)]
            )
            after = [rel_terms, loss_step(2)]
            rel_terms = rel_terms.reshape(rel_total, n * LANES)[:, :width]
            relation_grad = lax.psum_scatter(rel_terms, "edge", scatter_dimension=0, tiled=True)
        if k == chunks - 1:
            after = [relation_grad]
        if k > 0:
            total = collect(
                asked_counts, asked, arrived[k - 1], total, slices, bounds[k - 1], ent_rows, after
            )
            after = [total, rel_terms, loss_step(3)]
    k = chunks - 1
    total = collect(asked_counts, asked, arrived[k], total, slices, bounds[k], ent_rows, [])
    loss_pair = loss_step(groups)[0, :2]

    new_entity, new_entity_first, new_entity_second = update_entities(
        entity_table, total, entity_first, entity_second, slices
    )
    new_relation, new_relation_first, new_relation_second = adamw_update(
        relation_table, relation_grad, relation_first, relation_second
    )
    return (
        loss_pair,
        new_entity,
        new_entity_first,
        new_entity_second,
        new_relation,
        new_relation_first,
        new_relation_second,
    )


def solution(mesh):
    placed = (
        P("edge"),
        P("edge"),
        P("edge"),
        P("edge", None),
        P("edge"),
        P(),
        P(),
        P("col", "edge"),
        P("col", "edge"),
        P("col", "edge"),
        P("edge", "col"),
        P("edge", "col"),
        P("edge", "col"),
    )
    return jax.shard_map(
        shards,
        mesh=mesh,
        in_specs=placed,
        out_specs=(
            P(),
            P("col", "edge"),
            P("col", "edge"),
            P("col", "edge"),
            P("edge", "col"),
            P("edge", "col"),
            P("edge", "col"),
        ),
        check_vma=False,
    )
```

```python
import functools

import jax
import jax.numpy as jnp
from jax import lax
from jax.experimental import pallas as pl
from jax.experimental.pallas import tpu as pltpu
from jax.sharding import PartitionSpec as P

STEP = 5


MARGIN = 0.1
LEARN_RATE = 0.1
BETA_ONE = 0.5
BETA_TWO = 0.5
EPSILON = 1e-08
DECAY = 0.01
LANES = 128
UNROLL = 8
PARTS = 4
HALVES = 2
EARLY = 96
TURN = 512
REL_PAD = 256
TERMS = 3
NN = (((1,), (0,)), ((), ()))
NT = (((1,), (1,)), ((), ()))
TN = (((0,), (0,)), ((), ()))
F32 = jnp.float32
BF16 = jnp.bfloat16
SMEM = pltpu.SMEM
VMEM = pltpu.VMEM


def params():
    return pltpu.CompilerParams(vmem_limit_bytes=60 << 20)


def cost(flops, moved):
    return pl.CostEstimate(flops=int(flops), bytes_accessed=int(moved), transcendentals=0)


def whole(space):
    return pl.BlockSpec(memory_space=space)


def adamw_update(weights, gradient, first, second):
    new_first = BETA_ONE * first + (1.0 - BETA_ONE) * gradient
    new_second = BETA_TWO * second + (1.0 - BETA_TWO) * gradient * gradient
    first_hat = new_first / (1.0 - BETA_ONE**STEP)
    second_hat = new_second / (1.0 - BETA_TWO**STEP)
    updated = weights - LEARN_RATE * (
        first_hat / (jnp.sqrt(second_hat) + EPSILON) + DECAY * weights
    )
    return (updated, new_first, new_second)


def width_slices(width):
    return [(at, min(LANES, width - at)) for at in range(0, width, LANES)]


def owner_lists(all_ids, groups, capacity, ent_rows):
    count = all_ids.shape[0]
    owners = all_ids // ent_rows
    local_rows = all_ids - owners * ent_rows
    chunk = 256
    mine = owners[None, :] == jnp.arange(groups, dtype=jnp.int32)[:, None]
    mine = mine.astype(BF16).reshape(groups, count // chunk, chunk)
    before = jnp.triu(jnp.ones((chunk, chunk), BF16), 1)
    inner = jnp.dot(mine, before, preferred_element_type=F32)
    sums = jnp.sum(mine.astype(F32), axis=2)
    carry = jnp.cumsum(sums, axis=1) - sums
    ranks = jnp.sum(mine.astype(F32) * (inner + carry[:, :, None]), axis=0)
    ranks = ranks.astype(jnp.int32).reshape(count)
    counts = jnp.sum(sums, axis=1).astype(jnp.int32)
    high = owners * (capacity // LANES) + ranks // LANES
    low = ranks % LANES
    tall = groups * capacity // LANES
    left = (jnp.arange(tall, dtype=jnp.int32)[:, None] == high[None, :]).astype(BF16)
    right = (jnp.arange(LANES, dtype=jnp.int32)[:, None] == low[None, :]).astype(BF16)
    places = jnp.arange(1, count + 1, dtype=jnp.int32)
    parts = jnp.stack([places // 256, places % 256, local_rows // 256, local_rows % 256])
    right = (parts.astype(BF16)[:, None, :] * right[None]).reshape(PARTS * LANES, count)
    found = lax.dot_general(left, right, NT, preferred_element_type=F32).astype(jnp.int32)
    found = found.reshape(tall, PARTS, LANES)
    place = found[:, 0] * 256 + found[:, 1]
    place_list = jnp.where(place > 0, place - 1, count).reshape(groups, capacity)
    row_list = jnp.where(place > 0, found[:, 2] * 256 + found[:, 3], ent_rows)
    return place_list, row_list.reshape(groups, capacity), counts


def relation_rows_kernel(slices, ids_ref, scale_ref, *refs):
    n = len(slices)
    tables, outs = refs[:n], refs[-2 * n - 1 : -n - 1]
    columns, rows = refs[-n - 1], refs[-n:]
    groups = tables[0].shape[0]
    for (_, depth), table, into in zip(slices, tables, rows):
        columns[...] = jnp.zeros_like(columns)

        def turn(group, carry):
            columns[:depth, :] = table[group, :depth].astype(F32)
            if depth < LANES:
                columns[LANES - 1 :, :] = scale_ref[pl.ds(group, 1), :]
            into[pl.ds(pl.multiple_of(group * REL_PAD, REL_PAD), REL_PAD), :] = columns[...].T
            return carry

        lax.fori_loop(0, groups, turn, 0, unroll=4)

    def body(step, carry):
        for lane in range(UNROLL):
            at = step * UNROLL + lane
            row = ids_ref[at]
            for source, out in zip(rows, outs):
                out[pl.ds(at, 1), :] = source[pl.ds(row, 1), :]
        return carry

    lax.fori_loop(0, outs[0].shape[0] // UNROLL, body, 0)


def relation_rows(places, dense, scale, slices, after):
    count = places.shape[0]
    groups, depth, span = dense.shape
    n = len(slices)
    first = span // REL_PAD - n

    def columns(k):
        return pl.BlockSpec((groups, depth, REL_PAD), lambda i: (0, 0, first + k))

    return pl.pallas_call(
        functools.partial(relation_rows_kernel, slices),
        out_shape=[jax.ShapeDtypeStruct((count, LANES), F32)] * n,
        grid=(1,),
        in_specs=[whole(SMEM), whole(VMEM)]
        + [columns(k) for k in range(n)]
        + [whole(pl.ANY)] * len(after),
        out_specs=[whole(VMEM)] * n,
        scratch_shapes=[pltpu.VMEM((LANES, REL_PAD), F32)]
        + [pltpu.VMEM((groups * REL_PAD, LANES), F32)] * n,
        compiler_params=params(),
        cost_estimate=cost(0, 80e6),
        name="relation_rows",
    )(places, scale, *[dense] * n, *after)


def fetch_kernel(
    capacity, moves, ent_rows, counts_ref, place_ref, row_ref, dense_ref, *refs
):
    shard = pl.program_id(0)
    last = pl.num_programs(0) - 1
    out_ref, rows = refs[-3], refs[-2:]
    depth = dense_ref.shape[1]
    turns = ent_rows // TURN
    rest = ent_rows - turns * TURN

    if depth < LANES:

        @pl.when(shard == 0)
        def _():
            for ref in rows:
                ref[...] = jnp.zeros_like(ref)

    def turn(into, begin, size):
        cols = pl.ds(begin, size)
        into[cols, :depth] = dense_ref[0, :, cols].astype(F32).T

    def move(source, at):
        out_ref[pl.ds(place_ref[at], 1), :] = source[pl.ds(row_ref[at], 1), :]

    def step(into, source):
        base = (shard - 1) * capacity

        def remaining(first):
            def body(trip, carry):
                for lane in range(UNROLL):
                    move(source, base + first + trip * UNROLL + lane)
                return carry

            wanted = counts_ref[jnp.maximum(shard - 1, 0)] - first
            lax.fori_loop(0, (wanted + UNROLL - 1) // UNROLL, body, 0)

        def only_turn(trip, carry):
            turn(into, pl.multiple_of(trip * TURN, TURN), TURN)
            return carry

        def both(trip, carry):
            turn(into, pl.multiple_of(trip * TURN, TURN), TURN)
            for lane in range(moves):
                move(source, base + trip * moves + lane)
            return carry

        @pl.when(shard == 0)
        def _():
            lax.fori_loop(0, turns, only_turn, 0)

        @pl.when((shard > 0) & (shard < last))
        def _():
            lax.fori_loop(0, turns, both, 0)
            remaining(turns * moves)

        @pl.when(shard == last)
        def _():
            remaining(0)

        if rest:

            @pl.when(shard < last)
            def _():
                turn(into, turns * TURN, rest)

    for parity in range(2):

        @pl.when(lax.rem(shard, 2) == parity)
        def _():
            step(rows[parity], rows[1 - parity])


def fetch(counts, place_list, row_list, dense, id_count, ent_rows, after):
    groups, depth, _ = dense.shape
    capacity = place_list.shape[0] // groups
    moves = (id_count // groups) // (ent_rows // TURN) // UNROLL * UNROLL
    return pl.pallas_call(
        functools.partial(fetch_kernel, capacity, moves, ent_rows),
        out_shape=jax.ShapeDtypeStruct((id_count + 8, LANES), F32),
        grid=(groups + 1,),
        in_specs=[whole(SMEM)] * 3
        + [
            pl.BlockSpec(
                (1, depth, ent_rows), lambda shard: (jnp.minimum(shard, groups - 1), 0, 0)
            )
        ]
        + [whole(pl.ANY)] * len(after),
        out_specs=whole(VMEM),
        scratch_shapes=[pltpu.VMEM((ent_rows + 8, LANES), F32)] * 2,
        compiler_params=params(),
        cost_estimate=cost(0, 170e6),
        name="fetch_rows",
    )(counts, place_list, row_list, dense, *after)


def column_sum(values):
    return jnp.sum(values * values, axis=0, keepdims=True)


def negatives_kernel(neg_ref, early_ref, late_ref, norm_ref):
    neg_t = neg_ref[...].T
    early_ref[...] = neg_t[:EARLY].astype(BF16)
    late_ref[...] = neg_t[EARLY:].astype(BF16)
    norm_ref[...] = column_sum(neg_t)


def negatives(fetched, blocks, block_len):
    count = blocks * block_len
    return pl.pallas_call(
        negatives_kernel,
        out_shape=[
            jax.ShapeDtypeStruct((EARLY, count), BF16),
            jax.ShapeDtypeStruct((LANES - EARLY, count), BF16),
            jax.ShapeDtypeStruct((1, count), F32),
        ],
        grid=(blocks,),
        in_specs=[pl.BlockSpec((block_len, LANES), lambda b: (2 * blocks + b, 0))],
        out_specs=[
            pl.BlockSpec((EARLY, block_len), lambda b: (0, b)),
            pl.BlockSpec((LANES - EARLY, block_len), lambda b: (0, b)),
            pl.BlockSpec((1, block_len), lambda b: (0, b)),
        ],
        compiler_params=params(),
        cost_estimate=cost(0, 10e6),
        name="negatives",
    )(fetched)


def edge_parts(depth, head_ref, tail_ref, rel_ref, off_ref, tail_out):
    lane = lax.broadcasted_iota(jnp.int32, head_ref.shape, 1)
    inside = lane < depth
    rel = rel_ref[...]
    tail = tail_ref[...]
    shifted = head_ref[...] + jnp.where(inside, rel, 0.0)
    off_ref[...] = jnp.where(inside, shifted - tail, rel)
    tail_out[...] = tail.astype(BF16)
    shifted_t = shifted.T
    return shifted_t, column_sum((shifted - tail).T) - column_sum(shifted_t)


def edges_kernel(
    depth, head_ref, tail_ref, rel_ref, late_ref, off_ref, tail_out, low_ref, bias_ref
):
    shifted_t, bias = edge_parts(depth, head_ref, tail_ref, rel_ref, off_ref, tail_out)
    low_ref[:depth] = shifted_t[:depth].astype(BF16)
    low_ref[depth:] = late_ref[...]
    bias_ref[...] = bias


def edges(fetched, rel_rows, late, depth, blocks, block_len):
    count = blocks * block_len
    tall = depth + late.shape[0]

    def rows(at):
        return pl.BlockSpec((block_len, LANES), lambda b: (at * blocks + b, 0))

    return pl.pallas_call(
        functools.partial(edges_kernel, depth),
        out_shape=[
            jax.ShapeDtypeStruct((count, LANES), F32),
            jax.ShapeDtypeStruct((count, LANES), BF16),
            jax.ShapeDtypeStruct((tall, count), BF16),
            jax.ShapeDtypeStruct((1, count), F32),
        ],
        grid=(blocks,),
        in_specs=[rows(0), rows(1), rows(0)]
        + [pl.BlockSpec((tall - depth, block_len), lambda b: (0, b))],
        out_specs=[
            rows(0),
            rows(0),
            pl.BlockSpec((tall, block_len), lambda b: (0, b)),
            pl.BlockSpec((1, block_len), lambda b: (0, b)),
        ],
        compiler_params=params(),
        cost_estimate=cost(0, 30e6),
        name="edges",
    )(fetched, fetched, rel_rows, late)


def last_rows(depth):
    return (depth + 7) // 8 * 8


def with_terms(columns, total, depth):
    place = lax.broadcasted_iota(jnp.int32, (8, total.shape[1]), 0)
    left = total
    terms = jnp.zeros(place.shape, F32)
    for k in range(TERMS):
        term = left.astype(BF16).astype(F32)
        left = left - term
        terms = jnp.where(place == k, term, terms)
    return jnp.concatenate([columns[: last_rows(depth)], terms], axis=0).astype(BF16)


def last_kernel(depth, n_given, head_ref, tail_ref, neg_ref, rel_ref, *refs):
    biases, norms = refs[:n_given], refs[n_given : 2 * n_given]
    off_ref, tail_out, pair_ref = refs[-3:]
    shifted_t, bias = edge_parts(depth, head_ref, tail_ref, rel_ref, off_ref, tail_out)
    neg_t = neg_ref[...].T
    norm = column_sum(neg_t)
    for ref in biases:
        bias = bias + ref[...]
    for ref in norms:
        norm = norm + ref[...]
    pair_ref[0] = with_terms(shifted_t, bias, depth)
    pair_ref[1] = with_terms(neg_t, norm, depth)


def last_slice(fetched, rel_rows, biases, norms, depth, blocks, block_len, half, after):
    part = blocks // HALVES
    count = part * block_len
    tall = last_rows(depth) + 8

    def rows(at):
        return pl.BlockSpec((block_len, LANES), lambda b: (at * blocks + half * part + b, 0))

    return pl.pallas_call(
        functools.partial(last_kernel, depth, len(biases)),
        out_shape=[
            jax.ShapeDtypeStruct((count, LANES), F32),
            jax.ShapeDtypeStruct((count, LANES), BF16),
            jax.ShapeDtypeStruct((2, tall, count), BF16),
        ],
        grid=(part,),
        in_specs=[rows(0), rows(1), rows(2), rows(0)]
        + [pl.BlockSpec((1, block_len), lambda b: (0, half * part + b))]
        * (len(biases) + len(norms))
        + [whole(pl.ANY)] * len(after),
        out_specs=[
            pl.BlockSpec((block_len, LANES), lambda b: (b, 0)),
            pl.BlockSpec((block_len, LANES), lambda b: (b, 0)),
            pl.BlockSpec((2, tall, block_len), lambda b: (0, 0, b)),
        ],
        compiler_params=params(),
        cost_estimate=cost(0, 20e6),
        name="last_slice",
    )(fetched, fetched, fetched, rel_rows, *biases, *norms, *after)


def block_kernel(slices, n_col, half, me_ref, live_ref, *refs):
    n = len(slices)
    per_col = 2 * n - 1
    given = [refs[k * per_col : (k + 1) * per_col] for k in range(n_col)]
    refs = refs[n_col * per_col :]
    offs, tails, refs = refs[:n], refs[n : 2 * n], refs[2 * n :]
    grad, refs = refs[-9], refs[-8:]
    loss_ref, shift_scr, neg_scr, sums_scr, cross, slopes, row_bias, row_sum = refs
    block = pl.program_id(0)
    length = cross.shape[0]
    me = me_ref[0]
    for k in range(n_col):
        slot = lax.rem(me + (n_col - k), n_col)
        for m, (start, depth) in enumerate(slices):
            if m < n - 1:
                early, late = given[k][2 * m : 2 * m + 2]
                shift_scr[slot, start : start + depth, :] = 2.0 * late[:depth, :]
                neg_scr[slot, start : start + EARLY, :] = early[...]
                neg_scr[slot, start + EARLY : start + depth, :] = late[depth:, :]
            else:
                pair = given[k][-1]
                shift, neg = pair[0, :depth, :], pair[1, :depth, :]
                for row in range(2):
                    terms = pair[row, last_rows(depth) : last_rows(depth) + 8, :].astype(F32)
                    sums_scr[slot, row : row + 1] = jnp.sum(terms, axis=0, keepdims=True)
                shift_scr[slot, start : start + depth, :] = 2.0 * shift
                neg_scr[slot, start : start + depth, :] = neg
    bias = jnp.sum(sums_scr[:, 0, :], axis=0, keepdims=True) + MARGIN
    neg_norm = jnp.sum(sums_scr[:, 1, :], axis=0, keepdims=True)
    row_bias[...] = jnp.broadcast_to(bias, (LANES, length)).T

    live = live_ref[half * pl.num_programs(0) + block]
    tile = 256
    small = 128
    lane_tiles = [slice(at, at + LANES) for at in range(0, length, LANES)]
    cols = jnp.zeros((8, length), F32)
    loss = jnp.zeros((8, LANES), F32)
    def products(at):
        part = slice(at, at + tile)
        doubled = None
        for k in range(n_col):
            term = lax.dot_general(
                shift_scr[k, :, part], neg_scr[k], TN, preferred_element_type=F32
            )
            doubled = term if doubled is None else doubled + term
        cross[part, :] = doubled

    def moves(at):
        part = slice(at, at + tile)
        moved = lax.dot_general(slopes[part, :], neg_scr[me], NT, preferred_element_type=F32)
        fade = -row_sum[part, :]
        for m, (start, depth) in enumerate(slices):
            into = pl.ds(n * at + m, tile, stride=n)
            grad[0, into, :depth] = (
                fade[:, :depth] * tails[m][part, :depth].astype(F32)
                + moved[:, start : start + depth]
            )
            grad[1, into, :] = fade * offs[m][part, :]

    products(0)
    for begin in range(0, length, tile):
        if begin + tile < length:
            products(begin + tile)
        for at in range(begin, begin + tile, small):
            part = slice(at, at + small)
            place = at + lax.broadcasted_iota(jnp.int32, (small, 1), 0)
            scale = offs[-1][part, LANES - 1 : LANES]
            weight = jnp.where(place < live, scale, 0.0) / length
            margins = cross[part, :] + (row_bias[part, 0:1] - neg_norm)
            fall = jnp.exp(-jnp.abs(margins))
            under = 1.0 + fall
            guess = pl.reciprocal(under, approx=True)
            inverse = guess * (2.0 - under * guess)
            twice = (2.0 * weight) * (jnp.where(margins >= 0.0, 1.0, fall) * inverse)
            row_sum[part, :] = jnp.broadcast_to(
                jnp.sum(twice, axis=1, keepdims=True), (small, LANES)
            )
            slopes[part, :] = twice.astype(BF16)
            cols = cols + jnp.sum(twice.reshape(small // 8, 8, length), axis=0)
            over = jnp.maximum(margins, 0.0)
            lifts = [fall[:, lanes] for lanes in lane_tiles]
            while len(lifts) > 1:
                lifts = [a + b + a * b for a, b in zip(lifts[::2], lifts[1::2])]
            lift = lifts[0]
            soft = functools.reduce(jnp.add, [over[:, lanes] for lanes in lane_tiles]) + jnp.where(
                lift < 2.0**-11, lift * (1.0 - 0.5 * lift), jnp.log(1.0 + lift)
            )
            loss = loss + jnp.sum((weight * soft).reshape(small // 8, 8, LANES), axis=0)
        moves(begin)
    col_sum = jnp.sum(cols, axis=0, keepdims=True)

    @pl.when(block == 0)
    def _():
        loss_ref[...] = loss

    @pl.when(block > 0)
    def _():
        loss_ref[...] += loss

    moved = lax.dot_general(shift_scr[me], slopes[...], NN, preferred_element_type=F32)
    moved = 0.5 * moved - col_sum * neg_scr[me].astype(F32)
    for m, (start, depth) in enumerate(slices):
        grad[2, pl.ds(m, length, stride=n), :depth] = moved[start : start + depth, :].T


def block_math(me, live_counts, given, offs, tails, old, slices, block_len, half, after):
    n, n_col = len(slices), len(given)
    blocks = live_counts.shape[0]
    part = blocks // HALVES
    width = sum(depth for _, depth in slices)
    flat = [piece for per_col in given for piece in per_col]
    kept = [] if old is None else [old]

    def columns(piece):
        if piece.ndim == 3:
            return pl.BlockSpec((2, piece.shape[1], block_len), lambda b: (0, 0, b))
        return pl.BlockSpec((piece.shape[0], block_len), lambda b: (0, half * part + b))

    def rows(array):
        first = half * part if array.shape[0] > part * block_len else 0
        return pl.BlockSpec((block_len, LANES), lambda b: (first + b, 0))

    first_old = 2 + len(flat) + 2 * n
    return pl.pallas_call(
        functools.partial(block_kernel, slices, n_col, half),
        out_shape=[
            jax.ShapeDtypeStruct((3, n * blocks * block_len, LANES), F32),
            jax.ShapeDtypeStruct((8, LANES), F32),
        ],
        grid=(part,),
        in_specs=[whole(SMEM)] * 2
        + [columns(piece) for piece in flat]
        + [rows(array) for array in offs + tails]
        + [whole(pl.ANY)] * len(kept + after),
        out_specs=[
            pl.BlockSpec((3, n * block_len, LANES), lambda b: (0, half * part + b, 0)),
            pl.BlockSpec((8, LANES), lambda b: (0, 0)),
        ],
        input_output_aliases={first_old + k: k for k in range(len(kept))},
        scratch_shapes=[
            pltpu.VMEM((n_col, width, block_len), BF16),
            pltpu.VMEM((n_col, width, block_len), BF16),
            pltpu.VMEM((n_col, 2, block_len), F32),
            pltpu.VMEM((block_len, block_len), F32),
            pltpu.VMEM((block_len, block_len), BF16),
            pltpu.VMEM((block_len, LANES), F32),
            pltpu.VMEM((block_len, LANES), F32),
        ],
        compiler_params=params(),
        cost_estimate=cost(part * 8 * block_len * block_len * width, 120e6),
        name="block_math",
    )(me, live_counts, *flat, *offs, *tails, *kept, *after)


def pair_of(row, n):
    return pl.ds(pl.multiple_of(row * n, n), n)


def outgoing_kernel(slices, capacity, begin, counts_ref, place_ref, grad, *refs):
    n = len(slices)
    out_ref, tile = refs[-2:]
    groups, width, chunk = out_ref.shape

    def owner(group, carry):
        wanted = jnp.clip(counts_ref[group] - begin, 0, chunk)

        def body(step, inner):
            for lane in range(UNROLL):
                at = step * UNROLL + lane
                place = place_ref[group * capacity + begin + at]
                tile[pair_of(at, n), :] = grad[pair_of(place, n), :]
            return inner

        lax.fori_loop(0, (wanted + UNROLL - 1) // UNROLL, body, 0)
        for m, (start, depth) in enumerate(slices):
            piece = tile[pl.ds(m, chunk, stride=n), :].T
            out_ref[group, start : start + depth, :] = piece[:depth].astype(BF16)
        return carry

    lax.fori_loop(0, groups, owner, 0)


def outgoing(counts, place_list, grad, slices, begin, chunk, after):
    groups, capacity = place_list.shape
    n = len(slices)
    width = sum(depth for _, depth in slices)
    return pl.pallas_call(
        functools.partial(outgoing_kernel, slices, capacity, begin),
        out_shape=jax.ShapeDtypeStruct((groups, width, chunk), BF16),
        in_specs=[whole(SMEM)] * 2 + [whole(VMEM)] + [whole(pl.ANY)] * len(after),
        out_specs=whole(VMEM),
        scratch_shapes=[pltpu.VMEM((n * chunk, LANES), F32)],
        compiler_params=params(),
        cost_estimate=cost(0, 80e6),
        name="outgoing",
    )(counts, place_list.reshape(-1), grad, *after)


def collect_kernel(slices, capacity, begin, first, counts_ref, row_ref, came_ref, *refs):
    n = len(slices)
    total, tile = refs[-2:]
    groups, width, chunk = came_ref.shape
    total[...] = jnp.zeros_like(total) if first else refs[0][...]

    def source(group, carry):
        wanted = jnp.clip(counts_ref[group] - begin, 0, chunk)

        @pl.when(wanted > 0)
        def _():
            for m, (start, depth) in enumerate(slices):
                piece = came_ref[group, start : start + depth, :].astype(F32)
                tile[pl.ds(m, chunk, stride=n), :depth] = piece.T

            def body(step, inner):
                for lane in range(UNROLL):
                    at = step * UNROLL + lane
                    into = pair_of(row_ref[group * capacity + begin + at], n)
                    total[into, :] = total[into, :] + tile[pair_of(at, n), :]
                return inner

            lax.fori_loop(0, (wanted + UNROLL - 1) // UNROLL, body, 0)

        return carry

    lax.fori_loop(0, groups, source, 0)


def collect(counts, row_list, came, total, slices, begin, ent_rows, after):
    capacity = row_list.shape[1]
    chunk = came.shape[2]
    n = len(slices)
    given = [] if total is None else [total]
    return pl.pallas_call(
        functools.partial(collect_kernel, slices, capacity, begin, total is None),
        out_shape=jax.ShapeDtypeStruct((n * (ent_rows + 8), LANES), F32),
        in_specs=[whole(SMEM)] * 2
        + [whole(VMEM)] * (1 + len(given))
        + [whole(pl.ANY)] * len(after),
        out_specs=whole(VMEM),
        scratch_shapes=[pltpu.VMEM((n * chunk, LANES), F32)],
        compiler_params=params(),
        cost_estimate=cost(0, 120e6),
        name="collect",
    )(counts, row_list.reshape(-1), came, *given, *after)


def relation_sums_kernel(n, ids_ref, grad, *refs):
    total = refs[-1]
    total[...] = jnp.zeros_like(total)

    def body(step, carry):
        for lane in range(UNROLL):
            at = step * UNROLL + lane
            into = pair_of(ids_ref[at], n)
            total[into, :] = total[into, :] + grad[0, pair_of(at, n), :]
        return carry

    lax.fori_loop(0, grad.shape[1] // n // UNROLL, body, 0)


def relation_sums(relation_ids, grad, n, rel_total, after):
    count = relation_ids.shape[0]
    return pl.pallas_call(
        functools.partial(relation_sums_kernel, n),
        out_shape=jax.ShapeDtypeStruct((n * rel_total, LANES), F32),
        grid=(1,),
        in_specs=[whole(SMEM), pl.BlockSpec((1, n * count, LANES), lambda i: (0, 0, 0))]
        + [whole(pl.ANY)] * len(after),
        out_specs=whole(VMEM),
        compiler_params=params(),
        cost_estimate=cost(0, 120e6),
        name="relation_sums",
    )(relation_ids, grad, *after)


def update_kernel(slices, weights_ref, first_ref, second_ref, total, *refs):
    n = len(slices)
    outs, scr = refs[:3], refs[3]
    cols = weights_ref.shape[1]
    for m, (start, depth) in enumerate(slices):
        scr[start : start + depth, :] = total[pl.ds(m, cols, stride=n), :].T[:depth]
    results = adamw_update(weights_ref[...], scr[...], first_ref[...], second_ref[...])
    for out, result in zip(outs, results):
        out[...] = result


def update_entities(weights, total, first, second, slices):
    width, ent_rows = weights.shape
    cols = 1024
    n = len(slices)
    table = pl.BlockSpec((width, cols), lambda i: (0, i))
    return pl.pallas_call(
        functools.partial(update_kernel, slices),
        out_shape=[jax.ShapeDtypeStruct((width, ent_rows), F32)] * 3,
        grid=(pl.cdiv(ent_rows, cols),),
        in_specs=[table] * 3 + [pl.BlockSpec((n * cols, LANES), lambda i: (i, 0))],
        out_specs=[table] * 3,
        scratch_shapes=[pltpu.VMEM((width, cols), F32)],
        compiler_params=params(),
        cost_estimate=cost(0, 60e6),
        name="update_entities",
    )(weights, first, second, total)


def chunk_bounds(capacity):
    units = capacity // LANES
    sizes = [3, 6, 5, 2] if units == 16 else [units // 4] * 3 + [units - 3 * (units // 4)]
    bounds = [0]
    for size in sizes:
        bounds.append(bounds[-1] + size * LANES)
    return bounds


def shards(
    head_ids,
    relation_ids,
    tail_ids,
    negative_ids,
    live_counts,
    rel_weight,
    rel_count,
    entity_table,
    entity_first,
    entity_second,
    relation_table,
    relation_first,
    relation_second,
):
    groups = lax.axis_size("edge")
    n_col = lax.axis_size("col")
    width, ent_rows = entity_table.shape
    blocks, neg_count = negative_ids.shape
    block_len = head_ids.shape[0] // blocks
    edge_count = blocks * block_len
    slices = width_slices(width)
    n = len(slices)
    all_ids = jnp.concatenate([head_ids, tail_ids, negative_ids.reshape(-1)])
    id_count = all_ids.shape[0]
    capacity = (4 * id_count + 3 * groups - 1) // (3 * groups)
    rel_total = rel_weight.shape[0]

    rel_own = rel_total // groups
    rel_low = jnp.pad(relation_table.astype(BF16).T, ((0, 0), (0, REL_PAD - rel_own)))
    dense = []
    for k, (start, depth) in enumerate(slices):
        sent = entity_table[start : start + depth].astype(BF16)
        if k == 0:
            behind = [
                jnp.pad(rel_low[at : at + size], ((0, depth - size), (0, 0))) for at, size in slices
            ]
            sent = jnp.concatenate([sent] + behind, axis=1)
        dense.append(lax.all_gather(sent, "edge", axis=0, tiled=False))

    place_list, row_list, counts = owner_lists(all_ids, groups, capacity, ent_rows)
    safe_places = jnp.minimum(place_list, id_count - 1)
    place_flat, row_flat = place_list.reshape(-1), row_list.reshape(-1)

    rel_scale = rel_weight * (rel_total / jnp.sum(rel_weight)) / rel_count.astype(F32)
    rel_scale = jnp.pad(rel_scale.reshape(groups, rel_own), ((0, 0), (0, REL_PAD - rel_own)))
    rel_places = relation_ids + (relation_ids // rel_own) * (REL_PAD - rel_own)

    def from_others(array):
        turns = [[(c, (c + away) % n_col) for c in range(n_col)] for away in range(1, n_col)]
        return [lax.ppermute(array, "col", turn) for turn in turns]

    me = lax.axis_index("col").astype(jnp.int32).reshape(1)
    given = [[[] for _ in range(n_col)] for _ in range(HALVES)]
    offs = [[] for _ in range(HALVES)]
    tails = [[] for _ in range(HALVES)]
    biases, norms, first_sent, rel_rows = [], [], [], None
    for k, (start, depth) in enumerate(slices):
        sent = first_sent if k > 0 else []
        fetched = fetch(counts, place_flat, row_flat, dense[k], id_count, ent_rows, sent)
        if k < n - 1:
            early, late, norm = negatives(fetched, blocks, block_len)
            early_all = [early] + from_others(early)
            if rel_rows is None:
                rel_rows = relation_rows(rel_places, dense[0], rel_scale, slices, [early])
            off, tail, low, bias = edges(fetched, rel_rows[k], late, depth, blocks, block_len)
            low_all = [low] + from_others(low)
            first_sent = early_all[1:]
            biases.append(bias)
            norms.append(norm)
            for half in range(HALVES):
                offs[half].append(off)
                tails[half].append(tail)
                for col in range(n_col):
                    given[half][col] += [early_all[col], low_all[col]]
            continue
        if rel_rows is None:
            rel_rows = relation_rows(rel_places, dense[0], rel_scale, slices, [])

    def finish(half, after):
        off, tail, pair = last_slice(
            fetched, rel_rows[-1], biases, norms, slices[-1][1], blocks, block_len, half, after
        )
        offs[half].append(off)
        tails[half].append(tail)
        for col, piece in enumerate([pair] + from_others(pair)):
            given[half][col].append(piece)

    grad, loss_tiles = None, []
    for half in range(HALVES):
        finish(half, offs[half - 1][-1:] if half > 0 else [])
    row_list, _ = lax.optimization_barrier((row_list, offs[-1][-1]))
    asked = lax.all_to_all(row_list, "edge", split_axis=0, concat_axis=0, tiled=True)
    asked_counts = jnp.sum((asked < ent_rows).astype(jnp.int32), axis=1)
    for half in range(HALVES):
        after = [asked] if half == 0 else []
        grad, loss_tile = block_math(
            me,
            live_counts,
            given[half],
            offs[half],
            tails[half],
            grad,
            slices,
            block_len,
            half,
            after,
        )
        loss_tiles.append(loss_tile)
    live = jnp.sum(jnp.minimum(live_counts, block_len)).astype(F32)
    loss_own = jnp.sum(functools.reduce(jnp.add, loss_tiles))
    lane = jnp.arange(LANES, dtype=jnp.int32)
    loss_row = jnp.where(lane == 0, loss_own, jnp.where(lane == 1, live, 0.0))
    loss_all = lax.all_to_all(
        jnp.broadcast_to(loss_row, (groups, 1, LANES)), "edge", split_axis=0, concat_axis=0, tiled=True
    )
    loss_pair = jnp.sum(loss_all[:, 0, :2], axis=0)

    flat = grad.reshape(n * id_count, LANES)
    bounds = chunk_bounds(capacity)
    chunks = len(bounds) - 1
    arrived, total, after = [], None, []
    for k in range(chunks):
        sent = outgoing(
            counts, safe_places, flat, slices, bounds[k], bounds[k + 1] - bounds[k], after
        )
        arrived.append(lax.all_to_all(sent, "edge", split_axis=0, concat_axis=0, tiled=True))
        after = []
        if k == 1:
            rel_terms = relation_sums(relation_ids, grad, n, rel_total, [arrived[0], loss_all])
            after = [rel_terms]
            rel_terms = rel_terms.reshape(rel_total, n * LANES)[:, :width]
            relation_grad = lax.psum_scatter(rel_terms, "edge", scatter_dimension=0, tiled=True)
        if k == chunks - 1:
            after = [relation_grad]
        if k > 0:
            total = collect(
                asked_counts, asked, arrived[k - 1], total, slices, bounds[k - 1], ent_rows, after
            )
            after = [total, rel_terms]
    k = chunks - 1
    total = collect(asked_counts, asked, arrived[k], total, slices, bounds[k], ent_rows, [])

    new_entity, new_entity_first, new_entity_second = update_entities(
        entity_table, total, entity_first, entity_second, slices
    )
    new_relation, new_relation_first, new_relation_second = adamw_update(
        relation_table, relation_grad, relation_first, relation_second
    )
    return (
        loss_pair,
        new_entity,
        new_entity_first,
        new_entity_second,
        new_relation,
        new_relation_first,
        new_relation_second,
    )


def solution(mesh):
    placed = (
        P("edge"),
        P("edge"),
        P("edge"),
        P("edge", None),
        P("edge"),
        P(),
        P(),
        P("col", "edge"),
        P("col", "edge"),
        P("col", "edge"),
        P("edge", "col"),
        P("edge", "col"),
        P("edge", "col"),
    )
    return jax.shard_map(
        shards,
        mesh=mesh,
        in_specs=placed,
        out_specs=(
            P(),
            P("col", "edge"),
            P("col", "edge"),
            P("col", "edge"),
            P("edge", "col"),
            P("edge", "col"),
            P("edge", "col"),
        ),
        check_vma=False,
    )
```

```python
import functools

import jax
import jax.numpy as jnp
from jax import lax
from jax.experimental import pallas as pl
from jax.experimental.pallas import tpu as pltpu
from jax.sharding import PartitionSpec as P

STEP = 5


MARGIN = 0.1
LEARN_RATE = 0.1
BETA_ONE = 0.5
BETA_TWO = 0.5
EPSILON = 1e-08
DECAY = 0.01
LANES = 128
UNROLL = 8
PARTS = 4
HALVES = 2
EARLY = 96
TURN = 512
REL_PAD = 256
TERMS = 3
NN = (((1,), (0,)), ((), ()))
NT = (((1,), (1,)), ((), ()))
TN = (((0,), (0,)), ((), ()))
F32 = jnp.float32
BF16 = jnp.bfloat16
SMEM = pltpu.SMEM
VMEM = pltpu.VMEM


def params(mebibytes=60):
    return pltpu.CompilerParams(vmem_limit_bytes=mebibytes << 20)


def cost(flops, moved):
    return pl.CostEstimate(flops=int(flops), bytes_accessed=int(moved), transcendentals=0)


def whole(space):
    return pl.BlockSpec(memory_space=space)


def adamw_update(weights, gradient, first, second):
    new_first = BETA_ONE * first + (1.0 - BETA_ONE) * gradient
    new_second = BETA_TWO * second + (1.0 - BETA_TWO) * gradient * gradient
    first_hat = new_first / (1.0 - BETA_ONE**STEP)
    second_hat = new_second / (1.0 - BETA_TWO**STEP)
    updated = weights - LEARN_RATE * (
        first_hat / (jnp.sqrt(second_hat) + EPSILON) + DECAY * weights
    )
    return (updated, new_first, new_second)


def width_slices(width):
    return [(at, min(LANES, width - at)) for at in range(0, width, LANES)]


def owner_lists(all_ids, groups, capacity, ent_rows):
    count = all_ids.shape[0]
    owners = all_ids // ent_rows
    local_rows = all_ids - owners * ent_rows
    chunk = 256
    mine = owners[None, :] == jnp.arange(groups, dtype=jnp.int32)[:, None]
    mine = mine.astype(BF16).reshape(groups, count // chunk, chunk)
    before = jnp.triu(jnp.ones((chunk, chunk), BF16), 1)
    inner = jnp.dot(mine, before, preferred_element_type=F32)
    sums = jnp.sum(mine.astype(F32), axis=2)
    carry = jnp.cumsum(sums, axis=1) - sums
    ranks = jnp.sum(mine.astype(F32) * (inner + carry[:, :, None]), axis=0)
    ranks = ranks.astype(jnp.int32).reshape(count)
    counts = jnp.sum(sums, axis=1).astype(jnp.int32)
    high = owners * (capacity // LANES) + ranks // LANES
    low = ranks % LANES
    tall = groups * capacity // LANES
    left = (jnp.arange(tall, dtype=jnp.int32)[:, None] == high[None, :]).astype(BF16)
    right = (jnp.arange(LANES, dtype=jnp.int32)[:, None] == low[None, :]).astype(BF16)
    places = jnp.arange(1, count + 1, dtype=jnp.int32)
    parts = jnp.stack([places // 256, places % 256, local_rows // 256, local_rows % 256])
    right = (parts.astype(BF16)[:, None, :] * right[None]).reshape(PARTS * LANES, count)
    found = lax.dot_general(left, right, NT, preferred_element_type=F32).astype(jnp.int32)
    found = found.reshape(tall, PARTS, LANES)
    place = found[:, 0] * 256 + found[:, 1]
    place_list = jnp.where(place > 0, place - 1, count).reshape(groups, capacity)
    row_list = jnp.where(place > 0, found[:, 2] * 256 + found[:, 3], ent_rows)
    return place_list, row_list.reshape(groups, capacity), counts


def relation_rows_kernel(slices, ids_ref, scale_ref, *refs):
    n = len(slices)
    tables, outs = refs[:n], refs[-2 * n - 1 : -n - 1]
    columns, rows = refs[-n - 1], refs[-n:]
    groups = tables[0].shape[0]
    for (_, depth), table, into in zip(slices, tables, rows):
        columns[...] = jnp.zeros_like(columns)

        def turn(group, carry):
            columns[:depth, :] = table[group, :depth].astype(F32)
            if depth < LANES:
                columns[LANES - 1 :, :] = scale_ref[pl.ds(group, 1), :]
            into[pl.ds(pl.multiple_of(group * REL_PAD, REL_PAD), REL_PAD), :] = columns[...].T
            return carry

        lax.fori_loop(0, groups, turn, 0, unroll=4)

    def body(step, carry):
        for lane in range(UNROLL):
            at = step * UNROLL + lane
            row = ids_ref[at]
            for source, out in zip(rows, outs):
                out[pl.ds(at, 1), :] = source[pl.ds(row, 1), :]
        return carry

    lax.fori_loop(0, outs[0].shape[0] // UNROLL, body, 0)


def relation_rows(places, dense, scale, slices, after):
    count = places.shape[0]
    groups, depth, span = dense.shape
    n = len(slices)
    first = span // REL_PAD - n

    def columns(k):
        return pl.BlockSpec((groups, depth, REL_PAD), lambda i: (0, 0, first + k))

    return pl.pallas_call(
        functools.partial(relation_rows_kernel, slices),
        out_shape=[jax.ShapeDtypeStruct((count, LANES), F32)] * n,
        grid=(1,),
        in_specs=[whole(SMEM), whole(VMEM)]
        + [columns(k) for k in range(n)]
        + [whole(pl.ANY)] * len(after),
        out_specs=[whole(VMEM)] * n,
        scratch_shapes=[pltpu.VMEM((LANES, REL_PAD), F32)]
        + [pltpu.VMEM((groups * REL_PAD, LANES), F32)] * n,
        compiler_params=params(28),
        cost_estimate=cost(0, 80e6),
        name="relation_rows",
    )(places, scale, *[dense] * n, *after)


def fetch_kernel(
    capacity, moves, ent_rows, counts_ref, place_ref, row_ref, dense_ref, *refs
):
    shard = pl.program_id(0)
    last = pl.num_programs(0) - 1
    out_ref, rows = refs[-3], refs[-2:]
    depth = dense_ref.shape[1]
    turns = ent_rows // TURN
    rest = ent_rows - turns * TURN

    if depth < LANES:

        @pl.when(shard == 0)
        def _():
            for ref in rows:
                ref[...] = jnp.zeros_like(ref)

    def turn(into, begin, size):
        cols = pl.ds(begin, size)
        into[cols, :depth] = dense_ref[0, :, cols].astype(F32).T

    def move(source, at):
        out_ref[pl.ds(place_ref[at], 1), :] = source[pl.ds(row_ref[at], 1), :]

    def step(into, source):
        base = (shard - 1) * capacity

        def remaining(first):
            def body(trip, carry):
                for lane in range(UNROLL):
                    move(source, base + first + trip * UNROLL + lane)
                return carry

            wanted = counts_ref[jnp.maximum(shard - 1, 0)] - first
            lax.fori_loop(0, (wanted + UNROLL - 1) // UNROLL, body, 0)

        def only_turn(trip, carry):
            turn(into, pl.multiple_of(trip * TURN, TURN), TURN)
            return carry

        def both(trip, carry):
            turn(into, pl.multiple_of(trip * TURN, TURN), TURN)
            for lane in range(moves):
                move(source, base + trip * moves + lane)
            return carry

        @pl.when(shard == 0)
        def _():
            lax.fori_loop(0, turns, only_turn, 0)

        @pl.when((shard > 0) & (shard < last))
        def _():
            lax.fori_loop(0, turns, both, 0)
            remaining(turns * moves)

        @pl.when(shard == last)
        def _():
            remaining(0)

        if rest:

            @pl.when(shard < last)
            def _():
                turn(into, turns * TURN, rest)

    for parity in range(2):

        @pl.when(lax.rem(shard, 2) == parity)
        def _():
            step(rows[parity], rows[1 - parity])


def fetch(counts, place_list, row_list, dense, id_count, ent_rows, after):
    groups, depth, _ = dense.shape
    capacity = place_list.shape[0] // groups
    moves = (id_count // groups) // (ent_rows // TURN) // UNROLL * UNROLL
    return pl.pallas_call(
        functools.partial(fetch_kernel, capacity, moves, ent_rows),
        out_shape=jax.ShapeDtypeStruct((id_count + 8, LANES), F32),
        grid=(groups + 1,),
        in_specs=[whole(SMEM)] * 3
        + [
            pl.BlockSpec(
                (1, depth, ent_rows), lambda shard: (jnp.minimum(shard, groups - 1), 0, 0)
            )
        ]
        + [whole(pl.ANY)] * len(after),
        out_specs=whole(VMEM),
        scratch_shapes=[pltpu.VMEM((ent_rows + 8, LANES), F32)] * 2,
        compiler_params=params(32),
        cost_estimate=cost(0, 170e6),
        name="fetch_rows",
    )(counts, place_list, row_list, dense, *after)


def column_sum(values):
    return jnp.sum(values * values, axis=0, keepdims=True)


def negatives_kernel(neg_ref, early_ref, late_ref, norm_ref):
    neg_t = neg_ref[...].T
    early_ref[...] = neg_t[:EARLY].astype(BF16)
    late_ref[...] = neg_t[EARLY:].astype(BF16)
    norm_ref[...] = column_sum(neg_t)


def negatives(fetched, blocks, block_len):
    count = blocks * block_len
    return pl.pallas_call(
        negatives_kernel,
        out_shape=[
            jax.ShapeDtypeStruct((EARLY, count), BF16),
            jax.ShapeDtypeStruct((LANES - EARLY, count), BF16),
            jax.ShapeDtypeStruct((1, count), F32),
        ],
        grid=(blocks,),
        in_specs=[pl.BlockSpec((block_len, LANES), lambda b: (2 * blocks + b, 0))],
        out_specs=[
            pl.BlockSpec((EARLY, block_len), lambda b: (0, b)),
            pl.BlockSpec((LANES - EARLY, block_len), lambda b: (0, b)),
            pl.BlockSpec((1, block_len), lambda b: (0, b)),
        ],
        compiler_params=params(12),
        cost_estimate=cost(0, 10e6),
        name="negatives",
    )(fetched)


def edge_parts(depth, head_ref, tail_ref, rel_ref, off_ref, tail_out):
    lane = lax.broadcasted_iota(jnp.int32, head_ref.shape, 1)
    inside = lane < depth
    rel = rel_ref[...]
    tail = tail_ref[...]
    shifted = head_ref[...] + jnp.where(inside, rel, 0.0)
    off_ref[...] = jnp.where(inside, shifted - tail, rel)
    tail_out[...] = tail.astype(BF16)
    shifted_t = shifted.T
    return shifted_t, column_sum((shifted - tail).T) - column_sum(shifted_t)


def edges_kernel(
    depth, head_ref, tail_ref, rel_ref, late_ref, off_ref, tail_out, low_ref, bias_ref
):
    shifted_t, bias = edge_parts(depth, head_ref, tail_ref, rel_ref, off_ref, tail_out)
    low_ref[:depth] = shifted_t[:depth].astype(BF16)
    low_ref[depth:] = late_ref[...]
    bias_ref[...] = bias


def edges(fetched, rel_rows, late, depth, blocks, block_len):
    count = blocks * block_len
    tall = depth + late.shape[0]

    def rows(at):
        return pl.BlockSpec((block_len, LANES), lambda b: (at * blocks + b, 0))

    return pl.pallas_call(
        functools.partial(edges_kernel, depth),
        out_shape=[
            jax.ShapeDtypeStruct((count, LANES), F32),
            jax.ShapeDtypeStruct((count, LANES), BF16),
            jax.ShapeDtypeStruct((tall, count), BF16),
            jax.ShapeDtypeStruct((1, count), F32),
        ],
        grid=(blocks,),
        in_specs=[rows(0), rows(1), rows(0)]
        + [pl.BlockSpec((tall - depth, block_len), lambda b: (0, b))],
        out_specs=[
            rows(0),
            rows(0),
            pl.BlockSpec((tall, block_len), lambda b: (0, b)),
            pl.BlockSpec((1, block_len), lambda b: (0, b)),
        ],
        compiler_params=params(16),
        cost_estimate=cost(0, 30e6),
        name="edges",
    )(fetched, fetched, rel_rows, late)


def last_rows(depth):
    return (depth + 7) // 8 * 8


def with_terms(columns, total, depth):
    place = lax.broadcasted_iota(jnp.int32, (8, total.shape[1]), 0)
    left = total
    terms = jnp.zeros(place.shape, F32)
    for k in range(TERMS):
        term = left.astype(BF16).astype(F32)
        left = left - term
        terms = jnp.where(place == k, term, terms)
    return jnp.concatenate([columns[: last_rows(depth)], terms], axis=0).astype(BF16)


def last_kernel(depth, n_given, head_ref, tail_ref, neg_ref, rel_ref, *refs):
    biases, norms = refs[:n_given], refs[n_given : 2 * n_given]
    off_ref, tail_out, pair_ref = refs[-3:]
    shifted_t, bias = edge_parts(depth, head_ref, tail_ref, rel_ref, off_ref, tail_out)
    neg_t = neg_ref[...].T
    norm = column_sum(neg_t)
    for ref in biases:
        bias = bias + ref[...]
    for ref in norms:
        norm = norm + ref[...]
    pair_ref[0] = with_terms(shifted_t, bias, depth)
    pair_ref[1] = with_terms(neg_t, norm, depth)


def last_slice(fetched, rel_rows, biases, norms, depth, blocks, block_len, half, after):
    part = blocks // HALVES
    count = part * block_len
    tall = last_rows(depth) + 8

    def rows(at):
        return pl.BlockSpec((block_len, LANES), lambda b: (at * blocks + half * part + b, 0))

    return pl.pallas_call(
        functools.partial(last_kernel, depth, len(biases)),
        out_shape=[
            jax.ShapeDtypeStruct((count, LANES), F32),
            jax.ShapeDtypeStruct((count, LANES), BF16),
            jax.ShapeDtypeStruct((2, tall, count), BF16),
        ],
        grid=(part,),
        in_specs=[rows(0), rows(1), rows(2), rows(0)]
        + [pl.BlockSpec((1, block_len), lambda b: (0, half * part + b))]
        * (len(biases) + len(norms))
        + [whole(pl.ANY)] * len(after),
        out_specs=[
            pl.BlockSpec((block_len, LANES), lambda b: (b, 0)),
            pl.BlockSpec((block_len, LANES), lambda b: (b, 0)),
            pl.BlockSpec((2, tall, block_len), lambda b: (0, 0, b)),
        ],
        compiler_params=params(16),
        cost_estimate=cost(0, 20e6),
        name="last_slice",
    )(fetched, fetched, fetched, rel_rows, *biases, *norms, *after)


def block_kernel(slices, n_col, half, me_ref, live_ref, *refs):
    n = len(slices)
    per_col = 2 * n - 1
    given = [refs[k * per_col : (k + 1) * per_col] for k in range(n_col)]
    refs = refs[n_col * per_col :]
    offs, tails, refs = refs[:n], refs[n : 2 * n], refs[2 * n :]
    grad, refs = refs[-9], refs[-8:]
    loss_ref, shift_scr, neg_scr, sums_scr, cross, slopes, row_bias, row_sum = refs
    block = pl.program_id(0)
    length = cross.shape[0]
    me = me_ref[0]
    for k in range(n_col):
        slot = lax.rem(me + (n_col - k), n_col)
        for m, (start, depth) in enumerate(slices):
            if m < n - 1:
                early, late = given[k][2 * m : 2 * m + 2]
                shift_scr[slot, start : start + depth, :] = 2.0 * late[:depth, :]
                neg_scr[slot, start : start + EARLY, :] = early[...]
                neg_scr[slot, start + EARLY : start + depth, :] = late[depth:, :]
            else:
                pair = given[k][-1]
                shift, neg = pair[0, :depth, :], pair[1, :depth, :]
                for row in range(2):
                    terms = pair[row, last_rows(depth) : last_rows(depth) + 8, :].astype(F32)
                    sums_scr[slot, row : row + 1] = jnp.sum(terms, axis=0, keepdims=True)
                shift_scr[slot, start : start + depth, :] = 2.0 * shift
                neg_scr[slot, start : start + depth, :] = neg
    bias = jnp.sum(sums_scr[:, 0, :], axis=0, keepdims=True) + MARGIN
    neg_norm = jnp.sum(sums_scr[:, 1, :], axis=0, keepdims=True)
    row_bias[...] = jnp.broadcast_to(bias, (LANES, length)).T

    live = live_ref[half * pl.num_programs(0) + block]
    tile = 256
    small = 128
    lane_tiles = [slice(at, at + LANES) for at in range(0, length, LANES)]
    cols = jnp.zeros((8, length), F32)
    loss = jnp.zeros((8, LANES), F32)
    def products(at):
        part = slice(at, at + tile)
        doubled = None
        for k in range(n_col):
            term = lax.dot_general(
                shift_scr[k, :, part], neg_scr[k], TN, preferred_element_type=F32
            )
            doubled = term if doubled is None else doubled + term
        cross[part, :] = doubled

    def moves(at):
        part = slice(at, at + tile)
        moved = lax.dot_general(slopes[part, :], neg_scr[me], NT, preferred_element_type=F32)
        fade = -row_sum[part, :]
        for m, (start, depth) in enumerate(slices):
            into = pl.ds(n * at + m, tile, stride=n)
            grad[0, into, :depth] = (
                fade[:, :depth] * tails[m][part, :depth].astype(F32)
                + moved[:, start : start + depth]
            )
            grad[1, into, :] = fade * offs[m][part, :]

    products(0)
    for begin in range(0, length, tile):
        if begin + tile < length:
            products(begin + tile)
        for at in range(begin, begin + tile, small):
            part = slice(at, at + small)
            place = at + lax.broadcasted_iota(jnp.int32, (small, 1), 0)
            scale = offs[-1][part, LANES - 1 : LANES]
            weight = jnp.where(place < live, scale, 0.0) / length
            margins = cross[part, :] + (row_bias[part, 0:1] - neg_norm)
            fall = jnp.exp(-jnp.abs(margins))
            under = 1.0 + fall
            guess = pl.reciprocal(under, approx=True)
            inverse = guess * (2.0 - under * guess)
            twice = (2.0 * weight) * (jnp.where(margins >= 0.0, 1.0, fall) * inverse)
            row_sum[part, :] = jnp.broadcast_to(
                jnp.sum(twice, axis=1, keepdims=True), (small, LANES)
            )
            slopes[part, :] = twice.astype(BF16)
            cols = cols + jnp.sum(twice.reshape(small // 8, 8, length), axis=0)
            over = jnp.maximum(margins, 0.0)
            lifts = [fall[:, lanes] for lanes in lane_tiles]
            while len(lifts) > 1:
                lifts = [a + b + a * b for a, b in zip(lifts[::2], lifts[1::2])]
            lift = lifts[0]
            soft = functools.reduce(jnp.add, [over[:, lanes] for lanes in lane_tiles]) + jnp.where(
                lift < 2.0**-11, lift * (1.0 - 0.5 * lift), jnp.log(1.0 + lift)
            )
            loss = loss + jnp.sum((weight * soft).reshape(small // 8, 8, LANES), axis=0)
        moves(begin)
    col_sum = jnp.sum(cols, axis=0, keepdims=True)

    @pl.when(block == 0)
    def _():
        loss_ref[...] = loss

    @pl.when(block > 0)
    def _():
        loss_ref[...] += loss

    moved = lax.dot_general(shift_scr[me], slopes[...], NN, preferred_element_type=F32)
    moved = 0.5 * moved - col_sum * neg_scr[me].astype(F32)
    for m, (start, depth) in enumerate(slices):
        grad[2, pl.ds(m, length, stride=n), :depth] = moved[start : start + depth, :].T


def block_math(me, live_counts, given, offs, tails, old, slices, block_len, half, after):
    n, n_col = len(slices), len(given)
    blocks = live_counts.shape[0]
    part = blocks // HALVES
    width = sum(depth for _, depth in slices)
    flat = [piece for per_col in given for piece in per_col]
    kept = [] if old is None else [old]

    def columns(piece):
        if piece.ndim == 3:
            return pl.BlockSpec((2, piece.shape[1], block_len), lambda b: (0, 0, b))
        return pl.BlockSpec((piece.shape[0], block_len), lambda b: (0, half * part + b))

    def rows(array):
        first = half * part if array.shape[0] > part * block_len else 0
        return pl.BlockSpec((block_len, LANES), lambda b: (first + b, 0))

    first_old = 2 + len(flat) + 2 * n
    return pl.pallas_call(
        functools.partial(block_kernel, slices, n_col, half),
        out_shape=[
            jax.ShapeDtypeStruct((3, n * blocks * block_len, LANES), F32),
            jax.ShapeDtypeStruct((8, LANES), F32),
        ],
        grid=(part,),
        in_specs=[whole(SMEM)] * 2
        + [columns(piece) for piece in flat]
        + [rows(array) for array in offs + tails]
        + [whole(pl.ANY)] * len(kept + after),
        out_specs=[
            pl.BlockSpec((3, n * block_len, LANES), lambda b: (0, half * part + b, 0)),
            pl.BlockSpec((8, LANES), lambda b: (0, 0)),
        ],
        input_output_aliases={first_old + k: k for k in range(len(kept))},
        scratch_shapes=[
            pltpu.VMEM((n_col, width, block_len), BF16),
            pltpu.VMEM((n_col, width, block_len), BF16),
            pltpu.VMEM((n_col, 2, block_len), F32),
            pltpu.VMEM((block_len, block_len), F32),
            pltpu.VMEM((block_len, block_len), BF16),
            pltpu.VMEM((block_len, LANES), F32),
            pltpu.VMEM((block_len, LANES), F32),
        ],
        compiler_params=params(30),
        cost_estimate=cost(part * 8 * block_len * block_len * width, 120e6),
        name="block_math",
    )(me, live_counts, *flat, *offs, *tails, *kept, *after)


def pair_of(row, n):
    return pl.ds(pl.multiple_of(row * n, n), n)


def outgoing_kernel(slices, capacity, begin, counts_ref, place_ref, grad, *refs):
    n = len(slices)
    out_ref, tile = refs[-2:]
    groups, width, chunk = out_ref.shape

    def owner(group, carry):
        wanted = jnp.clip(counts_ref[group] - begin, 0, chunk)

        def body(step, inner):
            for lane in range(UNROLL):
                at = step * UNROLL + lane
                place = place_ref[group * capacity + begin + at]
                tile[pair_of(at, n), :] = grad[pair_of(place, n), :]
            return inner

        lax.fori_loop(0, (wanted + UNROLL - 1) // UNROLL, body, 0)
        for m, (start, depth) in enumerate(slices):
            piece = tile[pl.ds(m, chunk, stride=n), :].T
            out_ref[group, start : start + depth, :] = piece[:depth].astype(BF16)
        return carry

    lax.fori_loop(0, groups, owner, 0)


def outgoing(counts, place_list, grad, slices, begin, chunk, after):
    groups, capacity = place_list.shape
    n = len(slices)
    width = sum(depth for _, depth in slices)
    return pl.pallas_call(
        functools.partial(outgoing_kernel, slices, capacity, begin),
        out_shape=jax.ShapeDtypeStruct((groups, width, chunk), BF16),
        in_specs=[whole(SMEM)] * 2 + [whole(VMEM)] + [whole(pl.ANY)] * len(after),
        out_specs=whole(VMEM),
        scratch_shapes=[pltpu.VMEM((n * chunk, LANES), F32)],
        compiler_params=params(40),
        cost_estimate=cost(0, 80e6),
        name="outgoing",
    )(counts, place_list.reshape(-1), grad, *after)


def collect_kernel(slices, capacity, begin, first, counts_ref, row_ref, came_ref, *refs):
    n = len(slices)
    total, tile = refs[-2:]
    groups, width, chunk = came_ref.shape
    total[...] = jnp.zeros_like(total) if first else refs[0][...]

    def source(group, carry):
        wanted = jnp.clip(counts_ref[group] - begin, 0, chunk)

        @pl.when(wanted > 0)
        def _():
            for m, (start, depth) in enumerate(slices):
                piece = came_ref[group, start : start + depth, :].astype(F32)
                tile[pl.ds(m, chunk, stride=n), :depth] = piece.T

            def body(step, inner):
                for lane in range(UNROLL):
                    at = step * UNROLL + lane
                    into = pair_of(row_ref[group * capacity + begin + at], n)
                    total[into, :] = total[into, :] + tile[pair_of(at, n), :]
                return inner

            lax.fori_loop(0, (wanted + UNROLL - 1) // UNROLL, body, 0)

        return carry

    lax.fori_loop(0, groups, source, 0)


def collect(counts, row_list, came, total, slices, begin, ent_rows, after):
    capacity = row_list.shape[1]
    chunk = came.shape[2]
    n = len(slices)
    given = [] if total is None else [total]
    return pl.pallas_call(
        functools.partial(collect_kernel, slices, capacity, begin, total is None),
        out_shape=jax.ShapeDtypeStruct((n * (ent_rows + 8), LANES), F32),
        in_specs=[whole(SMEM)] * 2
        + [whole(VMEM)] * (1 + len(given))
        + [whole(pl.ANY)] * len(after),
        out_specs=whole(VMEM),
        scratch_shapes=[pltpu.VMEM((n * chunk, LANES), F32)],
        compiler_params=params(30),
        cost_estimate=cost(0, 120e6),
        name="collect",
    )(counts, row_list.reshape(-1), came, *given, *after)


def relation_sums_kernel(n, ids_ref, grad, *refs):
    total = refs[-1]
    total[...] = jnp.zeros_like(total)

    def body(step, carry):
        for lane in range(UNROLL):
            at = step * UNROLL + lane
            into = pair_of(ids_ref[at], n)
            total[into, :] = total[into, :] + grad[0, pair_of(at, n), :]
        return carry

    lax.fori_loop(0, grad.shape[1] // n // UNROLL, body, 0)


def relation_sums(relation_ids, grad, n, rel_total, after):
    count = relation_ids.shape[0]
    return pl.pallas_call(
        functools.partial(relation_sums_kernel, n),
        out_shape=jax.ShapeDtypeStruct((n * rel_total, LANES), F32),
        grid=(1,),
        in_specs=[whole(SMEM), pl.BlockSpec((1, n * count, LANES), lambda i: (0, 0, 0))]
        + [whole(pl.ANY)] * len(after),
        out_specs=whole(VMEM),
        compiler_params=params(30),
        cost_estimate=cost(0, 120e6),
        name="relation_sums",
    )(relation_ids, grad, *after)


def update_kernel(slices, weights_ref, first_ref, second_ref, total, *refs):
    n = len(slices)
    outs, scr = refs[:3], refs[3]
    cols = weights_ref.shape[1]
    for m, (start, depth) in enumerate(slices):
        scr[start : start + depth, :] = total[pl.ds(m, cols, stride=n), :].T[:depth]
    results = adamw_update(weights_ref[...], scr[...], first_ref[...], second_ref[...])
    for out, result in zip(outs, results):
        out[...] = result


def update_entities(weights, total, first, second, slices):
    width, ent_rows = weights.shape
    cols = 1024
    n = len(slices)
    table = pl.BlockSpec((width, cols), lambda i: (0, i))
    return pl.pallas_call(
        functools.partial(update_kernel, slices),
        out_shape=[jax.ShapeDtypeStruct((width, ent_rows), F32)] * 3,
        grid=(pl.cdiv(ent_rows, cols),),
        in_specs=[table] * 3 + [pl.BlockSpec((n * cols, LANES), lambda i: (i, 0))],
        out_specs=[table] * 3,
        scratch_shapes=[pltpu.VMEM((width, cols), F32)],
        compiler_params=params(20),
        cost_estimate=cost(0, 60e6),
        name="update_entities",
    )(weights, first, second, total)


def chunk_bounds(capacity):
    units = capacity // LANES
    sizes = [3, 6, 5, 2] if units == 16 else [units // 4] * 3 + [units - 3 * (units // 4)]
    bounds = [0]
    for size in sizes:
        bounds.append(bounds[-1] + size * LANES)
    return bounds


def shards(
    head_ids,
    relation_ids,
    tail_ids,
    negative_ids,
    live_counts,
    rel_weight,
    rel_count,
    entity_table,
    entity_first,
    entity_second,
    relation_table,
    relation_first,
    relation_second,
):
    groups = lax.axis_size("edge")
    n_col = lax.axis_size("col")
    width, ent_rows = entity_table.shape
    blocks, neg_count = negative_ids.shape
    block_len = head_ids.shape[0] // blocks
    edge_count = blocks * block_len
    slices = width_slices(width)
    n = len(slices)
    all_ids = jnp.concatenate([head_ids, tail_ids, negative_ids.reshape(-1)])
    id_count = all_ids.shape[0]
    capacity = (4 * id_count + 3 * groups - 1) // (3 * groups)
    rel_total = rel_weight.shape[0]

    rel_own = rel_total // groups
    rel_low = jnp.pad(relation_table.astype(BF16).T, ((0, 0), (0, REL_PAD - rel_own)))
    dense = []
    for k, (start, depth) in enumerate(slices):
        sent = entity_table[start : start + depth].astype(BF16)
        if k == 0:
            behind = [
                jnp.pad(rel_low[at : at + size], ((0, depth - size), (0, 0))) for at, size in slices
            ]
            sent = jnp.concatenate([sent] + behind, axis=1)
        dense.append(lax.all_gather(sent, "edge", axis=0, tiled=False))

    place_list, row_list, counts = owner_lists(all_ids, groups, capacity, ent_rows)
    safe_places = jnp.minimum(place_list, id_count - 1)
    place_flat, row_flat = place_list.reshape(-1), row_list.reshape(-1)

    rel_scale = rel_weight * (rel_total / jnp.sum(rel_weight)) / rel_count.astype(F32)
    rel_scale = jnp.pad(rel_scale.reshape(groups, rel_own), ((0, 0), (0, REL_PAD - rel_own)))
    rel_places = relation_ids + (relation_ids // rel_own) * (REL_PAD - rel_own)

    def from_others(array):
        turns = [[(c, (c + away) % n_col) for c in range(n_col)] for away in range(1, n_col)]
        return [lax.ppermute(array, "col", turn) for turn in turns]

    me = lax.axis_index("col").astype(jnp.int32).reshape(1)
    given = [[[] for _ in range(n_col)] for _ in range(HALVES)]
    offs = [[] for _ in range(HALVES)]
    tails = [[] for _ in range(HALVES)]
    biases, norms, first_sent, rel_rows = [], [], [], None
    for k, (start, depth) in enumerate(slices):
        sent = first_sent if k > 0 else []
        fetched = fetch(counts, place_flat, row_flat, dense[k], id_count, ent_rows, sent)
        if k < n - 1:
            early, late, norm = negatives(fetched, blocks, block_len)
            early_all = [early] + from_others(early)
            if rel_rows is None:
                rel_rows = relation_rows(rel_places, dense[0], rel_scale, slices, [early])
            off, tail, low, bias = edges(fetched, rel_rows[k], late, depth, blocks, block_len)
            low_all = [low] + from_others(low)
            first_sent = early_all[1:]
            biases.append(bias)
            norms.append(norm)
            for half in range(HALVES):
                offs[half].append(off)
                tails[half].append(tail)
                for col in range(n_col):
                    given[half][col] += [early_all[col], low_all[col]]
            continue
        if rel_rows is None:
            rel_rows = relation_rows(rel_places, dense[0], rel_scale, slices, [])

    def finish(half, after):
        off, tail, pair = last_slice(
            fetched, rel_rows[-1], biases, norms, slices[-1][1], blocks, block_len, half, after
        )
        offs[half].append(off)
        tails[half].append(tail)
        for col, piece in enumerate([pair] + from_others(pair)):
            given[half][col].append(piece)

    grad, loss_tiles = None, []
    for half in range(HALVES):
        finish(half, offs[half - 1][-1:] if half > 0 else [])
    row_list, _ = lax.optimization_barrier((row_list, offs[-1][-1]))
    asked = lax.all_to_all(row_list, "edge", split_axis=0, concat_axis=0, tiled=True)
    asked_counts = jnp.sum((asked < ent_rows).astype(jnp.int32), axis=1)
    for half in range(HALVES):
        after = [asked] if half == 0 else []
        grad, loss_tile = block_math(
            me,
            live_counts,
            given[half],
            offs[half],
            tails[half],
            grad,
            slices,
            block_len,
            half,
            after,
        )
        loss_tiles.append(loss_tile)
    live = jnp.sum(jnp.minimum(live_counts, block_len)).astype(F32)
    loss_own = jnp.sum(functools.reduce(jnp.add, loss_tiles))
    lane = jnp.arange(LANES, dtype=jnp.int32)
    loss_row = jnp.where(lane == 0, loss_own, jnp.where(lane == 1, live, 0.0))
    loss_all = lax.all_to_all(
        jnp.broadcast_to(loss_row, (groups, 1, LANES)), "edge", split_axis=0, concat_axis=0, tiled=True
    )
    loss_pair = jnp.sum(loss_all[:, 0, :2], axis=0)

    flat = grad.reshape(n * id_count, LANES)
    bounds = chunk_bounds(capacity)
    chunks = len(bounds) - 1
    arrived, total, after = [], None, []
    for k in range(chunks):
        sent = outgoing(
            counts, safe_places, flat, slices, bounds[k], bounds[k + 1] - bounds[k], after
        )
        arrived.append(lax.all_to_all(sent, "edge", split_axis=0, concat_axis=0, tiled=True))
        after = []
        if k == 1:
            rel_terms = relation_sums(relation_ids, grad, n, rel_total, [arrived[0], loss_all])
            after = [rel_terms]
            rel_terms = rel_terms.reshape(rel_total, n * LANES)[:, :width]
            relation_grad = lax.psum_scatter(rel_terms, "edge", scatter_dimension=0, tiled=True)
        if k == chunks - 1:
            after = [relation_grad]
        if k > 0:
            total = collect(
                asked_counts, asked, arrived[k - 1], total, slices, bounds[k - 1], ent_rows, after
            )
            after = [total, rel_terms]
    k = chunks - 1
    total = collect(asked_counts, asked, arrived[k], total, slices, bounds[k], ent_rows, [])

    new_entity, new_entity_first, new_entity_second = update_entities(
        entity_table, total, entity_first, entity_second, slices
    )
    new_relation, new_relation_first, new_relation_second = adamw_update(
        relation_table, relation_grad, relation_first, relation_second
    )
    return (
        loss_pair,
        new_entity,
        new_entity_first,
        new_entity_second,
        new_relation,
        new_relation_first,
        new_relation_second,
    )


def solution(mesh):
    placed = (
        P("edge"),
        P("edge"),
        P("edge"),
        P("edge", None),
        P("edge"),
        P(),
        P(),
        P("col", "edge"),
        P("col", "edge"),
        P("col", "edge"),
        P("edge", "col"),
        P("edge", "col"),
        P("edge", "col"),
    )
    return jax.shard_map(
        shards,
        mesh=mesh,
        in_specs=placed,
        out_specs=(
            P(),
            P("col", "edge"),
            P("col", "edge"),
            P("col", "edge"),
            P("edge", "col"),
            P("edge", "col"),
            P("edge", "col"),
        ),
        check_vma=False,
    )
```

```python
import functools

import jax
import jax.numpy as jnp
from jax import lax
from jax.experimental import pallas as pl
from jax.experimental.pallas import tpu as pltpu
from jax.sharding import PartitionSpec as P

STEP = 5


MARGIN = 0.1
LEARN_RATE = 0.1
BETA_ONE = 0.5
BETA_TWO = 0.5
EPSILON = 1e-08
DECAY = 0.01
LANES = 128
UNROLL = 8
PARTS = 4
HALVES = 2
EARLY = 96
TURN = 512
REL_PAD = 256
TERMS = 3
NN = (((1,), (0,)), ((), ()))
NT = (((1,), (1,)), ((), ()))
TN = (((0,), (0,)), ((), ()))
F32 = jnp.float32
BF16 = jnp.bfloat16
SMEM = pltpu.SMEM
VMEM = pltpu.VMEM


def params(mebibytes=60):
    return pltpu.CompilerParams(vmem_limit_bytes=mebibytes << 20)


def cost(flops, moved):
    return pl.CostEstimate(flops=int(flops), bytes_accessed=int(moved), transcendentals=0)


def corner(array):
    return array[(0,) * (array.ndim - 2) + (slice(0, 8), slice(0, LANES))]


def token_shape():
    return jax.ShapeDtypeStruct((8, LANES), F32)


def whole(space):
    return pl.BlockSpec(memory_space=space)


def adamw_update(weights, gradient, first, second):
    new_first = BETA_ONE * first + (1.0 - BETA_ONE) * gradient
    new_second = BETA_TWO * second + (1.0 - BETA_TWO) * gradient * gradient
    first_hat = new_first / (1.0 - BETA_ONE**STEP)
    second_hat = new_second / (1.0 - BETA_TWO**STEP)
    updated = weights - LEARN_RATE * (
        first_hat / (jnp.sqrt(second_hat) + EPSILON) + DECAY * weights
    )
    return (updated, new_first, new_second)


def width_slices(width):
    return [(at, min(LANES, width - at)) for at in range(0, width, LANES)]


def owner_lists(all_ids, groups, capacity, ent_rows):
    count = all_ids.shape[0]
    owners = all_ids // ent_rows
    local_rows = all_ids - owners * ent_rows
    chunk = 256
    mine = owners[None, :] == jnp.arange(groups, dtype=jnp.int32)[:, None]
    mine = mine.astype(BF16).reshape(groups, count // chunk, chunk)
    before = jnp.triu(jnp.ones((chunk, chunk), BF16), 1)
    inner = jnp.dot(mine, before, preferred_element_type=F32)
    sums = jnp.sum(mine.astype(F32), axis=2)
    carry = jnp.cumsum(sums, axis=1) - sums
    ranks = jnp.sum(mine.astype(F32) * (inner + carry[:, :, None]), axis=0)
    ranks = ranks.astype(jnp.int32).reshape(count)
    counts = jnp.sum(sums, axis=1).astype(jnp.int32)
    high = owners * (capacity // LANES) + ranks // LANES
    low = ranks % LANES
    tall = groups * capacity // LANES
    left = (jnp.arange(tall, dtype=jnp.int32)[:, None] == high[None, :]).astype(BF16)
    right = (jnp.arange(LANES, dtype=jnp.int32)[:, None] == low[None, :]).astype(BF16)
    places = jnp.arange(1, count + 1, dtype=jnp.int32)
    parts = jnp.stack([places // 256, places % 256, local_rows // 256, local_rows % 256])
    right = (parts.astype(BF16)[:, None, :] * right[None]).reshape(PARTS * LANES, count)
    found = lax.dot_general(left, right, NT, preferred_element_type=F32).astype(jnp.int32)
    found = found.reshape(tall, PARTS, LANES)
    place = found[:, 0] * 256 + found[:, 1]
    place_list = jnp.where(place > 0, place - 1, count).reshape(groups, capacity)
    row_list = jnp.where(place > 0, found[:, 2] * 256 + found[:, 3], ent_rows)
    return place_list, row_list.reshape(groups, capacity), counts


def relation_rows_kernel(slices, ids_ref, scale_ref, *refs):
    n = len(slices)
    tables, outs = refs[:n], refs[-2 * n - 1 : -n - 1]
    columns, rows = refs[-n - 1], refs[-n:]
    groups = tables[0].shape[0]
    for (_, depth), table, into in zip(slices, tables, rows):
        columns[...] = jnp.zeros_like(columns)

        def turn(group, carry):
            columns[:depth, :] = table[group, :depth].astype(F32)
            if depth < LANES:
                columns[LANES - 1 :, :] = scale_ref[pl.ds(group, 1), :]
            into[pl.ds(pl.multiple_of(group * REL_PAD, REL_PAD), REL_PAD), :] = columns[...].T
            return carry

        lax.fori_loop(0, groups, turn, 0, unroll=4)

    def body(step, carry):
        for lane in range(UNROLL):
            at = step * UNROLL + lane
            row = ids_ref[at]
            for source, out in zip(rows, outs):
                out[pl.ds(at, 1), :] = source[pl.ds(row, 1), :]
        return carry

    lax.fori_loop(0, outs[0].shape[0] // UNROLL, body, 0)


def relation_rows(places, dense, scale, slices, after):
    count = places.shape[0]
    groups, depth, span = dense.shape
    n = len(slices)
    first = span // REL_PAD - n

    def columns(k):
        return pl.BlockSpec((groups, depth, REL_PAD), lambda i: (0, 0, first + k))

    return pl.pallas_call(
        functools.partial(relation_rows_kernel, slices),
        out_shape=[jax.ShapeDtypeStruct((count, LANES), F32)] * n,
        grid=(1,),
        in_specs=[whole(SMEM), whole(VMEM)]
        + [columns(k) for k in range(n)]
        + [whole(pl.ANY)] * len(after),
        out_specs=[whole(VMEM)] * n,
        scratch_shapes=[pltpu.VMEM((LANES, REL_PAD), F32)]
        + [pltpu.VMEM((groups * REL_PAD, LANES), F32)] * n,
        compiler_params=params(28),
        cost_estimate=cost(0, 80e6),
        name="relation_rows",
    )(places, scale, *[dense] * n, *after)


def fetch_kernel(
    capacity, moves, ent_rows, counts_ref, place_ref, row_ref, dense_ref, *refs
):
    shard = pl.program_id(0)
    last = pl.num_programs(0) - 1
    out_ref, rows = refs[-3], refs[-2:]
    depth = dense_ref.shape[1]
    turns = ent_rows // TURN
    rest = ent_rows - turns * TURN

    if depth < LANES:

        @pl.when(shard == 0)
        def _():
            for ref in rows:
                ref[...] = jnp.zeros_like(ref)

    def turn(into, begin, size):
        cols = pl.ds(begin, size)
        into[cols, :depth] = dense_ref[0, :, cols].astype(F32).T

    def move(source, at):
        out_ref[pl.ds(place_ref[at], 1), :] = source[pl.ds(row_ref[at], 1), :]

    def step(into, source):
        base = (shard - 1) * capacity

        def remaining(first):
            def body(trip, carry):
                for lane in range(UNROLL):
                    move(source, base + first + trip * UNROLL + lane)
                return carry

            wanted = counts_ref[jnp.maximum(shard - 1, 0)] - first
            lax.fori_loop(0, (wanted + UNROLL - 1) // UNROLL, body, 0)

        def only_turn(trip, carry):
            turn(into, pl.multiple_of(trip * TURN, TURN), TURN)
            return carry

        def both(trip, carry):
            turn(into, pl.multiple_of(trip * TURN, TURN), TURN)
            for lane in range(moves):
                move(source, base + trip * moves + lane)
            return carry

        @pl.when(shard == 0)
        def _():
            lax.fori_loop(0, turns, only_turn, 0)

        @pl.when((shard > 0) & (shard < last))
        def _():
            lax.fori_loop(0, turns, both, 0)
            remaining(turns * moves)

        @pl.when(shard == last)
        def _():
            remaining(0)

        if rest:

            @pl.when(shard < last)
            def _():
                turn(into, turns * TURN, rest)

    for parity in range(2):

        @pl.when(lax.rem(shard, 2) == parity)
        def _():
            step(rows[parity], rows[1 - parity])


def fetch(counts, place_list, row_list, dense, id_count, ent_rows, after):
    groups, depth, _ = dense.shape
    capacity = place_list.shape[0] // groups
    moves = (id_count // groups) // (ent_rows // TURN) // UNROLL * UNROLL
    return pl.pallas_call(
        functools.partial(fetch_kernel, capacity, moves, ent_rows),
        out_shape=jax.ShapeDtypeStruct((id_count + 8, LANES), F32),
        grid=(groups + 1,),
        in_specs=[whole(SMEM)] * 3
        + [
            pl.BlockSpec(
                (1, depth, ent_rows), lambda shard: (jnp.minimum(shard, groups - 1), 0, 0)
            )
        ]
        + [whole(pl.ANY)] * len(after),
        out_specs=whole(VMEM),
        scratch_shapes=[pltpu.VMEM((ent_rows + 8, LANES), F32)] * 2,
        compiler_params=params(32),
        cost_estimate=cost(0, 170e6),
        name="fetch_rows",
    )(counts, place_list, row_list, dense, *after)


def column_sum(values):
    return jnp.sum(values * values, axis=0, keepdims=True)


def negatives_kernel(neg_ref, early_ref, late_ref, norm_ref):
    neg_t = neg_ref[...].T
    early_ref[...] = neg_t[:EARLY].astype(BF16)
    late_ref[...] = neg_t[EARLY:].astype(BF16)
    norm_ref[...] = column_sum(neg_t)


def negatives(fetched, blocks, block_len):
    count = blocks * block_len
    return pl.pallas_call(
        negatives_kernel,
        out_shape=[
            jax.ShapeDtypeStruct((EARLY, count), BF16),
            jax.ShapeDtypeStruct((LANES - EARLY, count), BF16),
            jax.ShapeDtypeStruct((1, count), F32),
        ],
        grid=(blocks,),
        in_specs=[pl.BlockSpec((block_len, LANES), lambda b: (2 * blocks + b, 0))],
        out_specs=[
            pl.BlockSpec((EARLY, block_len), lambda b: (0, b)),
            pl.BlockSpec((LANES - EARLY, block_len), lambda b: (0, b)),
            pl.BlockSpec((1, block_len), lambda b: (0, b)),
        ],
        compiler_params=params(12),
        cost_estimate=cost(0, 10e6),
        name="negatives",
    )(fetched)


def edge_parts(depth, head_ref, tail_ref, rel_ref, off_ref, tail_out):
    lane = lax.broadcasted_iota(jnp.int32, head_ref.shape, 1)
    inside = lane < depth
    rel = rel_ref[...]
    tail = tail_ref[...]
    shifted = head_ref[...] + jnp.where(inside, rel, 0.0)
    off_ref[...] = jnp.where(inside, shifted - tail, rel)
    tail_out[...] = tail.astype(BF16)
    shifted_t = shifted.T
    return shifted_t, column_sum((shifted - tail).T) - column_sum(shifted_t)


def edges_kernel(
    depth, head_ref, tail_ref, rel_ref, late_ref, off_ref, tail_out, low_ref, bias_ref
):
    shifted_t, bias = edge_parts(depth, head_ref, tail_ref, rel_ref, off_ref, tail_out)
    low_ref[:depth] = shifted_t[:depth].astype(BF16)
    low_ref[depth:] = late_ref[...]
    bias_ref[...] = bias


def edges(fetched, rel_rows, late, depth, blocks, block_len):
    count = blocks * block_len
    tall = depth + late.shape[0]

    def rows(at):
        return pl.BlockSpec((block_len, LANES), lambda b: (at * blocks + b, 0))

    return pl.pallas_call(
        functools.partial(edges_kernel, depth),
        out_shape=[
            jax.ShapeDtypeStruct((count, LANES), F32),
            jax.ShapeDtypeStruct((count, LANES), BF16),
            jax.ShapeDtypeStruct((tall, count), BF16),
            jax.ShapeDtypeStruct((1, count), F32),
        ],
        grid=(blocks,),
        in_specs=[rows(0), rows(1), rows(0)]
        + [pl.BlockSpec((tall - depth, block_len), lambda b: (0, b))],
        out_specs=[
            rows(0),
            rows(0),
            pl.BlockSpec((tall, block_len), lambda b: (0, b)),
            pl.BlockSpec((1, block_len), lambda b: (0, b)),
        ],
        compiler_params=params(16),
        cost_estimate=cost(0, 30e6),
        name="edges",
    )(fetched, fetched, rel_rows, late)


def last_rows(depth):
    return (depth + 7) // 8 * 8


def with_terms(columns, total, depth):
    place = lax.broadcasted_iota(jnp.int32, (8, total.shape[1]), 0)
    left = total
    terms = jnp.zeros(place.shape, F32)
    for k in range(TERMS):
        term = left.astype(BF16).astype(F32)
        left = left - term
        terms = jnp.where(place == k, term, terms)
    return jnp.concatenate([columns[: last_rows(depth)], terms], axis=0).astype(BF16)


def last_kernel(depth, n_given, head_ref, tail_ref, neg_ref, rel_ref, *refs):
    biases, norms = refs[:n_given], refs[n_given : 2 * n_given]
    off_ref, tail_out, pair_ref = refs[-3:]
    shifted_t, bias = edge_parts(depth, head_ref, tail_ref, rel_ref, off_ref, tail_out)
    neg_t = neg_ref[...].T
    norm = column_sum(neg_t)
    for ref in biases:
        bias = bias + ref[...]
    for ref in norms:
        norm = norm + ref[...]
    pair_ref[0] = with_terms(shifted_t, bias, depth)
    pair_ref[1] = with_terms(neg_t, norm, depth)


def last_slice(fetched, rel_rows, biases, norms, depth, blocks, block_len, half, after):
    part = blocks // HALVES
    count = part * block_len
    tall = last_rows(depth) + 8

    def rows(at):
        return pl.BlockSpec((block_len, LANES), lambda b: (at * blocks + half * part + b, 0))

    return pl.pallas_call(
        functools.partial(last_kernel, depth, len(biases)),
        out_shape=[
            jax.ShapeDtypeStruct((count, LANES), F32),
            jax.ShapeDtypeStruct((count, LANES), BF16),
            jax.ShapeDtypeStruct((2, tall, count), BF16),
        ],
        grid=(part,),
        in_specs=[rows(0), rows(1), rows(2), rows(0)]
        + [pl.BlockSpec((1, block_len), lambda b: (0, half * part + b))]
        * (len(biases) + len(norms))
        + [whole(pl.ANY)] * len(after),
        out_specs=[
            pl.BlockSpec((block_len, LANES), lambda b: (b, 0)),
            pl.BlockSpec((block_len, LANES), lambda b: (b, 0)),
            pl.BlockSpec((2, tall, block_len), lambda b: (0, 0, b)),
        ],
        compiler_params=params(16),
        cost_estimate=cost(0, 20e6),
        name="last_slice",
    )(fetched, fetched, fetched, rel_rows, *biases, *norms, *after)


def block_kernel(slices, n_col, half, me_ref, live_ref, *refs):
    n = len(slices)
    per_col = 2 * n - 1
    given = [refs[k * per_col : (k + 1) * per_col] for k in range(n_col)]
    refs = refs[n_col * per_col :]
    offs, tails, refs = refs[:n], refs[n : 2 * n], refs[2 * n :]
    grad, refs = refs[-9], refs[-8:]
    loss_ref, shift_scr, neg_scr, sums_scr, cross, slopes, row_bias, row_sum = refs
    block = pl.program_id(0)
    length = cross.shape[0]
    me = me_ref[0]
    for k in range(n_col):
        slot = lax.rem(me + (n_col - k), n_col)
        for m, (start, depth) in enumerate(slices):
            if m < n - 1:
                early, late = given[k][2 * m : 2 * m + 2]
                shift_scr[slot, start : start + depth, :] = 2.0 * late[:depth, :]
                neg_scr[slot, start : start + EARLY, :] = early[...]
                neg_scr[slot, start + EARLY : start + depth, :] = late[depth:, :]
            else:
                pair = given[k][-1]
                shift, neg = pair[0, :depth, :], pair[1, :depth, :]
                for row in range(2):
                    terms = pair[row, last_rows(depth) : last_rows(depth) + 8, :].astype(F32)
                    sums_scr[slot, row : row + 1] = jnp.sum(terms, axis=0, keepdims=True)
                shift_scr[slot, start : start + depth, :] = 2.0 * shift
                neg_scr[slot, start : start + depth, :] = neg
    bias = jnp.sum(sums_scr[:, 0, :], axis=0, keepdims=True) + MARGIN
    neg_norm = jnp.sum(sums_scr[:, 1, :], axis=0, keepdims=True)
    row_bias[...] = jnp.broadcast_to(bias, (LANES, length)).T

    live = live_ref[half * pl.num_programs(0) + block]
    tile = 256
    small = 128
    lane_tiles = [slice(at, at + LANES) for at in range(0, length, LANES)]
    cols = jnp.zeros((8, length), F32)
    loss = jnp.zeros((8, LANES), F32)
    def products(at):
        part = slice(at, at + tile)
        doubled = None
        for k in range(n_col):
            term = lax.dot_general(
                shift_scr[k, :, part], neg_scr[k], TN, preferred_element_type=F32
            )
            doubled = term if doubled is None else doubled + term
        cross[part, :] = doubled

    def moves(at):
        part = slice(at, at + tile)
        moved = lax.dot_general(slopes[part, :], neg_scr[me], NT, preferred_element_type=F32)
        fade = -row_sum[part, :]
        for m, (start, depth) in enumerate(slices):
            into = pl.ds(n * at + m, tile, stride=n)
            grad[0, into, :depth] = (
                fade[:, :depth] * tails[m][part, :depth].astype(F32)
                + moved[:, start : start + depth]
            )
            grad[1, into, :] = fade * offs[m][part, :]

    products(0)
    for begin in range(0, length, tile):
        if begin + tile < length:
            products(begin + tile)
        for at in range(begin, begin + tile, small):
            part = slice(at, at + small)
            place = at + lax.broadcasted_iota(jnp.int32, (small, 1), 0)
            scale = offs[-1][part, LANES - 1 : LANES]
            weight = jnp.where(place < live, scale, 0.0) / length
            margins = cross[part, :] + (row_bias[part, 0:1] - neg_norm)
            fall = jnp.exp(-jnp.abs(margins))
            under = 1.0 + fall
            guess = pl.reciprocal(under, approx=True)
            inverse = guess * (2.0 - under * guess)
            twice = (2.0 * weight) * (jnp.where(margins >= 0.0, 1.0, fall) * inverse)
            row_sum[part, :] = jnp.broadcast_to(
                jnp.sum(twice, axis=1, keepdims=True), (small, LANES)
            )
            slopes[part, :] = twice.astype(BF16)
            cols = cols + jnp.sum(twice.reshape(small // 8, 8, length), axis=0)
            over = jnp.maximum(margins, 0.0)
            lifts = [fall[:, lanes] for lanes in lane_tiles]
            while len(lifts) > 1:
                lifts = [a + b + a * b for a, b in zip(lifts[::2], lifts[1::2])]
            lift = lifts[0]
            soft = functools.reduce(jnp.add, [over[:, lanes] for lanes in lane_tiles]) + jnp.where(
                lift < 2.0**-11, lift * (1.0 - 0.5 * lift), jnp.log(1.0 + lift)
            )
            loss = loss + jnp.sum((weight * soft).reshape(small // 8, 8, LANES), axis=0)
        moves(begin)
    col_sum = jnp.sum(cols, axis=0, keepdims=True)

    @pl.when(block == 0)
    def _():
        loss_ref[...] = loss

    @pl.when(block > 0)
    def _():
        loss_ref[...] += loss

    moved = lax.dot_general(shift_scr[me], slopes[...], NN, preferred_element_type=F32)
    moved = 0.5 * moved - col_sum * neg_scr[me].astype(F32)
    for m, (start, depth) in enumerate(slices):
        grad[2, pl.ds(m, length, stride=n), :depth] = moved[start : start + depth, :].T


def block_math(me, live_counts, given, offs, tails, old, slices, block_len, half, after):
    n, n_col = len(slices), len(given)
    blocks = live_counts.shape[0]
    part = blocks // HALVES
    width = sum(depth for _, depth in slices)
    flat = [piece for per_col in given for piece in per_col]
    kept = [] if old is None else [old]

    def columns(piece):
        if piece.ndim == 3:
            return pl.BlockSpec((2, piece.shape[1], block_len), lambda b: (0, 0, b))
        return pl.BlockSpec((piece.shape[0], block_len), lambda b: (0, half * part + b))

    def rows(array):
        first = half * part if array.shape[0] > part * block_len else 0
        return pl.BlockSpec((block_len, LANES), lambda b: (first + b, 0))

    first_old = 2 + len(flat) + 2 * n
    return pl.pallas_call(
        functools.partial(block_kernel, slices, n_col, half),
        out_shape=[
            jax.ShapeDtypeStruct((3, n * blocks * block_len, LANES), F32),
            jax.ShapeDtypeStruct((8, LANES), F32),
        ],
        grid=(part,),
        in_specs=[whole(SMEM)] * 2
        + [columns(piece) for piece in flat]
        + [rows(array) for array in offs + tails]
        + [whole(pl.ANY)] * len(kept + after),
        out_specs=[
            pl.BlockSpec((3, n * block_len, LANES), lambda b: (0, half * part + b, 0)),
            pl.BlockSpec((8, LANES), lambda b: (0, 0)),
        ],
        input_output_aliases={first_old + k: k for k in range(len(kept))},
        scratch_shapes=[
            pltpu.VMEM((n_col, width, block_len), BF16),
            pltpu.VMEM((n_col, width, block_len), BF16),
            pltpu.VMEM((n_col, 2, block_len), F32),
            pltpu.VMEM((block_len, block_len), F32),
            pltpu.VMEM((block_len, block_len), BF16),
            pltpu.VMEM((block_len, LANES), F32),
            pltpu.VMEM((block_len, LANES), F32),
        ],
        compiler_params=params(30),
        cost_estimate=cost(part * 8 * block_len * block_len * width, 120e6),
        name="block_math",
    )(me, live_counts, *flat, *offs, *tails, *kept, *after)


def pair_of(row, n):
    return pl.ds(pl.multiple_of(row * n, n), n)


def outgoing_kernel(slices, capacity, begin, counts_ref, place_ref, grad, *refs):
    n = len(slices)
    out_ref, tile = refs[-2:]
    groups, width, chunk = out_ref.shape

    def owner(group, carry):
        wanted = jnp.clip(counts_ref[group] - begin, 0, chunk)

        def body(step, inner):
            for lane in range(UNROLL):
                at = step * UNROLL + lane
                place = place_ref[group * capacity + begin + at]
                tile[pair_of(at, n), :] = grad[pair_of(place, n), :]
            return inner

        lax.fori_loop(0, (wanted + UNROLL - 1) // UNROLL, body, 0)
        for m, (start, depth) in enumerate(slices):
            piece = tile[pl.ds(m, chunk, stride=n), :].T
            out_ref[group, start : start + depth, :] = piece[:depth].astype(BF16)
        return carry

    lax.fori_loop(0, groups, owner, 0)


def outgoing(counts, place_list, grad, slices, begin, chunk, after):
    groups, capacity = place_list.shape
    n = len(slices)
    width = sum(depth for _, depth in slices)
    return pl.pallas_call(
        functools.partial(outgoing_kernel, slices, capacity, begin),
        out_shape=jax.ShapeDtypeStruct((groups, width, chunk), BF16),
        in_specs=[whole(SMEM)] * 2 + [whole(VMEM)] + [whole(pl.ANY)] * len(after),
        out_specs=whole(VMEM),
        scratch_shapes=[pltpu.VMEM((n * chunk, LANES), F32)],
        compiler_params=params(34),
        cost_estimate=cost(0, 80e6),
        name="outgoing",
    )(counts, place_list.reshape(-1), grad, *after)


def collect_kernel(slices, capacity, begin, first, counts_ref, row_ref, came_ref, *refs):
    total, token, tile = refs[-3:]
    total[...] = jnp.zeros_like(total) if first else refs[0][...]
    token[...] = jnp.zeros_like(token)
    add_rows(slices, capacity, begin, counts_ref, row_ref, came_ref, total, tile)


def add_rows(slices, capacity, begin, counts_ref, row_ref, came_ref, total, tile):
    n = len(slices)
    groups, width, chunk = came_ref.shape

    def source(group, carry):
        wanted = jnp.clip(counts_ref[group] - begin, 0, chunk)

        @pl.when(wanted > 0)
        def _():
            for m, (start, depth) in enumerate(slices):
                piece = came_ref[group, start : start + depth, :].astype(F32)
                tile[pl.ds(m, chunk, stride=n), :depth] = piece.T

            def body(step, inner):
                for lane in range(UNROLL):
                    at = step * UNROLL + lane
                    into = pair_of(row_ref[group * capacity + begin + at], n)
                    total[into, :] = total[into, :] + tile[pair_of(at, n), :]
                return inner

            lax.fori_loop(0, (wanted + UNROLL - 1) // UNROLL, body, 0)

        return carry

    lax.fori_loop(0, groups, source, 0)


def collect(counts, row_list, came, total, slices, begin, ent_rows, after):
    capacity = row_list.shape[1]
    chunk = came.shape[2]
    n = len(slices)
    given = [] if total is None else [total]
    return pl.pallas_call(
        functools.partial(collect_kernel, slices, capacity, begin, total is None),
        out_shape=[jax.ShapeDtypeStruct((n * (ent_rows + 8), LANES), F32), token_shape()],
        input_output_aliases={3: 0} if given else {},
        in_specs=[whole(SMEM)] * 2
        + [whole(VMEM)] * (1 + len(given))
        + [whole(pl.ANY)] * len(after),
        out_specs=[whole(VMEM)] * 2,
        scratch_shapes=[pltpu.VMEM((n * chunk, LANES), F32)],
        compiler_params=params(26),
        cost_estimate=cost(0, 120e6),
        name="collect",
    )(counts, row_list.reshape(-1), came, *given, *after)


def relation_sums_kernel(n, ids_ref, grad, *refs):
    total, token = refs[-2:]
    total[...] = jnp.zeros_like(total)
    token[...] = jnp.zeros_like(token)

    def body(step, carry):
        for lane in range(UNROLL):
            at = step * UNROLL + lane
            into = pair_of(ids_ref[at], n)
            total[into, :] = total[into, :] + grad[0, pair_of(at, n), :]
        return carry

    lax.fori_loop(0, grad.shape[1] // n // UNROLL, body, 0)


def relation_sums(relation_ids, grad, n, rel_total, after):
    count = relation_ids.shape[0]
    return pl.pallas_call(
        functools.partial(relation_sums_kernel, n),
        out_shape=[jax.ShapeDtypeStruct((n * rel_total, LANES), F32), token_shape()],
        grid=(1,),
        in_specs=[whole(SMEM), pl.BlockSpec((1, n * count, LANES), lambda i: (0, 0, 0))]
        + [whole(pl.ANY)] * len(after),
        out_specs=[whole(VMEM)] * 2,
        compiler_params=params(30),
        cost_estimate=cost(0, 120e6),
        name="relation_sums",
    )(relation_ids, grad, *after)


def finish_kernel(
    slices,
    capacity,
    begin,
    counts_ref,
    row_ref,
    came_ref,
    total_ref,
    weights_ref,
    first_ref,
    second_ref,
    *refs,
):
    n = len(slices)
    outs, (total, tile, gradient) = refs[:3], refs[3:]
    cols = weights_ref.shape[1]
    step = pl.program_id(0)

    @pl.when(step == 0)
    def _():
        total[: total_ref.shape[0], :] = total_ref[...]
        add_rows(slices, capacity, begin, counts_ref, row_ref, came_ref, total, tile)

    for m, (start, depth) in enumerate(slices):
        part = total[pl.ds(step * (n * cols) + m, cols, stride=n), :]
        gradient[start : start + depth, :] = part.T[:depth]
    results = adamw_update(weights_ref[...], gradient[...], first_ref[...], second_ref[...])
    for out, result in zip(outs, results):
        out[...] = result


def finish_entities(counts, row_list, came, total, begin, weights, first, second, slices):
    width, ent_rows = weights.shape
    capacity = row_list.shape[1]
    cols = 1024
    steps = pl.cdiv(ent_rows, cols)
    n = len(slices)
    table = pl.BlockSpec((width, cols), lambda i: (0, i))
    tall = max(n * cols * steps, total.shape[0])
    return pl.pallas_call(
        functools.partial(finish_kernel, slices, capacity, begin),
        out_shape=[jax.ShapeDtypeStruct((width, ent_rows), F32)] * 3,
        grid=(steps,),
        in_specs=[whole(SMEM)] * 2 + [whole(VMEM)] * 2 + [table] * 3,
        out_specs=[table] * 3,
        scratch_shapes=[
            pltpu.VMEM((tall, LANES), F32),
            pltpu.VMEM((n * came.shape[2], LANES), F32),
            pltpu.VMEM((width, cols), F32),
        ],
        compiler_params=params(56),
        cost_estimate=cost(0, 60e6),
        name="finish_entities",
    )(counts, row_list.reshape(-1), came, total, weights, first, second)


def chunk_bounds(capacity):
    units = capacity // LANES
    sizes = [3, 6, 5, 2] if units == 16 else [units // 4] * 3 + [units - 3 * (units // 4)]
    bounds = [0]
    for size in sizes:
        bounds.append(bounds[-1] + size * LANES)
    return bounds


def shards(
    head_ids,
    relation_ids,
    tail_ids,
    negative_ids,
    live_counts,
    rel_weight,
    rel_count,
    entity_table,
    entity_first,
    entity_second,
    relation_table,
    relation_first,
    relation_second,
):
    groups = lax.axis_size("edge")
    n_col = lax.axis_size("col")
    width, ent_rows = entity_table.shape
    blocks, neg_count = negative_ids.shape
    block_len = head_ids.shape[0] // blocks
    edge_count = blocks * block_len
    slices = width_slices(width)
    n = len(slices)
    all_ids = jnp.concatenate([head_ids, tail_ids, negative_ids.reshape(-1)])
    id_count = all_ids.shape[0]
    capacity = (4 * id_count + 3 * groups - 1) // (3 * groups)
    rel_total = rel_weight.shape[0]

    rel_own = rel_total // groups
    rel_low = jnp.pad(relation_table.astype(BF16).T, ((0, 0), (0, REL_PAD - rel_own)))
    dense = []
    for k, (start, depth) in enumerate(slices):
        sent = entity_table[start : start + depth].astype(BF16)
        if k == 0:
            behind = [
                jnp.pad(rel_low[at : at + size], ((0, depth - size), (0, 0))) for at, size in slices
            ]
            sent = jnp.concatenate([sent] + behind, axis=1)
        dense.append(lax.all_gather(sent, "edge", axis=0, tiled=False))

    place_list, row_list, counts = owner_lists(all_ids, groups, capacity, ent_rows)
    safe_places = jnp.minimum(place_list, id_count - 1)
    place_flat, row_flat = place_list.reshape(-1), row_list.reshape(-1)

    rel_scale = rel_weight * (rel_total / jnp.sum(rel_weight)) / rel_count.astype(F32)
    rel_scale = jnp.pad(rel_scale.reshape(groups, rel_own), ((0, 0), (0, REL_PAD - rel_own)))
    rel_places = relation_ids + (relation_ids // rel_own) * (REL_PAD - rel_own)

    def from_others(array):
        turns = [[(c, (c + away) % n_col) for c in range(n_col)] for away in range(1, n_col)]
        return [lax.ppermute(array, "col", turn) for turn in turns]

    me = lax.axis_index("col").astype(jnp.int32).reshape(1)
    given = [[[] for _ in range(n_col)] for _ in range(HALVES)]
    offs = [[] for _ in range(HALVES)]
    tails = [[] for _ in range(HALVES)]
    biases, norms, first_sent, rel_rows = [], [], [], None
    for k, (start, depth) in enumerate(slices):
        sent = first_sent if k > 0 else []
        fetched = fetch(counts, place_flat, row_flat, dense[k], id_count, ent_rows, sent)
        if k < n - 1:
            early, late, norm = negatives(fetched, blocks, block_len)
            early_all = [early] + from_others(early)
            if rel_rows is None:
                rel_rows = relation_rows(rel_places, dense[0], rel_scale, slices, [norm])
            off, tail, low, bias = edges(fetched, rel_rows[k], late, depth, blocks, block_len)
            low_all = [low] + from_others(low)
            first_sent = [corner(piece) for piece in early_all[1:]]
            biases.append(bias)
            norms.append(norm)
            for half in range(HALVES):
                offs[half].append(off)
                tails[half].append(tail)
                for col in range(n_col):
                    given[half][col] += [early_all[col], low_all[col]]
            continue
        if rel_rows is None:
            rel_rows = relation_rows(rel_places, dense[0], rel_scale, slices, [])

    def finish(half, after):
        off, tail, pair = last_slice(
            fetched, rel_rows[-1], biases, norms, slices[-1][1], blocks, block_len, half, after
        )
        offs[half].append(off)
        tails[half].append(tail)
        for col, piece in enumerate([pair] + from_others(pair)):
            given[half][col].append(piece)

    grad, loss_tiles = None, []
    for half in range(HALVES):
        finish(half, [corner(offs[half - 1][-1])] if half > 0 else [])
    row_list, _ = lax.optimization_barrier((row_list, corner(offs[-1][-1])))
    asked = lax.all_to_all(row_list, "edge", split_axis=0, concat_axis=0, tiled=True)
    asked_counts = jnp.sum((asked < ent_rows).astype(jnp.int32), axis=1)
    for half in range(HALVES):
        after = [corner(asked)] if half == 0 else []
        grad, loss_tile = block_math(
            me,
            live_counts,
            given[half],
            offs[half],
            tails[half],
            grad,
            slices,
            block_len,
            half,
            after,
        )
        loss_tiles.append(loss_tile)
    live = jnp.sum(jnp.minimum(live_counts, block_len)).astype(F32)
    loss_own = jnp.sum(functools.reduce(jnp.add, loss_tiles))
    lane = jnp.arange(LANES, dtype=jnp.int32)
    loss_row = jnp.where(lane == 0, loss_own, jnp.where(lane == 1, live, 0.0))
    loss_all = lax.all_to_all(
        jnp.broadcast_to(loss_row, (groups, 1, LANES)), "edge", split_axis=0, concat_axis=0, tiled=True
    )
    loss_pair = jnp.sum(loss_all[:, 0, :2], axis=0)

    flat = grad.reshape(n * id_count, LANES)
    bounds = chunk_bounds(capacity)
    chunks = len(bounds) - 1
    arrived, total, after = [], None, []
    for k in range(chunks):
        sent = outgoing(
            counts, safe_places, flat, slices, bounds[k], bounds[k + 1] - bounds[k], after
        )
        arrived.append(lax.all_to_all(sent, "edge", split_axis=0, concat_axis=0, tiled=True))
        after = []
        if k == 1:
            before = [corner(arrived[0]), corner(loss_all)]
            rel_terms, token = relation_sums(relation_ids, grad, n, rel_total, before)
            after = [token]
            rel_terms = rel_terms.reshape(rel_total, n * LANES)[:, :width]
            relation_grad = lax.psum_scatter(rel_terms, "edge", scatter_dimension=0, tiled=True)
        if k == chunks - 1:
            after = [corner(relation_grad)]
        if k > 0:
            total, token = collect(
                asked_counts, asked, arrived[k - 1], total, slices, bounds[k - 1], ent_rows, after
            )
            after = [token, corner(rel_terms)]
    k = chunks - 1
    new_entity, new_entity_first, new_entity_second = finish_entities(
        asked_counts,
        asked,
        arrived[k],
        total,
        bounds[k],
        entity_table,
        entity_first,
        entity_second,
        slices,
    )
    new_relation, new_relation_first, new_relation_second = adamw_update(
        relation_table, relation_grad, relation_first, relation_second
    )
    return (
        loss_pair,
        new_entity,
        new_entity_first,
        new_entity_second,
        new_relation,
        new_relation_first,
        new_relation_second,
    )


def solution(mesh):
    placed = (
        P("edge"),
        P("edge"),
        P("edge"),
        P("edge", None),
        P("edge"),
        P(),
        P(),
        P("col", "edge"),
        P("col", "edge"),
        P("col", "edge"),
        P("edge", "col"),
        P("edge", "col"),
        P("edge", "col"),
    )
    return jax.shard_map(
        shards,
        mesh=mesh,
        in_specs=placed,
        out_specs=(
            P(),
            P("col", "edge"),
            P("col", "edge"),
            P("col", "edge"),
            P("edge", "col"),
            P("edge", "col"),
            P("edge", "col"),
        ),
        check_vma=False,
    )
```

```python
import functools

import jax
import jax.numpy as jnp
from jax import lax
from jax.experimental import pallas as pl
from jax.experimental.pallas import tpu as pltpu
from jax.sharding import PartitionSpec as P

STEP = 5


MARGIN = 0.1
LEARN_RATE = 0.1
BETA_ONE = 0.5
BETA_TWO = 0.5
EPSILON = 1e-08
DECAY = 0.01
LANES = 128
UNROLL = 8
PARTS = 4
EARLY = 48
TURN = 512
REL_PAD = 256
TERMS = 3
NN = (((1,), (0,)), ((), ()))
NT = (((1,), (1,)), ((), ()))
TN = (((0,), (0,)), ((), ()))
F32 = jnp.float32
BF16 = jnp.bfloat16
SMEM = pltpu.SMEM
VMEM = pltpu.VMEM


def params(mebibytes=60):
    return pltpu.CompilerParams(vmem_limit_bytes=mebibytes << 20)


def cost(flops, moved):
    return pl.CostEstimate(flops=int(flops), bytes_accessed=int(moved), transcendentals=0)


def corner(array):
    return array[(0,) * (array.ndim - 2) + (slice(0, 8), slice(0, LANES))]


def token_shape():
    return jax.ShapeDtypeStruct((8, LANES), F32)


def whole(space):
    return pl.BlockSpec(memory_space=space)


def adamw_update(weights, gradient, first, second):
    new_first = BETA_ONE * first + (1.0 - BETA_ONE) * gradient
    new_second = BETA_TWO * second + (1.0 - BETA_TWO) * gradient * gradient
    first_hat = new_first / (1.0 - BETA_ONE**STEP)
    second_hat = new_second / (1.0 - BETA_TWO**STEP)
    updated = weights - LEARN_RATE * (
        first_hat / (jnp.sqrt(second_hat) + EPSILON) + DECAY * weights
    )
    return (updated, new_first, new_second)


def block_parts(blocks):
    small = max(1, blocks // 4)
    middle = (blocks - small) // 2
    return [(0, small), (small, middle), (small + middle, blocks - small - middle)]


def width_slices(width):
    return [(at, min(LANES, width - at)) for at in range(0, width, LANES)]


def owner_lists(all_ids, groups, capacity, ent_rows):
    count = all_ids.shape[0]
    owners = all_ids // ent_rows
    local_rows = all_ids - owners * ent_rows
    chunk = 256
    mine = owners[None, :] == jnp.arange(groups, dtype=jnp.int32)[:, None]
    mine = mine.astype(BF16).reshape(groups, count // chunk, chunk)
    before = jnp.triu(jnp.ones((chunk, chunk), BF16), 1)
    inner = jnp.dot(mine, before, preferred_element_type=F32)
    sums = jnp.sum(mine.astype(F32), axis=2)
    carry = jnp.cumsum(sums, axis=1) - sums
    ranks = jnp.sum(mine.astype(F32) * (inner + carry[:, :, None]), axis=0)
    ranks = ranks.astype(jnp.int32).reshape(count)
    counts = jnp.sum(sums, axis=1).astype(jnp.int32)
    high = owners * (capacity // LANES) + ranks // LANES
    low = ranks % LANES
    tall = groups * capacity // LANES
    left = (jnp.arange(tall, dtype=jnp.int32)[:, None] == high[None, :]).astype(BF16)
    right = (jnp.arange(LANES, dtype=jnp.int32)[:, None] == low[None, :]).astype(BF16)
    places = jnp.arange(1, count + 1, dtype=jnp.int32)
    parts = jnp.stack([places // 256, places % 256, local_rows // 256, local_rows % 256])
    right = (parts.astype(BF16)[:, None, :] * right[None]).reshape(PARTS * LANES, count)
    found = lax.dot_general(left, right, NT, preferred_element_type=F32).astype(jnp.int32)
    found = found.reshape(tall, PARTS, LANES)
    place = found[:, 0] * 256 + found[:, 1]
    place_list = jnp.where(place > 0, place - 1, count).reshape(groups, capacity)
    row_list = jnp.where(place > 0, found[:, 2] * 256 + found[:, 3], ent_rows)
    return place_list, row_list.reshape(groups, capacity), counts


def relation_rows_kernel(slices, ids_ref, scale_ref, *refs):
    n = len(slices)
    tables, outs = refs[:n], refs[-2 * n - 1 : -n - 1]
    columns, rows = refs[-n - 1], refs[-n:]
    groups = tables[0].shape[0]
    for (_, depth), table, into in zip(slices, tables, rows):
        columns[...] = jnp.zeros_like(columns)

        def turn(group, carry):
            columns[:depth, :] = table[group, :depth].astype(F32)
            if depth < LANES:
                columns[LANES - 1 :, :] = scale_ref[pl.ds(group, 1), :]
            into[pl.ds(pl.multiple_of(group * REL_PAD, REL_PAD), REL_PAD), :] = columns[...].T
            return carry

        lax.fori_loop(0, groups, turn, 0, unroll=4)

    def body(step, carry):
        for lane in range(UNROLL):
            at = step * UNROLL + lane
            row = ids_ref[at]
            for source, out in zip(rows, outs):
                out[pl.ds(at, 1), :] = source[pl.ds(row, 1), :]
        return carry

    lax.fori_loop(0, outs[0].shape[0] // UNROLL, body, 0)


def relation_rows(places, dense, scale, slices, after):
    count = places.shape[0]
    groups, depth, span = dense.shape
    n = len(slices)
    first = span // REL_PAD - n

    def columns(k):
        return pl.BlockSpec((groups, depth, REL_PAD), lambda i: (0, 0, first + k))

    return pl.pallas_call(
        functools.partial(relation_rows_kernel, slices),
        out_shape=[jax.ShapeDtypeStruct((count, LANES), F32)] * n,
        grid=(1,),
        in_specs=[whole(SMEM), whole(VMEM)]
        + [columns(k) for k in range(n)]
        + [whole(pl.ANY)] * len(after),
        out_specs=[whole(VMEM)] * n,
        scratch_shapes=[pltpu.VMEM((LANES, REL_PAD), F32)]
        + [pltpu.VMEM((groups * REL_PAD, LANES), F32)] * n,
        compiler_params=params(28),
        cost_estimate=cost(0, 80e6),
        name="relation_rows",
    )(places, scale, *[dense] * n, *after)


def fetch_kernel(
    capacity, moves, ent_rows, counts_ref, place_ref, row_ref, dense_ref, *refs
):
    shard = pl.program_id(0)
    last = pl.num_programs(0) - 1
    out_ref, rows = refs[-3], refs[-2:]
    depth = dense_ref.shape[1]
    turns = ent_rows // TURN
    rest = ent_rows - turns * TURN

    if depth < LANES:

        @pl.when(shard == 0)
        def _():
            for ref in rows:
                ref[...] = jnp.zeros_like(ref)

    def turn(into, begin, size):
        cols = pl.ds(begin, size)
        into[cols, :depth] = dense_ref[0, :, cols].astype(F32).T

    def move(source, at):
        out_ref[pl.ds(place_ref[at], 1), :] = source[pl.ds(row_ref[at], 1), :]

    def step(into, source):
        base = (shard - 1) * capacity

        def remaining(first):
            def body(trip, carry):
                for lane in range(UNROLL):
                    move(source, base + first + trip * UNROLL + lane)
                return carry

            wanted = counts_ref[jnp.maximum(shard - 1, 0)] - first
            lax.fori_loop(0, (wanted + UNROLL - 1) // UNROLL, body, 0)

        def only_turn(trip, carry):
            turn(into, pl.multiple_of(trip * TURN, TURN), TURN)
            return carry

        def both(trip, carry):
            turn(into, pl.multiple_of(trip * TURN, TURN), TURN)
            for lane in range(moves):
                move(source, base + trip * moves + lane)
            return carry

        @pl.when(shard == 0)
        def _():
            lax.fori_loop(0, turns, only_turn, 0)

        @pl.when((shard > 0) & (shard < last))
        def _():
            lax.fori_loop(0, turns, both, 0)
            remaining(turns * moves)

        @pl.when(shard == last)
        def _():
            remaining(0)

        if rest:

            @pl.when(shard < last)
            def _():
                turn(into, turns * TURN, rest)

    for parity in range(2):

        @pl.when(lax.rem(shard, 2) == parity)
        def _():
            step(rows[parity], rows[1 - parity])


def fetch(counts, place_list, row_list, dense, id_count, ent_rows, after):
    groups, depth, _ = dense.shape
    capacity = place_list.shape[0] // groups
    moves = (id_count // groups) // (ent_rows // TURN) // UNROLL * UNROLL
    return pl.pallas_call(
        functools.partial(fetch_kernel, capacity, moves, ent_rows),
        out_shape=jax.ShapeDtypeStruct((id_count + 8, LANES), F32),
        grid=(groups + 1,),
        in_specs=[whole(SMEM)] * 3
        + [
            pl.BlockSpec(
                (1, depth, ent_rows), lambda shard: (jnp.minimum(shard, groups - 1), 0, 0)
            )
        ]
        + [whole(pl.ANY)] * len(after),
        out_specs=whole(VMEM),
        scratch_shapes=[pltpu.VMEM((ent_rows + 8, LANES), F32)] * 2,
        compiler_params=params(32),
        cost_estimate=cost(0, 170e6),
        name="fetch_rows",
    )(counts, place_list, row_list, dense, *after)


def column_sum(values):
    return jnp.sum(values * values, axis=0, keepdims=True)


def negatives_kernel(neg_ref, early_ref, late_ref, norm_ref):
    neg_t = neg_ref[...].T
    early_ref[...] = neg_t[:EARLY].astype(BF16)
    late_ref[...] = neg_t[EARLY:].astype(BF16)
    norm_ref[...] = column_sum(neg_t)


def negatives(fetched, blocks, block_len):
    count = blocks * block_len
    return pl.pallas_call(
        negatives_kernel,
        out_shape=[
            jax.ShapeDtypeStruct((EARLY, count), BF16),
            jax.ShapeDtypeStruct((LANES - EARLY, count), BF16),
            jax.ShapeDtypeStruct((1, count), F32),
        ],
        grid=(blocks,),
        in_specs=[pl.BlockSpec((block_len, LANES), lambda b: (2 * blocks + b, 0))],
        out_specs=[
            pl.BlockSpec((EARLY, block_len), lambda b: (0, b)),
            pl.BlockSpec((LANES - EARLY, block_len), lambda b: (0, b)),
            pl.BlockSpec((1, block_len), lambda b: (0, b)),
        ],
        compiler_params=params(12),
        cost_estimate=cost(0, 10e6),
        name="negatives",
    )(fetched)


def edge_parts(depth, head_ref, tail_ref, rel_ref, off_ref, tail_out):
    lane = lax.broadcasted_iota(jnp.int32, head_ref.shape, 1)
    inside = lane < depth
    rel = rel_ref[...]
    tail = tail_ref[...]
    shifted = head_ref[...] + jnp.where(inside, rel, 0.0)
    off_ref[...] = jnp.where(inside, shifted - tail, rel)
    tail_out[...] = tail.astype(BF16)
    shifted_t = shifted.T
    return shifted_t, column_sum((shifted - tail).T) - column_sum(shifted_t)


def edges_kernel(
    depth, head_ref, tail_ref, rel_ref, late_ref, *refs
):
    off_ref, tail_out, low_ref, bias_ref = refs[-4:]
    shifted_t, bias = edge_parts(depth, head_ref, tail_ref, rel_ref, off_ref, tail_out)
    low_ref[:depth] = shifted_t[:depth].astype(BF16)
    low_ref[depth:] = late_ref[...]
    bias_ref[...] = bias


def edges(fetched, rel_rows, late, depth, blocks, block_len, after):
    count = blocks * block_len
    tall = depth + late.shape[0]

    def rows(at):
        return pl.BlockSpec((block_len, LANES), lambda b: (at * blocks + b, 0))

    return pl.pallas_call(
        functools.partial(edges_kernel, depth),
        out_shape=[
            jax.ShapeDtypeStruct((count, LANES), F32),
            jax.ShapeDtypeStruct((count, LANES), BF16),
            jax.ShapeDtypeStruct((tall, count), BF16),
            jax.ShapeDtypeStruct((1, count), F32),
        ],
        grid=(blocks,),
        in_specs=[rows(0), rows(1), rows(0)]
        + [pl.BlockSpec((tall - depth, block_len), lambda b: (0, b))]
        + [whole(pl.ANY)] * len(after),
        out_specs=[
            rows(0),
            rows(0),
            pl.BlockSpec((tall, block_len), lambda b: (0, b)),
            pl.BlockSpec((1, block_len), lambda b: (0, b)),
        ],
        compiler_params=params(16),
        cost_estimate=cost(0, 30e6),
        name="edges",
    )(fetched, fetched, rel_rows, late, *after)


def last_rows(depth):
    return (depth + 7) // 8 * 8


def with_terms(columns, total, depth):
    place = lax.broadcasted_iota(jnp.int32, (8, total.shape[1]), 0)
    left = total
    terms = jnp.zeros(place.shape, F32)
    for k in range(TERMS):
        term = left.astype(BF16).astype(F32)
        left = left - term
        terms = jnp.where(place == k, term, terms)
    return jnp.concatenate([columns[: last_rows(depth)], terms], axis=0).astype(BF16)


def last_kernel(depth, n_given, head_ref, tail_ref, neg_ref, rel_ref, *refs):
    biases, norms = refs[:n_given], refs[n_given : 2 * n_given]
    off_ref, tail_out, pair_ref = refs[-3:]
    shifted_t, bias = edge_parts(depth, head_ref, tail_ref, rel_ref, off_ref, tail_out)
    neg_t = neg_ref[...].T
    norm = column_sum(neg_t)
    for ref in biases:
        bias = bias + ref[...]
    for ref in norms:
        norm = norm + ref[...]
    pair_ref[0] = with_terms(shifted_t, bias, depth)
    pair_ref[1] = with_terms(neg_t, norm, depth)


def last_slice(fetched, rel_rows, biases, norms, depth, blocks, block_len, part, after):
    first, size = part
    count = size * block_len
    tall = last_rows(depth) + 8

    def rows(at):
        return pl.BlockSpec((block_len, LANES), lambda b: (at * blocks + first + b, 0))

    return pl.pallas_call(
        functools.partial(last_kernel, depth, len(biases)),
        out_shape=[
            jax.ShapeDtypeStruct((count, LANES), F32),
            jax.ShapeDtypeStruct((count, LANES), BF16),
            jax.ShapeDtypeStruct((2, tall, count), BF16),
        ],
        grid=(size,),
        in_specs=[rows(0), rows(1), rows(2), rows(0)]
        + [pl.BlockSpec((1, block_len), lambda b: (0, first + b))]
        * (len(biases) + len(norms))
        + [whole(pl.ANY)] * len(after),
        out_specs=[
            pl.BlockSpec((block_len, LANES), lambda b: (b, 0)),
            pl.BlockSpec((block_len, LANES), lambda b: (b, 0)),
            pl.BlockSpec((2, tall, block_len), lambda b: (0, 0, b)),
        ],
        compiler_params=params(16),
        cost_estimate=cost(0, 20e6),
        name="last_slice",
    )(fetched, fetched, fetched, rel_rows, *biases, *norms, *after)


def block_kernel(slices, n_col, first_block, me_ref, live_ref, *refs):
    n = len(slices)
    per_col = 2 * n - 1
    given = [refs[k * per_col : (k + 1) * per_col] for k in range(n_col)]
    refs = refs[n_col * per_col :]
    offs, tails, refs = refs[:n], refs[n : 2 * n], refs[2 * n :]
    grad, refs = refs[-9], refs[-8:]
    loss_ref, shift_scr, neg_scr, sums_scr, cross, slopes, row_bias, row_sum = refs
    block = pl.program_id(0)
    length = cross.shape[0]
    me = me_ref[0]
    for k in range(n_col):
        slot = lax.rem(me + (n_col - k), n_col)
        for m, (start, depth) in enumerate(slices):
            if m < n - 1:
                early, late = given[k][2 * m : 2 * m + 2]
                shift_scr[slot, start : start + depth, :] = 2.0 * late[:depth, :]
                neg_scr[slot, start : start + EARLY, :] = early[...]
                neg_scr[slot, start + EARLY : start + depth, :] = late[depth:, :]
            else:
                pair = given[k][-1]
                shift, neg = pair[0, :depth, :], pair[1, :depth, :]
                for row in range(2):
                    terms = pair[row, last_rows(depth) : last_rows(depth) + 8, :].astype(F32)
                    sums_scr[slot, row : row + 1] = jnp.sum(terms, axis=0, keepdims=True)
                shift_scr[slot, start : start + depth, :] = 2.0 * shift
                neg_scr[slot, start : start + depth, :] = neg
    bias = jnp.sum(sums_scr[:, 0, :], axis=0, keepdims=True) + MARGIN
    neg_norm = jnp.sum(sums_scr[:, 1, :], axis=0, keepdims=True)
    row_bias[...] = jnp.broadcast_to(bias, (LANES, length)).T

    live = live_ref[first_block + block]
    tile = 256
    small = 128
    lane_tiles = [slice(at, at + LANES) for at in range(0, length, LANES)]
    cols = jnp.zeros((8, length), F32)
    loss = jnp.zeros((8, LANES), F32)
    def products(at):
        part = slice(at, at + tile)
        doubled = None
        for k in range(n_col):
            term = lax.dot_general(
                shift_scr[k, :, part], neg_scr[k], TN, preferred_element_type=F32
            )
            doubled = term if doubled is None else doubled + term
        cross[part, :] = doubled

    def moves(at):
        part = slice(at, at + tile)
        moved = lax.dot_general(slopes[part, :], neg_scr[me], NT, preferred_element_type=F32)
        fade = -row_sum[part, :]
        for m, (start, depth) in enumerate(slices):
            into = pl.ds(n * at + m, tile, stride=n)
            grad[0, into, :depth] = (
                fade[:, :depth] * tails[m][part, :depth].astype(F32)
                + moved[:, start : start + depth]
            )
            grad[1, into, :] = fade * offs[m][part, :]

    products(0)
    for begin in range(0, length, tile):
        if begin + tile < length:
            products(begin + tile)
        for at in range(begin, begin + tile, small):
            part = slice(at, at + small)
            place = at + lax.broadcasted_iota(jnp.int32, (small, 1), 0)
            scale = offs[-1][part, LANES - 1 : LANES]
            weight = jnp.where(place < live, scale, 0.0) / length
            margins = cross[part, :] + (row_bias[part, 0:1] - neg_norm)
            fall = jnp.exp(-jnp.abs(margins))
            under = 1.0 + fall
            guess = pl.reciprocal(under, approx=True)
            inverse = guess * (2.0 - under * guess)
            twice = (2.0 * weight) * (jnp.where(margins >= 0.0, 1.0, fall) * inverse)
            row_sum[part, :] = jnp.broadcast_to(
                jnp.sum(twice, axis=1, keepdims=True), (small, LANES)
            )
            slopes[part, :] = twice.astype(BF16)
            cols = cols + jnp.sum(twice.reshape(small // 8, 8, length), axis=0)
            over = jnp.maximum(margins, 0.0)
            lifts = [fall[:, lanes] for lanes in lane_tiles]
            while len(lifts) > 1:
                lifts = [a + b + a * b for a, b in zip(lifts[::2], lifts[1::2])]
            lift = lifts[0]
            soft = functools.reduce(jnp.add, [over[:, lanes] for lanes in lane_tiles]) + jnp.where(
                lift < 2.0**-11, lift * (1.0 - 0.5 * lift), jnp.log(1.0 + lift)
            )
            loss = loss + jnp.sum((weight * soft).reshape(small // 8, 8, LANES), axis=0)
        moves(begin)
    col_sum = jnp.sum(cols, axis=0, keepdims=True)

    @pl.when(block == 0)
    def _():
        loss_ref[...] = loss

    @pl.when(block > 0)
    def _():
        loss_ref[...] += loss

    moved = lax.dot_general(shift_scr[me], slopes[...], NN, preferred_element_type=F32)
    moved = 0.5 * moved - col_sum * neg_scr[me].astype(F32)
    for m, (start, depth) in enumerate(slices):
        grad[2, pl.ds(m, length, stride=n), :depth] = moved[start : start + depth, :].T


def block_math(me, live_counts, given, offs, tails, old, slices, block_len, part, after):
    n, n_col = len(slices), len(given)
    blocks = live_counts.shape[0]
    begin, size = part
    width = sum(depth for _, depth in slices)
    flat = [piece for per_col in given for piece in per_col]
    kept = [] if old is None else [old]

    def columns(piece):
        if piece.ndim == 3:
            return pl.BlockSpec((2, piece.shape[1], block_len), lambda b: (0, 0, b))
        return pl.BlockSpec((piece.shape[0], block_len), lambda b: (0, begin + b))

    def rows(array):
        first = begin if array.shape[0] > size * block_len else 0
        return pl.BlockSpec((block_len, LANES), lambda b: (first + b, 0))

    first_old = 2 + len(flat) + 2 * n
    return pl.pallas_call(
        functools.partial(block_kernel, slices, n_col, begin),
        out_shape=[
            jax.ShapeDtypeStruct((3, n * blocks * block_len, LANES), F32),
            jax.ShapeDtypeStruct((8, LANES), F32),
        ],
        grid=(size,),
        in_specs=[whole(SMEM)] * 2
        + [columns(piece) for piece in flat]
        + [rows(array) for array in offs + tails]
        + [whole(pl.ANY)] * len(kept + after),
        out_specs=[
            pl.BlockSpec((3, n * block_len, LANES), lambda b: (0, begin + b, 0)),
            pl.BlockSpec((8, LANES), lambda b: (0, 0)),
        ],
        input_output_aliases={first_old + k: k for k in range(len(kept))},
        scratch_shapes=[
            pltpu.VMEM((n_col, width, block_len), BF16),
            pltpu.VMEM((n_col, width, block_len), BF16),
            pltpu.VMEM((n_col, 2, block_len), F32),
            pltpu.VMEM((block_len, block_len), F32),
            pltpu.VMEM((block_len, block_len), BF16),
            pltpu.VMEM((block_len, LANES), F32),
            pltpu.VMEM((block_len, LANES), F32),
        ],
        compiler_params=params(60),
        cost_estimate=cost(size * 8 * block_len * block_len * width, 120e6),
        name="block_math",
    )(me, live_counts, *flat, *offs, *tails, *kept, *after)


def pair_of(row, n):
    return pl.ds(pl.multiple_of(row * n, n), n)


def outgoing_kernel(slices, capacity, begin, counts_ref, place_ref, grad, *refs):
    n = len(slices)
    out_ref, tile = refs[-2:]
    groups, width, chunk = out_ref.shape

    def owner(group, carry):
        wanted = jnp.clip(counts_ref[group] - begin, 0, chunk)

        def body(step, inner):
            for lane in range(UNROLL):
                at = step * UNROLL + lane
                place = place_ref[group * capacity + begin + at]
                tile[pair_of(at, n), :] = grad[pair_of(place, n), :]
            return inner

        lax.fori_loop(0, (wanted + UNROLL - 1) // UNROLL, body, 0)
        for m, (start, depth) in enumerate(slices):
            piece = tile[pl.ds(m, chunk, stride=n), :].T
            out_ref[group, start : start + depth, :] = piece[:depth].astype(BF16)
        return carry

    lax.fori_loop(0, groups, owner, 0)


def outgoing(counts, place_list, grad, slices, begin, chunk, after):
    groups, capacity = place_list.shape
    n = len(slices)
    width = sum(depth for _, depth in slices)
    return pl.pallas_call(
        functools.partial(outgoing_kernel, slices, capacity, begin),
        out_shape=jax.ShapeDtypeStruct((groups, width, chunk), BF16),
        in_specs=[whole(SMEM)] * 2 + [whole(VMEM)] + [whole(pl.ANY)] * len(after),
        out_specs=whole(VMEM),
        scratch_shapes=[pltpu.VMEM((n * chunk, LANES), F32)],
        compiler_params=params(34),
        cost_estimate=cost(0, 80e6),
        name="outgoing",
    )(counts, place_list.reshape(-1), grad, *after)


def collect_kernel(slices, capacity, begin, first, counts_ref, row_ref, came_ref, *refs):
    total, token, tile = refs[-3:]
    total[...] = jnp.zeros_like(total) if first else refs[0][...]
    token[...] = jnp.zeros_like(token)
    add_rows(slices, capacity, begin, counts_ref, row_ref, came_ref, total, tile)


def add_rows(slices, capacity, begin, counts_ref, row_ref, came_ref, total, tile):
    n = len(slices)
    groups, width, chunk = came_ref.shape

    def source(group, carry):
        wanted = jnp.clip(counts_ref[group] - begin, 0, chunk)

        @pl.when(wanted > 0)
        def _():
            for m, (start, depth) in enumerate(slices):
                piece = came_ref[group, start : start + depth, :].astype(F32)
                tile[pl.ds(m, chunk, stride=n), :depth] = piece.T

            def body(step, inner):
                for lane in range(UNROLL):
                    at = step * UNROLL + lane
                    into = pair_of(row_ref[group * capacity + begin + at], n)
                    total[into, :] = total[into, :] + tile[pair_of(at, n), :]
                return inner

            lax.fori_loop(0, (wanted + UNROLL - 1) // UNROLL, body, 0)

        return carry

    lax.fori_loop(0, groups, source, 0)


def collect(counts, row_list, came, total, slices, begin, ent_rows, after):
    capacity = row_list.shape[1]
    chunk = came.shape[2]
    n = len(slices)
    given = [] if total is None else [total]
    return pl.pallas_call(
        functools.partial(collect_kernel, slices, capacity, begin, total is None),
        out_shape=[jax.ShapeDtypeStruct((n * (ent_rows + 8), LANES), F32), token_shape()],
        input_output_aliases={3: 0} if given else {},
        in_specs=[whole(SMEM)] * 2
        + [whole(VMEM)] * (1 + len(given))
        + [whole(pl.ANY)] * len(after),
        out_specs=[whole(VMEM)] * 2,
        scratch_shapes=[pltpu.VMEM((n * chunk, LANES), F32)],
        compiler_params=params(26),
        cost_estimate=cost(0, 120e6),
        name="collect",
    )(counts, row_list.reshape(-1), came, *given, *after)


def relation_sums_kernel(n, ids_ref, grad, *refs):
    total, token = refs[-2:]
    total[...] = jnp.zeros_like(total)
    token[...] = jnp.zeros_like(token)

    def body(step, carry):
        for lane in range(UNROLL):
            at = step * UNROLL + lane
            into = pair_of(ids_ref[at], n)
            total[into, :] = total[into, :] + grad[0, pair_of(at, n), :]
        return carry

    lax.fori_loop(0, grad.shape[1] // n // UNROLL, body, 0)


def relation_sums(relation_ids, grad, n, rel_total, after):
    count = relation_ids.shape[0]
    return pl.pallas_call(
        functools.partial(relation_sums_kernel, n),
        out_shape=[jax.ShapeDtypeStruct((n * rel_total, LANES), F32), token_shape()],
        grid=(1,),
        in_specs=[whole(SMEM), pl.BlockSpec((1, n * count, LANES), lambda i: (0, 0, 0))]
        + [whole(pl.ANY)] * len(after),
        out_specs=[whole(VMEM)] * 2,
        compiler_params=params(30),
        cost_estimate=cost(0, 120e6),
        name="relation_sums",
    )(relation_ids, grad, *after)


def finish_kernel(
    slices,
    capacity,
    begin,
    counts_ref,
    row_ref,
    came_ref,
    total_ref,
    weights_ref,
    first_ref,
    second_ref,
    *refs,
):
    n = len(slices)
    outs, (total, tile, gradient) = refs[:3], refs[3:]
    cols = weights_ref.shape[1]
    step = pl.program_id(0)

    @pl.when(step == 0)
    def _():
        total[: total_ref.shape[0], :] = total_ref[...]
        add_rows(slices, capacity, begin, counts_ref, row_ref, came_ref, total, tile)

    for m, (start, depth) in enumerate(slices):
        part = total[pl.ds(step * (n * cols) + m, cols, stride=n), :]
        gradient[start : start + depth, :] = part.T[:depth]
    results = adamw_update(weights_ref[...], gradient[...], first_ref[...], second_ref[...])
    for out, result in zip(outs, results):
        out[...] = result


def finish_entities(counts, row_list, came, total, begin, weights, first, second, slices):
    width, ent_rows = weights.shape
    capacity = row_list.shape[1]
    cols = 1024
    steps = pl.cdiv(ent_rows, cols)
    n = len(slices)
    table = pl.BlockSpec((width, cols), lambda i: (0, i))
    tall = max(n * cols * steps, total.shape[0])
    return pl.pallas_call(
        functools.partial(finish_kernel, slices, capacity, begin),
        out_shape=[jax.ShapeDtypeStruct((width, ent_rows), F32)] * 3,
        grid=(steps,),
        in_specs=[whole(SMEM)] * 2 + [whole(VMEM)] * 2 + [table] * 3,
        out_specs=[table] * 3,
        scratch_shapes=[
            pltpu.VMEM((tall, LANES), F32),
            pltpu.VMEM((n * came.shape[2], LANES), F32),
            pltpu.VMEM((width, cols), F32),
        ],
        compiler_params=params(56),
        cost_estimate=cost(0, 60e6),
        name="finish_entities",
    )(counts, row_list.reshape(-1), came, total, weights, first, second)


def chunk_bounds(capacity):
    units = capacity // LANES
    sizes = [3, 6, 5, 2] if units == 16 else [units // 4] * 3 + [units - 3 * (units // 4)]
    bounds = [0]
    for size in sizes:
        bounds.append(bounds[-1] + size * LANES)
    return bounds


def shards(
    head_ids,
    relation_ids,
    tail_ids,
    negative_ids,
    live_counts,
    rel_weight,
    rel_count,
    entity_table,
    entity_first,
    entity_second,
    relation_table,
    relation_first,
    relation_second,
):
    groups = lax.axis_size("edge")
    n_col = lax.axis_size("col")
    width, ent_rows = entity_table.shape
    blocks, neg_count = negative_ids.shape
    block_len = head_ids.shape[0] // blocks
    edge_count = blocks * block_len
    slices = width_slices(width)
    n = len(slices)
    all_ids = jnp.concatenate([head_ids, tail_ids, negative_ids.reshape(-1)])
    id_count = all_ids.shape[0]
    capacity = (4 * id_count + 3 * groups - 1) // (3 * groups)
    rel_total = rel_weight.shape[0]

    rel_own = rel_total // groups
    rel_low = jnp.pad(relation_table.astype(BF16).T, ((0, 0), (0, REL_PAD - rel_own)))
    dense = []
    for k, (start, depth) in enumerate(slices):
        sent = entity_table[start : start + depth].astype(BF16)
        if k == 0:
            behind = [
                jnp.pad(rel_low[at : at + size], ((0, depth - size), (0, 0))) for at, size in slices
            ]
            sent = jnp.concatenate([sent] + behind, axis=1)
        dense.append(lax.all_gather(sent, "edge", axis=0, tiled=False))

    place_list, row_list, counts = owner_lists(all_ids, groups, capacity, ent_rows)
    safe_places = jnp.minimum(place_list, id_count - 1)
    place_flat, row_flat = place_list.reshape(-1), row_list.reshape(-1)

    rel_scale = rel_weight * (rel_total / jnp.sum(rel_weight)) / rel_count.astype(F32)
    rel_scale = jnp.pad(rel_scale.reshape(groups, rel_own), ((0, 0), (0, REL_PAD - rel_own)))
    rel_places = relation_ids + (relation_ids // rel_own) * (REL_PAD - rel_own)

    def from_others(array):
        turns = [[(c, (c + away) % n_col) for c in range(n_col)] for away in range(1, n_col)]
        return [lax.ppermute(array, "col", turn) for turn in turns]

    me = lax.axis_index("col").astype(jnp.int32).reshape(1)
    parts = block_parts(blocks)
    given = [[[] for _ in range(n_col)] for _ in range(len(parts))]
    offs = [[] for _ in range(len(parts))]
    tails = [[] for _ in range(len(parts))]
    biases, norms, rel_rows = [], [], None
    for k, (start, depth) in enumerate(slices):
        fetched = fetch(counts, place_flat, row_flat, dense[k], id_count, ent_rows, [])
        if k < n - 1:
            early, late, norm = negatives(fetched, blocks, block_len)
            early_all = [early] + from_others(early)
            first_sent = [corner(piece) for piece in early_all[1:]]
            if rel_rows is None:
                rel_rows = relation_rows(rel_places, dense[0], rel_scale, slices, [norm])
            off, tail, low, bias = edges(
                fetched, rel_rows[k], late, depth, blocks, block_len, first_sent
            )
            low_all = [low] + from_others(low)
            biases.append(bias)
            norms.append(norm)
            for half in range(len(parts)):
                offs[half].append(off)
                tails[half].append(tail)
                for col in range(n_col):
                    given[half][col] += [early_all[col], low_all[col]]
            continue
        if rel_rows is None:
            rel_rows = relation_rows(rel_places, dense[0], rel_scale, slices, [])

    def finish(half, after):
        off, tail, pair = last_slice(
            fetched, rel_rows[-1], biases, norms, slices[-1][1], blocks, block_len, parts[half], after
        )
        offs[half].append(off)
        tails[half].append(tail)
        for col, piece in enumerate([pair] + from_others(pair)):
            given[half][col].append(piece)

    grad, loss_tiles = None, []
    finish(0, [])
    finish(1, [corner(offs[0][-1])])
    finish(2, [corner(piece) for piece in given[0][-1][-1:]])
    row_list, _ = lax.optimization_barrier((row_list, corner(offs[1][-1])))
    asked = lax.all_to_all(row_list, "edge", split_axis=0, concat_axis=0, tiled=True)
    asked_counts = jnp.sum((asked < ent_rows).astype(jnp.int32), axis=1)
    for half in range(len(parts)):
        after = [corner(asked), corner(offs[2][-1])] if half == 0 else []
        grad, loss_tile = block_math(
            me,
            live_counts,
            given[half],
            offs[half],
            tails[half],
            grad,
            slices,
            block_len,
            parts[half],
            after,
        )
        loss_tiles.append(loss_tile)
    live = jnp.sum(jnp.minimum(live_counts, block_len)).astype(F32)
    loss_own = jnp.sum(functools.reduce(jnp.add, loss_tiles))
    lane = jnp.arange(LANES, dtype=jnp.int32)
    loss_row = jnp.where(lane == 0, loss_own, jnp.where(lane == 1, live, 0.0))
    loss_all = lax.all_to_all(
        jnp.broadcast_to(loss_row, (groups, 1, LANES)), "edge", split_axis=0, concat_axis=0, tiled=True
    )
    loss_pair = jnp.sum(loss_all[:, 0, :2], axis=0)

    flat = grad.reshape(n * id_count, LANES)
    bounds = chunk_bounds(capacity)
    chunks = len(bounds) - 1
    arrived, total, after = [], None, []
    for k in range(chunks):
        sent = outgoing(
            counts, safe_places, flat, slices, bounds[k], bounds[k + 1] - bounds[k], after
        )
        arrived.append(lax.all_to_all(sent, "edge", split_axis=0, concat_axis=0, tiled=True))
        after = []
        if k == 1:
            before = [corner(arrived[0]), corner(loss_all)]
            rel_terms, token = relation_sums(relation_ids, grad, n, rel_total, before)
            after = [token]
            relation_grad = lax.psum_scatter(rel_terms, "edge", scatter_dimension=0, tiled=True)
            relation_grad = relation_grad.reshape(rel_own, n * LANES)[:, :width]
        if k == chunks - 1:
            after = [corner(relation_grad)]
        if k > 0:
            total, token = collect(
                asked_counts, asked, arrived[k - 1], total, slices, bounds[k - 1], ent_rows, after
            )
            after = [token, corner(rel_terms)]
    k = chunks - 1
    new_entity, new_entity_first, new_entity_second = finish_entities(
        asked_counts,
        asked,
        arrived[k],
        total,
        bounds[k],
        entity_table,
        entity_first,
        entity_second,
        slices,
    )
    new_relation, new_relation_first, new_relation_second = adamw_update(
        relation_table, relation_grad, relation_first, relation_second
    )
    return (
        loss_pair,
        new_entity,
        new_entity_first,
        new_entity_second,
        new_relation,
        new_relation_first,
        new_relation_second,
    )


def solution(mesh):
    placed = (
        P("edge"),
        P("edge"),
        P("edge"),
        P("edge", None),
        P("edge"),
        P(),
        P(),
        P("col", "edge"),
        P("col", "edge"),
        P("col", "edge"),
        P("edge", "col"),
        P("edge", "col"),
        P("edge", "col"),
    )
    return jax.shard_map(
        shards,
        mesh=mesh,
        in_specs=placed,
        out_specs=(
            P(),
            P("col", "edge"),
            P("col", "edge"),
            P("col", "edge"),
            P("edge", "col"),
            P("edge", "col"),
            P("edge", "col"),
        ),
        check_vma=False,
    )
```

```python
import functools

import jax
import jax.numpy as jnp
from jax import lax
from jax.experimental import pallas as pl
from jax.experimental.pallas import tpu as pltpu
from jax.sharding import PartitionSpec as P

STEP = 5


MARGIN = 0.1
LEARN_RATE = 0.1
BETA_ONE = 0.5
BETA_TWO = 0.5
EPSILON = 1e-08
DECAY = 0.01
LANES = 128
UNROLL = 8
PARTS = 4
HALVES = 2
EARLY = 96
TURN = 512
REL_PAD = 256
TERMS = 3
NN = (((1,), (0,)), ((), ()))
NT = (((1,), (1,)), ((), ()))
TN = (((0,), (0,)), ((), ()))
F32 = jnp.float32
BF16 = jnp.bfloat16
SMEM = pltpu.SMEM
VMEM = pltpu.VMEM


def params(mebibytes=60):
    return pltpu.CompilerParams(vmem_limit_bytes=mebibytes << 20)


def cost(flops, moved):
    return pl.CostEstimate(flops=int(flops), bytes_accessed=int(moved), transcendentals=0)


def corner(array):
    return array[(0,) * (array.ndim - 2) + (slice(0, 8), slice(0, LANES))]


def token_shape():
    return jax.ShapeDtypeStruct((8, LANES), F32)


def whole(space):
    return pl.BlockSpec(memory_space=space)


def adamw_update(weights, gradient, first, second):
    new_first = BETA_ONE * first + (1.0 - BETA_ONE) * gradient
    new_second = BETA_TWO * second + (1.0 - BETA_TWO) * gradient * gradient
    first_hat = new_first / (1.0 - BETA_ONE**STEP)
    second_hat = new_second / (1.0 - BETA_TWO**STEP)
    updated = weights - LEARN_RATE * (
        first_hat / (jnp.sqrt(second_hat) + EPSILON) + DECAY * weights
    )
    return (updated, new_first, new_second)


def width_slices(width):
    return [(at, min(LANES, width - at)) for at in range(0, width, LANES)]


def owner_lists(all_ids, groups, capacity, ent_rows):
    count = all_ids.shape[0]
    owners = all_ids // ent_rows
    local_rows = all_ids - owners * ent_rows
    chunk = 256
    mine = owners[None, :] == jnp.arange(groups, dtype=jnp.int32)[:, None]
    mine = mine.astype(BF16).reshape(groups, count // chunk, chunk)
    before = jnp.triu(jnp.ones((chunk, chunk), BF16), 1)
    inner = jnp.dot(mine, before, preferred_element_type=F32)
    sums = jnp.sum(mine.astype(F32), axis=2)
    carry = jnp.cumsum(sums, axis=1) - sums
    ranks = jnp.sum(mine.astype(F32) * (inner + carry[:, :, None]), axis=0)
    ranks = ranks.astype(jnp.int32).reshape(count)
    counts = jnp.sum(sums, axis=1).astype(jnp.int32)
    high = owners * (capacity // LANES) + ranks // LANES
    low = ranks % LANES
    tall = groups * capacity // LANES
    left = (jnp.arange(tall, dtype=jnp.int32)[:, None] == high[None, :]).astype(BF16)
    right = (jnp.arange(LANES, dtype=jnp.int32)[:, None] == low[None, :]).astype(BF16)
    places = jnp.arange(1, count + 1, dtype=jnp.int32)
    parts = jnp.stack([places // 256, places % 256, local_rows // 256, local_rows % 256])
    right = (parts.astype(BF16)[:, None, :] * right[None]).reshape(PARTS * LANES, count)
    found = lax.dot_general(left, right, NT, preferred_element_type=F32).astype(jnp.int32)
    found = found.reshape(tall, PARTS, LANES)
    place = found[:, 0] * 256 + found[:, 1]
    place_list = jnp.where(place > 0, place - 1, count).reshape(groups, capacity)
    row_list = jnp.where(place > 0, found[:, 2] * 256 + found[:, 3], ent_rows)
    return place_list, row_list.reshape(groups, capacity), counts


def relation_rows_kernel(slices, ids_ref, scale_ref, *refs):
    n = len(slices)
    tables, outs = refs[:n], refs[-2 * n - 1 : -n - 1]
    columns, rows = refs[-n - 1], refs[-n:]
    groups = tables[0].shape[0]
    for (_, depth), table, into in zip(slices, tables, rows):
        columns[...] = jnp.zeros_like(columns)

        def turn(group, carry):
            columns[:depth, :] = table[group, :depth].astype(F32)
            if depth < LANES:
                columns[LANES - 1 :, :] = scale_ref[pl.ds(group, 1), :]
            into[pl.ds(pl.multiple_of(group * REL_PAD, REL_PAD), REL_PAD), :] = columns[...].T
            return carry

        lax.fori_loop(0, groups, turn, 0, unroll=4)

    def body(step, carry):
        for lane in range(UNROLL):
            at = step * UNROLL + lane
            row = ids_ref[at]
            for source, out in zip(rows, outs):
                out[pl.ds(at, 1), :] = source[pl.ds(row, 1), :]
        return carry

    lax.fori_loop(0, outs[0].shape[0] // UNROLL, body, 0)


def relation_rows(places, dense, scale, slices, after):
    count = places.shape[0]
    groups, depth, span = dense.shape
    n = len(slices)
    first = span // REL_PAD - n

    def columns(k):
        return pl.BlockSpec((groups, depth, REL_PAD), lambda i: (0, 0, first + k))

    return pl.pallas_call(
        functools.partial(relation_rows_kernel, slices),
        out_shape=[jax.ShapeDtypeStruct((count, LANES), F32)] * n,
        grid=(1,),
        in_specs=[whole(SMEM), whole(VMEM)]
        + [columns(k) for k in range(n)]
        + [whole(pl.ANY)] * len(after),
        out_specs=[whole(VMEM)] * n,
        scratch_shapes=[pltpu.VMEM((LANES, REL_PAD), F32)]
        + [pltpu.VMEM((groups * REL_PAD, LANES), F32)] * n,
        compiler_params=params(28),
        cost_estimate=cost(0, 80e6),
        name="relation_rows",
    )(places, scale, *[dense] * n, *after)


def fetch_kernel(
    capacity, moves, ent_rows, counts_ref, place_ref, row_ref, dense_ref, *refs
):
    shard = pl.program_id(0)
    last = pl.num_programs(0) - 1
    out_ref, rows = refs[-3], refs[-2:]
    depth = dense_ref.shape[1]
    turns = ent_rows // TURN
    rest = ent_rows - turns * TURN

    if depth < LANES:

        @pl.when(shard == 0)
        def _():
            for ref in rows:
                ref[...] = jnp.zeros_like(ref)

    def turn(into, begin, size):
        cols = pl.ds(begin, size)
        into[cols, :depth] = dense_ref[0, :, cols].astype(F32).T

    def move(source, at):
        out_ref[pl.ds(place_ref[at], 1), :] = source[pl.ds(row_ref[at], 1), :]

    def step(into, source):
        base = (shard - 1) * capacity

        def remaining(first):
            def body(trip, carry):
                for lane in range(UNROLL):
                    move(source, base + first + trip * UNROLL + lane)
                return carry

            wanted = counts_ref[jnp.maximum(shard - 1, 0)] - first
            lax.fori_loop(0, (wanted + UNROLL - 1) // UNROLL, body, 0)

        def only_turn(trip, carry):
            turn(into, pl.multiple_of(trip * TURN, TURN), TURN)
            return carry

        def both(trip, carry):
            turn(into, pl.multiple_of(trip * TURN, TURN), TURN)
            for lane in range(moves):
                move(source, base + trip * moves + lane)
            return carry

        @pl.when(shard == 0)
        def _():
            lax.fori_loop(0, turns, only_turn, 0)

        @pl.when((shard > 0) & (shard < last))
        def _():
            lax.fori_loop(0, turns, both, 0)
            remaining(turns * moves)

        @pl.when(shard == last)
        def _():
            remaining(0)

        if rest:

            @pl.when(shard < last)
            def _():
                turn(into, turns * TURN, rest)

    for parity in range(2):

        @pl.when(lax.rem(shard, 2) == parity)
        def _():
            step(rows[parity], rows[1 - parity])


def fetch(counts, place_list, row_list, dense, id_count, ent_rows, after):
    groups, depth, _ = dense.shape
    capacity = place_list.shape[0] // groups
    moves = (id_count // groups) // (ent_rows // TURN) // UNROLL * UNROLL
    return pl.pallas_call(
        functools.partial(fetch_kernel, capacity, moves, ent_rows),
        out_shape=jax.ShapeDtypeStruct((id_count + 8, LANES), F32),
        grid=(groups + 1,),
        in_specs=[whole(SMEM)] * 3
        + [
            pl.BlockSpec(
                (1, depth, ent_rows), lambda shard: (jnp.minimum(shard, groups - 1), 0, 0)
            )
        ]
        + [whole(pl.ANY)] * len(after),
        out_specs=whole(VMEM),
        scratch_shapes=[pltpu.VMEM((ent_rows + 8, LANES), F32)] * 2,
        compiler_params=params(32),
        cost_estimate=cost(0, 170e6),
        name="fetch_rows",
    )(counts, place_list, row_list, dense, *after)


def column_sum(values):
    return jnp.sum(values * values, axis=0, keepdims=True)


def negatives_kernel(neg_ref, early_ref, late_ref, norm_ref):
    neg_t = neg_ref[...].T
    early_ref[...] = neg_t[:EARLY].astype(BF16)
    late_ref[...] = neg_t[EARLY:].astype(BF16)
    norm_ref[...] = column_sum(neg_t)


def negatives(fetched, blocks, block_len):
    count = blocks * block_len
    return pl.pallas_call(
        negatives_kernel,
        out_shape=[
            jax.ShapeDtypeStruct((EARLY, count), BF16),
            jax.ShapeDtypeStruct((LANES - EARLY, count), BF16),
            jax.ShapeDtypeStruct((1, count), F32),
        ],
        grid=(blocks,),
        in_specs=[pl.BlockSpec((block_len, LANES), lambda b: (2 * blocks + b, 0))],
        out_specs=[
            pl.BlockSpec((EARLY, block_len), lambda b: (0, b)),
            pl.BlockSpec((LANES - EARLY, block_len), lambda b: (0, b)),
            pl.BlockSpec((1, block_len), lambda b: (0, b)),
        ],
        compiler_params=params(12),
        cost_estimate=cost(0, 10e6),
        name="negatives",
    )(fetched)


def edge_parts(depth, head_ref, tail_ref, rel_ref, off_ref, tail_out):
    lane = lax.broadcasted_iota(jnp.int32, head_ref.shape, 1)
    inside = lane < depth
    rel = rel_ref[...]
    tail = tail_ref[...]
    shifted = head_ref[...] + jnp.where(inside, rel, 0.0)
    off_ref[...] = jnp.where(inside, shifted - tail, rel)
    tail_out[...] = tail.astype(BF16)
    shifted_t = shifted.T
    return shifted_t, column_sum((shifted - tail).T) - column_sum(shifted_t)


def edges_kernel(
    depth, head_ref, tail_ref, rel_ref, late_ref, off_ref, tail_out, low_ref, bias_ref
):
    shifted_t, bias = edge_parts(depth, head_ref, tail_ref, rel_ref, off_ref, tail_out)
    low_ref[:depth] = shifted_t[:depth].astype(BF16)
    low_ref[depth:] = late_ref[...]
    bias_ref[...] = bias


def edges(fetched, rel_rows, late, depth, blocks, block_len):
    count = blocks * block_len
    tall = depth + late.shape[0]

    def rows(at):
        return pl.BlockSpec((block_len, LANES), lambda b: (at * blocks + b, 0))

    return pl.pallas_call(
        functools.partial(edges_kernel, depth),
        out_shape=[
            jax.ShapeDtypeStruct((count, LANES), F32),
            jax.ShapeDtypeStruct((count, LANES), BF16),
            jax.ShapeDtypeStruct((tall, count), BF16),
            jax.ShapeDtypeStruct((1, count), F32),
        ],
        grid=(blocks,),
        in_specs=[rows(0), rows(1), rows(0)]
        + [pl.BlockSpec((tall - depth, block_len), lambda b: (0, b))],
        out_specs=[
            rows(0),
            rows(0),
            pl.BlockSpec((tall, block_len), lambda b: (0, b)),
            pl.BlockSpec((1, block_len), lambda b: (0, b)),
        ],
        compiler_params=params(16),
        cost_estimate=cost(0, 30e6),
        name="edges",
    )(fetched, fetched, rel_rows, late)


def last_rows(depth):
    return (depth + 7) // 8 * 8


def with_terms(columns, total, depth):
    place = lax.broadcasted_iota(jnp.int32, (8, total.shape[1]), 0)
    left = total
    terms = jnp.zeros(place.shape, F32)
    for k in range(TERMS):
        term = left.astype(BF16).astype(F32)
        left = left - term
        terms = jnp.where(place == k, term, terms)
    return jnp.concatenate([columns[: last_rows(depth)], terms], axis=0).astype(BF16)


def last_kernel(depth, n_given, head_ref, tail_ref, neg_ref, rel_ref, *refs):
    biases, norms = refs[:n_given], refs[n_given : 2 * n_given]
    off_ref, tail_out, pair_ref = refs[-3:]
    shifted_t, bias = edge_parts(depth, head_ref, tail_ref, rel_ref, off_ref, tail_out)
    neg_t = neg_ref[...].T
    norm = column_sum(neg_t)
    for ref in biases:
        bias = bias + ref[...]
    for ref in norms:
        norm = norm + ref[...]
    pair_ref[0] = with_terms(shifted_t, bias, depth)
    pair_ref[1] = with_terms(neg_t, norm, depth)


def last_slice(fetched, rel_rows, biases, norms, depth, blocks, block_len, half, after):
    part = blocks // HALVES
    count = part * block_len
    tall = last_rows(depth) + 8

    def rows(at):
        return pl.BlockSpec((block_len, LANES), lambda b: (at * blocks + half * part + b, 0))

    return pl.pallas_call(
        functools.partial(last_kernel, depth, len(biases)),
        out_shape=[
            jax.ShapeDtypeStruct((count, LANES), F32),
            jax.ShapeDtypeStruct((count, LANES), BF16),
            jax.ShapeDtypeStruct((2, tall, count), BF16),
        ],
        grid=(part,),
        in_specs=[rows(0), rows(1), rows(2), rows(0)]
        + [pl.BlockSpec((1, block_len), lambda b: (0, half * part + b))]
        * (len(biases) + len(norms))
        + [whole(pl.ANY)] * len(after),
        out_specs=[
            pl.BlockSpec((block_len, LANES), lambda b: (b, 0)),
            pl.BlockSpec((block_len, LANES), lambda b: (b, 0)),
            pl.BlockSpec((2, tall, block_len), lambda b: (0, 0, b)),
        ],
        compiler_params=params(16),
        cost_estimate=cost(0, 20e6),
        name="last_slice",
    )(fetched, fetched, fetched, rel_rows, *biases, *norms, *after)


def block_kernel(slices, n_col, half, me_ref, live_ref, *refs):
    n = len(slices)
    per_col = 2 * n - 1
    given = [refs[k * per_col : (k + 1) * per_col] for k in range(n_col)]
    refs = refs[n_col * per_col :]
    offs, tails, refs = refs[:n], refs[n : 2 * n], refs[2 * n :]
    grad, refs = refs[-9], refs[-8:]
    loss_ref, shift_scr, neg_scr, sums_scr, cross, slopes, row_bias, row_sum = refs
    block = pl.program_id(0)
    length = cross.shape[0]
    me = me_ref[0]
    for k in range(n_col):
        slot = lax.rem(me + (n_col - k), n_col)
        for m, (start, depth) in enumerate(slices):
            if m < n - 1:
                early, late = given[k][2 * m : 2 * m + 2]
                shift_scr[slot, start : start + depth, :] = 2.0 * late[:depth, :]
                neg_scr[slot, start : start + EARLY, :] = early[...]
                neg_scr[slot, start + EARLY : start + depth, :] = late[depth:, :]
            else:
                pair = given[k][-1]
                shift, neg = pair[0, :depth, :], pair[1, :depth, :]
                for row in range(2):
                    terms = pair[row, last_rows(depth) : last_rows(depth) + 8, :].astype(F32)
                    sums_scr[slot, row : row + 1] = jnp.sum(terms, axis=0, keepdims=True)
                shift_scr[slot, start : start + depth, :] = 2.0 * shift
                neg_scr[slot, start : start + depth, :] = neg
    bias = jnp.sum(sums_scr[:, 0, :], axis=0, keepdims=True) + MARGIN
    neg_norm = jnp.sum(sums_scr[:, 1, :], axis=0, keepdims=True)
    row_bias[...] = jnp.broadcast_to(bias, (LANES, length)).T

    live = live_ref[half * pl.num_programs(0) + block]
    tile = 256
    small = 128
    lane_tiles = [slice(at, at + LANES) for at in range(0, length, LANES)]
    cols = jnp.zeros((8, length), F32)
    loss = jnp.zeros((8, LANES), F32)
    def products(at):
        part = slice(at, at + tile)
        doubled = None
        for k in range(n_col):
            term = lax.dot_general(
                shift_scr[k, :, part], neg_scr[k], TN, preferred_element_type=F32
            )
            doubled = term if doubled is None else doubled + term
        cross[part, :] = doubled

    def moves(at):
        part = slice(at, at + tile)
        moved = lax.dot_general(slopes[part, :], neg_scr[me], NT, preferred_element_type=F32)
        fade = -row_sum[part, :]
        for m, (start, depth) in enumerate(slices):
            into = pl.ds(n * at + m, tile, stride=n)
            grad[0, into, :depth] = (
                fade[:, :depth] * tails[m][part, :depth].astype(F32)
                + moved[:, start : start + depth]
            )
            grad[1, into, :] = fade * offs[m][part, :]

    products(0)
    for begin in range(0, length, tile):
        if begin + tile < length:
            products(begin + tile)
        for at in range(begin, begin + tile, small):
            part = slice(at, at + small)
            place = at + lax.broadcasted_iota(jnp.int32, (small, 1), 0)
            scale = offs[-1][part, LANES - 1 : LANES]
            weight = jnp.where(place < live, scale, 0.0) / length
            margins = cross[part, :] + (row_bias[part, 0:1] - neg_norm)
            fall = jnp.exp(-jnp.abs(margins))
            under = 1.0 + fall
            guess = pl.reciprocal(under, approx=True)
            inverse = guess * (2.0 - under * guess)
            twice = (2.0 * weight) * (jnp.where(margins >= 0.0, 1.0, fall) * inverse)
            row_sum[part, :] = jnp.broadcast_to(
                jnp.sum(twice, axis=1, keepdims=True), (small, LANES)
            )
            slopes[part, :] = twice.astype(BF16)
            cols = cols + jnp.sum(twice.reshape(small // 8, 8, length), axis=0)
            over = jnp.maximum(margins, 0.0)
            lifts = [fall[:, lanes] for lanes in lane_tiles]
            while len(lifts) > 1:
                lifts = [a + b + a * b for a, b in zip(lifts[::2], lifts[1::2])]
            lift = lifts[0]
            soft = functools.reduce(jnp.add, [over[:, lanes] for lanes in lane_tiles]) + jnp.where(
                lift < 2.0**-11, lift * (1.0 - 0.5 * lift), jnp.log(1.0 + lift)
            )
            loss = loss + jnp.sum((weight * soft).reshape(small // 8, 8, LANES), axis=0)
        moves(begin)
    col_sum = jnp.sum(cols, axis=0, keepdims=True)

    @pl.when(block == 0)
    def _():
        loss_ref[...] = loss

    @pl.when(block > 0)
    def _():
        loss_ref[...] += loss

    moved = lax.dot_general(shift_scr[me], slopes[...], NN, preferred_element_type=F32)
    moved = 0.5 * moved - col_sum * neg_scr[me].astype(F32)
    for m, (start, depth) in enumerate(slices):
        grad[2, pl.ds(m, length, stride=n), :depth] = moved[start : start + depth, :].T


def block_math(me, live_counts, given, offs, tails, old, slices, block_len, half, after):
    n, n_col = len(slices), len(given)
    blocks = live_counts.shape[0]
    part = blocks // HALVES
    width = sum(depth for _, depth in slices)
    flat = [piece for per_col in given for piece in per_col]
    kept = [] if old is None else [old]

    def columns(piece):
        if piece.ndim == 3:
            return pl.BlockSpec((2, piece.shape[1], block_len), lambda b: (0, 0, b))
        return pl.BlockSpec((piece.shape[0], block_len), lambda b: (0, half * part + b))

    def rows(array):
        first = half * part if array.shape[0] > part * block_len else 0
        return pl.BlockSpec((block_len, LANES), lambda b: (first + b, 0))

    first_old = 2 + len(flat) + 2 * n
    return pl.pallas_call(
        functools.partial(block_kernel, slices, n_col, half),
        out_shape=[
            jax.ShapeDtypeStruct((3, n * blocks * block_len, LANES), F32),
            jax.ShapeDtypeStruct((8, LANES), F32),
        ],
        grid=(part,),
        in_specs=[whole(SMEM)] * 2
        + [columns(piece) for piece in flat]
        + [rows(array) for array in offs + tails]
        + [whole(pl.ANY)] * len(kept + after),
        out_specs=[
            pl.BlockSpec((3, n * block_len, LANES), lambda b: (0, half * part + b, 0)),
            pl.BlockSpec((8, LANES), lambda b: (0, 0)),
        ],
        input_output_aliases={first_old + k: k for k in range(len(kept))},
        scratch_shapes=[
            pltpu.VMEM((n_col, width, block_len), BF16),
            pltpu.VMEM((n_col, width, block_len), BF16),
            pltpu.VMEM((n_col, 2, block_len), F32),
            pltpu.VMEM((block_len, block_len), F32),
            pltpu.VMEM((block_len, block_len), BF16),
            pltpu.VMEM((block_len, LANES), F32),
            pltpu.VMEM((block_len, LANES), F32),
        ],
        compiler_params=params(60),
        cost_estimate=cost(part * 8 * block_len * block_len * width, 120e6),
        name="block_math",
    )(me, live_counts, *flat, *offs, *tails, *kept, *after)


def pair_of(row, n):
    return pl.ds(pl.multiple_of(row * n, n), n)


def outgoing_kernel(slices, capacity, begin, counts_ref, place_ref, grad, *refs):
    n = len(slices)
    out_ref, tile = refs[-2:]
    groups, width, chunk = out_ref.shape

    def owner(group, carry):
        wanted = jnp.clip(counts_ref[group] - begin, 0, chunk)

        def body(step, inner):
            for lane in range(UNROLL):
                at = step * UNROLL + lane
                place = place_ref[group * capacity + begin + at]
                tile[pair_of(at, n), :] = grad[pair_of(place, n), :]
            return inner

        lax.fori_loop(0, (wanted + UNROLL - 1) // UNROLL, body, 0)
        for m, (start, depth) in enumerate(slices):
            piece = tile[pl.ds(m, chunk, stride=n), :].T
            out_ref[group, start : start + depth, :] = piece[:depth].astype(BF16)
        return carry

    lax.fori_loop(0, groups, owner, 0)


def outgoing(counts, place_list, grad, slices, begin, chunk, after):
    groups, capacity = place_list.shape
    n = len(slices)
    width = sum(depth for _, depth in slices)
    return pl.pallas_call(
        functools.partial(outgoing_kernel, slices, capacity, begin),
        out_shape=jax.ShapeDtypeStruct((groups, width, chunk), BF16),
        in_specs=[whole(SMEM)] * 2 + [whole(VMEM)] + [whole(pl.ANY)] * len(after),
        out_specs=whole(VMEM),
        scratch_shapes=[pltpu.VMEM((n * chunk, LANES), F32)],
        compiler_params=params(34),
        cost_estimate=cost(0, 80e6),
        name="outgoing",
    )(counts, place_list.reshape(-1), grad, *after)


def collect_kernel(slices, capacity, begin, first, counts_ref, row_ref, came_ref, *refs):
    total, token, tile = refs[-3:]
    total[...] = jnp.zeros_like(total) if first else refs[0][...]
    token[...] = jnp.zeros_like(token)
    add_rows(slices, capacity, begin, counts_ref, row_ref, came_ref, total, tile)


def add_rows(slices, capacity, begin, counts_ref, row_ref, came_ref, total, tile):
    n = len(slices)
    groups, width, chunk = came_ref.shape

    def source(group, carry):
        wanted = jnp.clip(counts_ref[group] - begin, 0, chunk)

        @pl.when(wanted > 0)
        def _():
            for m, (start, depth) in enumerate(slices):
                piece = came_ref[group, start : start + depth, :].astype(F32)
                tile[pl.ds(m, chunk, stride=n), :depth] = piece.T

            def body(step, inner):
                for lane in range(UNROLL):
                    at = step * UNROLL + lane
                    into = pair_of(row_ref[group * capacity + begin + at], n)
                    total[into, :] = total[into, :] + tile[pair_of(at, n), :]
                return inner

            lax.fori_loop(0, (wanted + UNROLL - 1) // UNROLL, body, 0)

        return carry

    lax.fori_loop(0, groups, source, 0)


def collect(counts, row_list, came, total, slices, begin, ent_rows, after):
    capacity = row_list.shape[1]
    chunk = came.shape[2]
    n = len(slices)
    given = [] if total is None else [total]
    return pl.pallas_call(
        functools.partial(collect_kernel, slices, capacity, begin, total is None),
        out_shape=[jax.ShapeDtypeStruct((n * (ent_rows + 8), LANES), F32), token_shape()],
        input_output_aliases={3: 0} if given else {},
        in_specs=[whole(SMEM)] * 2
        + [whole(VMEM)] * (1 + len(given))
        + [whole(pl.ANY)] * len(after),
        out_specs=[whole(VMEM)] * 2,
        scratch_shapes=[pltpu.VMEM((n * chunk, LANES), F32)],
        compiler_params=params(26),
        cost_estimate=cost(0, 120e6),
        name="collect",
    )(counts, row_list.reshape(-1), came, *given, *after)


def relation_sums_kernel(n, ids_ref, grad, *refs):
    total, token = refs[-2:]
    total[...] = jnp.zeros_like(total)
    token[...] = jnp.zeros_like(token)

    def body(step, carry):
        for lane in range(UNROLL):
            at = step * UNROLL + lane
            into = pair_of(ids_ref[at], n)
            total[into, :] = total[into, :] + grad[0, pair_of(at, n), :]
        return carry

    lax.fori_loop(0, grad.shape[1] // n // UNROLL, body, 0)


def relation_sums(relation_ids, grad, n, rel_total, after):
    count = relation_ids.shape[0]
    return pl.pallas_call(
        functools.partial(relation_sums_kernel, n),
        out_shape=[jax.ShapeDtypeStruct((n * rel_total, LANES), F32), token_shape()],
        grid=(1,),
        in_specs=[whole(SMEM), pl.BlockSpec((1, n * count, LANES), lambda i: (0, 0, 0))]
        + [whole(pl.ANY)] * len(after),
        out_specs=[whole(VMEM)] * 2,
        compiler_params=params(30),
        cost_estimate=cost(0, 120e6),
        name="relation_sums",
    )(relation_ids, grad, *after)


def finish_kernel(
    slices,
    capacity,
    begin,
    counts_ref,
    row_ref,
    came_ref,
    total_ref,
    weights_ref,
    first_ref,
    second_ref,
    *refs,
):
    n = len(slices)
    outs, (total, tile, gradient) = refs[:3], refs[3:]
    cols = weights_ref.shape[1]
    step = pl.program_id(0)

    @pl.when(step == 0)
    def _():
        total[: total_ref.shape[0], :] = total_ref[...]
        add_rows(slices, capacity, begin, counts_ref, row_ref, came_ref, total, tile)

    for m, (start, depth) in enumerate(slices):
        part = total[pl.ds(step * (n * cols) + m, cols, stride=n), :]
        gradient[start : start + depth, :] = part.T[:depth]
    results = adamw_update(weights_ref[...], gradient[...], first_ref[...], second_ref[...])
    for out, result in zip(outs, results):
        out[...] = result


def finish_entities(counts, row_list, came, total, begin, weights, first, second, slices):
    width, ent_rows = weights.shape
    capacity = row_list.shape[1]
    cols = 1024
    steps = pl.cdiv(ent_rows, cols)
    n = len(slices)
    table = pl.BlockSpec((width, cols), lambda i: (0, i))
    tall = max(n * cols * steps, total.shape[0])
    return pl.pallas_call(
        functools.partial(finish_kernel, slices, capacity, begin),
        out_shape=[jax.ShapeDtypeStruct((width, ent_rows), F32)] * 3,
        grid=(steps,),
        in_specs=[whole(SMEM)] * 2 + [whole(VMEM)] * 2 + [table] * 3,
        out_specs=[table] * 3,
        scratch_shapes=[
            pltpu.VMEM((tall, LANES), F32),
            pltpu.VMEM((n * came.shape[2], LANES), F32),
            pltpu.VMEM((width, cols), F32),
        ],
        compiler_params=params(56),
        cost_estimate=cost(0, 60e6),
        name="finish_entities",
    )(counts, row_list.reshape(-1), came, total, weights, first, second)


def chunk_bounds(capacity):
    units = capacity // LANES
    sizes = [4, 6, 3, 3] if units == 16 else [units // 4] * 3 + [units - 3 * (units // 4)]
    bounds = [0]
    for size in sizes:
        bounds.append(bounds[-1] + size * LANES)
    return bounds


def shards(
    head_ids,
    relation_ids,
    tail_ids,
    negative_ids,
    live_counts,
    rel_weight,
    rel_count,
    entity_table,
    entity_first,
    entity_second,
    relation_table,
    relation_first,
    relation_second,
):
    groups = lax.axis_size("edge")
    n_col = lax.axis_size("col")
    width, ent_rows = entity_table.shape
    blocks, neg_count = negative_ids.shape
    block_len = head_ids.shape[0] // blocks
    edge_count = blocks * block_len
    slices = width_slices(width)
    n = len(slices)
    all_ids = jnp.concatenate([head_ids, tail_ids, negative_ids.reshape(-1)])
    id_count = all_ids.shape[0]
    capacity = (4 * id_count + 3 * groups - 1) // (3 * groups)
    rel_total = rel_weight.shape[0]

    rel_own = rel_total // groups
    rel_low = jnp.pad(relation_table.astype(BF16).T, ((0, 0), (0, REL_PAD - rel_own)))
    dense = []
    for k, (start, depth) in enumerate(slices):
        sent = entity_table[start : start + depth].astype(BF16)
        if k == 0:
            behind = [
                jnp.pad(rel_low[at : at + size], ((0, depth - size), (0, 0))) for at, size in slices
            ]
            sent = jnp.concatenate([sent] + behind, axis=1)
        dense.append(lax.all_gather(sent, "edge", axis=0, tiled=False))

    place_list, row_list, counts = owner_lists(all_ids, groups, capacity, ent_rows)
    safe_places = jnp.minimum(place_list, id_count - 1)
    place_flat, row_flat = place_list.reshape(-1), row_list.reshape(-1)

    rel_scale = rel_weight * (rel_total / jnp.sum(rel_weight)) / rel_count.astype(F32)
    rel_scale = jnp.pad(rel_scale.reshape(groups, rel_own), ((0, 0), (0, REL_PAD - rel_own)))
    rel_places = relation_ids + (relation_ids // rel_own) * (REL_PAD - rel_own)

    def from_others(array):
        turns = [[(c, (c + away) % n_col) for c in range(n_col)] for away in range(1, n_col)]
        return [lax.ppermute(array, "col", turn) for turn in turns]

    me = lax.axis_index("col").astype(jnp.int32).reshape(1)
    given = [[[] for _ in range(n_col)] for _ in range(HALVES)]
    offs = [[] for _ in range(HALVES)]
    tails = [[] for _ in range(HALVES)]
    biases, norms, first_sent, rel_rows = [], [], [], None
    for k, (start, depth) in enumerate(slices):
        sent = first_sent if k > 0 else []
        fetched = fetch(counts, place_flat, row_flat, dense[k], id_count, ent_rows, sent)
        if k < n - 1:
            early, late, norm = negatives(fetched, blocks, block_len)
            early_all = [early] + from_others(early)
            if rel_rows is None:
                rel_rows = relation_rows(rel_places, dense[0], rel_scale, slices, [norm])
            off, tail, low, bias = edges(fetched, rel_rows[k], late, depth, blocks, block_len)
            low_all = [low] + from_others(low)
            first_sent = [corner(piece) for piece in early_all[1:]]
            biases.append(bias)
            norms.append(norm)
            for half in range(HALVES):
                offs[half].append(off)
                tails[half].append(tail)
                for col in range(n_col):
                    given[half][col] += [early_all[col], low_all[col]]
            continue
        if rel_rows is None:
            rel_rows = relation_rows(rel_places, dense[0], rel_scale, slices, [])

    def finish(half, after):
        off, tail, pair = last_slice(
            fetched, rel_rows[-1], biases, norms, slices[-1][1], blocks, block_len, half, after
        )
        offs[half].append(off)
        tails[half].append(tail)
        for col, piece in enumerate([pair] + from_others(pair)):
            given[half][col].append(piece)

    grad, loss_tiles = None, []
    for half in range(HALVES):
        finish(half, [corner(offs[half - 1][-1])] if half > 0 else [])
    row_list, _ = lax.optimization_barrier((row_list, corner(offs[-1][-1])))
    bounds = chunk_bounds(capacity)
    few = jnp.sum((counts > bounds[-2]).astype(jnp.int32)) <= 1
    flag = jnp.broadcast_to(few.astype(jnp.int32), (groups, LANES))
    asked = lax.all_to_all(
        jnp.concatenate([row_list, flag], axis=1), "edge", split_axis=0, concat_axis=0, tiled=True
    )
    all_few = jnp.min(asked[:, capacity]) > 0
    asked = asked[:, :capacity]
    asked_counts = jnp.sum((asked < ent_rows).astype(jnp.int32), axis=1)
    for half in range(HALVES):
        after = [corner(asked)] if half == 0 else []
        grad, loss_tile = block_math(
            me,
            live_counts,
            given[half],
            offs[half],
            tails[half],
            grad,
            slices,
            block_len,
            half,
            after,
        )
        loss_tiles.append(loss_tile)
    live = jnp.sum(jnp.minimum(live_counts, block_len)).astype(F32)
    loss_own = jnp.sum(functools.reduce(jnp.add, loss_tiles))
    lane = jnp.arange(LANES, dtype=jnp.int32)
    loss_row = jnp.where(lane == 0, loss_own, jnp.where(lane == 1, live, 0.0))
    loss_all = lax.all_to_all(
        jnp.broadcast_to(loss_row, (groups, 1, LANES)), "edge", split_axis=0, concat_axis=0, tiled=True
    )
    loss_pair = jnp.sum(loss_all[:, 0, :2], axis=0)

    flat = grad.reshape(n * id_count, LANES)
    chunks = len(bounds) - 1
    begin, size = bounds[-2], bounds[-1] - bounds[-2]
    most = jnp.argmax(counts)
    most_places = lax.dynamic_slice_in_dim(safe_places, most, 1, axis=0)
    most_count = lax.dynamic_slice_in_dim(counts, most, 1, axis=0)
    arrived, total, after = [], None, []
    for k in range(chunks - 1):
        sent = outgoing(
            counts, safe_places, flat, slices, bounds[k], bounds[k + 1] - bounds[k], after
        )
        arrived.append(lax.all_to_all(sent, "edge", split_axis=0, concat_axis=0, tiled=True))
        after = []
        if k == 1:
            before = [corner(arrived[0]), corner(loss_all)]
            excess = outgoing(most_count, most_places, flat, slices, begin, size, before)
            gathered = lax.all_gather(excess, "edge", axis=0, tiled=True)
            before = [corner(excess)]
            rel_terms, token = relation_sums(relation_ids, grad, n, rel_total, before)
            after = [token]
            rel_terms = rel_terms.reshape(rel_total, n * LANES)[:, :width]
            relation_grad = lax.psum_scatter(rel_terms, "edge", scatter_dimension=0, tiled=True)
        if k > 0:
            total, token = collect(
                asked_counts, asked, arrived[k - 1], total, slices, bounds[k - 1], ent_rows, after
            )
            after = [token, corner(rel_terms), corner(gathered)]

    def by_all_to_all():
        sent = outgoing(counts, safe_places, flat, slices, begin, size, [])
        return lax.all_to_all(sent, "edge", split_axis=0, concat_axis=0, tiled=True)

    k = chunks - 2
    total, token = collect(
        asked_counts,
        asked,
        arrived[k],
        total,
        slices,
        bounds[k],
        ent_rows,
        [],
    )
    ordered = (token[0, 0] == 0.0) & (relation_grad[0, 0] == relation_grad[0, 0])
    came = lax.cond(all_few & ordered, lambda: gathered, by_all_to_all)
    new_entity, new_entity_first, new_entity_second = finish_entities(
        asked_counts,
        asked,
        came,
        total,
        begin,
        entity_table,
        entity_first,
        entity_second,
        slices,
    )
    new_relation, new_relation_first, new_relation_second = adamw_update(
        relation_table, relation_grad, relation_first, relation_second
    )
    return (
        loss_pair,
        new_entity,
        new_entity_first,
        new_entity_second,
        new_relation,
        new_relation_first,
        new_relation_second,
    )


def solution(mesh):
    placed = (
        P("edge"),
        P("edge"),
        P("edge"),
        P("edge", None),
        P("edge"),
        P(),
        P(),
        P("col", "edge"),
        P("col", "edge"),
        P("col", "edge"),
        P("edge", "col"),
        P("edge", "col"),
        P("edge", "col"),
    )
    return jax.shard_map(
        shards,
        mesh=mesh,
        in_specs=placed,
        out_specs=(
            P(),
            P("col", "edge"),
            P("col", "edge"),
            P("col", "edge"),
            P("edge", "col"),
            P("edge", "col"),
            P("edge", "col"),
        ),
        check_vma=False,
    )
```

```python
import functools

import jax
import jax.numpy as jnp
from jax import lax
from jax.experimental import pallas as pl
from jax.experimental.pallas import tpu as pltpu
from jax.sharding import PartitionSpec as P

STEP = 5


MARGIN = 0.1
LEARN_RATE = 0.1
BETA_ONE = 0.5
BETA_TWO = 0.5
EPSILON = 1e-08
DECAY = 0.01
LANES = 128
UNROLL = 8
PARTS = 4
HALVES = 2
EARLY = 96
TURN = 512
REL_PAD = 256
TERMS = 3
NN = (((1,), (0,)), ((), ()))
NT = (((1,), (1,)), ((), ()))
TN = (((0,), (0,)), ((), ()))
F32 = jnp.float32
BF16 = jnp.bfloat16
SMEM = pltpu.SMEM
VMEM = pltpu.VMEM


def params(mebibytes=60):
    return pltpu.CompilerParams(vmem_limit_bytes=mebibytes << 20)


def cost(flops, moved):
    return pl.CostEstimate(flops=int(flops), bytes_accessed=int(moved), transcendentals=0)


def corner(array):
    return array[(0,) * (array.ndim - 2) + (slice(0, 8), slice(0, LANES))]


def token_shape():
    return jax.ShapeDtypeStruct((8, LANES), F32)


def whole(space):
    return pl.BlockSpec(memory_space=space)


def adamw_update(weights, gradient, first, second):
    new_first = BETA_ONE * first + (1.0 - BETA_ONE) * gradient
    new_second = BETA_TWO * second + (1.0 - BETA_TWO) * gradient * gradient
    first_hat = new_first / (1.0 - BETA_ONE**STEP)
    second_hat = new_second / (1.0 - BETA_TWO**STEP)
    updated = weights - LEARN_RATE * (
        first_hat / (jnp.sqrt(second_hat) + EPSILON) + DECAY * weights
    )
    return (updated, new_first, new_second)


def width_slices(width):
    return [(at, min(LANES, width - at)) for at in range(0, width, LANES)]


def owner_lists(all_ids, groups, capacity, ent_rows):
    count = all_ids.shape[0]
    owners = all_ids // ent_rows
    local_rows = all_ids - owners * ent_rows
    chunk = 256
    mine = owners[None, :] == jnp.arange(groups, dtype=jnp.int32)[:, None]
    mine = mine.astype(BF16).reshape(groups, count // chunk, chunk)
    before = jnp.triu(jnp.ones((chunk, chunk), BF16), 1)
    inner = jnp.dot(mine, before, preferred_element_type=F32)
    sums = jnp.sum(mine.astype(F32), axis=2)
    carry = jnp.cumsum(sums, axis=1) - sums
    ranks = jnp.sum(mine.astype(F32) * (inner + carry[:, :, None]), axis=0)
    ranks = ranks.astype(jnp.int32).reshape(count)
    counts = jnp.sum(sums, axis=1).astype(jnp.int32)
    high = owners * (capacity // LANES) + ranks // LANES
    low = ranks % LANES
    tall = groups * capacity // LANES
    left = (jnp.arange(tall, dtype=jnp.int32)[:, None] == high[None, :]).astype(BF16)
    right = (jnp.arange(LANES, dtype=jnp.int32)[:, None] == low[None, :]).astype(BF16)
    places = jnp.arange(1, count + 1, dtype=jnp.int32)
    parts = jnp.stack([places // 256, places % 256, local_rows // 256, local_rows % 256])
    right = (parts.astype(BF16)[:, None, :] * right[None]).reshape(PARTS * LANES, count)
    found = lax.dot_general(left, right, NT, preferred_element_type=F32).astype(jnp.int32)
    found = found.reshape(tall, PARTS, LANES)
    place = found[:, 0] * 256 + found[:, 1]
    place_list = jnp.where(place > 0, place - 1, count).reshape(groups, capacity)
    row_list = jnp.where(place > 0, found[:, 2] * 256 + found[:, 3], ent_rows)
    return place_list, row_list.reshape(groups, capacity), counts


def relation_rows_kernel(slices, ids_ref, scale_ref, *refs):
    n = len(slices)
    tables, outs = refs[:n], refs[-2 * n - 1 : -n - 1]
    columns, rows = refs[-n - 1], refs[-n:]
    groups = tables[0].shape[0]
    for (_, depth), table, into in zip(slices, tables, rows):
        columns[...] = jnp.zeros_like(columns)

        def turn(group, carry):
            columns[:depth, :] = table[group, :depth].astype(F32)
            if depth < LANES:
                columns[LANES - 1 :, :] = scale_ref[pl.ds(group, 1), :]
            into[pl.ds(pl.multiple_of(group * REL_PAD, REL_PAD), REL_PAD), :] = columns[...].T
            return carry

        lax.fori_loop(0, groups, turn, 0, unroll=4)

    def body(step, carry):
        for lane in range(UNROLL):
            at = step * UNROLL + lane
            row = ids_ref[at]
            for source, out in zip(rows, outs):
                out[pl.ds(at, 1), :] = source[pl.ds(row, 1), :]
        return carry

    lax.fori_loop(0, outs[0].shape[0] // UNROLL, body, 0)


def relation_rows(places, dense, scale, slices, after):
    count = places.shape[0]
    groups, depth, span = dense.shape
    n = len(slices)
    first = span // REL_PAD - n

    def columns(k):
        return pl.BlockSpec((groups, depth, REL_PAD), lambda i: (0, 0, first + k))

    return pl.pallas_call(
        functools.partial(relation_rows_kernel, slices),
        out_shape=[jax.ShapeDtypeStruct((count, LANES), F32)] * n,
        grid=(1,),
        in_specs=[whole(SMEM), whole(VMEM)]
        + [columns(k) for k in range(n)]
        + [whole(pl.ANY)] * len(after),
        out_specs=[whole(VMEM)] * n,
        scratch_shapes=[pltpu.VMEM((LANES, REL_PAD), F32)]
        + [pltpu.VMEM((groups * REL_PAD, LANES), F32)] * n,
        compiler_params=params(28),
        cost_estimate=cost(0, 80e6),
        name="relation_rows",
    )(places, scale, *[dense] * n, *after)


def fetch_kernel(
    capacity, moves, ent_rows, counts_ref, place_ref, row_ref, dense_ref, *refs
):
    shard = pl.program_id(0)
    last = pl.num_programs(0) - 1
    out_ref, rows = refs[-3], refs[-2:]
    depth = dense_ref.shape[1]
    turns = ent_rows // TURN
    rest = ent_rows - turns * TURN

    if depth < LANES:

        @pl.when(shard == 0)
        def _():
            for ref in rows:
                ref[...] = jnp.zeros_like(ref)

    def turn(into, begin, size):
        cols = pl.ds(begin, size)
        into[cols, :depth] = dense_ref[0, :, cols].astype(F32).T

    def move(source, at):
        out_ref[pl.ds(place_ref[at], 1), :] = source[pl.ds(row_ref[at], 1), :]

    def step(into, source):
        base = (shard - 1) * capacity

        def remaining(first):
            def body(trip, carry):
                for lane in range(UNROLL):
                    move(source, base + first + trip * UNROLL + lane)
                return carry

            wanted = counts_ref[jnp.maximum(shard - 1, 0)] - first
            lax.fori_loop(0, (wanted + UNROLL - 1) // UNROLL, body, 0)

        def only_turn(trip, carry):
            turn(into, pl.multiple_of(trip * TURN, TURN), TURN)
            return carry

        def both(trip, carry):
            turn(into, pl.multiple_of(trip * TURN, TURN), TURN)
            for lane in range(moves):
                move(source, base + trip * moves + lane)
            return carry

        @pl.when(shard == 0)
        def _():
            lax.fori_loop(0, turns, only_turn, 0)

        @pl.when((shard > 0) & (shard < last))
        def _():
            lax.fori_loop(0, turns, both, 0)
            remaining(turns * moves)

        @pl.when(shard == last)
        def _():
            remaining(0)

        if rest:

            @pl.when(shard < last)
            def _():
                turn(into, turns * TURN, rest)

    for parity in range(2):

        @pl.when(lax.rem(shard, 2) == parity)
        def _():
            step(rows[parity], rows[1 - parity])


def fetch(counts, place_list, row_list, dense, id_count, ent_rows, after):
    groups, depth, _ = dense.shape
    capacity = place_list.shape[0] // groups
    moves = (id_count // groups) // (ent_rows // TURN) // UNROLL * UNROLL
    return pl.pallas_call(
        functools.partial(fetch_kernel, capacity, moves, ent_rows),
        out_shape=jax.ShapeDtypeStruct((id_count + 8, LANES), F32),
        grid=(groups + 1,),
        in_specs=[whole(SMEM)] * 3
        + [
            pl.BlockSpec(
                (1, depth, ent_rows), lambda shard: (jnp.minimum(shard, groups - 1), 0, 0)
            )
        ]
        + [whole(pl.ANY)] * len(after),
        out_specs=whole(VMEM),
        scratch_shapes=[pltpu.VMEM((ent_rows + 8, LANES), F32)] * 2,
        compiler_params=params(32),
        cost_estimate=cost(0, 170e6),
        name="fetch_rows",
    )(counts, place_list, row_list, dense, *after)


def column_sum(values):
    return jnp.sum(values * values, axis=0, keepdims=True)


def negatives_kernel(neg_ref, early_ref, late_ref, norm_ref):
    neg_t = neg_ref[...].T
    early_ref[...] = neg_t[:EARLY].astype(BF16)
    late_ref[...] = neg_t[EARLY:].astype(BF16)
    norm_ref[...] = column_sum(neg_t)


def negatives(fetched, blocks, block_len):
    count = blocks * block_len
    return pl.pallas_call(
        negatives_kernel,
        out_shape=[
            jax.ShapeDtypeStruct((EARLY, count), BF16),
            jax.ShapeDtypeStruct((LANES - EARLY, count), BF16),
            jax.ShapeDtypeStruct((1, count), F32),
        ],
        grid=(blocks,),
        in_specs=[pl.BlockSpec((block_len, LANES), lambda b: (2 * blocks + b, 0))],
        out_specs=[
            pl.BlockSpec((EARLY, block_len), lambda b: (0, b)),
            pl.BlockSpec((LANES - EARLY, block_len), lambda b: (0, b)),
            pl.BlockSpec((1, block_len), lambda b: (0, b)),
        ],
        compiler_params=params(12),
        cost_estimate=cost(0, 10e6),
        name="negatives",
    )(fetched)


def edge_parts(depth, head_ref, tail_ref, rel_ref, off_ref, tail_out):
    lane = lax.broadcasted_iota(jnp.int32, head_ref.shape, 1)
    inside = lane < depth
    rel = rel_ref[...]
    tail = tail_ref[...]
    shifted = head_ref[...] + jnp.where(inside, rel, 0.0)
    off_ref[...] = jnp.where(inside, shifted - tail, rel)
    tail_out[...] = tail.astype(BF16)
    shifted_t = shifted.T
    return shifted_t, column_sum((shifted - tail).T) - column_sum(shifted_t)


def edges_kernel(
    depth, head_ref, tail_ref, rel_ref, late_ref, off_ref, tail_out, low_ref, bias_ref
):
    shifted_t, bias = edge_parts(depth, head_ref, tail_ref, rel_ref, off_ref, tail_out)
    low_ref[:depth] = shifted_t[:depth].astype(BF16)
    low_ref[depth:] = late_ref[...]
    bias_ref[...] = bias


def edges(fetched, rel_rows, late, depth, blocks, block_len):
    count = blocks * block_len
    tall = depth + late.shape[0]

    def rows(at):
        return pl.BlockSpec((block_len, LANES), lambda b: (at * blocks + b, 0))

    return pl.pallas_call(
        functools.partial(edges_kernel, depth),
        out_shape=[
            jax.ShapeDtypeStruct((count, LANES), F32),
            jax.ShapeDtypeStruct((count, LANES), BF16),
            jax.ShapeDtypeStruct((tall, count), BF16),
            jax.ShapeDtypeStruct((1, count), F32),
        ],
        grid=(blocks,),
        in_specs=[rows(0), rows(1), rows(0)]
        + [pl.BlockSpec((tall - depth, block_len), lambda b: (0, b))],
        out_specs=[
            rows(0),
            rows(0),
            pl.BlockSpec((tall, block_len), lambda b: (0, b)),
            pl.BlockSpec((1, block_len), lambda b: (0, b)),
        ],
        compiler_params=params(16),
        cost_estimate=cost(0, 30e6),
        name="edges",
    )(fetched, fetched, rel_rows, late)


def last_rows(depth):
    return (depth + 7) // 8 * 8


def with_terms(columns, total, depth):
    place = lax.broadcasted_iota(jnp.int32, (8, total.shape[1]), 0)
    left = total
    terms = jnp.zeros(place.shape, F32)
    for k in range(TERMS):
        term = left.astype(BF16).astype(F32)
        left = left - term
        terms = jnp.where(place == k, term, terms)
    return jnp.concatenate([columns[: last_rows(depth)], terms], axis=0).astype(BF16)


def last_kernel(depth, n_given, head_ref, tail_ref, neg_ref, rel_ref, *refs):
    biases, norms = refs[:n_given], refs[n_given : 2 * n_given]
    off_ref, tail_out, pair_ref = refs[-3:]
    shifted_t, bias = edge_parts(depth, head_ref, tail_ref, rel_ref, off_ref, tail_out)
    neg_t = neg_ref[...].T
    norm = column_sum(neg_t)
    for ref in biases:
        bias = bias + ref[...]
    for ref in norms:
        norm = norm + ref[...]
    pair_ref[0] = with_terms(shifted_t, bias, depth)
    pair_ref[1] = with_terms(neg_t, norm, depth)


def last_slice(fetched, rel_rows, biases, norms, depth, blocks, block_len, half, after):
    part = blocks // HALVES
    count = part * block_len
    tall = last_rows(depth) + 8

    def rows(at):
        return pl.BlockSpec((block_len, LANES), lambda b: (at * blocks + half * part + b, 0))

    return pl.pallas_call(
        functools.partial(last_kernel, depth, len(biases)),
        out_shape=[
            jax.ShapeDtypeStruct((count, LANES), F32),
            jax.ShapeDtypeStruct((count, LANES), BF16),
            jax.ShapeDtypeStruct((2, tall, count), BF16),
        ],
        grid=(part,),
        in_specs=[rows(0), rows(1), rows(2), rows(0)]
        + [pl.BlockSpec((1, block_len), lambda b: (0, half * part + b))]
        * (len(biases) + len(norms))
        + [whole(pl.ANY)] * len(after),
        out_specs=[
            pl.BlockSpec((block_len, LANES), lambda b: (b, 0)),
            pl.BlockSpec((block_len, LANES), lambda b: (b, 0)),
            pl.BlockSpec((2, tall, block_len), lambda b: (0, 0, b)),
        ],
        compiler_params=params(16),
        cost_estimate=cost(0, 20e6),
        name="last_slice",
    )(fetched, fetched, fetched, rel_rows, *biases, *norms, *after)


def block_kernel(slices, n_col, half, me_ref, live_ref, *refs):
    n = len(slices)
    per_col = 2 * n - 1
    given = [refs[k * per_col : (k + 1) * per_col] for k in range(n_col)]
    refs = refs[n_col * per_col :]
    offs, tails, refs = refs[:n], refs[n : 2 * n], refs[2 * n :]
    grad, refs = refs[-9], refs[-8:]
    loss_ref, shift_scr, neg_scr, sums_scr, cross, slopes, row_bias, row_sum = refs
    block = pl.program_id(0)
    length = cross.shape[0]
    me = me_ref[0]
    for k in range(n_col):
        slot = lax.rem(me + (n_col - k), n_col)
        for m, (start, depth) in enumerate(slices):
            if m < n - 1:
                early, late = given[k][2 * m : 2 * m + 2]
                shift_scr[slot, start : start + depth, :] = 2.0 * late[:depth, :]
                neg_scr[slot, start : start + EARLY, :] = early[...]
                neg_scr[slot, start + EARLY : start + depth, :] = late[depth:, :]
            else:
                pair = given[k][-1]
                shift, neg = pair[0, :depth, :], pair[1, :depth, :]
                for row in range(2):
                    terms = pair[row, last_rows(depth) : last_rows(depth) + 8, :].astype(F32)
                    sums_scr[slot, row : row + 1] = jnp.sum(terms, axis=0, keepdims=True)
                shift_scr[slot, start : start + depth, :] = 2.0 * shift
                neg_scr[slot, start : start + depth, :] = neg
    bias = jnp.sum(sums_scr[:, 0, :], axis=0, keepdims=True) + MARGIN
    neg_norm = jnp.sum(sums_scr[:, 1, :], axis=0, keepdims=True)
    row_bias[...] = jnp.broadcast_to(bias, (LANES, length)).T

    live = live_ref[half * pl.num_programs(0) + block]
    tile = 256
    small = 128
    lane_tiles = [slice(at, at + LANES) for at in range(0, length, LANES)]
    cols = jnp.zeros((8, length), F32)
    loss = jnp.zeros((8, LANES), F32)
    def products(at):
        part = slice(at, at + tile)
        doubled = None
        for k in range(n_col):
            term = lax.dot_general(
                shift_scr[k, :, part], neg_scr[k], TN, preferred_element_type=F32
            )
            doubled = term if doubled is None else doubled + term
        cross[part, :] = doubled

    def moves(at):
        part = slice(at, at + tile)
        moved = lax.dot_general(slopes[part, :], neg_scr[me], NT, preferred_element_type=F32)
        fade = -row_sum[part, :]
        for m, (start, depth) in enumerate(slices):
            into = pl.ds(n * at + m, tile, stride=n)
            grad[0, into, :depth] = (
                fade[:, :depth] * tails[m][part, :depth].astype(F32)
                + moved[:, start : start + depth]
            )
            grad[1, into, :] = fade * offs[m][part, :]

    products(0)
    for begin in range(0, length, tile):
        if begin + tile < length:
            products(begin + tile)
        for at in range(begin, begin + tile, small):
            part = slice(at, at + small)
            place = at + lax.broadcasted_iota(jnp.int32, (small, 1), 0)
            scale = offs[-1][part, LANES - 1 : LANES]
            weight = jnp.where(place < live, scale, 0.0) / length
            margins = cross[part, :] + (row_bias[part, 0:1] - neg_norm)
            fall = jnp.exp(-jnp.abs(margins))
            under = 1.0 + fall
            guess = pl.reciprocal(under, approx=True)
            inverse = guess * (2.0 - under * guess)
            twice = (2.0 * weight) * (jnp.where(margins >= 0.0, 1.0, fall) * inverse)
            row_sum[part, :] = jnp.broadcast_to(
                jnp.sum(twice, axis=1, keepdims=True), (small, LANES)
            )
            slopes[part, :] = twice.astype(BF16)
            cols = cols + jnp.sum(twice.reshape(small // 8, 8, length), axis=0)
            over = jnp.maximum(margins, 0.0)
            lifts = [fall[:, lanes] for lanes in lane_tiles]
            while len(lifts) > 1:
                lifts = [a + b + a * b for a, b in zip(lifts[::2], lifts[1::2])]
            lift = lifts[0]
            soft = functools.reduce(jnp.add, [over[:, lanes] for lanes in lane_tiles]) + jnp.where(
                lift < 2.0**-11, lift * (1.0 - 0.5 * lift), jnp.log(1.0 + lift)
            )
            loss = loss + jnp.sum((weight * soft).reshape(small // 8, 8, LANES), axis=0)
        moves(begin)
    col_sum = jnp.sum(cols, axis=0, keepdims=True)

    @pl.when(block == 0)
    def _():
        loss_ref[...] = loss

    @pl.when(block > 0)
    def _():
        loss_ref[...] += loss

    moved = lax.dot_general(shift_scr[me], slopes[...], NN, preferred_element_type=F32)
    moved = 0.5 * moved - col_sum * neg_scr[me].astype(F32)
    for m, (start, depth) in enumerate(slices):
        grad[2, pl.ds(m, length, stride=n), :depth] = moved[start : start + depth, :].T


def block_math(me, live_counts, given, offs, tails, old, slices, block_len, half, after):
    n, n_col = len(slices), len(given)
    blocks = live_counts.shape[0]
    part = blocks // HALVES
    width = sum(depth for _, depth in slices)
    flat = [piece for per_col in given for piece in per_col]
    kept = [] if old is None else [old]

    def columns(piece):
        if piece.ndim == 3:
            return pl.BlockSpec((2, piece.shape[1], block_len), lambda b: (0, 0, b))
        return pl.BlockSpec((piece.shape[0], block_len), lambda b: (0, half * part + b))

    def rows(array):
        first = half * part if array.shape[0] > part * block_len else 0
        return pl.BlockSpec((block_len, LANES), lambda b: (first + b, 0))

    first_old = 2 + len(flat) + 2 * n
    return pl.pallas_call(
        functools.partial(block_kernel, slices, n_col, half),
        out_shape=[
            jax.ShapeDtypeStruct((3, n * blocks * block_len, LANES), F32),
            jax.ShapeDtypeStruct((8, LANES), F32),
        ],
        grid=(part,),
        in_specs=[whole(SMEM)] * 2
        + [columns(piece) for piece in flat]
        + [rows(array) for array in offs + tails]
        + [whole(pl.ANY)] * len(kept + after),
        out_specs=[
            pl.BlockSpec((3, n * block_len, LANES), lambda b: (0, half * part + b, 0)),
            pl.BlockSpec((8, LANES), lambda b: (0, 0)),
        ],
        input_output_aliases={first_old + k: k for k in range(len(kept))},
        scratch_shapes=[
            pltpu.VMEM((n_col, width, block_len), BF16),
            pltpu.VMEM((n_col, width, block_len), BF16),
            pltpu.VMEM((n_col, 2, block_len), F32),
            pltpu.VMEM((block_len, block_len), F32),
            pltpu.VMEM((block_len, block_len), BF16),
            pltpu.VMEM((block_len, LANES), F32),
            pltpu.VMEM((block_len, LANES), F32),
        ],
        compiler_params=params(60),
        cost_estimate=cost(part * 8 * block_len * block_len * width, 120e6),
        name="block_math",
    )(me, live_counts, *flat, *offs, *tails, *kept, *after)


def pair_of(row, n):
    return pl.ds(pl.multiple_of(row * n, n), n)


def outgoing_kernel(slices, capacity, begin, counts_ref, place_ref, grad, *refs):
    n = len(slices)
    out_ref, tile = refs[-2:]
    groups, width, chunk = out_ref.shape

    def owner(group, carry):
        wanted = jnp.clip(counts_ref[group] - begin, 0, chunk)

        def body(step, inner):
            for lane in range(UNROLL):
                at = step * UNROLL + lane
                place = place_ref[group * capacity + begin + at]
                tile[pair_of(at, n), :] = grad[pair_of(place, n), :]
            return inner

        lax.fori_loop(0, (wanted + UNROLL - 1) // UNROLL, body, 0)
        for m, (start, depth) in enumerate(slices):
            piece = tile[pl.ds(m, chunk, stride=n), :].T
            out_ref[group, start : start + depth, :] = piece[:depth].astype(BF16)
        return carry

    lax.fori_loop(0, groups, owner, 0)


def outgoing(counts, place_list, grad, slices, begin, chunk, after):
    groups, capacity = place_list.shape
    n = len(slices)
    width = sum(depth for _, depth in slices)
    return pl.pallas_call(
        functools.partial(outgoing_kernel, slices, capacity, begin),
        out_shape=jax.ShapeDtypeStruct((groups, width, chunk), BF16),
        in_specs=[whole(SMEM)] * 2 + [whole(VMEM)] + [whole(pl.ANY)] * len(after),
        out_specs=whole(VMEM),
        scratch_shapes=[pltpu.VMEM((n * chunk, LANES), F32)],
        compiler_params=params(34),
        cost_estimate=cost(0, 80e6),
        name="outgoing",
    )(counts, place_list.reshape(-1), grad, *after)


def collect_kernel(slices, capacity, begin, first, counts_ref, row_ref, came_ref, *refs):
    total, token, tile = refs[-3:]
    total[...] = jnp.zeros_like(total) if first else refs[0][...]
    token[...] = jnp.zeros_like(token)
    add_rows(slices, capacity, begin, counts_ref, row_ref, came_ref, total, tile)


def add_rows(slices, capacity, begin, counts_ref, row_ref, came_ref, total, tile):
    n = len(slices)
    groups, width, chunk = came_ref.shape

    def source(group, carry):
        wanted = jnp.clip(counts_ref[group] - begin, 0, chunk)

        @pl.when(wanted > 0)
        def _():
            for m, (start, depth) in enumerate(slices):
                piece = came_ref[group, start : start + depth, :].astype(F32)
                tile[pl.ds(m, chunk, stride=n), :depth] = piece.T

            def body(step, inner):
                for lane in range(UNROLL):
                    at = step * UNROLL + lane
                    into = pair_of(row_ref[group * capacity + begin + at], n)
                    total[into, :] = total[into, :] + tile[pair_of(at, n), :]
                return inner

            lax.fori_loop(0, (wanted + UNROLL - 1) // UNROLL, body, 0)

        return carry

    lax.fori_loop(0, groups, source, 0)


def collect(counts, row_list, came, total, slices, begin, ent_rows, after):
    capacity = row_list.shape[1]
    chunk = came.shape[2]
    n = len(slices)
    given = [] if total is None else [total]
    return pl.pallas_call(
        functools.partial(collect_kernel, slices, capacity, begin, total is None),
        out_shape=[jax.ShapeDtypeStruct((n * (ent_rows + 8), LANES), F32), token_shape()],
        input_output_aliases={3: 0} if given else {},
        in_specs=[whole(SMEM)] * 2
        + [whole(VMEM)] * (1 + len(given))
        + [whole(pl.ANY)] * len(after),
        out_specs=[whole(VMEM)] * 2,
        scratch_shapes=[pltpu.VMEM((n * chunk, LANES), F32)],
        compiler_params=params(26),
        cost_estimate=cost(0, 120e6),
        name="collect",
    )(counts, row_list.reshape(-1), came, *given, *after)


def relation_sums_kernel(n, ids_ref, grad, *refs):
    total, token = refs[-2:]
    total[...] = jnp.zeros_like(total)
    token[...] = jnp.zeros_like(token)

    def body(step, carry):
        for lane in range(UNROLL):
            at = step * UNROLL + lane
            into = pair_of(ids_ref[at], n)
            total[into, :] = total[into, :] + grad[0, pair_of(at, n), :]
        return carry

    lax.fori_loop(0, grad.shape[1] // n // UNROLL, body, 0)


def relation_sums(relation_ids, grad, n, rel_total, after):
    count = relation_ids.shape[0]
    return pl.pallas_call(
        functools.partial(relation_sums_kernel, n),
        out_shape=[jax.ShapeDtypeStruct((n * rel_total, LANES), F32), token_shape()],
        grid=(1,),
        in_specs=[whole(SMEM), pl.BlockSpec((1, n * count, LANES), lambda i: (0, 0, 0))]
        + [whole(pl.ANY)] * len(after),
        out_specs=[whole(VMEM)] * 2,
        compiler_params=params(30),
        cost_estimate=cost(0, 120e6),
        name="relation_sums",
    )(relation_ids, grad, *after)


def finish_kernel(
    slices,
    capacity,
    begin,
    counts_ref,
    row_ref,
    came_ref,
    total_ref,
    weights_ref,
    first_ref,
    second_ref,
    *refs,
):
    n = len(slices)
    outs, (total, tile, gradient) = refs[:3], refs[3:]
    cols = weights_ref.shape[1]
    step = pl.program_id(0)

    @pl.when(step == 0)
    def _():
        total[: total_ref.shape[0], :] = total_ref[...]
        add_rows(slices, capacity, begin, counts_ref, row_ref, came_ref, total, tile)

    for m, (start, depth) in enumerate(slices):
        part = total[pl.ds(step * (n * cols) + m, cols, stride=n), :]
        gradient[start : start + depth, :] = part.T[:depth]
    results = adamw_update(weights_ref[...], gradient[...], first_ref[...], second_ref[...])
    for out, result in zip(outs, results):
        out[...] = result


def finish_entities(counts, row_list, came, total, begin, weights, first, second, slices):
    width, ent_rows = weights.shape
    capacity = row_list.shape[1]
    cols = 1024
    steps = pl.cdiv(ent_rows, cols)
    n = len(slices)
    table = pl.BlockSpec((width, cols), lambda i: (0, i))
    tall = max(n * cols * steps, total.shape[0])
    return pl.pallas_call(
        functools.partial(finish_kernel, slices, capacity, begin),
        out_shape=[jax.ShapeDtypeStruct((width, ent_rows), F32)] * 3,
        grid=(steps,),
        in_specs=[whole(SMEM)] * 2 + [whole(VMEM)] * 2 + [table] * 3,
        out_specs=[table] * 3,
        scratch_shapes=[
            pltpu.VMEM((tall, LANES), F32),
            pltpu.VMEM((n * came.shape[2], LANES), F32),
            pltpu.VMEM((width, cols), F32),
        ],
        compiler_params=params(56),
        cost_estimate=cost(0, 60e6),
        name="finish_entities",
    )(counts, row_list.reshape(-1), came, total, weights, first, second)


def chunk_bounds(capacity):
    units = capacity // LANES
    sizes = [4, 6, 3, 3] if units == 16 else [units // 4] * 3 + [units - 3 * (units // 4)]
    bounds = [0]
    for size in sizes:
        bounds.append(bounds[-1] + size * LANES)
    return bounds


def shards(
    head_ids,
    relation_ids,
    tail_ids,
    negative_ids,
    live_counts,
    rel_weight,
    rel_count,
    entity_table,
    entity_first,
    entity_second,
    relation_table,
    relation_first,
    relation_second,
):
    groups = lax.axis_size("edge")
    n_col = lax.axis_size("col")
    width, ent_rows = entity_table.shape
    blocks, neg_count = negative_ids.shape
    block_len = head_ids.shape[0] // blocks
    edge_count = blocks * block_len
    slices = width_slices(width)
    n = len(slices)
    all_ids = jnp.concatenate([head_ids, tail_ids, negative_ids.reshape(-1)])
    id_count = all_ids.shape[0]
    capacity = (4 * id_count + 3 * groups - 1) // (3 * groups)
    rel_total = rel_weight.shape[0]

    rel_own = rel_total // groups
    rel_low = jnp.pad(relation_table.astype(BF16).T, ((0, 0), (0, REL_PAD - rel_own)))
    dense = []
    for k, (start, depth) in enumerate(slices):
        sent = entity_table[start : start + depth].astype(BF16)
        if k == 0:
            behind = [
                jnp.pad(rel_low[at : at + size], ((0, depth - size), (0, 0))) for at, size in slices
            ]
            sent = jnp.concatenate([sent] + behind, axis=1)
        dense.append(lax.all_gather(sent, "edge", axis=0, tiled=False))

    place_list, row_list, counts = owner_lists(all_ids, groups, capacity, ent_rows)
    safe_places = jnp.minimum(place_list, id_count - 1)
    place_flat, row_flat = place_list.reshape(-1), row_list.reshape(-1)

    rel_scale = rel_weight * (rel_total / jnp.sum(rel_weight)) / rel_count.astype(F32)
    rel_scale = jnp.pad(rel_scale.reshape(groups, rel_own), ((0, 0), (0, REL_PAD - rel_own)))
    rel_places = relation_ids + (relation_ids // rel_own) * (REL_PAD - rel_own)

    def from_others(array):
        turns = [[(c, (c + away) % n_col) for c in range(n_col)] for away in range(1, n_col)]
        return [lax.ppermute(array, "col", turn) for turn in turns]

    me = lax.axis_index("col").astype(jnp.int32).reshape(1)
    given = [[[] for _ in range(n_col)] for _ in range(HALVES)]
    offs = [[] for _ in range(HALVES)]
    tails = [[] for _ in range(HALVES)]
    biases, norms, first_sent, rel_rows = [], [], [], None
    for k, (start, depth) in enumerate(slices):
        sent = first_sent if k > 0 else []
        fetched = fetch(counts, place_flat, row_flat, dense[k], id_count, ent_rows, sent)
        if k < n - 1:
            early, late, norm = negatives(fetched, blocks, block_len)
            early_all = [early] + from_others(early)
            if rel_rows is None:
                rel_rows = relation_rows(rel_places, dense[0], rel_scale, slices, [norm])
            off, tail, low, bias = edges(fetched, rel_rows[k], late, depth, blocks, block_len)
            low_all = [low] + from_others(low)
            first_sent = [corner(piece) for piece in early_all[1:]]
            biases.append(bias)
            norms.append(norm)
            for half in range(HALVES):
                offs[half].append(off)
                tails[half].append(tail)
                for col in range(n_col):
                    given[half][col] += [early_all[col], low_all[col]]
            continue
        if rel_rows is None:
            rel_rows = relation_rows(rel_places, dense[0], rel_scale, slices, [])

    def finish(half, after):
        off, tail, pair = last_slice(
            fetched, rel_rows[-1], biases, norms, slices[-1][1], blocks, block_len, half, after
        )
        offs[half].append(off)
        tails[half].append(tail)
        for col, piece in enumerate([pair] + from_others(pair)):
            given[half][col].append(piece)

    grad, loss_tiles = None, []
    for half in range(HALVES):
        finish(half, [corner(offs[half - 1][-1])] if half > 0 else [])
    row_list, _ = lax.optimization_barrier((row_list, corner(offs[-1][-1])))
    bounds = chunk_bounds(capacity)
    few = jnp.sum((counts > bounds[-2]).astype(jnp.int32)) <= 1
    flag = jnp.broadcast_to(few.astype(jnp.int32), (groups, LANES))
    asked = lax.all_to_all(
        jnp.concatenate([row_list, flag], axis=1), "edge", split_axis=0, concat_axis=0, tiled=True
    )
    all_few = jnp.min(asked[:, capacity]) > 0
    asked = asked[:, :capacity]
    asked_counts = jnp.sum((asked < ent_rows).astype(jnp.int32), axis=1)
    for half in range(HALVES):
        after = [corner(asked)] if half == 0 else []
        grad, loss_tile = block_math(
            me,
            live_counts,
            given[half],
            offs[half],
            tails[half],
            grad,
            slices,
            block_len,
            half,
            after,
        )
        loss_tiles.append(loss_tile)
    live = jnp.sum(jnp.minimum(live_counts, block_len)).astype(F32)
    loss_own = jnp.sum(functools.reduce(jnp.add, loss_tiles))
    lane = jnp.arange(LANES, dtype=jnp.int32)
    loss_row = jnp.where(lane == 0, loss_own, jnp.where(lane == 1, live, 0.0))
    loss_all = lax.all_to_all(
        jnp.broadcast_to(loss_row, (groups, 1, LANES)), "edge", split_axis=0, concat_axis=0, tiled=True
    )
    loss_pair = jnp.sum(loss_all[:, 0, :2], axis=0)

    flat = grad.reshape(n * id_count, LANES)
    chunks = len(bounds) - 1
    begin, size = bounds[-2], bounds[-1] - bounds[-2]
    most = jnp.argmax(counts)
    most_places = lax.dynamic_slice_in_dim(safe_places, most, 1, axis=0)
    most_count = lax.dynamic_slice_in_dim(counts, most, 1, axis=0)
    arrived, total, after = [], None, []
    for k in range(chunks - 1):
        sent = outgoing(
            counts, safe_places, flat, slices, bounds[k], bounds[k + 1] - bounds[k], after
        )
        arrived.append(lax.all_to_all(sent, "edge", split_axis=0, concat_axis=0, tiled=True))
        after = []
        if k == 0:
            excess = outgoing(
                most_count, most_places, flat, slices, begin, size, [corner(sent), corner(loss_all)]
            )
            gathered = lax.all_gather(excess, "edge", axis=0, tiled=True)
            after = [corner(excess)]
        if k == 1:
            before = [corner(arrived[0]), corner(loss_all), corner(excess)]
            rel_terms, token = relation_sums(relation_ids, grad, n, rel_total, before)
            after = [token]
            rel_terms = rel_terms.reshape(rel_total, n * LANES)[:, :width]
            relation_grad = lax.psum_scatter(rel_terms, "edge", scatter_dimension=0, tiled=True)
        if k == 2:
            after = [corner(relation_grad)]
        if k > 0:
            total, token = collect(
                asked_counts, asked, arrived[k - 1], total, slices, bounds[k - 1], ent_rows, after
            )
            after = [token, corner(rel_terms)]

    def by_all_to_all():
        sent = outgoing(counts, safe_places, flat, slices, begin, size, [])
        return lax.all_to_all(sent, "edge", split_axis=0, concat_axis=0, tiled=True)

    k = chunks - 2
    total, token = collect(
        asked_counts,
        asked,
        arrived[k],
        total,
        slices,
        bounds[k],
        ent_rows,
        [],
    )
    came = lax.cond(all_few & (token[0, 0] == 0.0), lambda: gathered, by_all_to_all)
    new_entity, new_entity_first, new_entity_second = finish_entities(
        asked_counts,
        asked,
        came,
        total,
        begin,
        entity_table,
        entity_first,
        entity_second,
        slices,
    )
    new_relation, new_relation_first, new_relation_second = adamw_update(
        relation_table, relation_grad, relation_first, relation_second
    )
    return (
        loss_pair,
        new_entity,
        new_entity_first,
        new_entity_second,
        new_relation,
        new_relation_first,
        new_relation_second,
    )


def solution(mesh):
    placed = (
        P("edge"),
        P("edge"),
        P("edge"),
        P("edge", None),
        P("edge"),
        P(),
        P(),
        P("col", "edge"),
        P("col", "edge"),
        P("col", "edge"),
        P("edge", "col"),
        P("edge", "col"),
        P("edge", "col"),
    )
    return jax.shard_map(
        shards,
        mesh=mesh,
        in_specs=placed,
        out_specs=(
            P(),
            P("col", "edge"),
            P("col", "edge"),
            P("col", "edge"),
            P("edge", "col"),
            P("edge", "col"),
            P("edge", "col"),
        ),
        check_vma=False,
    )
```

```python
import functools

import jax
import jax.numpy as jnp
from jax import lax
from jax.experimental import pallas as pl
from jax.experimental.pallas import tpu as pltpu
from jax.sharding import PartitionSpec as P

STEP = 5


MARGIN = 0.1
LEARN_RATE = 0.1
BETA_ONE = 0.5
BETA_TWO = 0.5
EPSILON = 1e-08
DECAY = 0.01
LANES = 128
UNROLL = 8
PARTS = 4
HALVES = 2
EARLY = 96
TURN = 512
REL_PAD = 256
TERMS = 3
SPARE = 8
NN = (((1,), (0,)), ((), ()))
NT = (((1,), (1,)), ((), ()))
TN = (((0,), (0,)), ((), ()))
F32 = jnp.float32
BF16 = jnp.bfloat16
SMEM = pltpu.SMEM
VMEM = pltpu.VMEM


def params(mebibytes=60):
    return pltpu.CompilerParams(vmem_limit_bytes=mebibytes << 20)


def cost(flops, moved):
    return pl.CostEstimate(flops=int(flops), bytes_accessed=int(moved), transcendentals=0)


def corner(array):
    return array[(0,) * (array.ndim - 2) + (slice(0, 8), slice(0, LANES))]


def token_shape():
    return jax.ShapeDtypeStruct((8, LANES), F32)


def whole(space):
    return pl.BlockSpec(memory_space=space)


def adamw_update(weights, gradient, first, second):
    new_first = BETA_ONE * first + (1.0 - BETA_ONE) * gradient
    new_second = BETA_TWO * second + (1.0 - BETA_TWO) * gradient * gradient
    first_hat = new_first / (1.0 - BETA_ONE**STEP)
    second_hat = new_second / (1.0 - BETA_TWO**STEP)
    updated = weights - LEARN_RATE * (
        first_hat / (jnp.sqrt(second_hat) + EPSILON) + DECAY * weights
    )
    return (updated, new_first, new_second)


def width_slices(width):
    return [(at, min(LANES, width - at)) for at in range(0, width, LANES)]


def owner_lists(all_ids, groups, capacity, ent_rows):
    count = all_ids.shape[0]
    owners = all_ids // ent_rows
    local_rows = all_ids - owners * ent_rows
    chunk = 256
    mine = owners[None, :] == jnp.arange(groups, dtype=jnp.int32)[:, None]
    mine = mine.astype(BF16).reshape(groups, count // chunk, chunk)
    before = jnp.triu(jnp.ones((chunk, chunk), BF16), 1)
    inner = jnp.dot(mine, before, preferred_element_type=F32)
    sums = jnp.sum(mine.astype(F32), axis=2)
    carry = jnp.cumsum(sums, axis=1) - sums
    ranks = jnp.sum(mine.astype(F32) * (inner + carry[:, :, None]), axis=0)
    ranks = ranks.astype(jnp.int32).reshape(count)
    counts = jnp.sum(sums, axis=1).astype(jnp.int32)
    high = owners * (capacity // LANES) + ranks // LANES
    low = ranks % LANES
    tall = groups * capacity // LANES
    left = (jnp.arange(tall, dtype=jnp.int32)[:, None] == high[None, :]).astype(BF16)
    right = (jnp.arange(LANES, dtype=jnp.int32)[:, None] == low[None, :]).astype(BF16)
    places = jnp.arange(1, count + 1, dtype=jnp.int32)
    parts = jnp.stack([places // 256, places % 256, local_rows // 256, local_rows % 256])
    right = (parts.astype(BF16)[:, None, :] * right[None]).reshape(PARTS * LANES, count)
    found = lax.dot_general(left, right, NT, preferred_element_type=F32).astype(jnp.int32)
    found = found.reshape(tall, PARTS, LANES)
    place = found[:, 0] * 256 + found[:, 1]
    place_list = jnp.where(place > 0, place - 1, count).reshape(groups, capacity)
    row_list = jnp.where(place > 0, found[:, 2] * 256 + found[:, 3], ent_rows)
    return place_list, row_list.reshape(groups, capacity), counts


def relation_rows_kernel(slices, ids_ref, scale_ref, *refs):
    n = len(slices)
    tables, outs = refs[:n], refs[-2 * n - 1 : -n - 1]
    columns, rows = refs[-n - 1], refs[-n:]
    groups = tables[0].shape[0]
    for (_, depth), table, into in zip(slices, tables, rows):
        columns[...] = jnp.zeros_like(columns)

        def turn(group, carry):
            columns[:depth, :] = table[group, :depth].astype(F32)
            if depth < LANES:
                columns[LANES - 1 :, :] = scale_ref[pl.ds(group, 1), :]
            into[pl.ds(pl.multiple_of(group * REL_PAD, REL_PAD), REL_PAD), :] = columns[...].T
            return carry

        lax.fori_loop(0, groups, turn, 0, unroll=4)

    def body(step, carry):
        for lane in range(UNROLL):
            at = step * UNROLL + lane
            row = ids_ref[at]
            for source, out in zip(rows, outs):
                out[pl.ds(at, 1), :] = source[pl.ds(row, 1), :]
        return carry

    lax.fori_loop(0, outs[0].shape[0] // UNROLL, body, 0)


def relation_rows(places, dense, scale, slices, after):
    count = places.shape[0]
    groups, depth, span = dense.shape
    n = len(slices)
    first = span // REL_PAD - n

    def columns(k):
        return pl.BlockSpec((groups, depth, REL_PAD), lambda i: (0, 0, first + k))

    return pl.pallas_call(
        functools.partial(relation_rows_kernel, slices),
        out_shape=[jax.ShapeDtypeStruct((count, LANES), F32)] * n,
        grid=(1,),
        in_specs=[whole(SMEM), whole(VMEM)]
        + [columns(k) for k in range(n)]
        + [whole(pl.ANY)] * len(after),
        out_specs=[whole(VMEM)] * n,
        scratch_shapes=[pltpu.VMEM((LANES, REL_PAD), F32)]
        + [pltpu.VMEM((groups * REL_PAD, LANES), F32)] * n,
        compiler_params=params(28),
        cost_estimate=cost(0, 80e6),
        name="relation_rows",
    )(places, scale, *[dense] * n, *after)


def fetch_kernel(
    capacity, moves, ent_rows, counts_ref, place_ref, row_ref, dense_ref, *refs
):
    shard = pl.program_id(0)
    last = pl.num_programs(0) - 1
    out_ref, rows = refs[-3], refs[-2:]
    depth = dense_ref.shape[1]
    turns = ent_rows // TURN
    rest = ent_rows - turns * TURN

    if depth < LANES:

        @pl.when(shard == 0)
        def _():
            for ref in rows:
                ref[...] = jnp.zeros_like(ref)

    def turn(into, begin, size):
        cols = pl.ds(begin, size)
        into[cols, :depth] = dense_ref[0, :, cols].astype(F32).T

    def move(source, at):
        out_ref[pl.ds(place_ref[at], 1), :] = source[pl.ds(row_ref[at], 1), :]

    def step(into, source):
        base = (shard - 1) * capacity

        def remaining(first):
            def body(trip, carry):
                for lane in range(UNROLL):
                    move(source, base + first + trip * UNROLL + lane)
                return carry

            wanted = counts_ref[jnp.maximum(shard - 1, 0)] - first
            lax.fori_loop(0, (wanted + UNROLL - 1) // UNROLL, body, 0)

        def only_turn(trip, carry):
            turn(into, pl.multiple_of(trip * TURN, TURN), TURN)
            return carry

        def both(trip, carry):
            turn(into, pl.multiple_of(trip * TURN, TURN), TURN)
            for lane in range(moves):
                move(source, base + trip * moves + lane)
            return carry

        @pl.when(shard == 0)
        def _():
            lax.fori_loop(0, turns, only_turn, 0)

        @pl.when((shard > 0) & (shard < last))
        def _():
            lax.fori_loop(0, turns, both, 0)
            remaining(turns * moves)

        @pl.when(shard == last)
        def _():
            remaining(0)

        if rest:

            @pl.when(shard < last)
            def _():
                turn(into, turns * TURN, rest)

    for parity in range(2):

        @pl.when(lax.rem(shard, 2) == parity)
        def _():
            step(rows[parity], rows[1 - parity])


def fetch(counts, place_list, row_list, dense, id_count, ent_rows, after):
    groups, depth, _ = dense.shape
    capacity = place_list.shape[0] // groups
    moves = (id_count // groups) // (ent_rows // TURN) // UNROLL * UNROLL
    return pl.pallas_call(
        functools.partial(fetch_kernel, capacity, moves, ent_rows),
        out_shape=jax.ShapeDtypeStruct((id_count + 8, LANES), F32),
        grid=(groups + 1,),
        in_specs=[whole(SMEM)] * 3
        + [
            pl.BlockSpec(
                (1, depth, ent_rows), lambda shard: (jnp.minimum(shard, groups - 1), 0, 0)
            )
        ]
        + [whole(pl.ANY)] * len(after),
        out_specs=whole(VMEM),
        scratch_shapes=[pltpu.VMEM((ent_rows + 8, LANES), F32)] * 2,
        compiler_params=params(32),
        cost_estimate=cost(0, 170e6),
        name="fetch_rows",
    )(counts, place_list, row_list, dense, *after)


def column_sum(values):
    return jnp.sum(values * values, axis=0, keepdims=True)


def negatives_kernel(neg_ref, early_ref, late_ref, norm_ref):
    neg_t = neg_ref[...].T
    early_ref[...] = neg_t[:EARLY].astype(BF16)
    late_ref[...] = neg_t[EARLY:].astype(BF16)
    norm_ref[...] = column_sum(neg_t)


def negatives(fetched, blocks, block_len):
    count = blocks * block_len
    return pl.pallas_call(
        negatives_kernel,
        out_shape=[
            jax.ShapeDtypeStruct((EARLY, count), BF16),
            jax.ShapeDtypeStruct((LANES - EARLY, count), BF16),
            jax.ShapeDtypeStruct((1, count), F32),
        ],
        grid=(blocks,),
        in_specs=[pl.BlockSpec((block_len, LANES), lambda b: (2 * blocks + b, 0))],
        out_specs=[
            pl.BlockSpec((EARLY, block_len), lambda b: (0, b)),
            pl.BlockSpec((LANES - EARLY, block_len), lambda b: (0, b)),
            pl.BlockSpec((1, block_len), lambda b: (0, b)),
        ],
        compiler_params=params(12),
        cost_estimate=cost(0, 10e6),
        name="negatives",
    )(fetched)


def edge_parts(depth, head_ref, tail_ref, rel_ref, off_ref, tail_out):
    lane = lax.broadcasted_iota(jnp.int32, head_ref.shape, 1)
    inside = lane < depth
    rel = rel_ref[...]
    tail = tail_ref[...]
    shifted = head_ref[...] + jnp.where(inside, rel, 0.0)
    off_ref[...] = jnp.where(inside, shifted - tail, rel)
    tail_out[...] = tail.astype(BF16)
    shifted_t = shifted.T
    return shifted_t, column_sum((shifted - tail).T) - column_sum(shifted_t)


def edges_kernel(
    depth, head_ref, tail_ref, rel_ref, late_ref, off_ref, tail_out, low_ref, bias_ref
):
    shifted_t, bias = edge_parts(depth, head_ref, tail_ref, rel_ref, off_ref, tail_out)
    low_ref[:depth] = shifted_t[:depth].astype(BF16)
    low_ref[depth:] = late_ref[...]
    bias_ref[...] = bias


def edges(fetched, rel_rows, late, depth, blocks, block_len):
    count = blocks * block_len
    tall = depth + late.shape[0]

    def rows(at):
        return pl.BlockSpec((block_len, LANES), lambda b: (at * blocks + b, 0))

    return pl.pallas_call(
        functools.partial(edges_kernel, depth),
        out_shape=[
            jax.ShapeDtypeStruct((count, LANES), F32),
            jax.ShapeDtypeStruct((count, LANES), BF16),
            jax.ShapeDtypeStruct((tall, count), BF16),
            jax.ShapeDtypeStruct((1, count), F32),
        ],
        grid=(blocks,),
        in_specs=[rows(0), rows(1), rows(0)]
        + [pl.BlockSpec((tall - depth, block_len), lambda b: (0, b))],
        out_specs=[
            rows(0),
            rows(0),
            pl.BlockSpec((tall, block_len), lambda b: (0, b)),
            pl.BlockSpec((1, block_len), lambda b: (0, b)),
        ],
        compiler_params=params(16),
        cost_estimate=cost(0, 30e6),
        name="edges",
    )(fetched, fetched, rel_rows, late)


def last_rows(depth):
    return (depth + 7) // 8 * 8


def with_terms(columns, total, depth):
    terms = term_rows(total, 0)
    return jnp.concatenate([columns[: last_rows(depth)], terms], axis=0).astype(BF16)


def term_rows(total, first):
    place = lax.broadcasted_iota(jnp.int32, (8, total.shape[1]), 0)
    left = total
    terms = jnp.zeros(place.shape, F32)
    for k in range(TERMS):
        term = left.astype(BF16).astype(F32)
        left = left - term
        terms = jnp.where(place == first + k, term, terms)
    return terms


def last_kernel(depth, n_given, head_ref, tail_ref, neg_ref, rel_ref, *refs):
    biases, norms = refs[:n_given], refs[n_given : 2 * n_given]
    off_ref, tail_out, pair_ref = refs[-3:]
    shifted_t, bias = edge_parts(depth, head_ref, tail_ref, rel_ref, off_ref, tail_out)
    neg_t = neg_ref[...].T
    norm = column_sum(neg_t)
    for ref in biases:
        bias = bias + ref[...]
    for ref in norms:
        norm = norm + ref[...]
    pair_ref[0] = with_terms(shifted_t, bias, depth)
    pair_ref[1] = with_terms(neg_t, norm, depth)


def last_slice(fetched, rel_rows, biases, norms, depth, blocks, block_len, half, after):
    part = blocks // HALVES
    count = part * block_len
    tall = last_rows(depth) + 8

    def rows(at):
        return pl.BlockSpec((block_len, LANES), lambda b: (at * blocks + half * part + b, 0))

    return pl.pallas_call(
        functools.partial(last_kernel, depth, len(biases)),
        out_shape=[
            jax.ShapeDtypeStruct((count, LANES), F32),
            jax.ShapeDtypeStruct((count, LANES), BF16),
            jax.ShapeDtypeStruct((2, tall, count), BF16),
        ],
        grid=(part,),
        in_specs=[rows(0), rows(1), rows(2), rows(0)]
        + [pl.BlockSpec((1, block_len), lambda b: (0, half * part + b))]
        * (len(biases) + len(norms))
        + [whole(pl.ANY)] * len(after),
        out_specs=[
            pl.BlockSpec((block_len, LANES), lambda b: (b, 0)),
            pl.BlockSpec((block_len, LANES), lambda b: (b, 0)),
            pl.BlockSpec((2, tall, block_len), lambda b: (0, 0, b)),
        ],
        compiler_params=params(16),
        cost_estimate=cost(0, 20e6),
        name="last_slice",
    )(fetched, fetched, fetched, rel_rows, *biases, *norms, *after)


def block_kernel(slices, n_col, half, me_ref, live_ref, *refs):
    n = len(slices)
    per_col = 2 * n - 1
    given = [refs[k * per_col : (k + 1) * per_col] for k in range(n_col)]
    refs = refs[n_col * per_col :]
    offs, tails, refs = refs[:n], refs[n : 2 * n], refs[2 * n :]
    grad, refs = refs[-9], refs[-8:]
    loss_ref, shift_scr, neg_scr, sums_scr, cross, slopes, row_bias, row_sum = refs
    block = pl.program_id(0)
    length = cross.shape[0]
    me = me_ref[0]
    for k in range(n_col):
        slot = lax.rem(me + (n_col - k), n_col)
        for m, (start, depth) in enumerate(slices):
            if m < n - 1:
                early, late = given[k][2 * m : 2 * m + 2]
                shift_scr[slot, start : start + depth, :] = 2.0 * late[:depth, :]
                neg_scr[slot, start : start + EARLY, :] = early[...]
                neg_scr[slot, start + EARLY : start + depth, :] = late[depth:, :]
            else:
                pair = given[k][-1]
                shift, neg = pair[0, :depth, :], pair[1, :depth, :]
                for row in range(2):
                    terms = pair[row, last_rows(depth) : last_rows(depth) + 8, :].astype(F32)
                    sums_scr[slot, row : row + 1] = jnp.sum(terms, axis=0, keepdims=True)
                shift_scr[slot, start : start + depth, :] = 2.0 * shift
                neg_scr[slot, start : start + depth, :] = neg
    bias = jnp.sum(sums_scr[:, 0, :], axis=0, keepdims=True) + MARGIN
    neg_norm = jnp.sum(sums_scr[:, 1, :], axis=0, keepdims=True)
    row_bias[...] = jnp.broadcast_to(bias, (LANES, length)).T

    live = live_ref[half * pl.num_programs(0) + block]
    tile = 256
    small = 128
    lane_tiles = [slice(at, at + LANES) for at in range(0, length, LANES)]
    cols = jnp.zeros((8, length), F32)
    loss = jnp.zeros((8, LANES), F32)
    def products(at):
        part = slice(at, at + tile)
        doubled = None
        for k in range(n_col):
            term = lax.dot_general(
                shift_scr[k, :, part], neg_scr[k], TN, preferred_element_type=F32
            )
            doubled = term if doubled is None else doubled + term
        cross[part, :] = doubled

    def moves(at):
        part = slice(at, at + tile)
        moved = lax.dot_general(slopes[part, :], neg_scr[me], NT, preferred_element_type=F32)
        fade = -row_sum[part, :]
        for m, (start, depth) in enumerate(slices):
            into = pl.ds(n * at + m, tile, stride=n)
            grad[0, into, :depth] = (
                fade[:, :depth] * tails[m][part, :depth].astype(F32)
                + moved[:, start : start + depth]
            )
            grad[1, into, :] = fade * offs[m][part, :]

    products(0)
    for begin in range(0, length, tile):
        if begin + tile < length:
            products(begin + tile)
        for at in range(begin, begin + tile, small):
            part = slice(at, at + small)
            place = at + lax.broadcasted_iota(jnp.int32, (small, 1), 0)
            scale = offs[-1][part, LANES - 1 : LANES]
            weight = jnp.where(place < live, scale, 0.0) / length
            margins = cross[part, :] + (row_bias[part, 0:1] - neg_norm)
            fall = jnp.exp(-jnp.abs(margins))
            under = 1.0 + fall
            guess = pl.reciprocal(under, approx=True)
            inverse = guess * (2.0 - under * guess)
            twice = (2.0 * weight) * (jnp.where(margins >= 0.0, 1.0, fall) * inverse)
            row_sum[part, :] = jnp.broadcast_to(
                jnp.sum(twice, axis=1, keepdims=True), (small, LANES)
            )
            slopes[part, :] = twice.astype(BF16)
            cols = cols + jnp.sum(twice.reshape(small // 8, 8, length), axis=0)
            over = jnp.maximum(margins, 0.0)
            lifts = [fall[:, lanes] for lanes in lane_tiles]
            while len(lifts) > 1:
                lifts = [a + b + a * b for a, b in zip(lifts[::2], lifts[1::2])]
            lift = lifts[0]
            soft = functools.reduce(jnp.add, [over[:, lanes] for lanes in lane_tiles]) + jnp.where(
                lift < 2.0**-11, lift * (1.0 - 0.5 * lift), jnp.log(1.0 + lift)
            )
            loss = loss + jnp.sum((weight * soft).reshape(small // 8, 8, LANES), axis=0)
        moves(begin)
    col_sum = jnp.sum(cols, axis=0, keepdims=True)

    @pl.when(block == 0)
    def _():
        loss_ref[...] = loss

    @pl.when(block > 0)
    def _():
        loss_ref[...] += loss

    moved = lax.dot_general(shift_scr[me], slopes[...], NN, preferred_element_type=F32)
    moved = 0.5 * moved - col_sum * neg_scr[me].astype(F32)
    for m, (start, depth) in enumerate(slices):
        grad[2, pl.ds(m, length, stride=n), :depth] = moved[start : start + depth, :].T


def block_math(me, live_counts, given, offs, tails, old, slices, block_len, half, after):
    n, n_col = len(slices), len(given)
    blocks = live_counts.shape[0]
    part = blocks // HALVES
    width = sum(depth for _, depth in slices)
    flat = [piece for per_col in given for piece in per_col]
    kept = [] if old is None else [old]

    def columns(piece):
        if piece.ndim == 3:
            return pl.BlockSpec((2, piece.shape[1], block_len), lambda b: (0, 0, b))
        return pl.BlockSpec((piece.shape[0], block_len), lambda b: (0, half * part + b))

    def rows(array):
        first = half * part if array.shape[0] > part * block_len else 0
        return pl.BlockSpec((block_len, LANES), lambda b: (first + b, 0))

    first_old = 2 + len(flat) + 2 * n
    return pl.pallas_call(
        functools.partial(block_kernel, slices, n_col, half),
        out_shape=[
            jax.ShapeDtypeStruct((3, n * blocks * block_len, LANES), F32),
            jax.ShapeDtypeStruct((8, LANES), F32),
        ],
        grid=(part,),
        in_specs=[whole(SMEM)] * 2
        + [columns(piece) for piece in flat]
        + [rows(array) for array in offs + tails]
        + [whole(pl.ANY)] * len(kept + after),
        out_specs=[
            pl.BlockSpec((3, n * block_len, LANES), lambda b: (0, half * part + b, 0)),
            pl.BlockSpec((8, LANES), lambda b: (0, 0)),
        ],
        input_output_aliases={first_old + k: k for k in range(len(kept))},
        scratch_shapes=[
            pltpu.VMEM((n_col, width, block_len), BF16),
            pltpu.VMEM((n_col, width, block_len), BF16),
            pltpu.VMEM((n_col, 2, block_len), F32),
            pltpu.VMEM((block_len, block_len), F32),
            pltpu.VMEM((block_len, block_len), BF16),
            pltpu.VMEM((block_len, LANES), F32),
            pltpu.VMEM((block_len, LANES), F32),
        ],
        compiler_params=params(60),
        cost_estimate=cost(part * 8 * block_len * block_len * width, 120e6),
        name="block_math",
    )(me, live_counts, *flat, *offs, *tails, *kept, *after)


def pair_of(row, n):
    return pl.ds(pl.multiple_of(row * n, n), n)


def outgoing_kernel(slices, capacity, begin, counts_ref, place_ref, grad, *refs):
    n = len(slices)
    out_ref, token, tile = refs[-3:]
    groups, _, chunk = out_ref.shape
    token[...] = jnp.zeros_like(token)

    def owner(group, carry):
        wanted = jnp.clip(counts_ref[group] - begin, 0, chunk)

        def body(step, inner):
            for lane in range(UNROLL):
                at = step * UNROLL + lane
                place = place_ref[group * capacity + begin + at]
                tile[pair_of(at, n), :] = grad[pair_of(place, n), :]
            return inner

        lax.fori_loop(0, (wanted + UNROLL - 1) // UNROLL, body, 0)
        for m, (start, depth) in enumerate(slices):
            piece = tile[pl.ds(m, chunk, stride=n), :].T
            out_ref[group, start : start + depth, :] = piece[:depth].astype(BF16)
        return carry

    lax.fori_loop(0, groups, owner, 0)


def excess_kernel(slices, capacity, begin, counts_ref, place_ref, live_ref, grad, loss_ref, *refs):
    outgoing_kernel(slices, capacity, begin, counts_ref, place_ref, grad, *refs)
    out_ref = refs[-3]
    loss = jnp.sum(jnp.sum(loss_ref[...], axis=0, keepdims=True), axis=1, keepdims=True)
    live = live_ref[0]
    for block in range(1, live_ref.shape[0]):
        live = live + live_ref[block]
    count = jnp.full((1, LANES), live.astype(F32))
    terms = term_rows(jnp.broadcast_to(loss, (1, LANES)), 0) + term_rows(count, TERMS)
    width = sum(depth for _, depth in slices)
    for at in range(0, out_ref.shape[2], LANES):
        out_ref[0, last_rows(width) :, at : at + LANES] = terms.astype(BF16)


def excess_rows(count, places, live, grad, loss, slices, begin, chunk, after):
    n = len(slices)
    width = sum(depth for _, depth in slices)
    return pl.pallas_call(
        functools.partial(excess_kernel, slices, places.shape[1], begin),
        out_shape=[
            jax.ShapeDtypeStruct((1, last_rows(width) + SPARE, chunk), BF16),
            token_shape(),
        ],
        in_specs=[whole(SMEM)] * 3 + [whole(VMEM)] * 2 + [whole(pl.ANY)] * len(after),
        out_specs=[whole(VMEM)] * 2,
        scratch_shapes=[pltpu.VMEM((n * chunk, LANES), F32)],
        compiler_params=params(34),
        cost_estimate=cost(0, 80e6),
        name="excess_rows",
    )(count, places.reshape(-1), live, grad, loss, *after)


def outgoing(counts, place_list, grad, slices, begin, chunk, after, spare=0):
    groups, capacity = place_list.shape
    n = len(slices)
    width = sum(depth for _, depth in slices) + spare
    return pl.pallas_call(
        functools.partial(outgoing_kernel, slices, capacity, begin),
        out_shape=[jax.ShapeDtypeStruct((groups, width, chunk), BF16), token_shape()],
        in_specs=[whole(SMEM)] * 2 + [whole(VMEM)] + [whole(pl.ANY)] * len(after),
        out_specs=[whole(VMEM)] * 2,
        scratch_shapes=[pltpu.VMEM((n * chunk, LANES), F32)],
        compiler_params=params(34),
        cost_estimate=cost(0, 80e6),
        name="outgoing",
    )(counts, place_list.reshape(-1), grad, *after)


def collect_kernel(slices, capacity, begin, first, counts_ref, row_ref, came_ref, *refs):
    total, token, tile = refs[-3:]
    total[...] = jnp.zeros_like(total) if first else refs[0][...]
    token[...] = jnp.zeros_like(token)
    add_rows(slices, capacity, begin, counts_ref, row_ref, came_ref, total, tile)


def add_rows(slices, capacity, begin, counts_ref, row_ref, came_ref, total, tile):
    n = len(slices)
    groups, _, chunk = came_ref.shape

    def source(group, carry):
        wanted = jnp.clip(counts_ref[group] - begin, 0, chunk)

        @pl.when(wanted > 0)
        def _():
            for m, (start, depth) in enumerate(slices):
                piece = came_ref[group, start : start + depth, :].astype(F32)
                tile[pl.ds(m, chunk, stride=n), :depth] = piece.T

            def body(step, inner):
                for lane in range(UNROLL):
                    at = step * UNROLL + lane
                    into = pair_of(row_ref[group * capacity + begin + at], n)
                    total[into, :] = total[into, :] + tile[pair_of(at, n), :]
                return inner

            lax.fori_loop(0, (wanted + UNROLL - 1) // UNROLL, body, 0)

        return carry

    lax.fori_loop(0, groups, source, 0)


def collect(counts, row_list, came, total, slices, begin, ent_rows, after):
    capacity = row_list.shape[1]
    chunk = came.shape[2]
    n = len(slices)
    given = [] if total is None else [total]
    return pl.pallas_call(
        functools.partial(collect_kernel, slices, capacity, begin, total is None),
        out_shape=[jax.ShapeDtypeStruct((n * (ent_rows + 8), LANES), F32), token_shape()],
        input_output_aliases={3: 0} if given else {},
        in_specs=[whole(SMEM)] * 2
        + [whole(VMEM)] * (1 + len(given))
        + [whole(pl.ANY)] * len(after),
        out_specs=[whole(VMEM)] * 2,
        scratch_shapes=[pltpu.VMEM((n * chunk, LANES), F32)],
        compiler_params=params(26),
        cost_estimate=cost(0, 120e6),
        name="collect",
    )(counts, row_list.reshape(-1), came, *given, *after)


def relation_sums_kernel(n, ids_ref, grad, *refs):
    total, token = refs[-2:]
    total[...] = jnp.zeros_like(total)
    token[...] = jnp.zeros_like(token)

    def body(step, carry):
        for lane in range(UNROLL):
            at = step * UNROLL + lane
            into = pair_of(ids_ref[at], n)
            total[into, :] = total[into, :] + grad[0, pair_of(at, n), :]
        return carry

    lax.fori_loop(0, grad.shape[1] // n // UNROLL, body, 0)


def relation_sums(relation_ids, grad, n, rel_total, after):
    count = relation_ids.shape[0]
    return pl.pallas_call(
        functools.partial(relation_sums_kernel, n),
        out_shape=[jax.ShapeDtypeStruct((n * rel_total, LANES), F32), token_shape()],
        grid=(1,),
        in_specs=[whole(SMEM), pl.BlockSpec((1, n * count, LANES), lambda i: (0, 0, 0))]
        + [whole(pl.ANY)] * len(after),
        out_specs=[whole(VMEM)] * 2,
        compiler_params=params(30),
        cost_estimate=cost(0, 120e6),
        name="relation_sums",
    )(relation_ids, grad, *after)


def finish_kernel(
    slices,
    capacity,
    begin,
    counts_ref,
    row_ref,
    came_ref,
    total_ref,
    weights_ref,
    first_ref,
    second_ref,
    *refs,
):
    n = len(slices)
    outs, (total, tile, gradient) = refs[:3], refs[3:]
    cols = weights_ref.shape[1]
    step = pl.program_id(0)

    @pl.when(step == 0)
    def _():
        total[: total_ref.shape[0], :] = total_ref[...]
        add_rows(slices, capacity, begin, counts_ref, row_ref, came_ref, total, tile)

    for m, (start, depth) in enumerate(slices):
        part = total[pl.ds(step * (n * cols) + m, cols, stride=n), :]
        gradient[start : start + depth, :] = part.T[:depth]
    grad = gradient[...]
    new_first = BETA_ONE * first_ref[...] + (1.0 - BETA_ONE) * grad
    new_second = BETA_TWO * second_ref[...] + (1.0 - BETA_TWO) * grad * grad
    under = jnp.sqrt(new_second * (1.0 / (1.0 - BETA_TWO**STEP))) + EPSILON
    guess = pl.reciprocal(under, approx=True)
    inverse = guess * (2.0 - under * guess)
    pace = LEARN_RATE / (1.0 - BETA_ONE**STEP)
    outs[0][...] = (1.0 - LEARN_RATE * DECAY) * weights_ref[...] - (pace * new_first) * inverse
    outs[1][...] = new_first
    outs[2][...] = new_second


def finish_entities(counts, row_list, came, total, begin, weights, first, second, slices):
    width, ent_rows = weights.shape
    capacity = row_list.shape[1]
    cols = 1024
    steps = pl.cdiv(ent_rows, cols)
    n = len(slices)
    table = pl.BlockSpec((width, cols), lambda i: (0, i))
    tall = max(n * cols * steps, total.shape[0])
    return pl.pallas_call(
        functools.partial(finish_kernel, slices, capacity, begin),
        out_shape=[jax.ShapeDtypeStruct((width, ent_rows), F32)] * 3,
        grid=(steps,),
        in_specs=[whole(SMEM)] * 2 + [whole(VMEM)] * 2 + [table] * 3,
        out_specs=[table] * 3,
        scratch_shapes=[
            pltpu.VMEM((tall, LANES), F32),
            pltpu.VMEM((n * came.shape[2], LANES), F32),
            pltpu.VMEM((width, cols), F32),
        ],
        compiler_params=params(56),
        cost_estimate=cost(0, 60e6),
        name="finish_entities",
    )(counts, row_list.reshape(-1), came, total, weights, first, second)


def chunk_bounds(capacity):
    units = capacity // LANES
    sizes = [3, 7, 3, 3] if units == 16 else [units // 4] * 3 + [units - 3 * (units // 4)]
    bounds = [0]
    for size in sizes:
        bounds.append(bounds[-1] + size * LANES)
    return bounds


def shards(
    head_ids,
    relation_ids,
    tail_ids,
    negative_ids,
    live_counts,
    rel_weight,
    rel_count,
    entity_table,
    entity_first,
    entity_second,
    relation_table,
    relation_first,
    relation_second,
):
    groups = lax.axis_size("edge")
    n_col = lax.axis_size("col")
    width, ent_rows = entity_table.shape
    blocks, neg_count = negative_ids.shape
    block_len = head_ids.shape[0] // blocks
    edge_count = blocks * block_len
    slices = width_slices(width)
    n = len(slices)
    all_ids = jnp.concatenate([head_ids, tail_ids, negative_ids.reshape(-1)])
    id_count = all_ids.shape[0]
    capacity = (4 * id_count + 3 * groups - 1) // (3 * groups)
    rel_total = rel_weight.shape[0]

    rel_own = rel_total // groups
    rel_low = jnp.pad(relation_table.astype(BF16).T, ((0, 0), (0, REL_PAD - rel_own)))
    dense = []
    for k, (start, depth) in enumerate(slices):
        sent = entity_table[start : start + depth].astype(BF16)
        if k == 0:
            behind = [
                jnp.pad(rel_low[at : at + size], ((0, depth - size), (0, 0))) for at, size in slices
            ]
            sent = jnp.concatenate([sent] + behind, axis=1)
        dense.append(lax.all_gather(sent, "edge", axis=0, tiled=False))

    place_list, row_list, counts = owner_lists(all_ids, groups, capacity, ent_rows)
    safe_places = jnp.minimum(place_list, id_count - 1)
    place_flat, row_flat = place_list.reshape(-1), row_list.reshape(-1)

    rel_scale = rel_weight * (rel_total / jnp.sum(rel_weight)) / rel_count.astype(F32)
    rel_scale = jnp.pad(rel_scale.reshape(groups, rel_own), ((0, 0), (0, REL_PAD - rel_own)))
    rel_places = relation_ids + (relation_ids // rel_own) * (REL_PAD - rel_own)

    def from_others(array):
        turns = [[(c, (c + away) % n_col) for c in range(n_col)] for away in range(1, n_col)]
        return [lax.ppermute(array, "col", turn) for turn in turns]

    me = lax.axis_index("col").astype(jnp.int32).reshape(1)
    given = [[[] for _ in range(n_col)] for _ in range(HALVES)]
    offs = [[] for _ in range(HALVES)]
    tails = [[] for _ in range(HALVES)]
    biases, norms, first_sent, rel_rows = [], [], [], None
    for k, (start, depth) in enumerate(slices):
        sent = first_sent if k > 0 else []
        fetched = fetch(counts, place_flat, row_flat, dense[k], id_count, ent_rows, sent)
        if k < n - 1:
            early, late, norm = negatives(fetched, blocks, block_len)
            early_all = [early] + from_others(early)
            if rel_rows is None:
                rel_rows = relation_rows(rel_places, dense[0], rel_scale, slices, [norm])
            off, tail, low, bias = edges(fetched, rel_rows[k], late, depth, blocks, block_len)
            low_all = [low] + from_others(low)
            first_sent = [corner(piece) for piece in early_all[1:]]
            biases.append(bias)
            norms.append(norm)
            for half in range(HALVES):
                offs[half].append(off)
                tails[half].append(tail)
                for col in range(n_col):
                    given[half][col] += [early_all[col], low_all[col]]
            continue
        if rel_rows is None:
            rel_rows = relation_rows(rel_places, dense[0], rel_scale, slices, [])

    def finish(half, after):
        off, tail, pair = last_slice(
            fetched, rel_rows[-1], biases, norms, slices[-1][1], blocks, block_len, half, after
        )
        offs[half].append(off)
        tails[half].append(tail)
        for col, piece in enumerate([pair] + from_others(pair)):
            given[half][col].append(piece)

    grad, loss_tiles = None, []
    for half in range(HALVES):
        finish(half, [corner(offs[half - 1][-1])] if half > 0 else [])
    row_list, _ = lax.optimization_barrier((row_list, corner(offs[-1][-1])))
    bounds = chunk_bounds(capacity)
    few = jnp.sum((counts > bounds[-2]).astype(jnp.int32)) <= 1
    flag = jnp.broadcast_to(few.astype(jnp.int32), (groups, LANES))
    asked = lax.all_to_all(
        jnp.concatenate([row_list, flag], axis=1), "edge", split_axis=0, concat_axis=0, tiled=True
    )
    all_few = jnp.min(asked[:, capacity]) > 0
    asked = asked[:, :capacity]
    asked_counts = jnp.sum((asked < ent_rows).astype(jnp.int32), axis=1)
    for half in range(HALVES):
        after = [corner(asked)] if half == 0 else []
        grad, loss_tile = block_math(
            me,
            live_counts,
            given[half],
            offs[half],
            tails[half],
            grad,
            slices,
            block_len,
            half,
            after,
        )
        loss_tiles.append(loss_tile)
    live = jnp.minimum(live_counts, block_len)
    loss_tile = functools.reduce(jnp.add, loss_tiles)

    flat = grad.reshape(n * id_count, LANES)
    chunks = len(bounds) - 1
    begin, size = bounds[-2], bounds[-1] - bounds[-2]
    most = jnp.argmax(counts)
    most_places = lax.dynamic_slice_in_dim(safe_places, most, 1, axis=0)
    most_count = lax.dynamic_slice_in_dim(counts, most, 1, axis=0)
    arrived, total, after = [], None, []
    for k in range(chunks - 1):
        sent, sent_token = outgoing(
            counts, safe_places, flat, slices, bounds[k], bounds[k + 1] - bounds[k], after
        )
        arrived.append(lax.all_to_all(sent, "edge", split_axis=0, concat_axis=0, tiled=True))
        after = []
        if k == 0:
            excess, excess_token = excess_rows(
                most_count,
                most_places,
                live,
                flat,
                loss_tile,
                slices,
                begin,
                size,
                [sent_token],
            )
            after = [excess_token]
        if k == 1:
            before = [corner(arrived[0]), excess_token]
            rel_terms, token = relation_sums(relation_ids, grad, n, rel_total, before)
            after = [token]
            rel_terms = rel_terms.reshape(rel_total, n * LANES)[:, :width]
            relation_grad = lax.psum_scatter(rel_terms, "edge", scatter_dimension=0, tiled=True)
        if k == 2:
            ready = (relation_grad[0, 0] == relation_grad[0, 0]) & (sent_token[0, 0] == 0.0)
            excess = jnp.where(ready, excess, jnp.zeros_like(excess))
            gathered = lax.all_gather(excess, "edge", axis=0, tiled=True)
            after = [corner(relation_grad)]
        if k > 0:
            total, token = collect(
                asked_counts, asked, arrived[k - 1], total, slices, bounds[k - 1], ent_rows, after
            )
            after = [token, corner(rel_terms)]

    def by_all_to_all():
        spare = last_rows(width) + SPARE - width
        sent, _ = outgoing(counts, safe_places, flat, slices, begin, size, [], spare)
        return lax.all_to_all(sent, "edge", split_axis=0, concat_axis=0, tiled=True)

    k = chunks - 2
    total, token = collect(
        asked_counts,
        asked,
        arrived[k],
        total,
        slices,
        bounds[k],
        ent_rows,
        [],
    )
    came = lax.cond(all_few & (token[0, 0] == 0.0), lambda: gathered, by_all_to_all)
    own_sums = gathered[:, last_rows(width) :, 0].astype(F32)
    loss_pair = jnp.stack(
        [
            jnp.sum(jnp.sum(own_sums[:, :TERMS], axis=1)),
            jnp.sum(jnp.sum(own_sums[:, TERMS : 2 * TERMS], axis=1)),
        ]
    )
    new_entity, new_entity_first, new_entity_second = finish_entities(
        asked_counts,
        asked,
        came,
        total,
        begin,
        entity_table,
        entity_first,
        entity_second,
        slices,
    )
    new_relation, new_relation_first, new_relation_second = adamw_update(
        relation_table, relation_grad, relation_first, relation_second
    )
    return (
        loss_pair,
        new_entity,
        new_entity_first,
        new_entity_second,
        new_relation,
        new_relation_first,
        new_relation_second,
    )


def solution(mesh):
    placed = (
        P("edge"),
        P("edge"),
        P("edge"),
        P("edge", None),
        P("edge"),
        P(),
        P(),
        P("col", "edge"),
        P("col", "edge"),
        P("col", "edge"),
        P("edge", "col"),
        P("edge", "col"),
        P("edge", "col"),
    )
    return jax.shard_map(
        shards,
        mesh=mesh,
        in_specs=placed,
        out_specs=(
            P(),
            P("col", "edge"),
            P("col", "edge"),
            P("col", "edge"),
            P("edge", "col"),
            P("edge", "col"),
            P("edge", "col"),
        ),
        check_vma=False,
    )
```

```python
import functools

import jax
import jax.numpy as jnp
from jax import lax
from jax.experimental import pallas as pl
from jax.experimental.pallas import tpu as pltpu
from jax.sharding import PartitionSpec as P

STEP = 5


MARGIN = 0.1
LEARN_RATE = 0.1
BETA_ONE = 0.5
BETA_TWO = 0.5
EPSILON = 1e-08
DECAY = 0.01
LANES = 128
UNROLL = 8
PARTS = 4
HALVES = 2
EARLY = 96
TURN = 512
REL_PAD = 256
TERMS = 3
SPARE = 8
NN = (((1,), (0,)), ((), ()))
NT = (((1,), (1,)), ((), ()))
TN = (((0,), (0,)), ((), ()))
F32 = jnp.float32
BF16 = jnp.bfloat16
SMEM = pltpu.SMEM
VMEM = pltpu.VMEM


def params(mebibytes=60):
    return pltpu.CompilerParams(vmem_limit_bytes=mebibytes << 20)


def cost(flops, moved):
    return pl.CostEstimate(flops=int(flops), bytes_accessed=int(moved), transcendentals=0)


def corner(array):
    return array[(0,) * (array.ndim - 2) + (slice(0, 8), slice(0, LANES))]


def token_shape():
    return jax.ShapeDtypeStruct((8, LANES), F32)


def whole(space):
    return pl.BlockSpec(memory_space=space)


def adamw_update(weights, gradient, first, second):
    new_first = BETA_ONE * first + (1.0 - BETA_ONE) * gradient
    new_second = BETA_TWO * second + (1.0 - BETA_TWO) * gradient * gradient
    first_hat = new_first / (1.0 - BETA_ONE**STEP)
    second_hat = new_second / (1.0 - BETA_TWO**STEP)
    updated = weights - LEARN_RATE * (
        first_hat / (jnp.sqrt(second_hat) + EPSILON) + DECAY * weights
    )
    return (updated, new_first, new_second)


def width_slices(width):
    return [(at, min(LANES, width - at)) for at in range(0, width, LANES)]


def owner_lists(all_ids, groups, capacity, ent_rows):
    count = all_ids.shape[0]
    owners = all_ids // ent_rows
    local_rows = all_ids - owners * ent_rows
    chunk = 256
    mine = owners[None, :] == jnp.arange(groups, dtype=jnp.int32)[:, None]
    mine = mine.astype(BF16).reshape(groups, count // chunk, chunk)
    before = jnp.triu(jnp.ones((chunk, chunk), BF16), 1)
    inner = jnp.dot(mine, before, preferred_element_type=F32)
    sums = jnp.sum(mine.astype(F32), axis=2)
    carry = jnp.cumsum(sums, axis=1) - sums
    ranks = jnp.sum(mine.astype(F32) * (inner + carry[:, :, None]), axis=0)
    ranks = ranks.astype(jnp.int32).reshape(count)
    counts = jnp.sum(sums, axis=1).astype(jnp.int32)
    high = owners * (capacity // LANES) + ranks // LANES
    low = ranks % LANES
    tall = groups * capacity // LANES
    left = (jnp.arange(tall, dtype=jnp.int32)[:, None] == high[None, :]).astype(BF16)
    right = (jnp.arange(LANES, dtype=jnp.int32)[:, None] == low[None, :]).astype(BF16)
    places = jnp.arange(1, count + 1, dtype=jnp.int32)
    parts = jnp.stack([places // 256, places % 256, local_rows // 256, local_rows % 256])
    right = (parts.astype(BF16)[:, None, :] * right[None]).reshape(PARTS * LANES, count)
    found = lax.dot_general(left, right, NT, preferred_element_type=F32).astype(jnp.int32)
    found = found.reshape(tall, PARTS, LANES)
    place = found[:, 0] * 256 + found[:, 1]
    place_list = jnp.where(place > 0, place - 1, count).reshape(groups, capacity)
    row_list = jnp.where(place > 0, found[:, 2] * 256 + found[:, 3], ent_rows)
    return place_list, row_list.reshape(groups, capacity), counts


def relation_rows_kernel(slices, ids_ref, scale_ref, *refs):
    n = len(slices)
    tables, outs = refs[:n], refs[-2 * n - 1 : -n - 1]
    columns, rows = refs[-n - 1], refs[-n:]
    groups = tables[0].shape[0]
    for (_, depth), table, into in zip(slices, tables, rows):
        columns[...] = jnp.zeros_like(columns)

        def turn(group, carry):
            columns[:depth, :] = table[group, :depth].astype(F32)
            if depth < LANES:
                columns[LANES - 1 :, :] = scale_ref[pl.ds(group, 1), :]
            into[pl.ds(pl.multiple_of(group * REL_PAD, REL_PAD), REL_PAD), :] = columns[...].T
            return carry

        lax.fori_loop(0, groups, turn, 0, unroll=4)

    def body(step, carry):
        for lane in range(UNROLL):
            at = step * UNROLL + lane
            row = ids_ref[at]
            for source, out in zip(rows, outs):
                out[pl.ds(at, 1), :] = source[pl.ds(row, 1), :]
        return carry

    lax.fori_loop(0, outs[0].shape[0] // UNROLL, body, 0)


def relation_rows(places, dense, scale, slices, after):
    count = places.shape[0]
    groups, depth, span = dense.shape
    n = len(slices)
    first = span // REL_PAD - n

    def columns(k):
        return pl.BlockSpec((groups, depth, REL_PAD), lambda i: (0, 0, first + k))

    return pl.pallas_call(
        functools.partial(relation_rows_kernel, slices),
        out_shape=[jax.ShapeDtypeStruct((count, LANES), F32)] * n,
        grid=(1,),
        in_specs=[whole(SMEM), whole(VMEM)]
        + [columns(k) for k in range(n)]
        + [whole(pl.ANY)] * len(after),
        out_specs=[whole(VMEM)] * n,
        scratch_shapes=[pltpu.VMEM((LANES, REL_PAD), F32)]
        + [pltpu.VMEM((groups * REL_PAD, LANES), F32)] * n,
        compiler_params=params(28),
        cost_estimate=cost(0, 80e6),
        name="relation_rows",
    )(places, scale, *[dense] * n, *after)


def fetch_kernel(
    capacity, moves, ent_rows, counts_ref, place_ref, row_ref, dense_ref, *refs
):
    shard = pl.program_id(0)
    last = pl.num_programs(0) - 1
    out_ref, rows = refs[-3], refs[-2:]
    depth = dense_ref.shape[1]
    turns = ent_rows // TURN
    rest = ent_rows - turns * TURN

    if depth < LANES:

        @pl.when(shard == 0)
        def _():
            for ref in rows:
                ref[...] = jnp.zeros_like(ref)

    def turn(into, begin, size):
        cols = pl.ds(begin, size)
        into[cols, :depth] = dense_ref[0, :, cols].astype(F32).T

    def move(source, at):
        out_ref[pl.ds(place_ref[at], 1), :] = source[pl.ds(row_ref[at], 1), :]

    def step(into, source):
        base = (shard - 1) * capacity

        def remaining(first):
            def body(trip, carry):
                for lane in range(UNROLL):
                    move(source, base + first + trip * UNROLL + lane)
                return carry

            wanted = counts_ref[jnp.maximum(shard - 1, 0)] - first
            lax.fori_loop(0, (wanted + UNROLL - 1) // UNROLL, body, 0)

        def only_turn(trip, carry):
            turn(into, pl.multiple_of(trip * TURN, TURN), TURN)
            return carry

        def both(trip, carry):
            turn(into, pl.multiple_of(trip * TURN, TURN), TURN)
            for lane in range(moves):
                move(source, base + trip * moves + lane)
            return carry

        @pl.when(shard == 0)
        def _():
            lax.fori_loop(0, turns, only_turn, 0)

        @pl.when((shard > 0) & (shard < last))
        def _():
            lax.fori_loop(0, turns, both, 0)
            remaining(turns * moves)

        @pl.when(shard == last)
        def _():
            remaining(0)

        if rest:

            @pl.when(shard < last)
            def _():
                turn(into, turns * TURN, rest)

    for parity in range(2):

        @pl.when(lax.rem(shard, 2) == parity)
        def _():
            step(rows[parity], rows[1 - parity])


def fetch(counts, place_list, row_list, dense, id_count, ent_rows, after):
    groups, depth, _ = dense.shape
    capacity = place_list.shape[0] // groups
    moves = (id_count // groups) // (ent_rows // TURN) // UNROLL * UNROLL
    return pl.pallas_call(
        functools.partial(fetch_kernel, capacity, moves, ent_rows),
        out_shape=jax.ShapeDtypeStruct((id_count + 8, LANES), F32),
        grid=(groups + 1,),
        in_specs=[whole(SMEM)] * 3
        + [
            pl.BlockSpec(
                (1, depth, ent_rows), lambda shard: (jnp.minimum(shard, groups - 1), 0, 0)
            )
        ]
        + [whole(pl.ANY)] * len(after),
        out_specs=whole(VMEM),
        scratch_shapes=[pltpu.VMEM((ent_rows + 8, LANES), F32)] * 2,
        compiler_params=params(32),
        cost_estimate=cost(0, 170e6),
        name="fetch_rows",
    )(counts, place_list, row_list, dense, *after)


def column_sum(values):
    return jnp.sum(values * values, axis=0, keepdims=True)


def negatives_kernel(neg_ref, early_ref, late_ref, norm_ref):
    neg_t = neg_ref[...].T
    early_ref[...] = neg_t[:EARLY].astype(BF16)
    late_ref[...] = neg_t[EARLY:].astype(BF16)
    norm_ref[...] = column_sum(neg_t)


def negatives(fetched, blocks, block_len):
    count = blocks * block_len
    return pl.pallas_call(
        negatives_kernel,
        out_shape=[
            jax.ShapeDtypeStruct((EARLY, count), BF16),
            jax.ShapeDtypeStruct((LANES - EARLY, count), BF16),
            jax.ShapeDtypeStruct((1, count), F32),
        ],
        grid=(blocks,),
        in_specs=[pl.BlockSpec((block_len, LANES), lambda b: (2 * blocks + b, 0))],
        out_specs=[
            pl.BlockSpec((EARLY, block_len), lambda b: (0, b)),
            pl.BlockSpec((LANES - EARLY, block_len), lambda b: (0, b)),
            pl.BlockSpec((1, block_len), lambda b: (0, b)),
        ],
        compiler_params=params(12),
        cost_estimate=cost(0, 10e6),
        name="negatives",
    )(fetched)


def edge_parts(depth, head_ref, tail_ref, rel_ref, off_ref, tail_out):
    lane = lax.broadcasted_iota(jnp.int32, head_ref.shape, 1)
    inside = lane < depth
    rel = rel_ref[...]
    tail = tail_ref[...]
    shifted = head_ref[...] + jnp.where(inside, rel, 0.0)
    off_ref[...] = jnp.where(inside, shifted - tail, rel)
    tail_out[...] = tail.astype(BF16)
    shifted_t = shifted.T
    return shifted_t, column_sum((shifted - tail).T) - column_sum(shifted_t)


def edges_kernel(
    depth, head_ref, tail_ref, rel_ref, late_ref, off_ref, tail_out, low_ref, bias_ref
):
    shifted_t, bias = edge_parts(depth, head_ref, tail_ref, rel_ref, off_ref, tail_out)
    low_ref[:depth] = shifted_t[:depth].astype(BF16)
    low_ref[depth:] = late_ref[...]
    bias_ref[...] = bias


def edges(fetched, rel_rows, late, depth, blocks, block_len):
    count = blocks * block_len
    tall = depth + late.shape[0]

    def rows(at):
        return pl.BlockSpec((block_len, LANES), lambda b: (at * blocks + b, 0))

    return pl.pallas_call(
        functools.partial(edges_kernel, depth),
        out_shape=[
            jax.ShapeDtypeStruct((count, LANES), F32),
            jax.ShapeDtypeStruct((count, LANES), BF16),
            jax.ShapeDtypeStruct((tall, count), BF16),
            jax.ShapeDtypeStruct((1, count), F32),
        ],
        grid=(blocks,),
        in_specs=[rows(0), rows(1), rows(0)]
        + [pl.BlockSpec((tall - depth, block_len), lambda b: (0, b))],
        out_specs=[
            rows(0),
            rows(0),
            pl.BlockSpec((tall, block_len), lambda b: (0, b)),
            pl.BlockSpec((1, block_len), lambda b: (0, b)),
        ],
        compiler_params=params(16),
        cost_estimate=cost(0, 30e6),
        name="edges",
    )(fetched, fetched, rel_rows, late)


def last_rows(depth):
    return (depth + 7) // 8 * 8


def with_terms(columns, total, depth):
    terms = term_rows(total, 0)
    return jnp.concatenate([columns[: last_rows(depth)], terms], axis=0).astype(BF16)


def term_rows(total, first):
    place = lax.broadcasted_iota(jnp.int32, (8, total.shape[1]), 0)
    left = total
    terms = jnp.zeros(place.shape, F32)
    for k in range(TERMS):
        term = left.astype(BF16).astype(F32)
        left = left - term
        terms = jnp.where(place == first + k, term, terms)
    return terms


def last_kernel(depth, n_given, head_ref, tail_ref, neg_ref, rel_ref, *refs):
    biases, norms = refs[:n_given], refs[n_given : 2 * n_given]
    off_ref, tail_out, pair_ref, token = refs[-4:]
    token[...] = jnp.zeros_like(token)
    shifted_t, bias = edge_parts(depth, head_ref, tail_ref, rel_ref, off_ref, tail_out)
    neg_t = neg_ref[...].T
    norm = column_sum(neg_t)
    for ref in biases:
        bias = bias + ref[...]
    for ref in norms:
        norm = norm + ref[...]
    pair_ref[0] = with_terms(shifted_t, bias, depth)
    pair_ref[1] = with_terms(neg_t, norm, depth)


def last_slice(fetched, rel_rows, biases, norms, depth, blocks, block_len, half, after):
    part = blocks // HALVES
    count = part * block_len
    tall = last_rows(depth) + 8

    def rows(at):
        return pl.BlockSpec((block_len, LANES), lambda b: (at * blocks + half * part + b, 0))

    return pl.pallas_call(
        functools.partial(last_kernel, depth, len(biases)),
        out_shape=[
            jax.ShapeDtypeStruct((count, LANES), F32),
            jax.ShapeDtypeStruct((count, LANES), BF16),
            jax.ShapeDtypeStruct((2, tall, count), BF16),
            token_shape(),
        ],
        grid=(part,),
        in_specs=[rows(0), rows(1), rows(2), rows(0)]
        + [pl.BlockSpec((1, block_len), lambda b: (0, half * part + b))]
        * (len(biases) + len(norms))
        + [whole(pl.ANY)] * len(after),
        out_specs=[
            pl.BlockSpec((block_len, LANES), lambda b: (b, 0)),
            pl.BlockSpec((block_len, LANES), lambda b: (b, 0)),
            pl.BlockSpec((2, tall, block_len), lambda b: (0, 0, b)),
            pl.BlockSpec((8, LANES), lambda b: (0, 0)),
        ],
        compiler_params=params(16),
        cost_estimate=cost(0, 20e6),
        name="last_slice",
    )(fetched, fetched, fetched, rel_rows, *biases, *norms, *after)


def block_kernel(slices, n_col, half, me_ref, live_ref, *refs):
    n = len(slices)
    per_col = 2 * n - 1
    given = [refs[k * per_col : (k + 1) * per_col] for k in range(n_col)]
    refs = refs[n_col * per_col :]
    offs, tails, refs = refs[:n], refs[n : 2 * n], refs[2 * n :]
    grad, refs = refs[-9], refs[-8:]
    loss_ref, shift_scr, neg_scr, sums_scr, cross, slopes, row_bias, row_sum = refs
    block = pl.program_id(0)
    length = cross.shape[0]
    me = me_ref[0]
    for k in range(n_col):
        slot = lax.rem(me + (n_col - k), n_col)
        for m, (start, depth) in enumerate(slices):
            if m < n - 1:
                early, late = given[k][2 * m : 2 * m + 2]
                shift_scr[slot, start : start + depth, :] = 2.0 * late[:depth, :]
                neg_scr[slot, start : start + EARLY, :] = early[...]
                neg_scr[slot, start + EARLY : start + depth, :] = late[depth:, :]
            else:
                pair = given[k][-1]
                shift, neg = pair[0, :depth, :], pair[1, :depth, :]
                for row in range(2):
                    terms = pair[row, last_rows(depth) : last_rows(depth) + 8, :].astype(F32)
                    sums_scr[slot, row : row + 1] = jnp.sum(terms, axis=0, keepdims=True)
                shift_scr[slot, start : start + depth, :] = 2.0 * shift
                neg_scr[slot, start : start + depth, :] = neg
    bias = jnp.sum(sums_scr[:, 0, :], axis=0, keepdims=True) + MARGIN
    neg_norm = jnp.sum(sums_scr[:, 1, :], axis=0, keepdims=True)
    row_bias[...] = jnp.broadcast_to(bias, (LANES, length)).T

    live = live_ref[half * pl.num_programs(0) + block]
    tile = 256
    small = 128
    lane_tiles = [slice(at, at + LANES) for at in range(0, length, LANES)]
    cols = jnp.zeros((8, length), F32)
    loss = jnp.zeros((8, LANES), F32)
    def products(at):
        part = slice(at, at + tile)
        doubled = None
        for k in range(n_col):
            term = lax.dot_general(
                shift_scr[k, :, part], neg_scr[k], TN, preferred_element_type=F32
            )
            doubled = term if doubled is None else doubled + term
        cross[part, :] = doubled

    def moves(at):
        part = slice(at, at + tile)
        moved = lax.dot_general(slopes[part, :], neg_scr[me], NT, preferred_element_type=F32)
        fade = -row_sum[part, :]
        for m, (start, depth) in enumerate(slices):
            into = pl.ds(n * at + m, tile, stride=n)
            grad[0, into, :depth] = (
                fade[:, :depth] * tails[m][part, :depth].astype(F32)
                + moved[:, start : start + depth]
            )
            grad[1, into, :] = fade * offs[m][part, :]

    products(0)
    for begin in range(0, length, tile):
        if begin + tile < length:
            products(begin + tile)
        for at in range(begin, begin + tile, small):
            part = slice(at, at + small)
            place = at + lax.broadcasted_iota(jnp.int32, (small, 1), 0)
            scale = offs[-1][part, LANES - 1 : LANES]
            weight = jnp.where(place < live, scale, 0.0) / length
            margins = cross[part, :] + (row_bias[part, 0:1] - neg_norm)
            fall = jnp.exp(-jnp.abs(margins))
            under = 1.0 + fall
            guess = pl.reciprocal(under, approx=True)
            inverse = guess * (2.0 - under * guess)
            twice = (2.0 * weight) * (jnp.where(margins >= 0.0, 1.0, fall) * inverse)
            row_sum[part, :] = jnp.broadcast_to(
                jnp.sum(twice, axis=1, keepdims=True), (small, LANES)
            )
            slopes[part, :] = twice.astype(BF16)
            cols = cols + jnp.sum(twice.reshape(small // 8, 8, length), axis=0)
            over = jnp.maximum(margins, 0.0)
            lifts = [fall[:, lanes] for lanes in lane_tiles]
            while len(lifts) > 1:
                lifts = [a + b + a * b for a, b in zip(lifts[::2], lifts[1::2])]
            lift = lifts[0]
            soft = functools.reduce(jnp.add, [over[:, lanes] for lanes in lane_tiles]) + jnp.where(
                lift < 2.0**-11, lift * (1.0 - 0.5 * lift), jnp.log(1.0 + lift)
            )
            loss = loss + jnp.sum((weight * soft).reshape(small // 8, 8, LANES), axis=0)
        moves(begin)
    col_sum = jnp.sum(cols, axis=0, keepdims=True)

    @pl.when(block == 0)
    def _():
        loss_ref[...] = loss

    @pl.when(block > 0)
    def _():
        loss_ref[...] += loss

    moved = lax.dot_general(shift_scr[me], slopes[...], NN, preferred_element_type=F32)
    moved = 0.5 * moved - col_sum * neg_scr[me].astype(F32)
    for m, (start, depth) in enumerate(slices):
        grad[2, pl.ds(m, length, stride=n), :depth] = moved[start : start + depth, :].T


def block_math(me, live_counts, given, offs, tails, old, slices, block_len, half, after):
    n, n_col = len(slices), len(given)
    blocks = live_counts.shape[0]
    part = blocks // HALVES
    width = sum(depth for _, depth in slices)
    flat = [piece for per_col in given for piece in per_col]
    kept = [] if old is None else [old]

    def columns(piece):
        if piece.ndim == 3:
            return pl.BlockSpec((2, piece.shape[1], block_len), lambda b: (0, 0, b))
        return pl.BlockSpec((piece.shape[0], block_len), lambda b: (0, half * part + b))

    def rows(array):
        first = half * part if array.shape[0] > part * block_len else 0
        return pl.BlockSpec((block_len, LANES), lambda b: (first + b, 0))

    first_old = 2 + len(flat) + 2 * n
    return pl.pallas_call(
        functools.partial(block_kernel, slices, n_col, half),
        out_shape=[
            jax.ShapeDtypeStruct((3, n * blocks * block_len, LANES), F32),
            jax.ShapeDtypeStruct((8, LANES), F32),
        ],
        grid=(part,),
        in_specs=[whole(SMEM)] * 2
        + [columns(piece) for piece in flat]
        + [rows(array) for array in offs + tails]
        + [whole(pl.ANY)] * len(kept + after),
        out_specs=[
            pl.BlockSpec((3, n * block_len, LANES), lambda b: (0, half * part + b, 0)),
            pl.BlockSpec((8, LANES), lambda b: (0, 0)),
        ],
        input_output_aliases={first_old + k: k for k in range(len(kept))},
        scratch_shapes=[
            pltpu.VMEM((n_col, width, block_len), BF16),
            pltpu.VMEM((n_col, width, block_len), BF16),
            pltpu.VMEM((n_col, 2, block_len), F32),
            pltpu.VMEM((block_len, block_len), F32),
            pltpu.VMEM((block_len, block_len), BF16),
            pltpu.VMEM((block_len, LANES), F32),
            pltpu.VMEM((block_len, LANES), F32),
        ],
        compiler_params=params(60),
        cost_estimate=cost(part * 8 * block_len * block_len * width, 120e6),
        name="block_math",
    )(me, live_counts, *flat, *offs, *tails, *kept, *after)


def pair_of(row, n):
    return pl.ds(pl.multiple_of(row * n, n), n)


def outgoing_kernel(slices, capacity, begin, counts_ref, place_ref, grad, *refs):
    n = len(slices)
    out_ref, token, tile = refs[-3:]
    groups, _, chunk = out_ref.shape
    token[...] = jnp.zeros_like(token)

    def owner(group, carry):
        wanted = jnp.clip(counts_ref[group] - begin, 0, chunk)

        def body(step, inner):
            for lane in range(UNROLL):
                at = step * UNROLL + lane
                place = place_ref[group * capacity + begin + at]
                tile[pair_of(at, n), :] = grad[pair_of(place, n), :]
            return inner

        lax.fori_loop(0, (wanted + UNROLL - 1) // UNROLL, body, 0)
        for m, (start, depth) in enumerate(slices):
            piece = tile[pl.ds(m, chunk, stride=n), :].T
            out_ref[group, start : start + depth, :] = piece[:depth].astype(BF16)
        return carry

    lax.fori_loop(0, groups, owner, 0)


def excess_kernel(slices, capacity, begin, counts_ref, place_ref, live_ref, grad, loss_ref, *refs):
    outgoing_kernel(slices, capacity, begin, counts_ref, place_ref, grad, *refs)
    out_ref = refs[-3]
    loss = jnp.sum(jnp.sum(loss_ref[...], axis=0, keepdims=True), axis=1, keepdims=True)
    live = live_ref[0]
    for block in range(1, live_ref.shape[0]):
        live = live + live_ref[block]
    count = jnp.full((1, LANES), live.astype(F32))
    terms = term_rows(jnp.broadcast_to(loss, (1, LANES)), 0) + term_rows(count, TERMS)
    width = sum(depth for _, depth in slices)
    for at in range(0, out_ref.shape[2], LANES):
        out_ref[0, last_rows(width) :, at : at + LANES] = terms.astype(BF16)


def excess_rows(count, places, live, grad, loss, slices, begin, chunk, after):
    n = len(slices)
    width = sum(depth for _, depth in slices)
    return pl.pallas_call(
        functools.partial(excess_kernel, slices, places.shape[1], begin),
        out_shape=[
            jax.ShapeDtypeStruct((1, last_rows(width) + SPARE, chunk), BF16),
            token_shape(),
        ],
        in_specs=[whole(SMEM)] * 3 + [whole(VMEM)] * 2 + [whole(pl.ANY)] * len(after),
        out_specs=[whole(VMEM)] * 2,
        scratch_shapes=[pltpu.VMEM((n * chunk, LANES), F32)],
        compiler_params=params(34),
        cost_estimate=cost(0, 80e6),
        name="excess_rows",
    )(count, places.reshape(-1), live, grad, loss, *after)


def outgoing(counts, place_list, grad, slices, begin, chunk, after, spare=0):
    groups, capacity = place_list.shape
    n = len(slices)
    width = sum(depth for _, depth in slices) + spare
    return pl.pallas_call(
        functools.partial(outgoing_kernel, slices, capacity, begin),
        out_shape=[jax.ShapeDtypeStruct((groups, width, chunk), BF16), token_shape()],
        in_specs=[whole(SMEM)] * 2 + [whole(VMEM)] + [whole(pl.ANY)] * len(after),
        out_specs=[whole(VMEM)] * 2,
        scratch_shapes=[pltpu.VMEM((n * chunk, LANES), F32)],
        compiler_params=params(34),
        cost_estimate=cost(0, 80e6),
        name="outgoing",
    )(counts, place_list.reshape(-1), grad, *after)


def collect_kernel(slices, capacity, begin, first, counts_ref, row_ref, came_ref, *refs):
    total, token, tile = refs[-3:]
    total[...] = jnp.zeros_like(total) if first else refs[0][...]
    token[...] = jnp.zeros_like(token)
    add_rows(slices, capacity, begin, counts_ref, row_ref, came_ref, total, tile)


def add_rows(slices, capacity, begin, counts_ref, row_ref, came_ref, total, tile):
    n = len(slices)
    groups, _, chunk = came_ref.shape

    def source(group, carry):
        wanted = jnp.clip(counts_ref[group] - begin, 0, chunk)

        @pl.when(wanted > 0)
        def _():
            for m, (start, depth) in enumerate(slices):
                piece = came_ref[group, start : start + depth, :].astype(F32)
                tile[pl.ds(m, chunk, stride=n), :depth] = piece.T

            def body(step, inner):
                for lane in range(UNROLL):
                    at = step * UNROLL + lane
                    into = pair_of(row_ref[group * capacity + begin + at], n)
                    total[into, :] = total[into, :] + tile[pair_of(at, n), :]
                return inner

            lax.fori_loop(0, (wanted + UNROLL - 1) // UNROLL, body, 0)

        return carry

    lax.fori_loop(0, groups, source, 0)


def collect(counts, row_list, came, total, slices, begin, ent_rows, after):
    capacity = row_list.shape[1]
    chunk = came.shape[2]
    n = len(slices)
    given = [] if total is None else [total]
    return pl.pallas_call(
        functools.partial(collect_kernel, slices, capacity, begin, total is None),
        out_shape=[jax.ShapeDtypeStruct((n * (ent_rows + 8), LANES), F32), token_shape()],
        input_output_aliases={3: 0} if given else {},
        in_specs=[whole(SMEM)] * 2
        + [whole(VMEM)] * (1 + len(given))
        + [whole(pl.ANY)] * len(after),
        out_specs=[whole(VMEM)] * 2,
        scratch_shapes=[pltpu.VMEM((n * chunk, LANES), F32)],
        compiler_params=params(26),
        cost_estimate=cost(0, 120e6),
        name="collect",
    )(counts, row_list.reshape(-1), came, *given, *after)


def relation_sums_kernel(n, ids_ref, grad, *refs):
    total, token = refs[-2:]
    total[...] = jnp.zeros_like(total)
    token[...] = jnp.zeros_like(token)

    def body(step, carry):
        for lane in range(UNROLL):
            at = step * UNROLL + lane
            into = pair_of(ids_ref[at], n)
            total[into, :] = total[into, :] + grad[0, pair_of(at, n), :]
        return carry

    lax.fori_loop(0, grad.shape[1] // n // UNROLL, body, 0)


def relation_sums(relation_ids, grad, n, rel_total, after):
    count = relation_ids.shape[0]
    return pl.pallas_call(
        functools.partial(relation_sums_kernel, n),
        out_shape=[jax.ShapeDtypeStruct((n * rel_total, LANES), F32), token_shape()],
        grid=(1,),
        in_specs=[whole(SMEM), pl.BlockSpec((1, n * count, LANES), lambda i: (0, 0, 0))]
        + [whole(pl.ANY)] * len(after),
        out_specs=[whole(VMEM)] * 2,
        compiler_params=params(30),
        cost_estimate=cost(0, 120e6),
        name="relation_sums",
    )(relation_ids, grad, *after)


def finish_kernel(
    slices,
    capacity,
    begin,
    last_begin,
    counts_ref,
    row_ref,
    came_ref,
    last_ref,
    total_ref,
    weights_ref,
    first_ref,
    second_ref,
    *refs,
):
    n = len(slices)
    width = sum(depth for _, depth in slices)
    outs, loss_ref, (total, tile, gradient) = refs[:3], refs[3], refs[4:]
    cols = weights_ref.shape[1]
    step = pl.program_id(0)

    @pl.when(step == 0)
    def _():
        total[: total_ref.shape[0], :] = total_ref[...]
        add_rows(slices, capacity, begin, counts_ref, row_ref, came_ref, total, tile)
        add_rows(slices, capacity, last_begin, counts_ref, row_ref, last_ref, total, tile)
        terms = jnp.zeros((SPARE, LANES), F32)
        for group in range(last_ref.shape[0]):
            terms = terms + last_ref[group, last_rows(width) :, :LANES].astype(F32)
        place = lax.broadcasted_iota(jnp.int32, terms.shape, 0)
        for k in range(2):
            own = (place >= k * TERMS) & (place < (k + 1) * TERMS)
            loss_ref[k : k + 1, :] = jnp.sum(jnp.where(own, terms, 0.0), axis=0, keepdims=True)
        loss_ref[2:, :] = jnp.zeros((6, LANES), F32)

    for m, (start, depth) in enumerate(slices):
        part = total[pl.ds(step * (n * cols) + m, cols, stride=n), :]
        gradient[start : start + depth, :] = part.T[:depth]
    grad = gradient[...]
    new_first = BETA_ONE * first_ref[...] + (1.0 - BETA_ONE) * grad
    new_second = BETA_TWO * second_ref[...] + (1.0 - BETA_TWO) * grad * grad
    under = jnp.sqrt(new_second * (1.0 / (1.0 - BETA_TWO**STEP))) + EPSILON
    guess = pl.reciprocal(under, approx=True)
    inverse = guess * (2.0 - under * guess)
    pace = LEARN_RATE / (1.0 - BETA_ONE**STEP)
    outs[0][...] = (1.0 - LEARN_RATE * DECAY) * weights_ref[...] - (pace * new_first) * inverse
    outs[1][...] = new_first
    outs[2][...] = new_second


def finish_entities(
    counts, row_list, came, last, total, begin, last_begin, weights, first, second, slices
):
    width, ent_rows = weights.shape
    capacity = row_list.shape[1]
    cols = 1024
    steps = pl.cdiv(ent_rows, cols)
    n = len(slices)
    table = pl.BlockSpec((width, cols), lambda i: (0, i))
    tall = max(n * cols * steps, total.shape[0])
    return pl.pallas_call(
        functools.partial(finish_kernel, slices, capacity, begin, last_begin),
        out_shape=[jax.ShapeDtypeStruct((width, ent_rows), F32)] * 3 + [token_shape()],
        grid=(steps,),
        in_specs=[whole(SMEM)] * 2 + [whole(VMEM)] * 3 + [table] * 3,
        out_specs=[table] * 3 + [pl.BlockSpec((8, LANES), lambda i: (0, 0))],
        scratch_shapes=[
            pltpu.VMEM((tall, LANES), F32),
            pltpu.VMEM((n * max(came.shape[2], last.shape[2]), LANES), F32),
            pltpu.VMEM((width, cols), F32),
        ],
        compiler_params=params(56),
        cost_estimate=cost(0, 60e6),
        name="finish_entities",
    )(counts, row_list.reshape(-1), came, last, total, weights, first, second)


def chunk_bounds(capacity):
    units = capacity // LANES
    sizes = [3, 7, 3, 3] if units == 16 else [units // 4] * 3 + [units - 3 * (units // 4)]
    bounds = [0]
    for size in sizes:
        bounds.append(bounds[-1] + size * LANES)
    return bounds


def shards(
    head_ids,
    relation_ids,
    tail_ids,
    negative_ids,
    live_counts,
    rel_weight,
    rel_count,
    entity_table,
    entity_first,
    entity_second,
    relation_table,
    relation_first,
    relation_second,
):
    groups = lax.axis_size("edge")
    n_col = lax.axis_size("col")
    width, ent_rows = entity_table.shape
    blocks, neg_count = negative_ids.shape
    block_len = head_ids.shape[0] // blocks
    edge_count = blocks * block_len
    slices = width_slices(width)
    n = len(slices)
    all_ids = jnp.concatenate([head_ids, tail_ids, negative_ids.reshape(-1)])
    id_count = all_ids.shape[0]
    capacity = (4 * id_count + 3 * groups - 1) // (3 * groups)
    rel_total = rel_weight.shape[0]

    rel_own = rel_total // groups
    rel_low = jnp.pad(relation_table.astype(BF16).T, ((0, 0), (0, REL_PAD - rel_own)))
    dense = []
    for k, (start, depth) in enumerate(slices):
        sent = entity_table[start : start + depth].astype(BF16)
        if k == 0:
            behind = [
                jnp.pad(rel_low[at : at + size], ((0, depth - size), (0, 0))) for at, size in slices
            ]
            sent = jnp.concatenate([sent] + behind, axis=1)
        dense.append(lax.all_gather(sent, "edge", axis=0, tiled=False))

    place_list, row_list, counts = owner_lists(all_ids, groups, capacity, ent_rows)
    safe_places = jnp.minimum(place_list, id_count - 1)
    place_flat, row_flat = place_list.reshape(-1), row_list.reshape(-1)

    rel_scale = rel_weight * (rel_total / jnp.sum(rel_weight)) / rel_count.astype(F32)
    rel_scale = jnp.pad(rel_scale.reshape(groups, rel_own), ((0, 0), (0, REL_PAD - rel_own)))
    rel_places = relation_ids + (relation_ids // rel_own) * (REL_PAD - rel_own)

    def from_others(array):
        turns = [[(c, (c + away) % n_col) for c in range(n_col)] for away in range(1, n_col)]
        return [lax.ppermute(array, "col", turn) for turn in turns]

    me = lax.axis_index("col").astype(jnp.int32).reshape(1)
    given = [[[] for _ in range(n_col)] for _ in range(HALVES)]
    offs = [[] for _ in range(HALVES)]
    tails = [[] for _ in range(HALVES)]
    biases, norms, first_sent, rel_rows = [], [], [], None
    for k, (start, depth) in enumerate(slices):
        sent = first_sent if k > 0 else []
        fetched = fetch(counts, place_flat, row_flat, dense[k], id_count, ent_rows, sent)
        if k < n - 1:
            early, late, norm = negatives(fetched, blocks, block_len)
            early_all = [early] + from_others(early)
            if rel_rows is None:
                rel_rows = relation_rows(rel_places, dense[0], rel_scale, slices, [norm])
            off, tail, low, bias = edges(fetched, rel_rows[k], late, depth, blocks, block_len)
            low_all = [low] + from_others(low)
            first_sent = [corner(piece) for piece in early_all[1:]]
            biases.append(bias)
            norms.append(norm)
            for half in range(HALVES):
                offs[half].append(off)
                tails[half].append(tail)
                for col in range(n_col):
                    given[half][col] += [early_all[col], low_all[col]]
            continue
        if rel_rows is None:
            rel_rows = relation_rows(rel_places, dense[0], rel_scale, slices, [])

    def finish(half, after):
        off, tail, pair, token = last_slice(
            fetched, rel_rows[-1], biases, norms, slices[-1][1], blocks, block_len, half, after
        )
        offs[half].append(off)
        tails[half].append(tail)
        for col, piece in enumerate([pair] + from_others(pair)):
            given[half][col].append(piece)
        return token

    grad, loss_tiles = None, []
    half_token = []
    for half in range(HALVES):
        half_token = [finish(half, half_token)]
    bounds = chunk_bounds(capacity)
    few = jnp.sum((counts > bounds[-2]).astype(jnp.int32)) <= 1
    flag = few.astype(jnp.int32) + half_token[0][0, 0].astype(jnp.int32)
    flag = jnp.broadcast_to(flag, (groups, LANES))
    asked = lax.all_to_all(
        jnp.concatenate([row_list, flag], axis=1), "edge", split_axis=0, concat_axis=0, tiled=True
    )
    all_few = jnp.min(asked[:, capacity]) > 0
    asked = asked[:, :capacity]
    asked_counts = jnp.sum((asked < ent_rows).astype(jnp.int32), axis=1)
    for half in range(HALVES):
        after = [corner(asked)] if half == 0 else []
        grad, loss_tile = block_math(
            me,
            live_counts,
            given[half],
            offs[half],
            tails[half],
            grad,
            slices,
            block_len,
            half,
            after,
        )
        loss_tiles.append(loss_tile)
    live = jnp.minimum(live_counts, block_len)
    loss_tile = functools.reduce(jnp.add, loss_tiles)

    flat = grad.reshape(n * id_count, LANES)
    chunks = len(bounds) - 1
    begin, size = bounds[-2], bounds[-1] - bounds[-2]
    most = jnp.argmax(counts)
    most_places = lax.dynamic_slice_in_dim(safe_places, most, 1, axis=0)
    most_count = lax.dynamic_slice_in_dim(counts, most, 1, axis=0)
    arrived, total, after = [], None, []
    for k in range(chunks - 1):
        sent, sent_token = outgoing(
            counts, safe_places, flat, slices, bounds[k], bounds[k + 1] - bounds[k], after
        )
        arrived.append(lax.all_to_all(sent, "edge", split_axis=0, concat_axis=0, tiled=True))
        after = []
        if k == 0:
            excess, excess_token = excess_rows(
                most_count,
                most_places,
                live,
                flat,
                loss_tile,
                slices,
                begin,
                size,
                [sent_token],
            )
            after = [excess_token]
        if k == 1:
            before = [corner(arrived[0]), excess_token, sent_token]
            rel_terms, token = relation_sums(relation_ids, grad, n, rel_total, before)
            after = [token]
            rel_terms = rel_terms.reshape(rel_total, n * LANES)[:, :width]
            relation_grad = lax.psum_scatter(rel_terms, "edge", scatter_dimension=0, tiled=True)
        if k == 2:
            ready = (relation_grad[0, 0] == relation_grad[0, 0]) & (sent_token[0, 0] == 0.0)
            excess = jnp.where(ready, excess, jnp.zeros_like(excess))
            gathered = lax.all_gather(excess, "edge", axis=0, tiled=True)
            after = [corner(relation_grad)]
        if k > 0:
            total, token = collect(
                asked_counts, asked, arrived[k - 1], total, slices, bounds[k - 1], ent_rows, after
            )
            after = [token, corner(relation_grad)]

    def by_all_to_all():
        spare = last_rows(width) + SPARE - width
        sent, _ = outgoing(counts, safe_places, flat, slices, begin, size, [], spare)
        rows = lax.all_to_all(sent, "edge", split_axis=0, concat_axis=0, tiled=True)
        return rows.at[:, last_rows(width) :].set(gathered[:, last_rows(width) :])

    k = chunks - 2
    here = jnp.where(arrived[k][0, 0, 0] > 0, 1, 2) > 0
    came = lax.cond(all_few & here & (token[0, 0] == 0.0), lambda: gathered, by_all_to_all)
    new_entity, new_entity_first, new_entity_second, sums = finish_entities(
        asked_counts,
        asked,
        arrived[k],
        came,
        total,
        bounds[k],
        begin,
        entity_table,
        entity_first,
        entity_second,
        slices,
    )
    loss_pair = sums[:2, 0]
    new_relation, new_relation_first, new_relation_second = adamw_update(
        relation_table, relation_grad, relation_first, relation_second
    )
    return (
        loss_pair,
        new_entity,
        new_entity_first,
        new_entity_second,
        new_relation,
        new_relation_first,
        new_relation_second,
    )


def solution(mesh):
    placed = (
        P("edge"),
        P("edge"),
        P("edge"),
        P("edge", None),
        P("edge"),
        P(),
        P(),
        P("col", "edge"),
        P("col", "edge"),
        P("col", "edge"),
        P("edge", "col"),
        P("edge", "col"),
        P("edge", "col"),
    )
    return jax.shard_map(
        shards,
        mesh=mesh,
        in_specs=placed,
        out_specs=(
            P(),
            P("col", "edge"),
            P("col", "edge"),
            P("col", "edge"),
            P("edge", "col"),
            P("edge", "col"),
            P("edge", "col"),
        ),
        check_vma=False,
    )
```

```python
import functools

import jax
import jax.numpy as jnp
from jax import lax
from jax.experimental import pallas as pl
from jax.experimental.pallas import tpu as pltpu
from jax.sharding import PartitionSpec as P

STEP = 5


MARGIN = 0.1
LEARN_RATE = 0.1
BETA_ONE = 0.5
BETA_TWO = 0.5
EPSILON = 1e-08
DECAY = 0.01
LANES = 128
UNROLL = 8
PARTS = 4
HALVES = 2
EARLY = 96
TURN = 512
REL_PAD = 256
TERMS = 3
SPARE = 8
NN = (((1,), (0,)), ((), ()))
NT = (((1,), (1,)), ((), ()))
TN = (((0,), (0,)), ((), ()))
F32 = jnp.float32
BF16 = jnp.bfloat16
SMEM = pltpu.SMEM
VMEM = pltpu.VMEM


def params(mebibytes=60):
    return pltpu.CompilerParams(vmem_limit_bytes=mebibytes << 20)


def cost(flops, moved):
    return pl.CostEstimate(flops=int(flops), bytes_accessed=int(moved), transcendentals=0)


def corner(array):
    return array[(0,) * (array.ndim - 2) + (slice(0, 8), slice(0, LANES))]


def token_shape():
    return jax.ShapeDtypeStruct((8, LANES), F32)


def whole(space):
    return pl.BlockSpec(memory_space=space)


def adamw_update(weights, gradient, first, second):
    new_first = BETA_ONE * first + (1.0 - BETA_ONE) * gradient
    new_second = BETA_TWO * second + (1.0 - BETA_TWO) * gradient * gradient
    first_hat = new_first / (1.0 - BETA_ONE**STEP)
    second_hat = new_second / (1.0 - BETA_TWO**STEP)
    updated = weights - LEARN_RATE * (
        first_hat / (jnp.sqrt(second_hat) + EPSILON) + DECAY * weights
    )
    return (updated, new_first, new_second)


def width_slices(width):
    return [(at, min(LANES, width - at)) for at in range(0, width, LANES)]


def owner_lists(all_ids, groups, capacity, ent_rows):
    count = all_ids.shape[0]
    owners = all_ids // ent_rows
    local_rows = all_ids - owners * ent_rows
    chunk = 256
    mine = owners[None, :] == jnp.arange(groups, dtype=jnp.int32)[:, None]
    mine = mine.astype(BF16).reshape(groups, count // chunk, chunk)
    before = jnp.triu(jnp.ones((chunk, chunk), BF16), 1)
    inner = jnp.dot(mine, before, preferred_element_type=F32)
    sums = jnp.sum(mine.astype(F32), axis=2)
    carry = jnp.cumsum(sums, axis=1) - sums
    ranks = jnp.sum(mine.astype(F32) * (inner + carry[:, :, None]), axis=0)
    ranks = ranks.astype(jnp.int32).reshape(count)
    counts = jnp.sum(sums, axis=1).astype(jnp.int32)
    high = owners * (capacity // LANES) + ranks // LANES
    low = ranks % LANES
    tall = groups * capacity // LANES
    left = (jnp.arange(tall, dtype=jnp.int32)[:, None] == high[None, :]).astype(BF16)
    right = (jnp.arange(LANES, dtype=jnp.int32)[:, None] == low[None, :]).astype(BF16)
    places = jnp.arange(1, count + 1, dtype=jnp.int32)
    parts = jnp.stack([places // 256, places % 256, local_rows // 256, local_rows % 256])
    right = (parts.astype(BF16)[:, None, :] * right[None]).reshape(PARTS * LANES, count)
    found = lax.dot_general(left, right, NT, preferred_element_type=F32).astype(jnp.int32)
    found = found.reshape(tall, PARTS, LANES)
    place = found[:, 0] * 256 + found[:, 1]
    place_list = jnp.where(place > 0, place - 1, count).reshape(groups, capacity)
    row_list = jnp.where(place > 0, found[:, 2] * 256 + found[:, 3], ent_rows)
    return place_list, row_list.reshape(groups, capacity), counts


def relation_rows_kernel(slices, ids_ref, scale_ref, *refs):
    n = len(slices)
    tables, outs = refs[:n], refs[-2 * n - 1 : -n - 1]
    columns, rows = refs[-n - 1], refs[-n:]
    groups = tables[0].shape[0]
    for (_, depth), table, into in zip(slices, tables, rows):
        columns[...] = jnp.zeros_like(columns)

        def turn(group, carry):
            columns[:depth, :] = table[group, :depth].astype(F32)
            if depth < LANES:
                columns[LANES - 1 :, :] = scale_ref[pl.ds(group, 1), :]
            into[pl.ds(pl.multiple_of(group * REL_PAD, REL_PAD), REL_PAD), :] = columns[...].T
            return carry

        lax.fori_loop(0, groups, turn, 0, unroll=4)

    def body(step, carry):
        for lane in range(UNROLL):
            at = step * UNROLL + lane
            row = ids_ref[at]
            for source, out in zip(rows, outs):
                out[pl.ds(at, 1), :] = source[pl.ds(row, 1), :]
        return carry

    lax.fori_loop(0, outs[0].shape[0] // UNROLL, body, 0)


def relation_rows(places, dense, scale, slices, after):
    count = places.shape[0]
    groups, depth, span = dense.shape
    n = len(slices)
    first = span // REL_PAD - n

    def columns(k):
        return pl.BlockSpec((groups, depth, REL_PAD), lambda i: (0, 0, first + k))

    return pl.pallas_call(
        functools.partial(relation_rows_kernel, slices),
        out_shape=[jax.ShapeDtypeStruct((count, LANES), F32)] * n,
        grid=(1,),
        in_specs=[whole(SMEM), whole(VMEM)]
        + [columns(k) for k in range(n)]
        + [whole(pl.ANY)] * len(after),
        out_specs=[whole(VMEM)] * n,
        scratch_shapes=[pltpu.VMEM((LANES, REL_PAD), F32)]
        + [pltpu.VMEM((groups * REL_PAD, LANES), F32)] * n,
        compiler_params=params(28),
        cost_estimate=cost(0, 80e6),
        name="relation_rows",
    )(places, scale, *[dense] * n, *after)


def fetch_kernel(
    capacity, moves, ent_rows, counts_ref, place_ref, row_ref, dense_ref, *refs
):
    shard = pl.program_id(0)
    last = pl.num_programs(0) - 1
    out_ref, rows = refs[-3], refs[-2:]
    depth = dense_ref.shape[1]
    turns = ent_rows // TURN
    rest = ent_rows - turns * TURN

    if depth < LANES:

        @pl.when(shard == 0)
        def _():
            for ref in rows:
                ref[...] = jnp.zeros_like(ref)

    def turn(into, begin, size):
        cols = pl.ds(begin, size)
        into[cols, :depth] = dense_ref[0, :, cols].astype(F32).T

    def move(source, at):
        out_ref[pl.ds(place_ref[at], 1), :] = source[pl.ds(row_ref[at], 1), :]

    def step(into, source):
        base = (shard - 1) * capacity

        def remaining(first):
            def body(trip, carry):
                for lane in range(UNROLL):
                    move(source, base + first + trip * UNROLL + lane)
                return carry

            wanted = counts_ref[jnp.maximum(shard - 1, 0)] - first
            lax.fori_loop(0, (wanted + UNROLL - 1) // UNROLL, body, 0)

        def only_turn(trip, carry):
            turn(into, pl.multiple_of(trip * TURN, TURN), TURN)
            return carry

        def both(trip, carry):
            turn(into, pl.multiple_of(trip * TURN, TURN), TURN)
            for lane in range(moves):
                move(source, base + trip * moves + lane)
            return carry

        @pl.when(shard == 0)
        def _():
            lax.fori_loop(0, turns, only_turn, 0)

        @pl.when((shard > 0) & (shard < last))
        def _():
            lax.fori_loop(0, turns, both, 0)
            remaining(turns * moves)

        @pl.when(shard == last)
        def _():
            remaining(0)

        if rest:

            @pl.when(shard < last)
            def _():
                turn(into, turns * TURN, rest)

    for parity in range(2):

        @pl.when(lax.rem(shard, 2) == parity)
        def _():
            step(rows[parity], rows[1 - parity])


def fetch(counts, place_list, row_list, dense, id_count, ent_rows, after):
    groups, depth, _ = dense.shape
    capacity = place_list.shape[0] // groups
    moves = (id_count // groups) // (ent_rows // TURN) // UNROLL * UNROLL
    return pl.pallas_call(
        functools.partial(fetch_kernel, capacity, moves, ent_rows),
        out_shape=jax.ShapeDtypeStruct((id_count + 8, LANES), F32),
        grid=(groups + 1,),
        in_specs=[whole(SMEM)] * 3
        + [
            pl.BlockSpec(
                (1, depth, ent_rows), lambda shard: (jnp.minimum(shard, groups - 1), 0, 0)
            )
        ]
        + [whole(pl.ANY)] * len(after),
        out_specs=whole(VMEM),
        scratch_shapes=[pltpu.VMEM((ent_rows + 8, LANES), F32)] * 2,
        compiler_params=params(26),
        cost_estimate=cost(0, 170e6),
        name="fetch_rows",
    )(counts, place_list, row_list, dense, *after)


def column_sum(values):
    return jnp.sum(values * values, axis=0, keepdims=True)


def negatives_kernel(neg_ref, early_ref, late_ref, norm_ref):
    neg_t = neg_ref[...].T
    early_ref[...] = neg_t[:EARLY].astype(BF16)
    late_ref[...] = neg_t[EARLY:].astype(BF16)
    norm_ref[...] = column_sum(neg_t)


def negatives(fetched, blocks, block_len):
    count = blocks * block_len
    return pl.pallas_call(
        negatives_kernel,
        out_shape=[
            jax.ShapeDtypeStruct((EARLY, count), BF16),
            jax.ShapeDtypeStruct((LANES - EARLY, count), BF16),
            jax.ShapeDtypeStruct((1, count), F32),
        ],
        grid=(blocks,),
        in_specs=[pl.BlockSpec((block_len, LANES), lambda b: (2 * blocks + b, 0))],
        out_specs=[
            pl.BlockSpec((EARLY, block_len), lambda b: (0, b)),
            pl.BlockSpec((LANES - EARLY, block_len), lambda b: (0, b)),
            pl.BlockSpec((1, block_len), lambda b: (0, b)),
        ],
        compiler_params=params(5),
        cost_estimate=cost(0, 10e6),
        name="negatives",
    )(fetched)


def edge_parts(depth, head_ref, tail_ref, rel_ref, off_ref, tail_out):
    lane = lax.broadcasted_iota(jnp.int32, head_ref.shape, 1)
    inside = lane < depth
    rel = rel_ref[...]
    tail = tail_ref[...]
    shifted = head_ref[...] + jnp.where(inside, rel, 0.0)
    off_ref[...] = jnp.where(inside, shifted - tail, rel)
    tail_out[...] = tail.astype(BF16)
    shifted_t = shifted.T
    return shifted_t, column_sum((shifted - tail).T) - column_sum(shifted_t)


def edges_kernel(
    depth, head_ref, tail_ref, rel_ref, late_ref, off_ref, tail_out, low_ref, bias_ref
):
    shifted_t, bias = edge_parts(depth, head_ref, tail_ref, rel_ref, off_ref, tail_out)
    low_ref[:depth] = shifted_t[:depth].astype(BF16)
    low_ref[depth:] = late_ref[...]
    bias_ref[...] = bias


def edges(fetched, rel_rows, late, depth, blocks, block_len):
    count = blocks * block_len
    tall = depth + late.shape[0]

    def rows(at):
        return pl.BlockSpec((block_len, LANES), lambda b: (at * blocks + b, 0))

    return pl.pallas_call(
        functools.partial(edges_kernel, depth),
        out_shape=[
            jax.ShapeDtypeStruct((count, LANES), F32),
            jax.ShapeDtypeStruct((count, LANES), BF16),
            jax.ShapeDtypeStruct((tall, count), BF16),
            jax.ShapeDtypeStruct((1, count), F32),
        ],
        grid=(blocks,),
        in_specs=[rows(0), rows(1), rows(0)]
        + [pl.BlockSpec((tall - depth, block_len), lambda b: (0, b))],
        out_specs=[
            rows(0),
            rows(0),
            pl.BlockSpec((tall, block_len), lambda b: (0, b)),
            pl.BlockSpec((1, block_len), lambda b: (0, b)),
        ],
        compiler_params=params(9),
        cost_estimate=cost(0, 30e6),
        name="edges",
    )(fetched, fetched, rel_rows, late)


def last_rows(depth):
    return (depth + 7) // 8 * 8


def with_terms(columns, total, depth):
    terms = term_rows(total, 0)
    return jnp.concatenate([columns[: last_rows(depth)], terms], axis=0).astype(BF16)


def term_rows(total, first):
    place = lax.broadcasted_iota(jnp.int32, (8, total.shape[1]), 0)
    left = total
    terms = jnp.zeros(place.shape, F32)
    for k in range(TERMS):
        term = left.astype(BF16).astype(F32)
        left = left - term
        terms = jnp.where(place == first + k, term, terms)
    return terms


def last_kernel(depth, n_given, head_ref, tail_ref, neg_ref, rel_ref, *refs):
    biases, norms = refs[:n_given], refs[n_given : 2 * n_given]
    off_ref, tail_out, pair_ref, token = refs[-4:]
    token[...] = jnp.zeros_like(token)
    shifted_t, bias = edge_parts(depth, head_ref, tail_ref, rel_ref, off_ref, tail_out)
    neg_t = neg_ref[...].T
    norm = column_sum(neg_t)
    for ref in biases:
        bias = bias + ref[...]
    for ref in norms:
        norm = norm + ref[...]
    pair_ref[0] = with_terms(shifted_t, bias, depth)
    pair_ref[1] = with_terms(neg_t, norm, depth)


def last_slice(fetched, rel_rows, biases, norms, depth, blocks, block_len, half, after):
    part = blocks // HALVES
    count = part * block_len
    tall = last_rows(depth) + 8

    def rows(at):
        return pl.BlockSpec((block_len, LANES), lambda b: (at * blocks + half * part + b, 0))

    return pl.pallas_call(
        functools.partial(last_kernel, depth, len(biases)),
        out_shape=[
            jax.ShapeDtypeStruct((count, LANES), F32),
            jax.ShapeDtypeStruct((count, LANES), BF16),
            jax.ShapeDtypeStruct((2, tall, count), BF16),
            token_shape(),
        ],
        grid=(part,),
        in_specs=[rows(0), rows(1), rows(2), rows(0)]
        + [pl.BlockSpec((1, block_len), lambda b: (0, half * part + b))]
        * (len(biases) + len(norms))
        + [whole(pl.ANY)] * len(after),
        out_specs=[
            pl.BlockSpec((block_len, LANES), lambda b: (b, 0)),
            pl.BlockSpec((block_len, LANES), lambda b: (b, 0)),
            pl.BlockSpec((2, tall, block_len), lambda b: (0, 0, b)),
            pl.BlockSpec((8, LANES), lambda b: (0, 0)),
        ],
        compiler_params=params(9),
        cost_estimate=cost(0, 20e6),
        name="last_slice",
    )(fetched, fetched, fetched, rel_rows, *biases, *norms, *after)


def block_kernel(slices, n_col, half, me_ref, live_ref, *refs):
    n = len(slices)
    per_col = 2 * n - 1
    given = [refs[k * per_col : (k + 1) * per_col] for k in range(n_col)]
    refs = refs[n_col * per_col :]
    offs, tails, refs = refs[:n], refs[n : 2 * n], refs[2 * n :]
    grad, refs = refs[-9], refs[-8:]
    loss_ref, shift_scr, neg_scr, sums_scr, cross, slopes, row_bias, row_sum = refs
    block = pl.program_id(0)
    length = cross.shape[0]
    me = me_ref[0]
    for k in range(n_col):
        slot = lax.rem(me + (n_col - k), n_col)
        for m, (start, depth) in enumerate(slices):
            if m < n - 1:
                early, late = given[k][2 * m : 2 * m + 2]
                shift_scr[slot, start : start + depth, :] = 2.0 * late[:depth, :]
                neg_scr[slot, start : start + EARLY, :] = early[...]
                neg_scr[slot, start + EARLY : start + depth, :] = late[depth:, :]
            else:
                pair = given[k][-1]
                shift, neg = pair[0, :depth, :], pair[1, :depth, :]
                for row in range(2):
                    terms = pair[row, last_rows(depth) : last_rows(depth) + 8, :].astype(F32)
                    sums_scr[slot, row : row + 1] = jnp.sum(terms, axis=0, keepdims=True)
                shift_scr[slot, start : start + depth, :] = 2.0 * shift
                neg_scr[slot, start : start + depth, :] = neg
    bias = jnp.sum(sums_scr[:, 0, :], axis=0, keepdims=True) + MARGIN
    neg_norm = jnp.sum(sums_scr[:, 1, :], axis=0, keepdims=True)
    row_bias[...] = jnp.broadcast_to(bias, (LANES, length)).T

    live = live_ref[half * pl.num_programs(0) + block]
    tile = 256
    small = 128
    lane_tiles = [slice(at, at + LANES) for at in range(0, length, LANES)]
    cols = jnp.zeros((8, length), F32)
    loss = jnp.zeros((8, LANES), F32)
    def products(at):
        part = slice(at, at + tile)
        doubled = None
        for k in range(n_col):
            term = lax.dot_general(
                shift_scr[k, :, part], neg_scr[k], TN, preferred_element_type=F32
            )
            doubled = term if doubled is None else doubled + term
        cross[part, :] = doubled

    def moves(at):
        part = slice(at, at + tile)
        moved = lax.dot_general(slopes[part, :], neg_scr[me], NT, preferred_element_type=F32)
        fade = -row_sum[part, :]
        for m, (start, depth) in enumerate(slices):
            into = pl.ds(n * at + m, tile, stride=n)
            grad[0, into, :depth] = (
                fade[:, :depth] * tails[m][part, :depth].astype(F32)
                + moved[:, start : start + depth]
            )
            grad[1, into, :] = fade * offs[m][part, :]

    products(0)
    for begin in range(0, length, tile):
        if begin + tile < length:
            products(begin + tile)
        for at in range(begin, begin + tile, small):
            part = slice(at, at + small)
            place = at + lax.broadcasted_iota(jnp.int32, (small, 1), 0)
            scale = offs[-1][part, LANES - 1 : LANES]
            weight = jnp.where(place < live, scale, 0.0) / length
            margins = cross[part, :] + (row_bias[part, 0:1] - neg_norm)
            fall = jnp.exp(-jnp.abs(margins))
            under = 1.0 + fall
            guess = pl.reciprocal(under, approx=True)
            inverse = guess * (2.0 - under * guess)
            twice = (2.0 * weight) * (jnp.where(margins >= 0.0, 1.0, fall) * inverse)
            row_sum[part, :] = jnp.broadcast_to(
                jnp.sum(twice, axis=1, keepdims=True), (small, LANES)
            )
            slopes[part, :] = twice.astype(BF16)
            cols = cols + jnp.sum(twice.reshape(small // 8, 8, length), axis=0)
            over = jnp.maximum(margins, 0.0)
            lifts = [fall[:, lanes] for lanes in lane_tiles]
            while len(lifts) > 1:
                lifts = [a + b + a * b for a, b in zip(lifts[::2], lifts[1::2])]
            lift = lifts[0]
            soft = functools.reduce(jnp.add, [over[:, lanes] for lanes in lane_tiles]) + jnp.where(
                lift < 2.0**-11, lift * (1.0 - 0.5 * lift), jnp.log(1.0 + lift)
            )
            loss = loss + jnp.sum((weight * soft).reshape(small // 8, 8, LANES), axis=0)
        moves(begin)
    col_sum = jnp.sum(cols, axis=0, keepdims=True)

    @pl.when(block == 0)
    def _():
        loss_ref[...] = loss

    @pl.when(block > 0)
    def _():
        loss_ref[...] += loss

    moved = lax.dot_general(shift_scr[me], slopes[...], NN, preferred_element_type=F32)
    moved = 0.5 * moved - col_sum * neg_scr[me].astype(F32)
    for m, (start, depth) in enumerate(slices):
        grad[2, pl.ds(m, length, stride=n), :depth] = moved[start : start + depth, :].T


def block_math(me, live_counts, given, offs, tails, old, slices, block_len, half, after):
    n, n_col = len(slices), len(given)
    blocks = live_counts.shape[0]
    part = blocks // HALVES
    width = sum(depth for _, depth in slices)
    flat = [piece for per_col in given for piece in per_col]
    kept = [] if old is None else [old]

    def columns(piece):
        if piece.ndim == 3:
            return pl.BlockSpec((2, piece.shape[1], block_len), lambda b: (0, 0, b))
        return pl.BlockSpec((piece.shape[0], block_len), lambda b: (0, half * part + b))

    def rows(array):
        first = half * part if array.shape[0] > part * block_len else 0
        return pl.BlockSpec((block_len, LANES), lambda b: (first + b, 0))

    first_old = 2 + len(flat) + 2 * n
    return pl.pallas_call(
        functools.partial(block_kernel, slices, n_col, half),
        out_shape=[
            jax.ShapeDtypeStruct((3, n * blocks * block_len, LANES), F32),
            jax.ShapeDtypeStruct((8, LANES), F32),
        ],
        grid=(part,),
        in_specs=[whole(SMEM)] * 2
        + [columns(piece) for piece in flat]
        + [rows(array) for array in offs + tails]
        + [whole(pl.ANY)] * len(kept + after),
        out_specs=[
            pl.BlockSpec((3, n * block_len, LANES), lambda b: (0, half * part + b, 0)),
            pl.BlockSpec((8, LANES), lambda b: (0, 0)),
        ],
        input_output_aliases={first_old + k: k for k in range(len(kept))},
        scratch_shapes=[
            pltpu.VMEM((n_col, width, block_len), BF16),
            pltpu.VMEM((n_col, width, block_len), BF16),
            pltpu.VMEM((n_col, 2, block_len), F32),
            pltpu.VMEM((block_len, block_len), F32),
            pltpu.VMEM((block_len, block_len), BF16),
            pltpu.VMEM((block_len, LANES), F32),
            pltpu.VMEM((block_len, LANES), F32),
        ],
        compiler_params=params(60),
        cost_estimate=cost(part * 8 * block_len * block_len * width, 120e6),
        name="block_math",
    )(me, live_counts, *flat, *offs, *tails, *kept, *after)


def pair_of(row, n):
    return pl.ds(pl.multiple_of(row * n, n), n)


def pass_on_kernel(array_ref, *refs):
    refs[-1][...] = jnp.zeros((8, LANES), F32)


def pass_on(array, after):
    return pl.pallas_call(
        pass_on_kernel,
        out_shape=[jax.ShapeDtypeStruct(array.shape, array.dtype), token_shape()],
        in_specs=[whole(pl.ANY)] * (1 + len(after)),
        out_specs=[whole(pl.ANY), whole(VMEM)],
        input_output_aliases={0: 0},
        compiler_params=params(2),
        cost_estimate=cost(0, 1e3),
        name="pass_on",
    )(array, *after)[0]


def outgoing_kernel(slices, capacity, begin, counts_ref, place_ref, grad, *refs):
    n = len(slices)
    out_ref, token, tile = refs[-3:]
    groups, _, chunk = out_ref.shape
    token[...] = jnp.zeros_like(token)

    def owner(group, carry):
        wanted = jnp.clip(counts_ref[group] - begin, 0, chunk)

        def body(step, inner):
            for lane in range(UNROLL):
                at = step * UNROLL + lane
                place = place_ref[group * capacity + begin + at]
                tile[pair_of(at, n), :] = grad[pair_of(place, n), :]
            return inner

        lax.fori_loop(0, (wanted + UNROLL - 1) // UNROLL, body, 0)
        for m, (start, depth) in enumerate(slices):
            piece = tile[pl.ds(m, chunk, stride=n), :].T
            out_ref[group, start : start + depth, :] = piece[:depth].astype(BF16)
        return carry

    lax.fori_loop(0, groups, owner, 0)


def excess_kernel(slices, capacity, begin, counts_ref, place_ref, live_ref, grad, loss_ref, *refs):
    outgoing_kernel(slices, capacity, begin, counts_ref, place_ref, grad, *refs)
    out_ref = refs[-3]
    loss = jnp.sum(jnp.sum(loss_ref[...], axis=0, keepdims=True), axis=1, keepdims=True)
    live = live_ref[0]
    for block in range(1, live_ref.shape[0]):
        live = live + live_ref[block]
    count = jnp.full((1, LANES), live.astype(F32))
    terms = term_rows(jnp.broadcast_to(loss, (1, LANES)), 0) + term_rows(count, TERMS)
    width = sum(depth for _, depth in slices)
    for at in range(0, out_ref.shape[2], LANES):
        out_ref[0, last_rows(width) :, at : at + LANES] = terms.astype(BF16)


def excess_rows(count, places, live, grad, loss, slices, begin, chunk, after):
    n = len(slices)
    width = sum(depth for _, depth in slices)
    return pl.pallas_call(
        functools.partial(excess_kernel, slices, places.shape[1], begin),
        out_shape=[
            jax.ShapeDtypeStruct((1, last_rows(width) + SPARE, chunk), BF16),
            token_shape(),
        ],
        in_specs=[whole(SMEM)] * 3 + [whole(VMEM)] * 2 + [whole(pl.ANY)] * len(after),
        out_specs=[whole(VMEM)] * 2,
        scratch_shapes=[pltpu.VMEM((n * chunk, LANES), F32)],
        compiler_params=params(34),
        cost_estimate=cost(0, 80e6),
        name="excess_rows",
    )(count, places.reshape(-1), live, grad, loss, *after)


def outgoing(counts, place_list, grad, slices, begin, chunk, after, spare=0):
    groups, capacity = place_list.shape
    n = len(slices)
    width = sum(depth for _, depth in slices) + spare
    return pl.pallas_call(
        functools.partial(outgoing_kernel, slices, capacity, begin),
        out_shape=[jax.ShapeDtypeStruct((groups, width, chunk), BF16), token_shape()],
        in_specs=[whole(SMEM)] * 2 + [whole(VMEM)] + [whole(pl.ANY)] * len(after),
        out_specs=[whole(VMEM)] * 2,
        scratch_shapes=[pltpu.VMEM((n * chunk, LANES), F32)],
        compiler_params=params(34),
        cost_estimate=cost(0, 80e6),
        name="outgoing",
    )(counts, place_list.reshape(-1), grad, *after)


def collect_kernel(slices, capacity, begin, first, counts_ref, row_ref, came_ref, *refs):
    total, token, tile = refs[-3:]
    total[...] = jnp.zeros_like(total) if first else refs[0][...]
    token[...] = jnp.zeros_like(token)
    add_rows(slices, capacity, begin, counts_ref, row_ref, came_ref, total, tile)


def add_rows(slices, capacity, begin, counts_ref, row_ref, came_ref, total, tile):
    n = len(slices)
    groups, _, chunk = came_ref.shape

    def source(group, carry):
        wanted = jnp.clip(counts_ref[group] - begin, 0, chunk)

        @pl.when(wanted > 0)
        def _():
            for m, (start, depth) in enumerate(slices):
                piece = came_ref[group, start : start + depth, :].astype(F32)
                tile[pl.ds(m, chunk, stride=n), :depth] = piece.T

            def body(step, inner):
                for lane in range(UNROLL):
                    at = step * UNROLL + lane
                    into = pair_of(row_ref[group * capacity + begin + at], n)
                    total[into, :] = total[into, :] + tile[pair_of(at, n), :]
                return inner

            lax.fori_loop(0, (wanted + UNROLL - 1) // UNROLL, body, 0)

        return carry

    lax.fori_loop(0, groups, source, 0)


def collect(counts, row_list, came, total, slices, begin, ent_rows, after):
    capacity = row_list.shape[1]
    chunk = came.shape[2]
    n = len(slices)
    given = [] if total is None else [total]
    return pl.pallas_call(
        functools.partial(collect_kernel, slices, capacity, begin, total is None),
        out_shape=[jax.ShapeDtypeStruct((n * (ent_rows + 8), LANES), F32), token_shape()],
        input_output_aliases={3: 0} if given else {},
        in_specs=[whole(SMEM)] * 2
        + [whole(VMEM)] * (1 + len(given))
        + [whole(pl.ANY)] * len(after),
        out_specs=[whole(VMEM)] * 2,
        scratch_shapes=[pltpu.VMEM((n * chunk, LANES), F32)],
        compiler_params=params(26),
        cost_estimate=cost(0, 120e6),
        name="collect",
    )(counts, row_list.reshape(-1), came, *given, *after)


def relation_sums_kernel(n, ids_ref, grad, *refs):
    total, token = refs[-2:]
    total[...] = jnp.zeros_like(total)
    token[...] = jnp.zeros_like(token)

    def body(step, carry):
        for lane in range(UNROLL):
            at = step * UNROLL + lane
            into = pair_of(ids_ref[at], n)
            total[into, :] = total[into, :] + grad[0, pair_of(at, n), :]
        return carry

    lax.fori_loop(0, grad.shape[1] // n // UNROLL, body, 0)


def relation_sums(relation_ids, grad, n, rel_total, after):
    count = relation_ids.shape[0]
    return pl.pallas_call(
        functools.partial(relation_sums_kernel, n),
        out_shape=[jax.ShapeDtypeStruct((n * rel_total, LANES), F32), token_shape()],
        grid=(1,),
        in_specs=[whole(SMEM), pl.BlockSpec((1, n * count, LANES), lambda i: (0, 0, 0))]
        + [whole(pl.ANY)] * len(after),
        out_specs=[whole(VMEM)] * 2,
        compiler_params=params(30),
        cost_estimate=cost(0, 120e6),
        name="relation_sums",
    )(relation_ids, grad, *after)


def finish_kernel(
    slices,
    capacity,
    begin,
    last_begin,
    counts_ref,
    row_ref,
    came_ref,
    last_ref,
    total_ref,
    weights_ref,
    first_ref,
    second_ref,
    *refs,
):
    n = len(slices)
    width = sum(depth for _, depth in slices)
    outs, loss_ref, (total, tile, gradient) = refs[:3], refs[3], refs[4:]
    cols = weights_ref.shape[1]
    step = pl.program_id(0)

    @pl.when(step == 0)
    def _():
        total[: total_ref.shape[0], :] = total_ref[...]
        add_rows(slices, capacity, begin, counts_ref, row_ref, came_ref, total, tile)
        add_rows(slices, capacity, last_begin, counts_ref, row_ref, last_ref, total, tile)
        terms = jnp.zeros((SPARE, LANES), F32)
        for group in range(last_ref.shape[0]):
            terms = terms + last_ref[group, last_rows(width) :, :LANES].astype(F32)
        place = lax.broadcasted_iota(jnp.int32, terms.shape, 0)
        for k in range(2):
            own = (place >= k * TERMS) & (place < (k + 1) * TERMS)
            loss_ref[k : k + 1, :] = jnp.sum(jnp.where(own, terms, 0.0), axis=0, keepdims=True)
        loss_ref[2:, :] = jnp.zeros((6, LANES), F32)

    for m, (start, depth) in enumerate(slices):
        part = total[pl.ds(step * (n * cols) + m, cols, stride=n), :]
        gradient[start : start + depth, :] = part.T[:depth]
    grad = gradient[...]
    new_first = BETA_ONE * first_ref[...] + (1.0 - BETA_ONE) * grad
    new_second = BETA_TWO * second_ref[...] + (1.0 - BETA_TWO) * grad * grad
    under = jnp.sqrt(new_second * (1.0 / (1.0 - BETA_TWO**STEP))) + EPSILON
    guess = pl.reciprocal(under, approx=True)
    inverse = guess * (2.0 - under * guess)
    pace = LEARN_RATE / (1.0 - BETA_ONE**STEP)
    outs[0][...] = (1.0 - LEARN_RATE * DECAY) * weights_ref[...] - (pace * new_first) * inverse
    outs[1][...] = new_first
    outs[2][...] = new_second


def finish_entities(
    counts, row_list, came, last, total, begin, last_begin, weights, first, second, slices
):
    width, ent_rows = weights.shape
    capacity = row_list.shape[1]
    cols = 1024
    steps = pl.cdiv(ent_rows, cols)
    n = len(slices)
    table = pl.BlockSpec((width, cols), lambda i: (0, i))
    tall = max(n * cols * steps, total.shape[0])
    return pl.pallas_call(
        functools.partial(finish_kernel, slices, capacity, begin, last_begin),
        out_shape=[jax.ShapeDtypeStruct((width, ent_rows), F32)] * 3 + [token_shape()],
        grid=(steps,),
        in_specs=[whole(SMEM)] * 2 + [whole(VMEM)] * 3 + [table] * 3,
        out_specs=[table] * 3 + [pl.BlockSpec((8, LANES), lambda i: (0, 0))],
        scratch_shapes=[
            pltpu.VMEM((tall, LANES), F32),
            pltpu.VMEM((n * max(came.shape[2], last.shape[2]), LANES), F32),
            pltpu.VMEM((width, cols), F32),
        ],
        compiler_params=params(56),
        cost_estimate=cost(0, 60e6),
        name="finish_entities",
    )(counts, row_list.reshape(-1), came, last, total, weights, first, second)


def chunk_bounds(capacity):
    units = capacity // LANES
    sizes = [3, 7, 3, 3] if units == 16 else [units // 4] * 3 + [units - 3 * (units // 4)]
    bounds = [0]
    for size in sizes:
        bounds.append(bounds[-1] + size * LANES)
    return bounds


def shards(
    head_ids,
    relation_ids,
    tail_ids,
    negative_ids,
    live_counts,
    rel_weight,
    rel_count,
    entity_table,
    entity_first,
    entity_second,
    relation_table,
    relation_first,
    relation_second,
):
    groups = lax.axis_size("edge")
    n_col = lax.axis_size("col")
    width, ent_rows = entity_table.shape
    blocks, neg_count = negative_ids.shape
    block_len = head_ids.shape[0] // blocks
    edge_count = blocks * block_len
    slices = width_slices(width)
    n = len(slices)
    all_ids = jnp.concatenate([head_ids, tail_ids, negative_ids.reshape(-1)])
    id_count = all_ids.shape[0]
    capacity = (4 * id_count + 3 * groups - 1) // (3 * groups)
    rel_total = rel_weight.shape[0]

    rel_own = rel_total // groups
    rel_low = jnp.pad(relation_table.astype(BF16).T, ((0, 0), (0, REL_PAD - rel_own)))
    dense = []
    for k, (start, depth) in enumerate(slices):
        sent = entity_table[start : start + depth].astype(BF16)
        if k == 0:
            behind = [
                jnp.pad(rel_low[at : at + size], ((0, depth - size), (0, 0))) for at, size in slices
            ]
            sent = jnp.concatenate([sent] + behind, axis=1)
        dense.append(lax.all_gather(sent, "edge", axis=0, tiled=False))

    place_list, row_list, counts = owner_lists(all_ids, groups, capacity, ent_rows)
    safe_places = jnp.minimum(place_list, id_count - 1)
    place_flat, row_flat = place_list.reshape(-1), row_list.reshape(-1)

    rel_scale = rel_weight * (rel_total / jnp.sum(rel_weight)) / rel_count.astype(F32)
    rel_scale = jnp.pad(rel_scale.reshape(groups, rel_own), ((0, 0), (0, REL_PAD - rel_own)))
    rel_places = relation_ids + (relation_ids // rel_own) * (REL_PAD - rel_own)

    def from_others(array):
        turns = [[(c, (c + away) % n_col) for c in range(n_col)] for away in range(1, n_col)]
        return [lax.ppermute(array, "col", turn) for turn in turns]

    bounds = chunk_bounds(capacity)
    few = jnp.sum((counts > bounds[-2]).astype(jnp.int32)) <= 1
    flag = jnp.broadcast_to(few.astype(jnp.int32), (groups, LANES))
    me = lax.axis_index("col").astype(jnp.int32).reshape(1)
    given = [[[] for _ in range(n_col)] for _ in range(HALVES)]
    offs = [[] for _ in range(HALVES)]
    tails = [[] for _ in range(HALVES)]
    biases, norms, first_sent, rel_rows = [], [], [], None
    for k, (start, depth) in enumerate(slices):
        sent = first_sent if k > 0 else [flag]
        fetched = fetch(counts, place_flat, row_flat, dense[k], id_count, ent_rows, sent)
        if k < n - 1:
            early, late, norm = negatives(fetched, blocks, block_len)
            early_all = [early] + from_others(early)
            if rel_rows is None:
                rel_rows = relation_rows(rel_places, dense[0], rel_scale, slices, [norm])
            off, tail, low, bias = edges(fetched, rel_rows[k], late, depth, blocks, block_len)
            low_all = [low] + from_others(low)
            first_sent = [corner(piece) for piece in early_all[1:]]
            biases.append(bias)
            norms.append(norm)
            for half in range(HALVES):
                offs[half].append(off)
                tails[half].append(tail)
                for col in range(n_col):
                    given[half][col] += [early_all[col], low_all[col]]
            continue
        if rel_rows is None:
            rel_rows = relation_rows(rel_places, dense[0], rel_scale, slices, [])

    def finish(half, after):
        off, tail, pair, token = last_slice(
            fetched, rel_rows[-1], biases, norms, slices[-1][1], blocks, block_len, half, after
        )
        offs[half].append(off)
        tails[half].append(tail)
        for col, piece in enumerate([pair] + from_others(pair)):
            given[half][col].append(piece)
        return token

    grad, loss_tiles = None, []
    half_token = []
    for half in range(HALVES):
        half_token = [finish(half, half_token)]
    flag = flag + half_token[0][0, 0].astype(jnp.int32)
    asked = lax.all_to_all(
        jnp.concatenate([row_list, flag], axis=1), "edge", split_axis=0, concat_axis=0, tiled=True
    )
    all_few = jnp.min(asked[:, capacity]) > 0
    asked = asked[:, :capacity]
    asked_counts = jnp.sum((asked < ent_rows).astype(jnp.int32), axis=1)
    for half in range(HALVES):
        after = [corner(asked)] if half == 0 else []
        grad, loss_tile = block_math(
            me,
            live_counts,
            given[half],
            offs[half],
            tails[half],
            grad,
            slices,
            block_len,
            half,
            after,
        )
        loss_tiles.append(loss_tile)
    live = jnp.minimum(live_counts, block_len)
    loss_tile = functools.reduce(jnp.add, loss_tiles)

    flat = grad.reshape(n * id_count, LANES)
    chunks = len(bounds) - 1
    begin, size = bounds[-2], bounds[-1] - bounds[-2]
    most = jnp.argmax(counts)
    most_places = lax.dynamic_slice_in_dim(safe_places, most, 1, axis=0)
    most_count = lax.dynamic_slice_in_dim(counts, most, 1, axis=0)
    arrived, total, after = [], None, []
    for k in range(chunks - 1):
        sent, sent_token = outgoing(
            counts, safe_places, flat, slices, bounds[k], bounds[k + 1] - bounds[k], after
        )
        if k == chunks - 2:
            sent = pass_on(sent, [corner(relation_grad)])
        arrived.append(lax.all_to_all(sent, "edge", split_axis=0, concat_axis=0, tiled=True))
        after = []
        if k == 0:
            excess, excess_token = excess_rows(
                most_count,
                most_places,
                live,
                flat,
                loss_tile,
                slices,
                begin,
                size,
                [sent_token],
            )
            after = [excess_token]
        if k == 1:
            before = [corner(arrived[0]), excess_token, sent_token]
            rel_terms, token = relation_sums(relation_ids, grad, n, rel_total, before)
            after = [token]
            rel_terms = rel_terms.reshape(rel_total, n * LANES)[:, :width]
            relation_grad = lax.psum_scatter(rel_terms, "edge", scatter_dimension=0, tiled=True)
        if k == 2:
            ready = (relation_grad[0, 0] == relation_grad[0, 0]) & (sent_token[0, 0] == 0.0)
            excess = jnp.where(ready, excess, jnp.zeros_like(excess))
            gathered = lax.all_gather(excess, "edge", axis=0, tiled=True)
            after = [corner(relation_grad)]
        if k > 0:
            total, token = collect(
                asked_counts, asked, arrived[k - 1], total, slices, bounds[k - 1], ent_rows, after
            )
            after = [token]

    def by_all_to_all():
        spare = last_rows(width) + SPARE - width
        sent, _ = outgoing(counts, safe_places, flat, slices, begin, size, [], spare)
        rows = lax.all_to_all(sent, "edge", split_axis=0, concat_axis=0, tiled=True)
        return rows.at[:, last_rows(width) :].set(gathered[:, last_rows(width) :])

    k = chunks - 2
    here = jnp.where(arrived[k][0, 0, 0] > 0, 1, 2) > 0
    came = lax.cond(all_few & here & (token[0, 0] == 0.0), lambda: gathered, by_all_to_all)
    new_entity, new_entity_first, new_entity_second, sums = finish_entities(
        asked_counts,
        asked,
        arrived[k],
        came,
        total,
        bounds[k],
        begin,
        entity_table,
        entity_first,
        entity_second,
        slices,
    )
    loss_pair = sums[:2, 0]
    new_relation, new_relation_first, new_relation_second = adamw_update(
        relation_table, relation_grad, relation_first, relation_second
    )
    return (
        loss_pair,
        new_entity,
        new_entity_first,
        new_entity_second,
        new_relation,
        new_relation_first,
        new_relation_second,
    )


def solution(mesh):
    placed = (
        P("edge"),
        P("edge"),
        P("edge"),
        P("edge", None),
        P("edge"),
        P(),
        P(),
        P("col", "edge"),
        P("col", "edge"),
        P("col", "edge"),
        P("edge", "col"),
        P("edge", "col"),
        P("edge", "col"),
    )
    return jax.shard_map(
        shards,
        mesh=mesh,
        in_specs=placed,
        out_specs=(
            P(),
            P("col", "edge"),
            P("col", "edge"),
            P("col", "edge"),
            P("edge", "col"),
            P("edge", "col"),
            P("edge", "col"),
        ),
        check_vma=False,
    )
```

```python
import functools

import jax
import jax.numpy as jnp
from jax import lax
from jax.experimental import pallas as pl
from jax.experimental.pallas import tpu as pltpu
from jax.sharding import PartitionSpec as P

STEP = 5


MARGIN = 0.1
LEARN_RATE = 0.1
BETA_ONE = 0.5
BETA_TWO = 0.5
EPSILON = 1e-08
DECAY = 0.01
LANES = 128
UNROLL = 8
PARTS = 4
HALVES = 2
EARLY = 96
TURN = 512
REL_PAD = 256
TERMS = 3
SPARE = 8
NN = (((1,), (0,)), ((), ()))
NT = (((1,), (1,)), ((), ()))
TN = (((0,), (0,)), ((), ()))
F32 = jnp.float32
BF16 = jnp.bfloat16
SMEM = pltpu.SMEM
VMEM = pltpu.VMEM


def params(mebibytes=60):
    return pltpu.CompilerParams(vmem_limit_bytes=mebibytes << 20)


def cost(flops, moved):
    return pl.CostEstimate(flops=int(flops), bytes_accessed=int(moved), transcendentals=0)


def corner(array):
    return array[(0,) * (array.ndim - 2) + (slice(0, 8), slice(0, LANES))]


def token_shape():
    return jax.ShapeDtypeStruct((8, LANES), F32)


def whole(space):
    return pl.BlockSpec(memory_space=space)


def adamw_update(weights, gradient, first, second):
    new_first = BETA_ONE * first + (1.0 - BETA_ONE) * gradient
    new_second = BETA_TWO * second + (1.0 - BETA_TWO) * gradient * gradient
    first_hat = new_first / (1.0 - BETA_ONE**STEP)
    second_hat = new_second / (1.0 - BETA_TWO**STEP)
    updated = weights - LEARN_RATE * (
        first_hat / (jnp.sqrt(second_hat) + EPSILON) + DECAY * weights
    )
    return (updated, new_first, new_second)


def width_slices(width):
    return [(at, min(LANES, width - at)) for at in range(0, width, LANES)]


def owner_lists(all_ids, groups, capacity, ent_rows):
    count = all_ids.shape[0]
    owners = all_ids // ent_rows
    local_rows = all_ids - owners * ent_rows
    chunk = 256
    mine = owners[None, :] == jnp.arange(groups, dtype=jnp.int32)[:, None]
    mine = mine.astype(BF16).reshape(groups, count // chunk, chunk)
    before = jnp.triu(jnp.ones((chunk, chunk), BF16), 1)
    inner = jnp.dot(mine, before, preferred_element_type=F32)
    sums = jnp.sum(mine.astype(F32), axis=2)
    carry = jnp.cumsum(sums, axis=1) - sums
    ranks = jnp.sum(mine.astype(F32) * (inner + carry[:, :, None]), axis=0)
    ranks = ranks.astype(jnp.int32).reshape(count)
    counts = jnp.sum(sums, axis=1).astype(jnp.int32)
    high = owners * (capacity // LANES) + ranks // LANES
    low = ranks % LANES
    tall = groups * capacity // LANES
    left = (jnp.arange(tall, dtype=jnp.int32)[:, None] == high[None, :]).astype(BF16)
    right = (jnp.arange(LANES, dtype=jnp.int32)[:, None] == low[None, :]).astype(BF16)
    places = jnp.arange(1, count + 1, dtype=jnp.int32)
    parts = jnp.stack([places // 256, places % 256, local_rows // 256, local_rows % 256])
    right = (parts.astype(BF16)[:, None, :] * right[None]).reshape(PARTS * LANES, count)
    found = lax.dot_general(left, right, NT, preferred_element_type=F32).astype(jnp.int32)
    found = found.reshape(tall, PARTS, LANES)
    place = found[:, 0] * 256 + found[:, 1]
    place_list = jnp.where(place > 0, place - 1, count).reshape(groups, capacity)
    row_list = jnp.where(place > 0, found[:, 2] * 256 + found[:, 3], ent_rows)
    return place_list, row_list.reshape(groups, capacity), counts


def relation_rows_kernel(slices, ids_ref, scale_ref, *refs):
    n = len(slices)
    tables, outs = refs[:n], refs[-2 * n - 1 : -n - 1]
    columns, rows = refs[-n - 1], refs[-n:]
    groups = tables[0].shape[0]
    for (_, depth), table, into in zip(slices, tables, rows):
        columns[...] = jnp.zeros_like(columns)

        def turn(group, carry):
            columns[:depth, :] = table[group, :depth].astype(F32)
            if depth < LANES:
                columns[LANES - 1 :, :] = scale_ref[pl.ds(group, 1), :]
            into[pl.ds(pl.multiple_of(group * REL_PAD, REL_PAD), REL_PAD), :] = columns[...].T
            return carry

        lax.fori_loop(0, groups, turn, 0, unroll=4)

    def body(step, carry):
        for lane in range(UNROLL):
            at = step * UNROLL + lane
            row = ids_ref[at]
            for source, out in zip(rows, outs):
                out[pl.ds(at, 1), :] = source[pl.ds(row, 1), :]
        return carry

    lax.fori_loop(0, outs[0].shape[0] // UNROLL, body, 0)


def relation_rows(places, dense, scale, slices, after):
    count = places.shape[0]
    groups, depth, span = dense.shape
    n = len(slices)
    first = span // REL_PAD - n

    def columns(k):
        return pl.BlockSpec((groups, depth, REL_PAD), lambda i: (0, 0, first + k))

    return pl.pallas_call(
        functools.partial(relation_rows_kernel, slices),
        out_shape=[jax.ShapeDtypeStruct((count, LANES), F32)] * n,
        grid=(1,),
        in_specs=[whole(SMEM), whole(VMEM)]
        + [columns(k) for k in range(n)]
        + [whole(pl.ANY)] * len(after),
        out_specs=[whole(VMEM)] * n,
        scratch_shapes=[pltpu.VMEM((LANES, REL_PAD), F32)]
        + [pltpu.VMEM((groups * REL_PAD, LANES), F32)] * n,
        compiler_params=params(28),
        cost_estimate=cost(0, 80e6),
        name="relation_rows",
    )(places, scale, *[dense] * n, *after)


def fetch_kernel(
    capacity, moves, ent_rows, counts_ref, place_ref, row_ref, dense_ref, *refs
):
    shard = pl.program_id(0)
    last = pl.num_programs(0) - 1
    out_ref, rows = refs[-3], refs[-2:]
    depth = dense_ref.shape[1]
    turns = ent_rows // TURN
    rest = ent_rows - turns * TURN

    if depth < LANES:

        @pl.when(shard == 0)
        def _():
            for ref in rows:
                ref[...] = jnp.zeros_like(ref)

    def turn(into, begin, size):
        cols = pl.ds(begin, size)
        into[cols, :depth] = dense_ref[0, :, cols].astype(F32).T

    def move(source, at):
        out_ref[pl.ds(place_ref[at], 1), :] = source[pl.ds(row_ref[at], 1), :]

    def step(into, source):
        base = (shard - 1) * capacity

        def remaining(first):
            def body(trip, carry):
                for lane in range(UNROLL):
                    move(source, base + first + trip * UNROLL + lane)
                return carry

            wanted = counts_ref[jnp.maximum(shard - 1, 0)] - first
            lax.fori_loop(0, (wanted + UNROLL - 1) // UNROLL, body, 0)

        def only_turn(trip, carry):
            turn(into, pl.multiple_of(trip * TURN, TURN), TURN)
            return carry

        def both(trip, carry):
            turn(into, pl.multiple_of(trip * TURN, TURN), TURN)
            for lane in range(moves):
                move(source, base + trip * moves + lane)
            return carry

        @pl.when(shard == 0)
        def _():
            lax.fori_loop(0, turns, only_turn, 0)

        @pl.when((shard > 0) & (shard < last))
        def _():
            lax.fori_loop(0, turns, both, 0)
            remaining(turns * moves)

        @pl.when(shard == last)
        def _():
            remaining(0)

        if rest:

            @pl.when(shard < last)
            def _():
                turn(into, turns * TURN, rest)

    for parity in range(2):

        @pl.when(lax.rem(shard, 2) == parity)
        def _():
            step(rows[parity], rows[1 - parity])


def fetch(counts, place_list, row_list, dense, id_count, ent_rows, after):
    groups, depth, _ = dense.shape
    capacity = place_list.shape[0] // groups
    moves = (id_count // groups) // (ent_rows // TURN) // UNROLL * UNROLL
    return pl.pallas_call(
        functools.partial(fetch_kernel, capacity, moves, ent_rows),
        out_shape=jax.ShapeDtypeStruct((id_count + 8, LANES), F32),
        grid=(groups + 1,),
        in_specs=[whole(SMEM)] * 3
        + [
            pl.BlockSpec(
                (1, depth, ent_rows), lambda shard: (jnp.minimum(shard, groups - 1), 0, 0)
            )
        ]
        + [whole(pl.ANY)] * len(after),
        out_specs=whole(VMEM),
        scratch_shapes=[pltpu.VMEM((ent_rows + 8, LANES), F32)] * 2,
        compiler_params=params(26),
        cost_estimate=cost(0, 170e6),
        name="fetch_rows",
    )(counts, place_list, row_list, dense, *after)


def column_sum(values):
    return jnp.sum(values * values, axis=0, keepdims=True)


def negatives_kernel(neg_ref, early_ref, late_ref, norm_ref):
    neg_t = neg_ref[...].T
    early_ref[...] = neg_t[:EARLY].astype(BF16)
    late_ref[...] = neg_t[EARLY:].astype(BF16)
    norm_ref[...] = column_sum(neg_t)


def negatives(fetched, blocks, block_len):
    count = blocks * block_len
    return pl.pallas_call(
        negatives_kernel,
        out_shape=[
            jax.ShapeDtypeStruct((EARLY, count), BF16),
            jax.ShapeDtypeStruct((LANES - EARLY, count), BF16),
            jax.ShapeDtypeStruct((1, count), F32),
        ],
        grid=(blocks,),
        in_specs=[pl.BlockSpec((block_len, LANES), lambda b: (2 * blocks + b, 0))],
        out_specs=[
            pl.BlockSpec((EARLY, block_len), lambda b: (0, b)),
            pl.BlockSpec((LANES - EARLY, block_len), lambda b: (0, b)),
            pl.BlockSpec((1, block_len), lambda b: (0, b)),
        ],
        compiler_params=params(5),
        cost_estimate=cost(0, 10e6),
        name="negatives",
    )(fetched)


def edge_parts(depth, head_ref, tail_ref, rel_ref, off_ref, tail_out):
    lane = lax.broadcasted_iota(jnp.int32, head_ref.shape, 1)
    inside = lane < depth
    rel = rel_ref[...]
    tail = tail_ref[...]
    shifted = head_ref[...] + jnp.where(inside, rel, 0.0)
    off_ref[...] = jnp.where(inside, shifted - tail, rel)
    tail_out[...] = tail.astype(BF16)
    shifted_t = shifted.T
    return shifted_t, column_sum((shifted - tail).T) - column_sum(shifted_t)


def edges_kernel(
    depth, head_ref, tail_ref, rel_ref, late_ref, off_ref, tail_out, low_ref, bias_ref
):
    shifted_t, bias = edge_parts(depth, head_ref, tail_ref, rel_ref, off_ref, tail_out)
    low_ref[:depth] = shifted_t[:depth].astype(BF16)
    low_ref[depth:] = late_ref[...]
    bias_ref[...] = bias


def edges(fetched, rel_rows, late, depth, blocks, block_len):
    count = blocks * block_len
    tall = depth + late.shape[0]

    def rows(at):
        return pl.BlockSpec((block_len, LANES), lambda b: (at * blocks + b, 0))

    return pl.pallas_call(
        functools.partial(edges_kernel, depth),
        out_shape=[
            jax.ShapeDtypeStruct((count, LANES), F32),
            jax.ShapeDtypeStruct((count, LANES), BF16),
            jax.ShapeDtypeStruct((tall, count), BF16),
            jax.ShapeDtypeStruct((1, count), F32),
        ],
        grid=(blocks,),
        in_specs=[rows(0), rows(1), rows(0)]
        + [pl.BlockSpec((tall - depth, block_len), lambda b: (0, b))],
        out_specs=[
            rows(0),
            rows(0),
            pl.BlockSpec((tall, block_len), lambda b: (0, b)),
            pl.BlockSpec((1, block_len), lambda b: (0, b)),
        ],
        compiler_params=params(9),
        cost_estimate=cost(0, 30e6),
        name="edges",
    )(fetched, fetched, rel_rows, late)


def last_rows(depth):
    return (depth + 7) // 8 * 8


def with_terms(columns, total, depth):
    terms = term_rows(total, 0)
    return jnp.concatenate([columns[: last_rows(depth)], terms], axis=0).astype(BF16)


def term_rows(total, first):
    place = lax.broadcasted_iota(jnp.int32, (8, total.shape[1]), 0)
    left = total
    terms = jnp.zeros(place.shape, F32)
    for k in range(TERMS):
        term = left.astype(BF16).astype(F32)
        left = left - term
        terms = jnp.where(place == first + k, term, terms)
    return terms


def last_kernel(depth, n_given, head_ref, tail_ref, neg_ref, rel_ref, *refs):
    biases, norms = refs[:n_given], refs[n_given : 2 * n_given]
    off_ref, tail_out, pair_ref, token = refs[-4:]
    token[...] = jnp.zeros_like(token)
    shifted_t, bias = edge_parts(depth, head_ref, tail_ref, rel_ref, off_ref, tail_out)
    neg_t = neg_ref[...].T
    norm = column_sum(neg_t)
    for ref in biases:
        bias = bias + ref[...]
    for ref in norms:
        norm = norm + ref[...]
    pair_ref[0] = with_terms(shifted_t, bias, depth)
    pair_ref[1] = with_terms(neg_t, norm, depth)


def last_slice(fetched, rel_rows, biases, norms, depth, blocks, block_len, half, after):
    part = blocks // HALVES
    count = part * block_len
    tall = last_rows(depth) + 8

    def rows(at):
        return pl.BlockSpec((block_len, LANES), lambda b: (at * blocks + half * part + b, 0))

    return pl.pallas_call(
        functools.partial(last_kernel, depth, len(biases)),
        out_shape=[
            jax.ShapeDtypeStruct((count, LANES), F32),
            jax.ShapeDtypeStruct((count, LANES), BF16),
            jax.ShapeDtypeStruct((2, tall, count), BF16),
            token_shape(),
        ],
        grid=(part,),
        in_specs=[rows(0), rows(1), rows(2), rows(0)]
        + [pl.BlockSpec((1, block_len), lambda b: (0, half * part + b))]
        * (len(biases) + len(norms))
        + [whole(pl.ANY)] * len(after),
        out_specs=[
            pl.BlockSpec((block_len, LANES), lambda b: (b, 0)),
            pl.BlockSpec((block_len, LANES), lambda b: (b, 0)),
            pl.BlockSpec((2, tall, block_len), lambda b: (0, 0, b)),
            pl.BlockSpec((8, LANES), lambda b: (0, 0)),
        ],
        compiler_params=params(9),
        cost_estimate=cost(0, 20e6),
        name="last_slice",
    )(fetched, fetched, fetched, rel_rows, *biases, *norms, *after)


def block_kernel(slices, n_col, half, me_ref, live_ref, *refs):
    n = len(slices)
    per_col = 2 * n - 1
    given = [refs[k * per_col : (k + 1) * per_col] for k in range(n_col)]
    refs = refs[n_col * per_col :]
    offs, tails, refs = refs[:n], refs[n : 2 * n], refs[2 * n :]
    grad, refs = refs[-9], refs[-8:]
    loss_ref, shift_scr, neg_scr, sums_scr, cross, slopes, row_bias, row_sum = refs
    block = pl.program_id(0)
    length = cross.shape[0]
    me = me_ref[0]
    for k in range(n_col):
        slot = lax.rem(me + (n_col - k), n_col)
        for m, (start, depth) in enumerate(slices):
            if m < n - 1:
                early, late = given[k][2 * m : 2 * m + 2]
                shift_scr[slot, start : start + depth, :] = 2.0 * late[:depth, :]
                neg_scr[slot, start : start + EARLY, :] = early[...]
                neg_scr[slot, start + EARLY : start + depth, :] = late[depth:, :]
            else:
                pair = given[k][-1]
                shift, neg = pair[0, :depth, :], pair[1, :depth, :]
                for row in range(2):
                    terms = pair[row, last_rows(depth) : last_rows(depth) + 8, :].astype(F32)
                    sums_scr[slot, row : row + 1] = jnp.sum(terms, axis=0, keepdims=True)
                shift_scr[slot, start : start + depth, :] = 2.0 * shift
                neg_scr[slot, start : start + depth, :] = neg
    bias = jnp.sum(sums_scr[:, 0, :], axis=0, keepdims=True) + MARGIN
    neg_norm = jnp.sum(sums_scr[:, 1, :], axis=0, keepdims=True)
    row_bias[...] = jnp.broadcast_to(bias, (LANES, length)).T

    live = live_ref[half * pl.num_programs(0) + block]
    tile = 256
    small = 128
    lane_tiles = [slice(at, at + LANES) for at in range(0, length, LANES)]
    cols = jnp.zeros((8, length), F32)
    loss = jnp.zeros((8, LANES), F32)
    def products(at):
        part = slice(at, at + tile)
        doubled = None
        for k in range(n_col):
            term = lax.dot_general(
                shift_scr[k, :, part], neg_scr[k], TN, preferred_element_type=F32
            )
            doubled = term if doubled is None else doubled + term
        cross[part, :] = doubled

    def moves(at):
        part = slice(at, at + tile)
        moved = lax.dot_general(slopes[part, :], neg_scr[me], NT, preferred_element_type=F32)
        fade = -row_sum[part, :]
        for m, (start, depth) in enumerate(slices):
            into = pl.ds(n * at + m, tile, stride=n)
            grad[0, into, :depth] = (
                fade[:, :depth] * tails[m][part, :depth].astype(F32)
                + moved[:, start : start + depth]
            )
            grad[1, into, :] = fade * offs[m][part, :]

    products(0)
    for begin in range(0, length, tile):
        if begin + tile < length:
            products(begin + tile)
        for at in range(begin, begin + tile, small):
            part = slice(at, at + small)
            place = at + lax.broadcasted_iota(jnp.int32, (small, 1), 0)
            scale = offs[-1][part, LANES - 1 : LANES]
            weight = jnp.where(place < live, scale, 0.0) / length
            margins = cross[part, :] + (row_bias[part, 0:1] - neg_norm)
            fall = jnp.exp(-jnp.abs(margins))
            under = 1.0 + fall
            guess = pl.reciprocal(under, approx=True)
            inverse = guess * (2.0 - under * guess)
            twice = (2.0 * weight) * (jnp.where(margins >= 0.0, 1.0, fall) * inverse)
            row_sum[part, :] = jnp.broadcast_to(
                jnp.sum(twice, axis=1, keepdims=True), (small, LANES)
            )
            slopes[part, :] = twice.astype(BF16)
            cols = cols + jnp.sum(twice.reshape(small // 8, 8, length), axis=0)
            over = jnp.maximum(margins, 0.0)
            lifts = [fall[:, lanes] for lanes in lane_tiles]
            while len(lifts) > 1:
                lifts = [a + b + a * b for a, b in zip(lifts[::2], lifts[1::2])]
            lift = lifts[0]
            soft = functools.reduce(jnp.add, [over[:, lanes] for lanes in lane_tiles]) + jnp.where(
                lift < 2.0**-11, lift * (1.0 - 0.5 * lift), jnp.log(1.0 + lift)
            )
            loss = loss + jnp.sum((weight * soft).reshape(small // 8, 8, LANES), axis=0)
        moves(begin)
    col_sum = jnp.sum(cols, axis=0, keepdims=True)

    @pl.when(block == 0)
    def _():
        loss_ref[...] = loss

    @pl.when(block > 0)
    def _():
        loss_ref[...] += loss

    moved = lax.dot_general(shift_scr[me], slopes[...], NN, preferred_element_type=F32)
    moved = 0.5 * moved - col_sum * neg_scr[me].astype(F32)
    for m, (start, depth) in enumerate(slices):
        grad[2, pl.ds(m, length, stride=n), :depth] = moved[start : start + depth, :].T


def block_math(me, live_counts, given, offs, tails, old, slices, block_len, half, after):
    n, n_col = len(slices), len(given)
    blocks = live_counts.shape[0]
    part = blocks // HALVES
    width = sum(depth for _, depth in slices)
    flat = [piece for per_col in given for piece in per_col]
    kept = [] if old is None else [old]

    def columns(piece):
        if piece.ndim == 3:
            return pl.BlockSpec((2, piece.shape[1], block_len), lambda b: (0, 0, b))
        return pl.BlockSpec((piece.shape[0], block_len), lambda b: (0, half * part + b))

    def rows(array):
        first = half * part if array.shape[0] > part * block_len else 0
        return pl.BlockSpec((block_len, LANES), lambda b: (first + b, 0))

    first_old = 2 + len(flat) + 2 * n
    return pl.pallas_call(
        functools.partial(block_kernel, slices, n_col, half),
        out_shape=[
            jax.ShapeDtypeStruct((3, n * blocks * block_len, LANES), F32),
            jax.ShapeDtypeStruct((8, LANES), F32),
        ],
        grid=(part,),
        in_specs=[whole(SMEM)] * 2
        + [columns(piece) for piece in flat]
        + [rows(array) for array in offs + tails]
        + [whole(pl.ANY)] * len(kept + after),
        out_specs=[
            pl.BlockSpec((3, n * block_len, LANES), lambda b: (0, half * part + b, 0)),
            pl.BlockSpec((8, LANES), lambda b: (0, 0)),
        ],
        input_output_aliases={first_old + k: k for k in range(len(kept))},
        scratch_shapes=[
            pltpu.VMEM((n_col, width, block_len), BF16),
            pltpu.VMEM((n_col, width, block_len), BF16),
            pltpu.VMEM((n_col, 2, block_len), F32),
            pltpu.VMEM((block_len, block_len), F32),
            pltpu.VMEM((block_len, block_len), BF16),
            pltpu.VMEM((block_len, LANES), F32),
            pltpu.VMEM((block_len, LANES), F32),
        ],
        compiler_params=params(60),
        cost_estimate=cost(part * 8 * block_len * block_len * width, 120e6),
        name="block_math",
    )(me, live_counts, *flat, *offs, *tails, *kept, *after)


def pair_of(row, n):
    return pl.ds(pl.multiple_of(row * n, n), n)


def pass_on_kernel(array_ref, *refs):
    refs[-1][...] = jnp.zeros((8, LANES), F32)


def pass_on(array, after):
    return pl.pallas_call(
        pass_on_kernel,
        out_shape=[jax.ShapeDtypeStruct(array.shape, array.dtype), token_shape()],
        in_specs=[whole(pl.ANY)] * (1 + len(after)),
        out_specs=[whole(pl.ANY), whole(VMEM)],
        input_output_aliases={0: 0},
        compiler_params=params(2),
        cost_estimate=cost(0, 1e3),
        name="pass_on",
    )(array, *after)[0]


def outgoing_kernel(slices, capacity, begin, counts_ref, place_ref, grad, *refs):
    n = len(slices)
    out_ref, token, tile = refs[-3:]
    groups, _, chunk = out_ref.shape
    token[...] = jnp.zeros_like(token)

    def owner(group, carry):
        wanted = jnp.clip(counts_ref[group] - begin, 0, chunk)

        def body(step, inner):
            for lane in range(UNROLL):
                at = step * UNROLL + lane
                place = place_ref[group * capacity + begin + at]
                tile[pair_of(at, n), :] = grad[pair_of(place, n), :]
            return inner

        lax.fori_loop(0, (wanted + UNROLL - 1) // UNROLL, body, 0)
        for m, (start, depth) in enumerate(slices):
            piece = tile[pl.ds(m, chunk, stride=n), :].T
            out_ref[group, start : start + depth, :] = piece[:depth].astype(BF16)
        return carry

    lax.fori_loop(0, groups, owner, 0)


def excess_kernel(slices, capacity, begin, counts_ref, place_ref, live_ref, grad, loss_ref, *refs):
    outgoing_kernel(slices, capacity, begin, counts_ref, place_ref, grad, *refs)
    out_ref = refs[-3]
    loss = jnp.sum(jnp.sum(loss_ref[...], axis=0, keepdims=True), axis=1, keepdims=True)
    live = live_ref[0]
    for block in range(1, live_ref.shape[0]):
        live = live + live_ref[block]
    count = jnp.full((1, LANES), live.astype(F32))
    terms = term_rows(jnp.broadcast_to(loss, (1, LANES)), 0) + term_rows(count, TERMS)
    width = sum(depth for _, depth in slices)
    for at in range(0, out_ref.shape[2], LANES):
        out_ref[0, last_rows(width) :, at : at + LANES] = terms.astype(BF16)


def excess_rows(count, places, live, grad, loss, slices, begin, chunk, after):
    n = len(slices)
    width = sum(depth for _, depth in slices)
    return pl.pallas_call(
        functools.partial(excess_kernel, slices, places.shape[1], begin),
        out_shape=[
            jax.ShapeDtypeStruct((1, last_rows(width) + SPARE, chunk), BF16),
            token_shape(),
        ],
        in_specs=[whole(SMEM)] * 3 + [whole(VMEM)] * 2 + [whole(pl.ANY)] * len(after),
        out_specs=[whole(VMEM)] * 2,
        scratch_shapes=[pltpu.VMEM((n * chunk, LANES), F32)],
        compiler_params=params(34),
        cost_estimate=cost(0, 80e6),
        name="excess_rows",
    )(count, places.reshape(-1), live, grad, loss, *after)


def outgoing(counts, place_list, grad, slices, begin, chunk, after, spare=0):
    groups, capacity = place_list.shape
    n = len(slices)
    width = sum(depth for _, depth in slices) + spare
    return pl.pallas_call(
        functools.partial(outgoing_kernel, slices, capacity, begin),
        out_shape=[jax.ShapeDtypeStruct((groups, width, chunk), BF16), token_shape()],
        in_specs=[whole(SMEM)] * 2 + [whole(VMEM)] + [whole(pl.ANY)] * len(after),
        out_specs=[whole(VMEM)] * 2,
        scratch_shapes=[pltpu.VMEM((n * chunk, LANES), F32)],
        compiler_params=params(34),
        cost_estimate=cost(0, 80e6),
        name="outgoing",
    )(counts, place_list.reshape(-1), grad, *after)


def collect_kernel(slices, capacity, begin, first, counts_ref, row_ref, came_ref, *refs):
    total, token, tile = refs[-3:]
    total[...] = jnp.zeros_like(total) if first else refs[0][...]
    token[...] = jnp.zeros_like(token)
    add_rows(slices, capacity, begin, counts_ref, row_ref, came_ref, total, tile)


def add_rows(slices, capacity, begin, counts_ref, row_ref, came_ref, total, tile):
    n = len(slices)
    groups, _, chunk = came_ref.shape

    def source(group, carry):
        wanted = jnp.clip(counts_ref[group] - begin, 0, chunk)

        @pl.when(wanted > 0)
        def _():
            for m, (start, depth) in enumerate(slices):
                piece = came_ref[group, start : start + depth, :].astype(F32)
                tile[pl.ds(m, chunk, stride=n), :depth] = piece.T

            def body(step, inner):
                for lane in range(UNROLL):
                    at = step * UNROLL + lane
                    into = pair_of(row_ref[group * capacity + begin + at], n)
                    total[into, :] = total[into, :] + tile[pair_of(at, n), :]
                return inner

            lax.fori_loop(0, (wanted + UNROLL - 1) // UNROLL, body, 0)

        return carry

    lax.fori_loop(0, groups, source, 0)


def collect(counts, row_list, came, total, slices, begin, ent_rows, after):
    capacity = row_list.shape[1]
    chunk = came.shape[2]
    n = len(slices)
    given = [] if total is None else [total]
    return pl.pallas_call(
        functools.partial(collect_kernel, slices, capacity, begin, total is None),
        out_shape=[jax.ShapeDtypeStruct((n * (ent_rows + 8), LANES), F32), token_shape()],
        input_output_aliases={3: 0} if given else {},
        in_specs=[whole(SMEM)] * 2
        + [whole(VMEM)] * (1 + len(given))
        + [whole(pl.ANY)] * len(after),
        out_specs=[whole(VMEM)] * 2,
        scratch_shapes=[pltpu.VMEM((n * chunk, LANES), F32)],
        compiler_params=params(60),
        cost_estimate=cost(0, 120e6),
        name="collect",
    )(counts, row_list.reshape(-1), came, *given, *after)


def relation_sums_kernel(n, ids_ref, grad, *refs):
    total, token = refs[-2:]
    total[...] = jnp.zeros_like(total)
    token[...] = jnp.zeros_like(token)

    def body(step, carry):
        for lane in range(UNROLL):
            at = step * UNROLL + lane
            into = pair_of(ids_ref[at], n)
            total[into, :] = total[into, :] + grad[0, pair_of(at, n), :]
        return carry

    lax.fori_loop(0, grad.shape[1] // n // UNROLL, body, 0)


def relation_sums(relation_ids, grad, n, rel_total, after):
    count = relation_ids.shape[0]
    return pl.pallas_call(
        functools.partial(relation_sums_kernel, n),
        out_shape=[jax.ShapeDtypeStruct((n * rel_total, LANES), F32), token_shape()],
        grid=(1,),
        in_specs=[whole(SMEM), pl.BlockSpec((1, n * count, LANES), lambda i: (0, 0, 0))]
        + [whole(pl.ANY)] * len(after),
        out_specs=[whole(VMEM)] * 2,
        compiler_params=params(30),
        cost_estimate=cost(0, 120e6),
        name="relation_sums",
    )(relation_ids, grad, *after)


def finish_kernel(
    slices,
    capacity,
    begin,
    last_begin,
    counts_ref,
    row_ref,
    came_ref,
    last_ref,
    total_ref,
    weights_ref,
    first_ref,
    second_ref,
    *refs,
):
    n = len(slices)
    width = sum(depth for _, depth in slices)
    outs, loss_ref, (total, tile, gradient) = refs[:3], refs[3], refs[4:]
    cols = weights_ref.shape[1]
    step = pl.program_id(0)

    @pl.when(step == 0)
    def _():
        total[: total_ref.shape[0], :] = total_ref[...]
        add_rows(slices, capacity, begin, counts_ref, row_ref, came_ref, total, tile)
        add_rows(slices, capacity, last_begin, counts_ref, row_ref, last_ref, total, tile)
        terms = jnp.zeros((SPARE, LANES), F32)
        for group in range(last_ref.shape[0]):
            terms = terms + last_ref[group, last_rows(width) :, :LANES].astype(F32)
        place = lax.broadcasted_iota(jnp.int32, terms.shape, 0)
        for k in range(2):
            own = (place >= k * TERMS) & (place < (k + 1) * TERMS)
            loss_ref[k : k + 1, :] = jnp.sum(jnp.where(own, terms, 0.0), axis=0, keepdims=True)
        loss_ref[2:, :] = jnp.zeros((6, LANES), F32)

    for m, (start, depth) in enumerate(slices):
        part = total[pl.ds(step * (n * cols) + m, cols, stride=n), :]
        gradient[start : start + depth, :] = part.T[:depth]
    grad = gradient[...]
    new_first = BETA_ONE * first_ref[...] + (1.0 - BETA_ONE) * grad
    new_second = BETA_TWO * second_ref[...] + (1.0 - BETA_TWO) * grad * grad
    under = jnp.sqrt(new_second * (1.0 / (1.0 - BETA_TWO**STEP))) + EPSILON
    guess = pl.reciprocal(under, approx=True)
    inverse = guess * (2.0 - under * guess)
    pace = LEARN_RATE / (1.0 - BETA_ONE**STEP)
    outs[0][...] = (1.0 - LEARN_RATE * DECAY) * weights_ref[...] - (pace * new_first) * inverse
    outs[1][...] = new_first
    outs[2][...] = new_second


def finish_entities(
    counts, row_list, came, last, total, begin, last_begin, weights, first, second, slices
):
    width, ent_rows = weights.shape
    capacity = row_list.shape[1]
    cols = 1024
    steps = pl.cdiv(ent_rows, cols)
    n = len(slices)
    table = pl.BlockSpec((width, cols), lambda i: (0, i))
    tall = max(n * cols * steps, total.shape[0])
    return pl.pallas_call(
        functools.partial(finish_kernel, slices, capacity, begin, last_begin),
        out_shape=[jax.ShapeDtypeStruct((width, ent_rows), F32)] * 3 + [token_shape()],
        grid=(steps,),
        in_specs=[whole(SMEM)] * 2 + [whole(VMEM)] * 3 + [table] * 3,
        out_specs=[table] * 3 + [pl.BlockSpec((8, LANES), lambda i: (0, 0))],
        scratch_shapes=[
            pltpu.VMEM((tall, LANES), F32),
            pltpu.VMEM((n * max(came.shape[2], last.shape[2]), LANES), F32),
            pltpu.VMEM((width, cols), F32),
        ],
        compiler_params=params(56),
        cost_estimate=cost(0, 60e6),
        name="finish_entities",
    )(counts, row_list.reshape(-1), came, last, total, weights, first, second)


def chunk_bounds(capacity):
    units = capacity // LANES
    sizes = [3, 7, 3, 3] if units == 16 else [units // 4] * 3 + [units - 3 * (units // 4)]
    bounds = [0]
    for size in sizes:
        bounds.append(bounds[-1] + size * LANES)
    return bounds


def shards(
    head_ids,
    relation_ids,
    tail_ids,
    negative_ids,
    live_counts,
    rel_weight,
    rel_count,
    entity_table,
    entity_first,
    entity_second,
    relation_table,
    relation_first,
    relation_second,
):
    groups = lax.axis_size("edge")
    n_col = lax.axis_size("col")
    width, ent_rows = entity_table.shape
    blocks, neg_count = negative_ids.shape
    block_len = head_ids.shape[0] // blocks
    edge_count = blocks * block_len
    slices = width_slices(width)
    n = len(slices)
    all_ids = jnp.concatenate([head_ids, tail_ids, negative_ids.reshape(-1)])
    id_count = all_ids.shape[0]
    capacity = (4 * id_count + 3 * groups - 1) // (3 * groups)
    rel_total = rel_weight.shape[0]

    rel_own = rel_total // groups
    rel_low = jnp.pad(relation_table.astype(BF16).T, ((0, 0), (0, REL_PAD - rel_own)))
    dense = []
    for k, (start, depth) in enumerate(slices):
        sent = entity_table[start : start + depth].astype(BF16)
        if k == 0:
            behind = [
                jnp.pad(rel_low[at : at + size], ((0, depth - size), (0, 0))) for at, size in slices
            ]
            sent = jnp.concatenate([sent] + behind, axis=1)
        dense.append(lax.all_gather(sent, "edge", axis=0, tiled=False))

    place_list, row_list, counts = owner_lists(all_ids, groups, capacity, ent_rows)
    safe_places = jnp.minimum(place_list, id_count - 1)
    place_flat, row_flat = place_list.reshape(-1), row_list.reshape(-1)

    rel_scale = rel_weight * (rel_total / jnp.sum(rel_weight)) / rel_count.astype(F32)
    rel_scale = jnp.pad(rel_scale.reshape(groups, rel_own), ((0, 0), (0, REL_PAD - rel_own)))
    rel_places = relation_ids + (relation_ids // rel_own) * (REL_PAD - rel_own)

    def from_others(array):
        turns = [[(c, (c + away) % n_col) for c in range(n_col)] for away in range(1, n_col)]
        return [lax.ppermute(array, "col", turn) for turn in turns]

    bounds = chunk_bounds(capacity)
    few = jnp.sum((counts > bounds[-2]).astype(jnp.int32)) <= 1
    flag = jnp.broadcast_to(few.astype(jnp.int32), (groups, LANES))
    me = lax.axis_index("col").astype(jnp.int32).reshape(1)
    given = [[[] for _ in range(n_col)] for _ in range(HALVES)]
    offs = [[] for _ in range(HALVES)]
    tails = [[] for _ in range(HALVES)]
    biases, norms, first_sent, rel_rows = [], [], [], None
    for k, (start, depth) in enumerate(slices):
        sent = first_sent if k > 0 else [flag]
        fetched = fetch(counts, place_flat, row_flat, dense[k], id_count, ent_rows, sent)
        if k < n - 1:
            early, late, norm = negatives(fetched, blocks, block_len)
            early_all = [early] + from_others(early)
            if rel_rows is None:
                rel_rows = relation_rows(rel_places, dense[0], rel_scale, slices, [norm])
            off, tail, low, bias = edges(fetched, rel_rows[k], late, depth, blocks, block_len)
            low_all = [low] + from_others(low)
            first_sent = [corner(piece) for piece in early_all[1:]]
            biases.append(bias)
            norms.append(norm)
            for half in range(HALVES):
                offs[half].append(off)
                tails[half].append(tail)
                for col in range(n_col):
                    given[half][col] += [early_all[col], low_all[col]]
            continue
        if rel_rows is None:
            rel_rows = relation_rows(rel_places, dense[0], rel_scale, slices, [])

    def finish(half, after):
        off, tail, pair, token = last_slice(
            fetched, rel_rows[-1], biases, norms, slices[-1][1], blocks, block_len, half, after
        )
        offs[half].append(off)
        tails[half].append(tail)
        for col, piece in enumerate([pair] + from_others(pair)):
            given[half][col].append(piece)
        return token

    grad, loss_tiles = None, []
    half_token = []
    for half in range(HALVES):
        half_token = [finish(half, half_token)]
    flag = flag + half_token[0][0, 0].astype(jnp.int32)
    asked = lax.all_to_all(
        jnp.concatenate([row_list, flag], axis=1), "edge", split_axis=0, concat_axis=0, tiled=True
    )
    all_few = jnp.min(asked[:, capacity]) > 0
    asked = asked[:, :capacity]
    asked_counts = jnp.sum((asked < ent_rows).astype(jnp.int32), axis=1)
    for half in range(HALVES):
        after = [corner(asked)] if half == 0 else []
        grad, loss_tile = block_math(
            me,
            live_counts,
            given[half],
            offs[half],
            tails[half],
            grad,
            slices,
            block_len,
            half,
            after,
        )
        loss_tiles.append(loss_tile)
    live = jnp.minimum(live_counts, block_len)
    loss_tile = functools.reduce(jnp.add, loss_tiles)

    flat = grad.reshape(n * id_count, LANES)
    chunks = len(bounds) - 1
    begin, size = bounds[-2], bounds[-1] - bounds[-2]
    most = jnp.argmax(counts)
    most_places = lax.dynamic_slice_in_dim(safe_places, most, 1, axis=0)
    most_count = lax.dynamic_slice_in_dim(counts, most, 1, axis=0)
    arrived, total, after = [], None, []
    for k in range(chunks - 1):
        sent, sent_token = outgoing(
            counts, safe_places, flat, slices, bounds[k], bounds[k + 1] - bounds[k], after
        )
        if k == chunks - 2:
            sent = pass_on(sent, [corner(relation_grad)])
        arrived.append(lax.all_to_all(sent, "edge", split_axis=0, concat_axis=0, tiled=True))
        after = []
        if k == 0:
            excess, excess_token = excess_rows(
                most_count,
                most_places,
                live,
                flat,
                loss_tile,
                slices,
                begin,
                size,
                [sent_token],
            )
            after = [excess_token]
        if k == 1:
            before = [corner(arrived[0]), excess_token, sent_token]
            rel_terms, token = relation_sums(relation_ids, grad, n, rel_total, before)
            after = [token]
            rel_terms = rel_terms.reshape(rel_total, n * LANES)[:, :width]
            relation_grad = lax.psum_scatter(rel_terms, "edge", scatter_dimension=0, tiled=True)
        if k == 2:
            ready = (relation_grad[0, 0] == relation_grad[0, 0]) & (sent_token[0, 0] == 0.0)
            excess = jnp.where(ready, excess, jnp.zeros_like(excess))
            gathered = lax.all_gather(excess, "edge", axis=0, tiled=True)
            after = [corner(relation_grad)]
        if k > 0:
            total, token = collect(
                asked_counts, asked, arrived[k - 1], total, slices, bounds[k - 1], ent_rows, after
            )
            after = [token]

    def by_all_to_all():
        spare = last_rows(width) + SPARE - width
        sent, _ = outgoing(counts, safe_places, flat, slices, begin, size, [], spare)
        rows = lax.all_to_all(sent, "edge", split_axis=0, concat_axis=0, tiled=True)
        return rows.at[:, last_rows(width) :].set(gathered[:, last_rows(width) :])

    k = chunks - 2
    here = jnp.where(arrived[k][0, 0, 0] > 0, 1, 2) > 0
    came = lax.cond(all_few & here & (token[0, 0] == 0.0), lambda: gathered, by_all_to_all)
    new_entity, new_entity_first, new_entity_second, sums = finish_entities(
        asked_counts,
        asked,
        arrived[k],
        came,
        total,
        bounds[k],
        begin,
        entity_table,
        entity_first,
        entity_second,
        slices,
    )
    loss_pair = sums[:2, 0]
    new_relation, new_relation_first, new_relation_second = adamw_update(
        relation_table, relation_grad, relation_first, relation_second
    )
    return (
        loss_pair,
        new_entity,
        new_entity_first,
        new_entity_second,
        new_relation,
        new_relation_first,
        new_relation_second,
    )


def solution(mesh):
    placed = (
        P("edge"),
        P("edge"),
        P("edge"),
        P("edge", None),
        P("edge"),
        P(),
        P(),
        P("col", "edge"),
        P("col", "edge"),
        P("col", "edge"),
        P("edge", "col"),
        P("edge", "col"),
        P("edge", "col"),
    )
    return jax.shard_map(
        shards,
        mesh=mesh,
        in_specs=placed,
        out_specs=(
            P(),
            P("col", "edge"),
            P("col", "edge"),
            P("col", "edge"),
            P("edge", "col"),
            P("edge", "col"),
            P("edge", "col"),
        ),
        check_vma=False,
    )
```

```python
import functools

import jax
import jax.numpy as jnp
from jax import lax
from jax.experimental import pallas as pl
from jax.experimental.pallas import tpu as pltpu
from jax.sharding import PartitionSpec as P

STEP = 5


MARGIN = 0.1
LEARN_RATE = 0.1
BETA_ONE = 0.5
BETA_TWO = 0.5
EPSILON = 1e-08
DECAY = 0.01
LANES = 128
UNROLL = 8
PARTS = 4
HALVES = 2
EARLY = 96
TURN = 512
REL_PAD = 256
TERMS = 3
SPARE = 8
NN = (((1,), (0,)), ((), ()))
NT = (((1,), (1,)), ((), ()))
TN = (((0,), (0,)), ((), ()))
F32 = jnp.float32
BF16 = jnp.bfloat16
SMEM = pltpu.SMEM
VMEM = pltpu.VMEM


def params(mebibytes=60):
    return pltpu.CompilerParams(vmem_limit_bytes=mebibytes << 20)


def cost(flops, moved):
    return pl.CostEstimate(flops=int(flops), bytes_accessed=int(moved), transcendentals=0)


def corner(array):
    return array[(0,) * (array.ndim - 2) + (slice(0, 8), slice(0, LANES))]


def token_shape():
    return jax.ShapeDtypeStruct((8, LANES), F32)


def whole(space):
    return pl.BlockSpec(memory_space=space)


def adamw_update(weights, gradient, first, second):
    new_first = BETA_ONE * first + (1.0 - BETA_ONE) * gradient
    new_second = BETA_TWO * second + (1.0 - BETA_TWO) * gradient * gradient
    first_hat = new_first / (1.0 - BETA_ONE**STEP)
    second_hat = new_second / (1.0 - BETA_TWO**STEP)
    updated = weights - LEARN_RATE * (
        first_hat / (jnp.sqrt(second_hat) + EPSILON) + DECAY * weights
    )
    return (updated, new_first, new_second)


def width_slices(width):
    return [(at, min(LANES, width - at)) for at in range(0, width, LANES)]


def owner_lists(all_ids, groups, capacity, ent_rows):
    count = all_ids.shape[0]
    owners = all_ids // ent_rows
    local_rows = all_ids - owners * ent_rows
    chunk = 256
    mine = owners[None, :] == jnp.arange(groups, dtype=jnp.int32)[:, None]
    mine = mine.astype(BF16).reshape(groups, count // chunk, chunk)
    before = jnp.triu(jnp.ones((chunk, chunk), BF16), 1)
    inner = jnp.dot(mine, before, preferred_element_type=F32)
    sums = jnp.sum(mine.astype(F32), axis=2)
    carry = jnp.cumsum(sums, axis=1) - sums
    ranks = jnp.sum(mine.astype(F32) * (inner + carry[:, :, None]), axis=0)
    ranks = ranks.astype(jnp.int32).reshape(count)
    counts = jnp.sum(sums, axis=1).astype(jnp.int32)
    high = owners * (capacity // LANES) + ranks // LANES
    low = ranks % LANES
    tall = groups * capacity // LANES
    left = (jnp.arange(tall, dtype=jnp.int32)[:, None] == high[None, :]).astype(BF16)
    right = (jnp.arange(LANES, dtype=jnp.int32)[:, None] == low[None, :]).astype(BF16)
    places = jnp.arange(1, count + 1, dtype=jnp.int32)
    parts = jnp.stack([places // 256, places % 256, local_rows // 256, local_rows % 256])
    right = (parts.astype(BF16)[:, None, :] * right[None]).reshape(PARTS * LANES, count)
    found = lax.dot_general(left, right, NT, preferred_element_type=F32).astype(jnp.int32)
    found = found.reshape(tall, PARTS, LANES)
    place = found[:, 0] * 256 + found[:, 1]
    place_list = jnp.where(place > 0, place - 1, count).reshape(groups, capacity)
    row_list = jnp.where(place > 0, found[:, 2] * 256 + found[:, 3], ent_rows)
    return place_list, row_list.reshape(groups, capacity), counts


def relation_rows_kernel(slices, ids_ref, scale_ref, *refs):
    n = len(slices)
    tables, outs = refs[:n], refs[-2 * n - 1 : -n - 1]
    columns, rows = refs[-n - 1], refs[-n:]
    groups = tables[0].shape[0]
    for (_, depth), table, into in zip(slices, tables, rows):
        columns[...] = jnp.zeros_like(columns)

        def turn(group, carry):
            columns[:depth, :] = table[group, :depth].astype(F32)
            if depth < LANES:
                columns[LANES - 1 :, :] = scale_ref[pl.ds(group, 1), :]
            into[pl.ds(pl.multiple_of(group * REL_PAD, REL_PAD), REL_PAD), :] = columns[...].T
            return carry

        lax.fori_loop(0, groups, turn, 0, unroll=4)

    def body(step, carry):
        for lane in range(UNROLL):
            at = step * UNROLL + lane
            row = ids_ref[at]
            for source, out in zip(rows, outs):
                out[pl.ds(at, 1), :] = source[pl.ds(row, 1), :]
        return carry

    lax.fori_loop(0, outs[0].shape[0] // UNROLL, body, 0)


def relation_rows(places, dense, scale, slices, after):
    count = places.shape[0]
    groups, depth, span = dense.shape
    n = len(slices)
    first = span // REL_PAD - n

    def columns(k):
        return pl.BlockSpec((groups, depth, REL_PAD), lambda i: (0, 0, first + k))

    return pl.pallas_call(
        functools.partial(relation_rows_kernel, slices),
        out_shape=[jax.ShapeDtypeStruct((count, LANES), F32)] * n,
        grid=(1,),
        in_specs=[whole(SMEM), whole(VMEM)]
        + [columns(k) for k in range(n)]
        + [whole(pl.ANY)] * len(after),
        out_specs=[whole(VMEM)] * n,
        scratch_shapes=[pltpu.VMEM((LANES, REL_PAD), F32)]
        + [pltpu.VMEM((groups * REL_PAD, LANES), F32)] * n,
        compiler_params=params(28),
        cost_estimate=cost(0, 80e6),
        name="relation_rows",
    )(places, scale, *[dense] * n, *after)


def fetch_kernel(
    capacity, moves, ent_rows, counts_ref, place_ref, row_ref, dense_ref, *refs
):
    shard = pl.program_id(0)
    last = pl.num_programs(0) - 1
    out_ref, rows = refs[-3], refs[-2:]
    depth = dense_ref.shape[1]
    turns = ent_rows // TURN
    rest = ent_rows - turns * TURN

    if depth < LANES:

        @pl.when(shard == 0)
        def _():
            for ref in rows:
                ref[...] = jnp.zeros_like(ref)

    def turn(into, begin, size):
        cols = pl.ds(begin, size)
        into[cols, :depth] = dense_ref[0, :, cols].astype(F32).T

    def move(source, at):
        out_ref[pl.ds(place_ref[at], 1), :] = source[pl.ds(row_ref[at], 1), :]

    def step(into, source):
        base = (shard - 1) * capacity

        def remaining(first):
            def body(trip, carry):
                for lane in range(UNROLL):
                    move(source, base + first + trip * UNROLL + lane)
                return carry

            wanted = counts_ref[jnp.maximum(shard - 1, 0)] - first
            lax.fori_loop(0, (wanted + UNROLL - 1) // UNROLL, body, 0)

        def only_turn(trip, carry):
            turn(into, pl.multiple_of(trip * TURN, TURN), TURN)
            return carry

        def both(trip, carry):
            turn(into, pl.multiple_of(trip * TURN, TURN), TURN)
            for lane in range(moves):
                move(source, base + trip * moves + lane)
            return carry

        @pl.when(shard == 0)
        def _():
            lax.fori_loop(0, turns, only_turn, 0)

        @pl.when((shard > 0) & (shard < last))
        def _():
            lax.fori_loop(0, turns, both, 0)
            remaining(turns * moves)

        @pl.when(shard == last)
        def _():
            remaining(0)

        if rest:

            @pl.when(shard < last)
            def _():
                turn(into, turns * TURN, rest)

    for parity in range(2):

        @pl.when(lax.rem(shard, 2) == parity)
        def _():
            step(rows[parity], rows[1 - parity])


def fetch(counts, place_list, row_list, dense, id_count, ent_rows, after):
    groups, depth, _ = dense.shape
    capacity = place_list.shape[0] // groups
    moves = (id_count // groups) // (ent_rows // TURN) // UNROLL * UNROLL
    return pl.pallas_call(
        functools.partial(fetch_kernel, capacity, moves, ent_rows),
        out_shape=jax.ShapeDtypeStruct((id_count + 8, LANES), F32),
        grid=(groups + 1,),
        in_specs=[whole(SMEM)] * 3
        + [
            pl.BlockSpec(
                (1, depth, ent_rows), lambda shard: (jnp.minimum(shard, groups - 1), 0, 0)
            )
        ]
        + [whole(pl.ANY)] * len(after),
        out_specs=whole(VMEM),
        scratch_shapes=[pltpu.VMEM((ent_rows + 8, LANES), F32)] * 2,
        compiler_params=params(26),
        cost_estimate=cost(0, 170e6),
        name="fetch_rows",
    )(counts, place_list, row_list, dense, *after)


def column_sum(values):
    return jnp.sum(values * values, axis=0, keepdims=True)


def negatives_kernel(neg_ref, early_ref, late_ref, norm_ref):
    neg_t = neg_ref[...].T
    early_ref[...] = neg_t[:EARLY].astype(BF16)
    late_ref[...] = neg_t[EARLY:].astype(BF16)
    norm_ref[...] = column_sum(neg_t)


def negatives(fetched, blocks, block_len):
    count = blocks * block_len
    return pl.pallas_call(
        negatives_kernel,
        out_shape=[
            jax.ShapeDtypeStruct((EARLY, count), BF16),
            jax.ShapeDtypeStruct((LANES - EARLY, count), BF16),
            jax.ShapeDtypeStruct((1, count), F32),
        ],
        grid=(blocks,),
        in_specs=[pl.BlockSpec((block_len, LANES), lambda b: (2 * blocks + b, 0))],
        out_specs=[
            pl.BlockSpec((EARLY, block_len), lambda b: (0, b)),
            pl.BlockSpec((LANES - EARLY, block_len), lambda b: (0, b)),
            pl.BlockSpec((1, block_len), lambda b: (0, b)),
        ],
        compiler_params=params(5),
        cost_estimate=cost(0, 10e6),
        name="negatives",
    )(fetched)


def edge_parts(depth, head_ref, tail_ref, rel_ref, off_ref, tail_out):
    lane = lax.broadcasted_iota(jnp.int32, head_ref.shape, 1)
    inside = lane < depth
    rel = rel_ref[...]
    tail = tail_ref[...]
    shifted = head_ref[...] + jnp.where(inside, rel, 0.0)
    off_ref[...] = jnp.where(inside, shifted - tail, rel)
    tail_out[...] = tail.astype(BF16)
    shifted_t = shifted.T
    return shifted_t, column_sum((shifted - tail).T) - column_sum(shifted_t)


def edges_kernel(
    depth, head_ref, tail_ref, rel_ref, late_ref, off_ref, tail_out, low_ref, bias_ref
):
    shifted_t, bias = edge_parts(depth, head_ref, tail_ref, rel_ref, off_ref, tail_out)
    low_ref[:depth] = shifted_t[:depth].astype(BF16)
    low_ref[depth:] = late_ref[...]
    bias_ref[...] = bias


def edges(fetched, rel_rows, late, depth, blocks, block_len):
    count = blocks * block_len
    tall = depth + late.shape[0]

    def rows(at):
        return pl.BlockSpec((block_len, LANES), lambda b: (at * blocks + b, 0))

    return pl.pallas_call(
        functools.partial(edges_kernel, depth),
        out_shape=[
            jax.ShapeDtypeStruct((count, LANES), F32),
            jax.ShapeDtypeStruct((count, LANES), BF16),
            jax.ShapeDtypeStruct((tall, count), BF16),
            jax.ShapeDtypeStruct((1, count), F32),
        ],
        grid=(blocks,),
        in_specs=[rows(0), rows(1), rows(0)]
        + [pl.BlockSpec((tall - depth, block_len), lambda b: (0, b))],
        out_specs=[
            rows(0),
            rows(0),
            pl.BlockSpec((tall, block_len), lambda b: (0, b)),
            pl.BlockSpec((1, block_len), lambda b: (0, b)),
        ],
        compiler_params=params(9),
        cost_estimate=cost(0, 30e6),
        name="edges",
    )(fetched, fetched, rel_rows, late)


def last_rows(depth):
    return (depth + 7) // 8 * 8


def with_terms(columns, total, depth):
    terms = term_rows(total, 0)
    return jnp.concatenate([columns[: last_rows(depth)], terms], axis=0).astype(BF16)


def term_rows(total, first):
    place = lax.broadcasted_iota(jnp.int32, (8, total.shape[1]), 0)
    left = total
    terms = jnp.zeros(place.shape, F32)
    for k in range(TERMS):
        term = left.astype(BF16).astype(F32)
        left = left - term
        terms = jnp.where(place == first + k, term, terms)
    return terms


def last_kernel(depth, n_given, head_ref, tail_ref, neg_ref, rel_ref, *refs):
    biases, norms = refs[:n_given], refs[n_given : 2 * n_given]
    off_ref, tail_out, pair_ref, token = refs[-4:]
    token[...] = jnp.zeros_like(token)
    shifted_t, bias = edge_parts(depth, head_ref, tail_ref, rel_ref, off_ref, tail_out)
    neg_t = neg_ref[...].T
    norm = column_sum(neg_t)
    for ref in biases:
        bias = bias + ref[...]
    for ref in norms:
        norm = norm + ref[...]
    pair_ref[0] = with_terms(shifted_t, bias, depth)
    pair_ref[1] = with_terms(neg_t, norm, depth)


def last_slice(fetched, rel_rows, biases, norms, depth, blocks, block_len, half, after):
    part = blocks // HALVES
    count = part * block_len
    tall = last_rows(depth) + 8

    def rows(at):
        return pl.BlockSpec((block_len, LANES), lambda b: (at * blocks + half * part + b, 0))

    return pl.pallas_call(
        functools.partial(last_kernel, depth, len(biases)),
        out_shape=[
            jax.ShapeDtypeStruct((count, LANES), F32),
            jax.ShapeDtypeStruct((count, LANES), BF16),
            jax.ShapeDtypeStruct((2, tall, count), BF16),
            token_shape(),
        ],
        grid=(part,),
        in_specs=[rows(0), rows(1), rows(2), rows(0)]
        + [pl.BlockSpec((1, block_len), lambda b: (0, half * part + b))]
        * (len(biases) + len(norms))
        + [whole(pl.ANY)] * len(after),
        out_specs=[
            pl.BlockSpec((block_len, LANES), lambda b: (b, 0)),
            pl.BlockSpec((block_len, LANES), lambda b: (b, 0)),
            pl.BlockSpec((2, tall, block_len), lambda b: (0, 0, b)),
            pl.BlockSpec((8, LANES), lambda b: (0, 0)),
        ],
        compiler_params=params(9),
        cost_estimate=cost(0, 20e6),
        name="last_slice",
    )(fetched, fetched, fetched, rel_rows, *biases, *norms, *after)


def block_kernel(slices, n_col, half, me_ref, live_ref, *refs):
    n = len(slices)
    per_col = 2 * n - 1
    given = [refs[k * per_col : (k + 1) * per_col] for k in range(n_col)]
    refs = refs[n_col * per_col :]
    offs, tails, refs = refs[:n], refs[n : 2 * n], refs[2 * n :]
    grad, refs = refs[-9], refs[-8:]
    loss_ref, shift_scr, neg_scr, sums_scr, cross, slopes, row_bias, row_sum = refs
    block = pl.program_id(0)
    length = cross.shape[0]
    me = me_ref[0]
    for k in range(n_col):
        slot = lax.rem(me + (n_col - k), n_col)
        for m, (start, depth) in enumerate(slices):
            if m < n - 1:
                early, late = given[k][2 * m : 2 * m + 2]
                shift_scr[slot, start : start + depth, :] = 2.0 * late[:depth, :]
                neg_scr[slot, start : start + EARLY, :] = early[...]
                neg_scr[slot, start + EARLY : start + depth, :] = late[depth:, :]
            else:
                pair = given[k][-1]
                shift, neg = pair[0, :depth, :], pair[1, :depth, :]
                for row in range(2):
                    terms = pair[row, last_rows(depth) : last_rows(depth) + 8, :].astype(F32)
                    sums_scr[slot, row : row + 1] = jnp.sum(terms, axis=0, keepdims=True)
                shift_scr[slot, start : start + depth, :] = 2.0 * shift
                neg_scr[slot, start : start + depth, :] = neg
    bias = jnp.sum(sums_scr[:, 0, :], axis=0, keepdims=True) + MARGIN
    neg_norm = jnp.sum(sums_scr[:, 1, :], axis=0, keepdims=True)
    row_bias[...] = jnp.broadcast_to(bias, (LANES, length)).T

    live = live_ref[half * pl.num_programs(0) + block]
    tile = 256
    small = 128
    lane_tiles = [slice(at, at + LANES) for at in range(0, length, LANES)]
    cols = jnp.zeros((8, length), F32)
    loss = jnp.zeros((8, LANES), F32)
    def products(at):
        part = slice(at, at + tile)
        doubled = None
        for k in range(n_col):
            term = lax.dot_general(
                shift_scr[k, :, part], neg_scr[k], TN, preferred_element_type=F32
            )
            doubled = term if doubled is None else doubled + term
        cross[part, :] = doubled

    def moves(at):
        part = slice(at, at + tile)
        moved = lax.dot_general(slopes[part, :], neg_scr[me], NT, preferred_element_type=F32)
        fade = -row_sum[part, :]
        for m, (start, depth) in enumerate(slices):
            into = pl.ds(n * at + m, tile, stride=n)
            grad[0, into, :depth] = (
                fade[:, :depth] * tails[m][part, :depth].astype(F32)
                + moved[:, start : start + depth]
            )
            grad[1, into, :] = fade * offs[m][part, :]

    products(0)
    for begin in range(0, length, tile):
        if begin + tile < length:
            products(begin + tile)
        for at in range(begin, begin + tile, small):
            part = slice(at, at + small)
            place = at + lax.broadcasted_iota(jnp.int32, (small, 1), 0)
            scale = offs[-1][part, LANES - 1 : LANES]
            weight = jnp.where(place < live, scale, 0.0) / length
            margins = cross[part, :] + (row_bias[part, 0:1] - neg_norm)
            fall = jnp.exp(-jnp.abs(margins))
            under = 1.0 + fall
            guess = pl.reciprocal(under, approx=True)
            inverse = guess * (2.0 - under * guess)
            twice = (2.0 * weight) * (jnp.where(margins >= 0.0, 1.0, fall) * inverse)
            row_sum[part, :] = jnp.broadcast_to(
                jnp.sum(twice, axis=1, keepdims=True), (small, LANES)
            )
            slopes[part, :] = twice.astype(BF16)
            cols = cols + jnp.sum(twice.reshape(small // 8, 8, length), axis=0)
            over = jnp.maximum(margins, 0.0)
            lifts = [fall[:, lanes] for lanes in lane_tiles]
            while len(lifts) > 1:
                lifts = [a + b + a * b for a, b in zip(lifts[::2], lifts[1::2])]
            lift = lifts[0]
            soft = functools.reduce(jnp.add, [over[:, lanes] for lanes in lane_tiles]) + jnp.where(
                lift < 2.0**-11, lift * (1.0 - 0.5 * lift), jnp.log(1.0 + lift)
            )
            loss = loss + jnp.sum((weight * soft).reshape(small // 8, 8, LANES), axis=0)
        moves(begin)
    col_sum = jnp.sum(cols, axis=0, keepdims=True)

    @pl.when(block == 0)
    def _():
        loss_ref[...] = loss

    @pl.when(block > 0)
    def _():
        loss_ref[...] += loss

    moved = lax.dot_general(shift_scr[me], slopes[...], NN, preferred_element_type=F32)
    moved = 0.5 * moved - col_sum * neg_scr[me].astype(F32)
    for m, (start, depth) in enumerate(slices):
        grad[2, pl.ds(m, length, stride=n), :depth] = moved[start : start + depth, :].T


def block_math(me, live_counts, given, offs, tails, old, slices, block_len, half, after):
    n, n_col = len(slices), len(given)
    blocks = live_counts.shape[0]
    part = blocks // HALVES
    width = sum(depth for _, depth in slices)
    flat = [piece for per_col in given for piece in per_col]
    kept = [] if old is None else [old]

    def columns(piece):
        if piece.ndim == 3:
            return pl.BlockSpec((2, piece.shape[1], block_len), lambda b: (0, 0, b))
        return pl.BlockSpec((piece.shape[0], block_len), lambda b: (0, half * part + b))

    def rows(array):
        first = half * part if array.shape[0] > part * block_len else 0
        return pl.BlockSpec((block_len, LANES), lambda b: (first + b, 0))

    first_old = 2 + len(flat) + 2 * n
    return pl.pallas_call(
        functools.partial(block_kernel, slices, n_col, half),
        out_shape=[
            jax.ShapeDtypeStruct((3, n * blocks * block_len, LANES), F32),
            jax.ShapeDtypeStruct((8, LANES), F32),
        ],
        grid=(part,),
        in_specs=[whole(SMEM)] * 2
        + [columns(piece) for piece in flat]
        + [rows(array) for array in offs + tails]
        + [whole(pl.ANY)] * len(kept + after),
        out_specs=[
            pl.BlockSpec((3, n * block_len, LANES), lambda b: (0, half * part + b, 0)),
            pl.BlockSpec((8, LANES), lambda b: (0, 0)),
        ],
        input_output_aliases={first_old + k: k for k in range(len(kept))},
        scratch_shapes=[
            pltpu.VMEM((n_col, width, block_len), BF16),
            pltpu.VMEM((n_col, width, block_len), BF16),
            pltpu.VMEM((n_col, 2, block_len), F32),
            pltpu.VMEM((block_len, block_len), F32),
            pltpu.VMEM((block_len, block_len), BF16),
            pltpu.VMEM((block_len, LANES), F32),
            pltpu.VMEM((block_len, LANES), F32),
        ],
        compiler_params=params(60),
        cost_estimate=cost(part * 8 * block_len * block_len * width, 120e6),
        name="block_math",
    )(me, live_counts, *flat, *offs, *tails, *kept, *after)


def pair_of(row, n):
    return pl.ds(pl.multiple_of(row * n, n), n)


def pass_on_kernel(array_ref, *refs):
    refs[-1][...] = jnp.zeros((8, LANES), F32)


def pass_on(array, after):
    return pl.pallas_call(
        pass_on_kernel,
        out_shape=[jax.ShapeDtypeStruct(array.shape, array.dtype), token_shape()],
        in_specs=[whole(pl.ANY)] * (1 + len(after)),
        out_specs=[whole(pl.ANY), whole(VMEM)],
        input_output_aliases={0: 0},
        compiler_params=params(2),
        cost_estimate=cost(0, 1e3),
        name="pass_on",
    )(array, *after)[0]


def outgoing_kernel(slices, capacity, begin, counts_ref, place_ref, grad, *refs):
    n = len(slices)
    out_ref, token, tile = refs[-3:]
    groups, _, chunk = out_ref.shape
    token[...] = jnp.zeros_like(token)

    def owner(group, carry):
        wanted = jnp.clip(counts_ref[group] - begin, 0, chunk)

        def body(step, inner):
            for lane in range(UNROLL):
                at = step * UNROLL + lane
                place = place_ref[group * capacity + begin + at]
                tile[pair_of(at, n), :] = grad[pair_of(place, n), :]
            return inner

        lax.fori_loop(0, (wanted + UNROLL - 1) // UNROLL, body, 0)
        for m, (start, depth) in enumerate(slices):
            piece = tile[pl.ds(m, chunk, stride=n), :].T
            out_ref[group, start : start + depth, :] = piece[:depth].astype(BF16)
        return carry

    lax.fori_loop(0, groups, owner, 0)


def excess_kernel(slices, capacity, begin, counts_ref, place_ref, live_ref, grad, loss_ref, *refs):
    outgoing_kernel(slices, capacity, begin, counts_ref, place_ref, grad, *refs)
    out_ref = refs[-3]
    loss = jnp.sum(jnp.sum(loss_ref[...], axis=0, keepdims=True), axis=1, keepdims=True)
    live = live_ref[0]
    for block in range(1, live_ref.shape[0]):
        live = live + live_ref[block]
    count = jnp.full((1, LANES), live.astype(F32))
    terms = term_rows(jnp.broadcast_to(loss, (1, LANES)), 0) + term_rows(count, TERMS)
    width = sum(depth for _, depth in slices)
    for at in range(0, out_ref.shape[2], LANES):
        out_ref[0, last_rows(width) :, at : at + LANES] = terms.astype(BF16)


def excess_rows(count, places, live, grad, loss, slices, begin, chunk, after):
    n = len(slices)
    width = sum(depth for _, depth in slices)
    return pl.pallas_call(
        functools.partial(excess_kernel, slices, places.shape[1], begin),
        out_shape=[
            jax.ShapeDtypeStruct((1, last_rows(width) + SPARE, chunk), BF16),
            token_shape(),
        ],
        in_specs=[whole(SMEM)] * 3 + [whole(VMEM)] * 2 + [whole(pl.ANY)] * len(after),
        out_specs=[whole(VMEM)] * 2,
        scratch_shapes=[pltpu.VMEM((n * chunk, LANES), F32)],
        compiler_params=params(34),
        cost_estimate=cost(0, 80e6),
        name="excess_rows",
    )(count, places.reshape(-1), live, grad, loss, *after)


def outgoing(counts, place_list, grad, slices, begin, chunk, after, spare=0):
    groups, capacity = place_list.shape
    n = len(slices)
    width = sum(depth for _, depth in slices) + spare
    return pl.pallas_call(
        functools.partial(outgoing_kernel, slices, capacity, begin),
        out_shape=[jax.ShapeDtypeStruct((groups, width, chunk), BF16), token_shape()],
        in_specs=[whole(SMEM)] * 2 + [whole(VMEM)] + [whole(pl.ANY)] * len(after),
        out_specs=[whole(VMEM)] * 2,
        scratch_shapes=[pltpu.VMEM((n * chunk, LANES), F32)],
        compiler_params=params(34),
        cost_estimate=cost(0, 80e6),
        name="outgoing",
    )(counts, place_list.reshape(-1), grad, *after)


def collect_kernel(slices, capacity, begin, first, counts_ref, row_ref, came_ref, *refs):
    total, token, tile = refs[-3:]
    total[...] = jnp.zeros_like(total) if first else refs[0][...]
    token[...] = jnp.zeros_like(token)
    add_rows(slices, capacity, begin, counts_ref, row_ref, came_ref, total, tile)


def add_rows(slices, capacity, begin, counts_ref, row_ref, came_ref, total, tile):
    n = len(slices)
    groups, _, chunk = came_ref.shape

    def source(group, carry):
        wanted = jnp.clip(counts_ref[group] - begin, 0, chunk)

        @pl.when(wanted > 0)
        def _():
            for m, (start, depth) in enumerate(slices):
                piece = came_ref[group, start : start + depth, :].astype(F32)
                tile[pl.ds(m, chunk, stride=n), :depth] = piece.T

            def body(step, inner):
                for lane in range(UNROLL):
                    at = step * UNROLL + lane
                    into = pair_of(row_ref[group * capacity + begin + at], n)
                    total[into, :] = total[into, :] + tile[pair_of(at, n), :]
                return inner

            lax.fori_loop(0, (wanted + UNROLL - 1) // UNROLL, body, 0)

        return carry

    lax.fori_loop(0, groups, source, 0)


def collect(counts, row_list, came, total, slices, begin, ent_rows, after):
    capacity = row_list.shape[1]
    chunk = came.shape[2]
    n = len(slices)
    given = [] if total is None else [total]
    return pl.pallas_call(
        functools.partial(collect_kernel, slices, capacity, begin, total is None),
        out_shape=[jax.ShapeDtypeStruct((n * (ent_rows + 8), LANES), F32), token_shape()],
        input_output_aliases={3: 0} if given else {},
        in_specs=[whole(SMEM)] * 2
        + [whole(VMEM)] * (1 + len(given))
        + [whole(pl.ANY)] * len(after),
        out_specs=[whole(VMEM)] * 2,
        scratch_shapes=[pltpu.VMEM((n * chunk, LANES), F32)],
        compiler_params=params(60),
        cost_estimate=cost(0, 120e6),
        name="collect",
    )(counts, row_list.reshape(-1), came, *given, *after)


def relation_sums_kernel(n, ids_ref, grad, *refs):
    total, token = refs[-2:]
    total[...] = jnp.zeros_like(total)
    token[...] = jnp.zeros_like(token)

    def body(step, carry):
        for lane in range(UNROLL):
            at = step * UNROLL + lane
            into = pair_of(ids_ref[at], n)
            total[into, :] = total[into, :] + grad[0, pair_of(at, n), :]
        return carry

    lax.fori_loop(0, grad.shape[1] // n // UNROLL, body, 0)


def relation_sums(relation_ids, grad, n, rel_total, after):
    count = relation_ids.shape[0]
    return pl.pallas_call(
        functools.partial(relation_sums_kernel, n),
        out_shape=[jax.ShapeDtypeStruct((n * rel_total, LANES), F32), token_shape()],
        grid=(1,),
        in_specs=[whole(SMEM), pl.BlockSpec((1, n * count, LANES), lambda i: (0, 0, 0))]
        + [whole(pl.ANY)] * len(after),
        out_specs=[whole(VMEM)] * 2,
        compiler_params=params(30),
        cost_estimate=cost(0, 120e6),
        name="relation_sums",
    )(relation_ids, grad, *after)


def finish_kernel(
    slices,
    capacity,
    begin,
    last_begin,
    counts_ref,
    row_ref,
    came_ref,
    last_ref,
    total_ref,
    weights_ref,
    first_ref,
    second_ref,
    *refs,
):
    n = len(slices)
    width = sum(depth for _, depth in slices)
    outs, loss_ref, (total, tile, gradient) = refs[:3], refs[3], refs[4:]
    cols = weights_ref.shape[1]
    step = pl.program_id(0)

    @pl.when(step == 0)
    def _():
        total[: total_ref.shape[0], :] = total_ref[...]
        add_rows(slices, capacity, begin, counts_ref, row_ref, came_ref, total, tile)
        add_rows(slices, capacity, last_begin, counts_ref, row_ref, last_ref, total, tile)
        terms = jnp.zeros((SPARE, LANES), F32)
        for group in range(last_ref.shape[0]):
            terms = terms + last_ref[group, last_rows(width) :, :LANES].astype(F32)
        place = lax.broadcasted_iota(jnp.int32, terms.shape, 0)
        for k in range(2):
            own = (place >= k * TERMS) & (place < (k + 1) * TERMS)
            loss_ref[k : k + 1, :] = jnp.sum(jnp.where(own, terms, 0.0), axis=0, keepdims=True)
        loss_ref[2:, :] = jnp.zeros((6, LANES), F32)

    for m, (start, depth) in enumerate(slices):
        part = total[pl.ds(step * (n * cols) + m, cols, stride=n), :]
        gradient[start : start + depth, :] = part.T[:depth]
    grad = gradient[...]
    new_first = BETA_ONE * first_ref[...] + (1.0 - BETA_ONE) * grad
    new_second = BETA_TWO * second_ref[...] + (1.0 - BETA_TWO) * grad * grad
    under = jnp.sqrt(new_second * (1.0 / (1.0 - BETA_TWO**STEP))) + EPSILON
    guess = pl.reciprocal(under, approx=True)
    inverse = guess * (2.0 - under * guess)
    pace = LEARN_RATE / (1.0 - BETA_ONE**STEP)
    outs[0][...] = (1.0 - LEARN_RATE * DECAY) * weights_ref[...] - (pace * new_first) * inverse
    outs[1][...] = new_first
    outs[2][...] = new_second


def finish_entities(
    counts, row_list, came, last, total, begin, last_begin, weights, first, second, slices
):
    width, ent_rows = weights.shape
    capacity = row_list.shape[1]
    cols = 1024
    steps = pl.cdiv(ent_rows, cols)
    n = len(slices)
    table = pl.BlockSpec((width, cols), lambda i: (0, i))
    tall = max(n * cols * steps, total.shape[0])
    return pl.pallas_call(
        functools.partial(finish_kernel, slices, capacity, begin, last_begin),
        out_shape=[jax.ShapeDtypeStruct((width, ent_rows), F32)] * 3 + [token_shape()],
        grid=(steps,),
        in_specs=[whole(SMEM)] * 2 + [whole(VMEM)] * 3 + [table] * 3,
        out_specs=[table] * 3 + [pl.BlockSpec((8, LANES), lambda i: (0, 0))],
        scratch_shapes=[
            pltpu.VMEM((tall, LANES), F32),
            pltpu.VMEM((n * max(came.shape[2], last.shape[2]), LANES), F32),
            pltpu.VMEM((width, cols), F32),
        ],
        compiler_params=params(56),
        cost_estimate=cost(0, 60e6),
        name="finish_entities",
    )(counts, row_list.reshape(-1), came, last, total, weights, first, second)


def chunk_bounds(capacity):
    units = capacity // LANES
    sizes = [3, 7, 3, 3] if units == 16 else [units // 4] * 3 + [units - 3 * (units // 4)]
    bounds = [0]
    for size in sizes:
        bounds.append(bounds[-1] + size * LANES)
    return bounds


def shards(
    head_ids,
    relation_ids,
    tail_ids,
    negative_ids,
    live_counts,
    rel_weight,
    rel_count,
    entity_table,
    entity_first,
    entity_second,
    relation_table,
    relation_first,
    relation_second,
):
    groups = lax.axis_size("edge")
    n_col = lax.axis_size("col")
    width, ent_rows = entity_table.shape
    blocks, neg_count = negative_ids.shape
    block_len = head_ids.shape[0] // blocks
    edge_count = blocks * block_len
    slices = width_slices(width)
    n = len(slices)
    all_ids = jnp.concatenate([head_ids, tail_ids, negative_ids.reshape(-1)])
    id_count = all_ids.shape[0]
    capacity = (4 * id_count + 3 * groups - 1) // (3 * groups)
    rel_total = rel_weight.shape[0]

    rel_own = rel_total // groups
    rel_low = jnp.pad(relation_table.astype(BF16).T, ((0, 0), (0, REL_PAD - rel_own)))
    dense = []
    for k, (start, depth) in enumerate(slices):
        sent = entity_table[start : start + depth].astype(BF16)
        if k == 0:
            behind = [
                jnp.pad(rel_low[at : at + size], ((0, depth - size), (0, 0))) for at, size in slices
            ]
            sent = jnp.concatenate([sent] + behind, axis=1)
        dense.append(lax.all_gather(sent, "edge", axis=0, tiled=False))

    place_list, row_list, counts = owner_lists(all_ids, groups, capacity, ent_rows)
    safe_places = jnp.minimum(place_list, id_count - 1)
    place_flat, row_flat = place_list.reshape(-1), row_list.reshape(-1)

    rel_scale = rel_weight * (rel_total / jnp.sum(rel_weight)) / rel_count.astype(F32)
    rel_scale = jnp.pad(rel_scale.reshape(groups, rel_own), ((0, 0), (0, REL_PAD - rel_own)))
    rel_places = relation_ids + (relation_ids // rel_own) * (REL_PAD - rel_own)

    def from_others(array):
        turns = [[(c, (c + away) % n_col) for c in range(n_col)] for away in range(1, n_col)]
        return [lax.ppermute(array, "col", turn) for turn in turns]

    bounds = chunk_bounds(capacity)
    few = jnp.sum((counts > bounds[-2]).astype(jnp.int32)) <= 1
    flag = jnp.broadcast_to(few.astype(jnp.int32), (groups, LANES))
    me = lax.axis_index("col").astype(jnp.int32).reshape(1)
    given = [[[] for _ in range(n_col)] for _ in range(HALVES)]
    offs = [[] for _ in range(HALVES)]
    tails = [[] for _ in range(HALVES)]
    biases, norms, first_sent, rel_rows = [], [], [], None
    for k, (start, depth) in enumerate(slices):
        sent = first_sent if k > 0 else [flag]
        fetched = fetch(counts, place_flat, row_flat, dense[k], id_count, ent_rows, sent)
        if k < n - 1:
            early, late, norm = negatives(fetched, blocks, block_len)
            early_all = [early] + from_others(early)
            if rel_rows is None:
                rel_rows = relation_rows(rel_places, dense[0], rel_scale, slices, [norm])
            off, tail, low, bias = edges(fetched, rel_rows[k], late, depth, blocks, block_len)
            low_all = [low] + from_others(low)
            first_sent = [corner(piece) for piece in early_all[1:]]
            biases.append(bias)
            norms.append(norm)
            for half in range(HALVES):
                offs[half].append(off)
                tails[half].append(tail)
                for col in range(n_col):
                    given[half][col] += [early_all[col], low_all[col]]
            continue
        if rel_rows is None:
            rel_rows = relation_rows(rel_places, dense[0], rel_scale, slices, [])

    def finish(half, after):
        off, tail, pair, token = last_slice(
            fetched, rel_rows[-1], biases, norms, slices[-1][1], blocks, block_len, half, after
        )
        offs[half].append(off)
        tails[half].append(tail)
        for col, piece in enumerate([pair] + from_others(pair)):
            given[half][col].append(piece)
        return token

    grad, loss_tiles = None, []
    half_token = []
    for half in range(HALVES):
        half_token = [finish(half, half_token)]
    flag = flag + half_token[0][0, 0].astype(jnp.int32)
    asked = lax.all_to_all(
        jnp.concatenate([row_list, flag], axis=1), "edge", split_axis=0, concat_axis=0, tiled=True
    )
    all_few = jnp.min(asked[:, capacity]) > 0
    asked = asked[:, :capacity]
    asked_counts = jnp.sum((asked < ent_rows).astype(jnp.int32), axis=1)
    for half in range(HALVES):
        after = [corner(asked)] if half == 0 else []
        grad, loss_tile = block_math(
            me,
            live_counts,
            given[half],
            offs[half],
            tails[half],
            grad,
            slices,
            block_len,
            half,
            after,
        )
        loss_tiles.append(loss_tile)
    live = jnp.minimum(live_counts, block_len)
    loss_tile = functools.reduce(jnp.add, loss_tiles)

    flat = grad.reshape(n * id_count, LANES)
    chunks = len(bounds) - 1
    begin, size = bounds[-2], bounds[-1] - bounds[-2]
    most = jnp.argmax(counts)
    most_places = lax.dynamic_slice_in_dim(safe_places, most, 1, axis=0)
    most_count = lax.dynamic_slice_in_dim(counts, most, 1, axis=0)
    arrived, total, after = [], None, []
    for k in range(chunks - 1):
        sent, sent_token = outgoing(
            counts, safe_places, flat, slices, bounds[k], bounds[k + 1] - bounds[k], after
        )
        if k == chunks - 2:
            sent = pass_on(sent, [corner(relation_pairs)])
        arrived.append(lax.all_to_all(sent, "edge", split_axis=0, concat_axis=0, tiled=True))
        after = []
        if k == 0:
            excess, excess_token = excess_rows(
                most_count,
                most_places,
                live,
                flat,
                loss_tile,
                slices,
                begin,
                size,
                [sent_token],
            )
            after = [excess_token]
        if k == 1:
            before = [corner(arrived[0]), excess_token, sent_token]
            rel_terms, token = relation_sums(relation_ids, grad, n, rel_total, before)
            after = [token]
            relation_pairs = lax.psum_scatter(rel_terms, "edge", scatter_dimension=0, tiled=True)
        if k == 2:
            ready = (relation_pairs[0, 0] == relation_pairs[0, 0]) & (sent_token[0, 0] == 0.0)
            excess = jnp.where(ready, excess, jnp.zeros_like(excess))
            gathered = lax.all_gather(excess, "edge", axis=0, tiled=True)
            after = [corner(relation_pairs)]
        if k > 0:
            total, token = collect(
                asked_counts, asked, arrived[k - 1], total, slices, bounds[k - 1], ent_rows, after
            )
            after = [token]

    def by_all_to_all():
        spare = last_rows(width) + SPARE - width
        sent, _ = outgoing(counts, safe_places, flat, slices, begin, size, [], spare)
        rows = lax.all_to_all(sent, "edge", split_axis=0, concat_axis=0, tiled=True)
        return rows.at[:, last_rows(width) :].set(gathered[:, last_rows(width) :])

    k = chunks - 2
    here = jnp.where(arrived[k][0, 0, 0] > 0, 1, 2) > 0
    came = lax.cond(all_few & here & (token[0, 0] == 0.0), lambda: gathered, by_all_to_all)
    new_entity, new_entity_first, new_entity_second, sums = finish_entities(
        asked_counts,
        asked,
        arrived[k],
        came,
        total,
        bounds[k],
        begin,
        entity_table,
        entity_first,
        entity_second,
        slices,
    )
    loss_pair = sums[:2, 0]
    relation_grad = relation_pairs.reshape(rel_own, n * LANES)[:, :width]
    new_relation, new_relation_first, new_relation_second = adamw_update(
        relation_table, relation_grad, relation_first, relation_second
    )
    return (
        loss_pair,
        new_entity,
        new_entity_first,
        new_entity_second,
        new_relation,
        new_relation_first,
        new_relation_second,
    )


def solution(mesh):
    placed = (
        P("edge"),
        P("edge"),
        P("edge"),
        P("edge", None),
        P("edge"),
        P(),
        P(),
        P("col", "edge"),
        P("col", "edge"),
        P("col", "edge"),
        P("edge", "col"),
        P("edge", "col"),
        P("edge", "col"),
    )
    return jax.shard_map(
        shards,
        mesh=mesh,
        in_specs=placed,
        out_specs=(
            P(),
            P("col", "edge"),
            P("col", "edge"),
            P("col", "edge"),
            P("edge", "col"),
            P("edge", "col"),
            P("edge", "col"),
        ),
        check_vma=False,
    )
```

```python
import functools

import jax
import jax.numpy as jnp
from jax import lax
from jax.experimental import pallas as pl
from jax.experimental.pallas import tpu as pltpu
from jax.sharding import PartitionSpec as P

STEP = 5


MARGIN = 0.1
LEARN_RATE = 0.1
BETA_ONE = 0.5
BETA_TWO = 0.5
EPSILON = 1e-08
DECAY = 0.01
LANES = 128
UNROLL = 8
PARTS = 4
HALVES = 2
EARLY = 96
TURN = 512
REL_PAD = 256
TERMS = 3
SPARE = 8
NN = (((1,), (0,)), ((), ()))
NT = (((1,), (1,)), ((), ()))
TN = (((0,), (0,)), ((), ()))
F32 = jnp.float32
BF16 = jnp.bfloat16
SMEM = pltpu.SMEM
VMEM = pltpu.VMEM


def params(mebibytes=60):
    return pltpu.CompilerParams(vmem_limit_bytes=mebibytes << 20)


def cost(flops, moved):
    return pl.CostEstimate(flops=int(flops), bytes_accessed=int(moved), transcendentals=0)


def corner(array):
    return array[(0,) * (array.ndim - 2) + (slice(0, 8), slice(0, LANES))]


def token_shape():
    return jax.ShapeDtypeStruct((8, LANES), F32)


def whole(space):
    return pl.BlockSpec(memory_space=space)


def adamw_update(weights, gradient, first, second):
    new_first = BETA_ONE * first + (1.0 - BETA_ONE) * gradient
    new_second = BETA_TWO * second + (1.0 - BETA_TWO) * gradient * gradient
    first_hat = new_first / (1.0 - BETA_ONE**STEP)
    second_hat = new_second / (1.0 - BETA_TWO**STEP)
    updated = weights - LEARN_RATE * (
        first_hat / (jnp.sqrt(second_hat) + EPSILON) + DECAY * weights
    )
    return (updated, new_first, new_second)


def width_slices(width):
    return [(at, min(LANES, width - at)) for at in range(0, width, LANES)]


def owner_lists(all_ids, groups, capacity, ent_rows):
    count = all_ids.shape[0]
    owners = all_ids // ent_rows
    local_rows = all_ids - owners * ent_rows
    chunk = 256
    mine = owners[None, :] == jnp.arange(groups, dtype=jnp.int32)[:, None]
    mine = mine.astype(BF16).reshape(groups, count // chunk, chunk)
    before = jnp.triu(jnp.ones((chunk, chunk), BF16), 1)
    inner = jnp.dot(mine, before, preferred_element_type=F32)
    sums = jnp.sum(mine.astype(F32), axis=2)
    carry = jnp.cumsum(sums, axis=1) - sums
    ranks = jnp.sum(mine.astype(F32) * (inner + carry[:, :, None]), axis=0)
    ranks = ranks.astype(jnp.int32).reshape(count)
    counts = jnp.sum(sums, axis=1).astype(jnp.int32)
    high = owners * (capacity // LANES) + ranks // LANES
    low = ranks % LANES
    tall = groups * capacity // LANES
    left = (jnp.arange(tall, dtype=jnp.int32)[:, None] == high[None, :]).astype(BF16)
    right = (jnp.arange(LANES, dtype=jnp.int32)[:, None] == low[None, :]).astype(BF16)
    places = jnp.arange(1, count + 1, dtype=jnp.int32)
    parts = jnp.stack([places // 256, places % 256, local_rows // 256, local_rows % 256])
    right = (parts.astype(BF16)[:, None, :] * right[None]).reshape(PARTS * LANES, count)
    found = lax.dot_general(left, right, NT, preferred_element_type=F32).astype(jnp.int32)
    found = found.reshape(tall, PARTS, LANES)
    place = found[:, 0] * 256 + found[:, 1]
    place_list = jnp.where(place > 0, place - 1, count).reshape(groups, capacity)
    row_list = jnp.where(place > 0, found[:, 2] * 256 + found[:, 3], ent_rows)
    return place_list, row_list.reshape(groups, capacity), counts


def relation_rows_kernel(slices, ids_ref, scale_ref, *refs):
    n = len(slices)
    tables, outs = refs[:n], refs[-2 * n - 1 : -n - 1]
    columns, rows = refs[-n - 1], refs[-n:]
    groups = tables[0].shape[0]
    for (_, depth), table, into in zip(slices, tables, rows):
        columns[...] = jnp.zeros_like(columns)

        def turn(group, carry):
            columns[:depth, :] = table[group, :depth].astype(F32)
            if depth < LANES:
                columns[LANES - 1 :, :] = scale_ref[pl.ds(group, 1), :]
            into[pl.ds(pl.multiple_of(group * REL_PAD, REL_PAD), REL_PAD), :] = columns[...].T
            return carry

        lax.fori_loop(0, groups, turn, 0, unroll=4)

    def body(step, carry):
        for lane in range(UNROLL):
            at = step * UNROLL + lane
            row = ids_ref[at]
            for source, out in zip(rows, outs):
                out[pl.ds(at, 1), :] = source[pl.ds(row, 1), :]
        return carry

    lax.fori_loop(0, outs[0].shape[0] // UNROLL, body, 0)


def relation_rows(places, dense, scale, slices, after):
    count = places.shape[0]
    groups, depth, span = dense.shape
    n = len(slices)
    first = span // REL_PAD - n

    def columns(k):
        return pl.BlockSpec((groups, depth, REL_PAD), lambda i: (0, 0, first + k))

    return pl.pallas_call(
        functools.partial(relation_rows_kernel, slices),
        out_shape=[jax.ShapeDtypeStruct((count, LANES), F32)] * n,
        grid=(1,),
        in_specs=[whole(SMEM), whole(VMEM)]
        + [columns(k) for k in range(n)]
        + [whole(pl.ANY)] * len(after),
        out_specs=[whole(VMEM)] * n,
        scratch_shapes=[pltpu.VMEM((LANES, REL_PAD), F32)]
        + [pltpu.VMEM((groups * REL_PAD, LANES), F32)] * n,
        compiler_params=params(28),
        cost_estimate=cost(0, 80e6),
        name="relation_rows",
    )(places, scale, *[dense] * n, *after)


def fetch_kernel(
    capacity, moves, ent_rows, counts_ref, place_ref, row_ref, dense_ref, *refs
):
    shard = pl.program_id(0)
    last = pl.num_programs(0) - 1
    out_ref, rows = refs[-3], refs[-2:]
    depth = dense_ref.shape[1]
    turns = ent_rows // TURN
    rest = ent_rows - turns * TURN

    if depth < LANES:

        @pl.when(shard == 0)
        def _():
            for ref in rows:
                ref[...] = jnp.zeros_like(ref)

    def turn(into, begin, size):
        cols = pl.ds(begin, size)
        into[cols, :depth] = dense_ref[0, :, cols].astype(F32).T

    def move(source, at):
        out_ref[pl.ds(place_ref[at], 1), :] = source[pl.ds(row_ref[at], 1), :]

    def step(into, source):
        base = (shard - 1) * capacity

        def remaining(first):
            def body(trip, carry):
                for lane in range(UNROLL):
                    move(source, base + first + trip * UNROLL + lane)
                return carry

            wanted = counts_ref[jnp.maximum(shard - 1, 0)] - first
            lax.fori_loop(0, (wanted + UNROLL - 1) // UNROLL, body, 0)

        def only_turn(trip, carry):
            turn(into, pl.multiple_of(trip * TURN, TURN), TURN)
            return carry

        def both(trip, carry):
            turn(into, pl.multiple_of(trip * TURN, TURN), TURN)
            for lane in range(moves):
                move(source, base + trip * moves + lane)
            return carry

        @pl.when(shard == 0)
        def _():
            lax.fori_loop(0, turns, only_turn, 0)

        @pl.when((shard > 0) & (shard < last))
        def _():
            lax.fori_loop(0, turns, both, 0)
            remaining(turns * moves)

        @pl.when(shard == last)
        def _():
            remaining(0)

        if rest:

            @pl.when(shard < last)
            def _():
                turn(into, turns * TURN, rest)

    for parity in range(2):

        @pl.when(lax.rem(shard, 2) == parity)
        def _():
            step(rows[parity], rows[1 - parity])


def fetch(counts, place_list, row_list, dense, id_count, ent_rows, after):
    groups, depth, _ = dense.shape
    capacity = place_list.shape[0] // groups
    moves = (id_count // groups) // (ent_rows // TURN) // UNROLL * UNROLL
    return pl.pallas_call(
        functools.partial(fetch_kernel, capacity, moves, ent_rows),
        out_shape=jax.ShapeDtypeStruct((id_count + 8, LANES), F32),
        grid=(groups + 1,),
        in_specs=[whole(SMEM)] * 3
        + [
            pl.BlockSpec(
                (1, depth, ent_rows), lambda shard: (jnp.minimum(shard, groups - 1), 0, 0)
            )
        ]
        + [whole(pl.ANY)] * len(after),
        out_specs=whole(VMEM),
        scratch_shapes=[pltpu.VMEM((ent_rows + 8, LANES), F32)] * 2,
        compiler_params=params(26),
        cost_estimate=cost(0, 170e6),
        name="fetch_rows",
    )(counts, place_list, row_list, dense, *after)


def column_sum(values):
    return jnp.sum(values * values, axis=0, keepdims=True)


def negatives_kernel(neg_ref, early_ref, late_ref, norm_ref):
    neg_t = neg_ref[...].T
    early_ref[...] = neg_t[:EARLY].astype(BF16)
    late_ref[...] = neg_t[EARLY:].astype(BF16)
    norm_ref[...] = column_sum(neg_t)


def negatives(fetched, blocks, block_len):
    count = blocks * block_len
    return pl.pallas_call(
        negatives_kernel,
        out_shape=[
            jax.ShapeDtypeStruct((EARLY, count), BF16),
            jax.ShapeDtypeStruct((LANES - EARLY, count), BF16),
            jax.ShapeDtypeStruct((1, count), F32),
        ],
        grid=(blocks,),
        in_specs=[pl.BlockSpec((block_len, LANES), lambda b: (2 * blocks + b, 0))],
        out_specs=[
            pl.BlockSpec((EARLY, block_len), lambda b: (0, b)),
            pl.BlockSpec((LANES - EARLY, block_len), lambda b: (0, b)),
            pl.BlockSpec((1, block_len), lambda b: (0, b)),
        ],
        compiler_params=params(5),
        cost_estimate=cost(0, 10e6),
        name="negatives",
    )(fetched)


def edge_parts(depth, head_ref, tail_ref, rel_ref, off_ref, tail_out):
    lane = lax.broadcasted_iota(jnp.int32, head_ref.shape, 1)
    inside = lane < depth
    rel = rel_ref[...]
    tail = tail_ref[...]
    shifted = head_ref[...] + jnp.where(inside, rel, 0.0)
    off_ref[...] = jnp.where(inside, shifted - tail, rel)
    tail_out[...] = tail.astype(BF16)
    shifted_t = shifted.T
    return shifted_t, column_sum((shifted - tail).T) - column_sum(shifted_t)


def edges_kernel(
    depth, head_ref, tail_ref, rel_ref, late_ref, off_ref, tail_out, low_ref, bias_ref
):
    shifted_t, bias = edge_parts(depth, head_ref, tail_ref, rel_ref, off_ref, tail_out)
    low_ref[:depth] = shifted_t[:depth].astype(BF16)
    low_ref[depth:] = late_ref[...]
    bias_ref[...] = bias


def edges(fetched, rel_rows, late, depth, blocks, block_len):
    count = blocks * block_len
    tall = depth + late.shape[0]

    def rows(at):
        return pl.BlockSpec((block_len, LANES), lambda b: (at * blocks + b, 0))

    return pl.pallas_call(
        functools.partial(edges_kernel, depth),
        out_shape=[
            jax.ShapeDtypeStruct((count, LANES), F32),
            jax.ShapeDtypeStruct((count, LANES), BF16),
            jax.ShapeDtypeStruct((tall, count), BF16),
            jax.ShapeDtypeStruct((1, count), F32),
        ],
        grid=(blocks,),
        in_specs=[rows(0), rows(1), rows(0)]
        + [pl.BlockSpec((tall - depth, block_len), lambda b: (0, b))],
        out_specs=[
            rows(0),
            rows(0),
            pl.BlockSpec((tall, block_len), lambda b: (0, b)),
            pl.BlockSpec((1, block_len), lambda b: (0, b)),
        ],
        compiler_params=params(9),
        cost_estimate=cost(0, 30e6),
        name="edges",
    )(fetched, fetched, rel_rows, late)


def last_rows(depth):
    return (depth + 7) // 8 * 8


def with_terms(columns, total, depth):
    terms = term_rows(total, 0)
    return jnp.concatenate([columns[: last_rows(depth)], terms], axis=0).astype(BF16)


def term_rows(total, first):
    place = lax.broadcasted_iota(jnp.int32, (8, total.shape[1]), 0)
    left = total
    terms = jnp.zeros(place.shape, F32)
    for k in range(TERMS):
        term = left.astype(BF16).astype(F32)
        left = left - term
        terms = jnp.where(place == first + k, term, terms)
    return terms


def last_kernel(depth, n_given, head_ref, tail_ref, neg_ref, rel_ref, *refs):
    biases, norms = refs[:n_given], refs[n_given : 2 * n_given]
    off_ref, tail_out, pair_ref, token = refs[-4:]
    token[...] = jnp.zeros_like(token)
    shifted_t, bias = edge_parts(depth, head_ref, tail_ref, rel_ref, off_ref, tail_out)
    neg_t = neg_ref[...].T
    norm = column_sum(neg_t)
    for ref in biases:
        bias = bias + ref[...]
    for ref in norms:
        norm = norm + ref[...]
    pair_ref[0] = with_terms(shifted_t, bias, depth)
    pair_ref[1] = with_terms(neg_t, norm, depth)


def last_slice(fetched, rel_rows, biases, norms, depth, blocks, block_len, half, after):
    part = blocks // HALVES
    count = part * block_len
    tall = last_rows(depth) + 8

    def rows(at):
        return pl.BlockSpec((block_len, LANES), lambda b: (at * blocks + half * part + b, 0))

    return pl.pallas_call(
        functools.partial(last_kernel, depth, len(biases)),
        out_shape=[
            jax.ShapeDtypeStruct((count, LANES), F32),
            jax.ShapeDtypeStruct((count, LANES), BF16),
            jax.ShapeDtypeStruct((2, tall, count), BF16),
            token_shape(),
        ],
        grid=(part,),
        in_specs=[rows(0), rows(1), rows(2), rows(0)]
        + [pl.BlockSpec((1, block_len), lambda b: (0, half * part + b))]
        * (len(biases) + len(norms))
        + [whole(pl.ANY)] * len(after),
        out_specs=[
            pl.BlockSpec((block_len, LANES), lambda b: (b, 0)),
            pl.BlockSpec((block_len, LANES), lambda b: (b, 0)),
            pl.BlockSpec((2, tall, block_len), lambda b: (0, 0, b)),
            pl.BlockSpec((8, LANES), lambda b: (0, 0)),
        ],
        compiler_params=params(9),
        cost_estimate=cost(0, 20e6),
        name="last_slice",
    )(fetched, fetched, fetched, rel_rows, *biases, *norms, *after)


def block_kernel(slices, n_col, half, me_ref, live_ref, *refs):
    n = len(slices)
    per_col = 2 * n - 1
    given = [refs[k * per_col : (k + 1) * per_col] for k in range(n_col)]
    refs = refs[n_col * per_col :]
    offs, tails, refs = refs[:n], refs[n : 2 * n], refs[2 * n :]
    grad, refs = refs[-9], refs[-8:]
    loss_ref, shift_scr, neg_scr, sums_scr, cross, slopes, row_bias, row_sum = refs
    block = pl.program_id(0)
    length = cross.shape[0]
    me = me_ref[0]
    for k in range(n_col):
        slot = lax.rem(me + (n_col - k), n_col)
        for m, (start, depth) in enumerate(slices):
            if m < n - 1:
                early, late = given[k][2 * m : 2 * m + 2]
                shift_scr[slot, start : start + depth, :] = 2.0 * late[:depth, :]
                neg_scr[slot, start : start + EARLY, :] = early[...]
                neg_scr[slot, start + EARLY : start + depth, :] = late[depth:, :]
            else:
                pair = given[k][-1]
                shift, neg = pair[0, :depth, :], pair[1, :depth, :]
                for row in range(2):
                    terms = pair[row, last_rows(depth) : last_rows(depth) + 8, :].astype(F32)
                    sums_scr[slot, row : row + 1] = jnp.sum(terms, axis=0, keepdims=True)
                shift_scr[slot, start : start + depth, :] = 2.0 * shift
                neg_scr[slot, start : start + depth, :] = neg
    bias = jnp.sum(sums_scr[:, 0, :], axis=0, keepdims=True) + MARGIN
    neg_norm = jnp.sum(sums_scr[:, 1, :], axis=0, keepdims=True)
    row_bias[...] = jnp.broadcast_to(bias, (LANES, length)).T

    live = live_ref[half * pl.num_programs(0) + block]
    tile = 256
    small = 128
    lane_tiles = [slice(at, at + LANES) for at in range(0, length, LANES)]
    cols = jnp.zeros((8, length), F32)
    loss = jnp.zeros((8, LANES), F32)
    def products(at):
        part = slice(at, at + tile)
        doubled = None
        for k in range(n_col):
            term = lax.dot_general(
                shift_scr[k, :, part], neg_scr[k], TN, preferred_element_type=F32
            )
            doubled = term if doubled is None else doubled + term
        cross[part, :] = doubled

    def moves(at):
        part = slice(at, at + tile)
        moved = lax.dot_general(slopes[part, :], neg_scr[me], NT, preferred_element_type=F32)
        fade = -row_sum[part, :]
        for m, (start, depth) in enumerate(slices):
            into = pl.ds(n * at + m, tile, stride=n)
            grad[0, into, :depth] = (
                fade[:, :depth] * tails[m][part, :depth].astype(F32)
                + moved[:, start : start + depth]
            )
            grad[1, into, :] = fade * offs[m][part, :]

    products(0)
    for begin in range(0, length, tile):
        if begin + tile < length:
            products(begin + tile)
        for at in range(begin, begin + tile, small):
            part = slice(at, at + small)
            place = at + lax.broadcasted_iota(jnp.int32, (small, 1), 0)
            scale = offs[-1][part, LANES - 1 : LANES]
            weight = jnp.where(place < live, scale, 0.0) / length
            margins = cross[part, :] + (row_bias[part, 0:1] - neg_norm)
            fall = jnp.exp(-jnp.abs(margins))
            under = 1.0 + fall
            guess = pl.reciprocal(under, approx=True)
            inverse = guess * (2.0 - under * guess)
            twice = (2.0 * weight) * (jnp.where(margins >= 0.0, 1.0, fall) * inverse)
            row_sum[part, :] = jnp.broadcast_to(
                jnp.sum(twice, axis=1, keepdims=True), (small, LANES)
            )
            slopes[part, :] = twice.astype(BF16)
            cols = cols + jnp.sum(twice.reshape(small // 8, 8, length), axis=0)
            over = jnp.maximum(margins, 0.0)
            lifts = [fall[:, lanes] for lanes in lane_tiles]
            while len(lifts) > 1:
                lifts = [a + b + a * b for a, b in zip(lifts[::2], lifts[1::2])]
            lift = lifts[0]
            soft = functools.reduce(jnp.add, [over[:, lanes] for lanes in lane_tiles]) + jnp.where(
                lift < 2.0**-11, lift * (1.0 - 0.5 * lift), jnp.log(1.0 + lift)
            )
            loss = loss + jnp.sum((weight * soft).reshape(small // 8, 8, LANES), axis=0)
        moves(begin)
    col_sum = jnp.sum(cols, axis=0, keepdims=True)

    @pl.when(block == 0)
    def _():
        loss_ref[...] = loss

    @pl.when(block > 0)
    def _():
        loss_ref[...] += loss

    moved = lax.dot_general(shift_scr[me], slopes[...], NN, preferred_element_type=F32)
    moved = 0.5 * moved - col_sum * neg_scr[me].astype(F32)
    for m, (start, depth) in enumerate(slices):
        grad[2, pl.ds(m, length, stride=n), :depth] = moved[start : start + depth, :].T


def block_math(me, live_counts, given, offs, tails, old, slices, block_len, half, after):
    n, n_col = len(slices), len(given)
    blocks = live_counts.shape[0]
    part = blocks // HALVES
    width = sum(depth for _, depth in slices)
    flat = [piece for per_col in given for piece in per_col]
    kept = [] if old is None else [old]

    def columns(piece):
        if piece.ndim == 3:
            return pl.BlockSpec((2, piece.shape[1], block_len), lambda b: (0, 0, b))
        return pl.BlockSpec((piece.shape[0], block_len), lambda b: (0, half * part + b))

    def rows(array):
        first = half * part if array.shape[0] > part * block_len else 0
        return pl.BlockSpec((block_len, LANES), lambda b: (first + b, 0))

    first_old = 2 + len(flat) + 2 * n
    return pl.pallas_call(
        functools.partial(block_kernel, slices, n_col, half),
        out_shape=[
            jax.ShapeDtypeStruct((3, n * blocks * block_len, LANES), F32),
            jax.ShapeDtypeStruct((8, LANES), F32),
        ],
        grid=(part,),
        in_specs=[whole(SMEM)] * 2
        + [columns(piece) for piece in flat]
        + [rows(array) for array in offs + tails]
        + [whole(pl.ANY)] * len(kept + after),
        out_specs=[
            pl.BlockSpec((3, n * block_len, LANES), lambda b: (0, half * part + b, 0)),
            pl.BlockSpec((8, LANES), lambda b: (0, 0)),
        ],
        input_output_aliases={first_old + k: k for k in range(len(kept))},
        scratch_shapes=[
            pltpu.VMEM((n_col, width, block_len), BF16),
            pltpu.VMEM((n_col, width, block_len), BF16),
            pltpu.VMEM((n_col, 2, block_len), F32),
            pltpu.VMEM((block_len, block_len), F32),
            pltpu.VMEM((block_len, block_len), BF16),
            pltpu.VMEM((block_len, LANES), F32),
            pltpu.VMEM((block_len, LANES), F32),
        ],
        compiler_params=params(60),
        cost_estimate=cost(part * 8 * block_len * block_len * width, 120e6),
        name="block_math",
    )(me, live_counts, *flat, *offs, *tails, *kept, *after)


def pair_of(row, n):
    return pl.ds(pl.multiple_of(row * n, n), n)


def pass_on_kernel(array_ref, *refs):
    refs[-1][...] = jnp.zeros((8, LANES), F32)


def pass_on(array, after):
    return pl.pallas_call(
        pass_on_kernel,
        out_shape=[jax.ShapeDtypeStruct(array.shape, array.dtype), token_shape()],
        in_specs=[whole(pl.ANY)] * (1 + len(after)),
        out_specs=[whole(pl.ANY), whole(VMEM)],
        input_output_aliases={0: 0},
        compiler_params=params(2),
        cost_estimate=cost(0, 1e3),
        name="pass_on",
    )(array, *after)[0]


def outgoing_kernel(slices, capacity, begin, counts_ref, place_ref, grad, *refs):
    n = len(slices)
    out_ref, token, tile = refs[-3:]
    groups, _, chunk = out_ref.shape
    token[...] = jnp.zeros_like(token)

    def owner(group, carry):
        wanted = jnp.clip(counts_ref[group] - begin, 0, chunk)

        def body(step, inner):
            for lane in range(UNROLL):
                at = step * UNROLL + lane
                place = place_ref[group * capacity + begin + at]
                tile[pair_of(at, n), :] = grad[pair_of(place, n), :]
            return inner

        lax.fori_loop(0, (wanted + UNROLL - 1) // UNROLL, body, 0)
        for m, (start, depth) in enumerate(slices):
            piece = tile[pl.ds(m, chunk, stride=n), :].T
            out_ref[group, start : start + depth, :] = piece[:depth].astype(BF16)
        return carry

    lax.fori_loop(0, groups, owner, 0)


def excess_kernel(slices, capacity, begin, counts_ref, place_ref, live_ref, grad, loss_ref, *refs):
    outgoing_kernel(slices, capacity, begin, counts_ref, place_ref, grad, *refs)
    out_ref = refs[-3]
    loss = jnp.sum(jnp.sum(loss_ref[...], axis=0, keepdims=True), axis=1, keepdims=True)
    live = live_ref[0]
    for block in range(1, live_ref.shape[0]):
        live = live + live_ref[block]
    count = jnp.full((1, LANES), live.astype(F32))
    terms = term_rows(jnp.broadcast_to(loss, (1, LANES)), 0) + term_rows(count, TERMS)
    width = sum(depth for _, depth in slices)
    for at in range(0, out_ref.shape[2], LANES):
        out_ref[0, last_rows(width) :, at : at + LANES] = terms.astype(BF16)


def excess_rows(count, places, live, grad, loss, slices, begin, chunk, after):
    n = len(slices)
    width = sum(depth for _, depth in slices)
    return pl.pallas_call(
        functools.partial(excess_kernel, slices, places.shape[1], begin),
        out_shape=[
            jax.ShapeDtypeStruct((1, last_rows(width) + SPARE, chunk), BF16),
            token_shape(),
        ],
        in_specs=[whole(SMEM)] * 3 + [whole(VMEM)] * 2 + [whole(pl.ANY)] * len(after),
        out_specs=[whole(VMEM)] * 2,
        scratch_shapes=[pltpu.VMEM((n * chunk, LANES), F32)],
        compiler_params=params(34),
        cost_estimate=cost(0, 80e6),
        name="excess_rows",
    )(count, places.reshape(-1), live, grad, loss, *after)


def outgoing(counts, place_list, grad, slices, begin, chunk, after, spare=0):
    groups, capacity = place_list.shape
    n = len(slices)
    width = sum(depth for _, depth in slices) + spare
    return pl.pallas_call(
        functools.partial(outgoing_kernel, slices, capacity, begin),
        out_shape=[jax.ShapeDtypeStruct((groups, width, chunk), BF16), token_shape()],
        in_specs=[whole(SMEM)] * 2 + [whole(VMEM)] + [whole(pl.ANY)] * len(after),
        out_specs=[whole(VMEM)] * 2,
        scratch_shapes=[pltpu.VMEM((n * chunk, LANES), F32)],
        compiler_params=params(34),
        cost_estimate=cost(0, 80e6),
        name="outgoing",
    )(counts, place_list.reshape(-1), grad, *after)


def collect_kernel(slices, capacity, begin, first, counts_ref, row_ref, came_ref, *refs):
    total, token, tile = refs[-3:]
    total[...] = jnp.zeros_like(total) if first else refs[0][...]
    token[...] = jnp.zeros_like(token)
    add_rows(slices, capacity, begin, counts_ref, row_ref, came_ref, total, tile)


def add_rows(slices, capacity, begin, counts_ref, row_ref, came_ref, total, tile):
    n = len(slices)
    groups, _, chunk = came_ref.shape

    def source(group, carry):
        wanted = jnp.clip(counts_ref[group] - begin, 0, chunk)

        @pl.when(wanted > 0)
        def _():
            for m, (start, depth) in enumerate(slices):
                piece = came_ref[group, start : start + depth, :].astype(F32)
                tile[pl.ds(m, chunk, stride=n), :depth] = piece.T

            def body(step, inner):
                for lane in range(UNROLL):
                    at = step * UNROLL + lane
                    into = pair_of(row_ref[group * capacity + begin + at], n)
                    total[into, :] = total[into, :] + tile[pair_of(at, n), :]
                return inner

            lax.fori_loop(0, (wanted + UNROLL - 1) // UNROLL, body, 0)

        return carry

    lax.fori_loop(0, groups, source, 0)


def collect(counts, row_list, came, total, slices, begin, ent_rows, after):
    capacity = row_list.shape[1]
    chunk = came.shape[2]
    n = len(slices)
    given = [] if total is None else [total]
    return pl.pallas_call(
        functools.partial(collect_kernel, slices, capacity, begin, total is None),
        out_shape=[jax.ShapeDtypeStruct((n * (ent_rows + 8), LANES), F32), token_shape()],
        input_output_aliases={3: 0} if given else {},
        in_specs=[whole(SMEM)] * 2
        + [whole(VMEM)] * (1 + len(given))
        + [whole(pl.ANY)] * len(after),
        out_specs=[whole(VMEM)] * 2,
        scratch_shapes=[pltpu.VMEM((n * chunk, LANES), F32)],
        compiler_params=params(60),
        cost_estimate=cost(0, 120e6),
        name="collect",
    )(counts, row_list.reshape(-1), came, *given, *after)


def relation_sums_kernel(n, ids_ref, grad, *refs):
    total, token = refs[-2:]
    total[...] = jnp.zeros_like(total)
    token[...] = jnp.zeros_like(token)

    def body(step, carry):
        for lane in range(UNROLL):
            at = step * UNROLL + lane
            into = pair_of(ids_ref[at], n)
            total[into, :] = total[into, :] + grad[0, pair_of(at, n), :]
        return carry

    lax.fori_loop(0, grad.shape[1] // n // UNROLL, body, 0)


def relation_sums(relation_ids, grad, n, rel_total, after):
    count = relation_ids.shape[0]
    return pl.pallas_call(
        functools.partial(relation_sums_kernel, n),
        out_shape=[jax.ShapeDtypeStruct((n * rel_total, LANES), F32), token_shape()],
        grid=(1,),
        in_specs=[whole(SMEM), pl.BlockSpec((1, n * count, LANES), lambda i: (0, 0, 0))]
        + [whole(pl.ANY)] * len(after),
        out_specs=[whole(VMEM)] * 2,
        compiler_params=params(30),
        cost_estimate=cost(0, 120e6),
        name="relation_sums",
    )(relation_ids, grad, *after)


def finish_kernel(
    slices,
    capacity,
    begin,
    last_begin,
    counts_ref,
    row_ref,
    came_ref,
    last_ref,
    total_ref,
    weights_ref,
    first_ref,
    second_ref,
    *refs,
):
    n = len(slices)
    width = sum(depth for _, depth in slices)
    outs, loss_ref, (total, tile, gradient) = refs[:3], refs[3], refs[4:]
    cols = weights_ref.shape[1]
    step = pl.program_id(0)

    @pl.when(step == 0)
    def _():
        total[: total_ref.shape[0], :] = total_ref[...]
        add_rows(slices, capacity, begin, counts_ref, row_ref, came_ref, total, tile)
        add_rows(slices, capacity, last_begin, counts_ref, row_ref, last_ref, total, tile)
        terms = jnp.zeros((SPARE, LANES), F32)
        for group in range(last_ref.shape[0]):
            terms = terms + last_ref[group, last_rows(width) :, :LANES].astype(F32)
        place = lax.broadcasted_iota(jnp.int32, terms.shape, 0)
        for k in range(2):
            own = (place >= k * TERMS) & (place < (k + 1) * TERMS)
            loss_ref[k : k + 1, :] = jnp.sum(jnp.where(own, terms, 0.0), axis=0, keepdims=True)
        loss_ref[2:, :] = jnp.zeros((6, LANES), F32)

    for m, (start, depth) in enumerate(slices):
        part = total[pl.ds(step * (n * cols) + m, cols, stride=n), :]
        gradient[start : start + depth, :] = part.T[:depth]
    grad = gradient[...]
    new_first = BETA_ONE * first_ref[...] + (1.0 - BETA_ONE) * grad
    new_second = BETA_TWO * second_ref[...] + (1.0 - BETA_TWO) * grad * grad
    under = jnp.sqrt(new_second * (1.0 / (1.0 - BETA_TWO**STEP))) + EPSILON
    guess = pl.reciprocal(under, approx=True)
    inverse = guess * (2.0 - under * guess)
    pace = LEARN_RATE / (1.0 - BETA_ONE**STEP)
    outs[0][...] = (1.0 - LEARN_RATE * DECAY) * weights_ref[...] - (pace * new_first) * inverse
    outs[1][...] = new_first
    outs[2][...] = new_second


def finish_entities(
    counts, row_list, came, last, total, begin, last_begin, weights, first, second, slices
):
    width, ent_rows = weights.shape
    capacity = row_list.shape[1]
    cols = 2048
    steps = pl.cdiv(ent_rows, cols)
    n = len(slices)
    table = pl.BlockSpec((width, cols), lambda i: (0, i))
    tall = max(n * cols * steps, total.shape[0])
    return pl.pallas_call(
        functools.partial(finish_kernel, slices, capacity, begin, last_begin),
        out_shape=[jax.ShapeDtypeStruct((width, ent_rows), F32)] * 3 + [token_shape()],
        grid=(steps,),
        in_specs=[whole(SMEM)] * 2 + [whole(VMEM)] * 3 + [table] * 3,
        out_specs=[table] * 3 + [pl.BlockSpec((8, LANES), lambda i: (0, 0))],
        scratch_shapes=[
            pltpu.VMEM((tall, LANES), F32),
            pltpu.VMEM((n * max(came.shape[2], last.shape[2]), LANES), F32),
            pltpu.VMEM((width, cols), F32),
        ],
        compiler_params=params(56),
        cost_estimate=cost(0, 60e6),
        name="finish_entities",
    )(counts, row_list.reshape(-1), came, last, total, weights, first, second)


def chunk_bounds(capacity):
    units = capacity // LANES
    sizes = [3, 7, 3, 3] if units == 16 else [units // 4] * 3 + [units - 3 * (units // 4)]
    bounds = [0]
    for size in sizes:
        bounds.append(bounds[-1] + size * LANES)
    return bounds


def shards(
    head_ids,
    relation_ids,
    tail_ids,
    negative_ids,
    live_counts,
    rel_weight,
    rel_count,
    entity_table,
    entity_first,
    entity_second,
    relation_table,
    relation_first,
    relation_second,
):
    groups = lax.axis_size("edge")
    n_col = lax.axis_size("col")
    width, ent_rows = entity_table.shape
    blocks, neg_count = negative_ids.shape
    block_len = head_ids.shape[0] // blocks
    edge_count = blocks * block_len
    slices = width_slices(width)
    n = len(slices)
    all_ids = jnp.concatenate([head_ids, tail_ids, negative_ids.reshape(-1)])
    id_count = all_ids.shape[0]
    capacity = (4 * id_count + 3 * groups - 1) // (3 * groups)
    rel_total = rel_weight.shape[0]

    rel_own = rel_total // groups
    rel_low = jnp.pad(relation_table.astype(BF16).T, ((0, 0), (0, REL_PAD - rel_own)))
    dense = []
    for k, (start, depth) in enumerate(slices):
        sent = entity_table[start : start + depth].astype(BF16)
        if k == 0:
            behind = [
                jnp.pad(rel_low[at : at + size], ((0, depth - size), (0, 0))) for at, size in slices
            ]
            sent = jnp.concatenate([sent] + behind, axis=1)
        dense.append(lax.all_gather(sent, "edge", axis=0, tiled=False))

    place_list, row_list, counts = owner_lists(all_ids, groups, capacity, ent_rows)
    safe_places = jnp.minimum(place_list, id_count - 1)
    place_flat, row_flat = place_list.reshape(-1), row_list.reshape(-1)

    rel_scale = rel_weight * (rel_total / jnp.sum(rel_weight)) / rel_count.astype(F32)
    rel_scale = jnp.pad(rel_scale.reshape(groups, rel_own), ((0, 0), (0, REL_PAD - rel_own)))
    rel_places = relation_ids + (relation_ids // rel_own) * (REL_PAD - rel_own)

    def from_others(array):
        turns = [[(c, (c + away) % n_col) for c in range(n_col)] for away in range(1, n_col)]
        return [lax.ppermute(array, "col", turn) for turn in turns]

    bounds = chunk_bounds(capacity)
    few = jnp.sum((counts > bounds[-2]).astype(jnp.int32)) <= 1
    flag = jnp.broadcast_to(few.astype(jnp.int32), (groups, LANES))
    me = lax.axis_index("col").astype(jnp.int32).reshape(1)
    given = [[[] for _ in range(n_col)] for _ in range(HALVES)]
    offs = [[] for _ in range(HALVES)]
    tails = [[] for _ in range(HALVES)]
    biases, norms, first_sent, rel_rows = [], [], [], None
    for k, (start, depth) in enumerate(slices):
        sent = first_sent if k > 0 else [flag]
        fetched = fetch(counts, place_flat, row_flat, dense[k], id_count, ent_rows, sent)
        if k < n - 1:
            early, late, norm = negatives(fetched, blocks, block_len)
            early_all = [early] + from_others(early)
            if rel_rows is None:
                rel_rows = relation_rows(rel_places, dense[0], rel_scale, slices, [norm])
            off, tail, low, bias = edges(fetched, rel_rows[k], late, depth, blocks, block_len)
            low_all = [low] + from_others(low)
            first_sent = [corner(piece) for piece in early_all[1:]]
            biases.append(bias)
            norms.append(norm)
            for half in range(HALVES):
                offs[half].append(off)
                tails[half].append(tail)
                for col in range(n_col):
                    given[half][col] += [early_all[col], low_all[col]]
            continue
        if rel_rows is None:
            rel_rows = relation_rows(rel_places, dense[0], rel_scale, slices, [])

    def finish(half, after):
        off, tail, pair, token = last_slice(
            fetched, rel_rows[-1], biases, norms, slices[-1][1], blocks, block_len, half, after
        )
        offs[half].append(off)
        tails[half].append(tail)
        for col, piece in enumerate([pair] + from_others(pair)):
            given[half][col].append(piece)
        return token

    grad, loss_tiles = None, []
    half_token = []
    for half in range(HALVES):
        half_token = [finish(half, half_token)]
    flag = flag + half_token[0][0, 0].astype(jnp.int32)
    asked = lax.all_to_all(
        jnp.concatenate([row_list, flag], axis=1), "edge", split_axis=0, concat_axis=0, tiled=True
    )
    all_few = jnp.min(asked[:, capacity]) > 0
    asked = asked[:, :capacity]
    asked_counts = jnp.sum((asked < ent_rows).astype(jnp.int32), axis=1)
    for half in range(HALVES):
        after = [corner(asked)] if half == 0 else []
        grad, loss_tile = block_math(
            me,
            live_counts,
            given[half],
            offs[half],
            tails[half],
            grad,
            slices,
            block_len,
            half,
            after,
        )
        loss_tiles.append(loss_tile)
    live = jnp.minimum(live_counts, block_len)
    loss_tile = functools.reduce(jnp.add, loss_tiles)

    flat = grad.reshape(n * id_count, LANES)
    chunks = len(bounds) - 1
    begin, size = bounds[-2], bounds[-1] - bounds[-2]
    most = jnp.argmax(counts)
    most_places = lax.dynamic_slice_in_dim(safe_places, most, 1, axis=0)
    most_count = lax.dynamic_slice_in_dim(counts, most, 1, axis=0)
    arrived, total, after = [], None, []
    for k in range(chunks - 1):
        sent, sent_token = outgoing(
            counts, safe_places, flat, slices, bounds[k], bounds[k + 1] - bounds[k], after
        )
        if k == chunks - 2:
            sent = pass_on(sent, [corner(relation_grad)])
        arrived.append(lax.all_to_all(sent, "edge", split_axis=0, concat_axis=0, tiled=True))
        after = []
        if k == 0:
            excess, excess_token = excess_rows(
                most_count,
                most_places,
                live,
                flat,
                loss_tile,
                slices,
                begin,
                size,
                [sent_token],
            )
            after = [excess_token]
        if k == 1:
            before = [corner(arrived[0]), excess_token, sent_token]
            rel_terms, token = relation_sums(relation_ids, grad, n, rel_total, before)
            after = [token]
            rel_terms = rel_terms.reshape(rel_total, n * LANES)[:, :width]
            relation_grad = lax.psum_scatter(rel_terms, "edge", scatter_dimension=0, tiled=True)
        if k == 2:
            ready = (relation_grad[0, 0] == relation_grad[0, 0]) & (sent_token[0, 0] == 0.0)
            excess = jnp.where(ready, excess, jnp.zeros_like(excess))
            gathered = lax.all_gather(excess, "edge", axis=0, tiled=True)
            after = [corner(relation_grad)]
        if k > 0:
            total, token = collect(
                asked_counts, asked, arrived[k - 1], total, slices, bounds[k - 1], ent_rows, after
            )
            after = [token]

    def by_all_to_all():
        spare = last_rows(width) + SPARE - width
        sent, _ = outgoing(counts, safe_places, flat, slices, begin, size, [], spare)
        rows = lax.all_to_all(sent, "edge", split_axis=0, concat_axis=0, tiled=True)
        return rows.at[:, last_rows(width) :].set(gathered[:, last_rows(width) :])

    k = chunks - 2
    here = jnp.where(arrived[k][0, 0, 0] > 0, 1, 2) > 0
    came = lax.cond(all_few & here & (token[0, 0] == 0.0), lambda: gathered, by_all_to_all)
    new_entity, new_entity_first, new_entity_second, sums = finish_entities(
        asked_counts,
        asked,
        arrived[k],
        came,
        total,
        bounds[k],
        begin,
        entity_table,
        entity_first,
        entity_second,
        slices,
    )
    loss_pair = sums[:2, 0]
    new_relation, new_relation_first, new_relation_second = adamw_update(
        relation_table, relation_grad, relation_first, relation_second
    )
    return (
        loss_pair,
        new_entity,
        new_entity_first,
        new_entity_second,
        new_relation,
        new_relation_first,
        new_relation_second,
    )


def solution(mesh):
    placed = (
        P("edge"),
        P("edge"),
        P("edge"),
        P("edge", None),
        P("edge"),
        P(),
        P(),
        P("col", "edge"),
        P("col", "edge"),
        P("col", "edge"),
        P("edge", "col"),
        P("edge", "col"),
        P("edge", "col"),
    )
    return jax.shard_map(
        shards,
        mesh=mesh,
        in_specs=placed,
        out_specs=(
            P(),
            P("col", "edge"),
            P("col", "edge"),
            P("col", "edge"),
            P("edge", "col"),
            P("edge", "col"),
            P("edge", "col"),
        ),
        check_vma=False,
    )
```
